32 devices in a mesh: frame: 16 (over z, y, x), pix: 2 (over core).
Axes of the slice: x: 2, y: 2, z: 4, core: 2. Of those that a mesh axis runs over, the one named last changes fastest.
Arguments:
- frames: bfloat16 [1024, 32768], P('frame', 'pix'), as said below
- cycle_map: int32 [32768], P('pix'), may hold values from -1 to 15, as said below
Outputs:
- correlation: bfloat16 [16, 1024, 1024], P('frame', 'pix')
The draws below stay inside these ranges and needn't reach their ends.
Inputs may be any that keep to these rules, and one draw needn't show every extreme that they name: `frames`: every entry is positive. `cycle_map`: pixels come in aligned blocks of 128; every pixel of a block is either -1 or one common cycle, and the first pixel of a block that holds a cycle belongs to it. Within each sector (aligned blocks of 16384 pixels, one a pix group) every cycle holds at least one and at most 8 blocks, and every cycle holds exactly 1024 pixels in some sector.
All inputs are finite; a program needn't handle non-finite values.
Results may differ from the reference program's by a relative error of at most 0.012.
Values may be sent and summed in bfloat16 or wider, within the bound.
No kernel may reach another device: no remote copies, remote signals or barrier semaphores. Data moves between devices by JAX's collectives and lax.ppermute only.
A program may use at most 64 MiB of HBM per device.

```python
import math
import jax
import jax.numpy as jnp
from jax import lax

F = 1024
BLOCK = 128
CAP = 1024
HALF_WIN = 2
CYCLES = 16
P_SEC = 16384
NPIX = 32768
N_PIX = 2


def draw_frames(key, part):
    key_scale, key_speckle, key_omega, key_phase, key_drift = jax.random.split(key, 5)
    frame_pos = jnp.arange(F, dtype=jnp.float32)[:, None]
    scale = jnp.exp(jax.random.uniform(key_scale, (1, NPIX), jnp.float32) * math.log(10.0))
    uniform_part = jax.random.uniform(key_speckle, (F, NPIX), jnp.float32)
    speckle = 0.05 - jnp.log(1.0 - 0.99 * uniform_part)
    omega = jnp.exp(jax.random.uniform(key_omega, (1, NPIX), jnp.float32, math.log(0.005), math.log(0.3)))
    phase = jax.random.uniform(key_phase, (1, NPIX), jnp.float32, -math.pi, math.pi)
    drift = jax.random.uniform(key_drift, (F, 1), jnp.float32, 0.7, 1.3)
    values = scale * drift * speckle * (1.0 + 0.5 * jnp.sin(omega * frame_pos + phase))
    return values.astype(jnp.bfloat16)


def draw_cycle_map(key, part):
    key_flip, key_jitter, key_keep, key_perm = jax.random.split(key, 4)
    block_count = P_SEC // BLOCK
    cap_blocks = CAP // BLOCK
    sector = jnp.arange(N_PIX, dtype=jnp.int32)[:, None]
    flip = jax.random.randint(key_flip, (1, CYCLES), 0, 2, dtype=jnp.int32)
    position = jnp.where(flip == 1, N_PIX - 1 - sector, sector)
    last = position == N_PIX - 1
    base = cap_blocks // 3 + (cap_blocks - cap_blocks // 3) * position // (N_PIX - 1)
    jitter = jax.random.randint(key_jitter, (N_PIX, CYCLES), 0, cap_blocks // 8 + 1, dtype=jnp.int32)
    blocks_used = jnp.where(last, cap_blocks, jnp.maximum(base - jitter, 1))
    threshold = jnp.where(last, 8, 3 + 5 * position // (N_PIX - 1))
    block_slot = jnp.arange(block_count, dtype=jnp.int32)
    cycle_of = block_slot // cap_blocks
    rank_of = block_slot % cap_blocks
    live_block = rank_of[None, :] < blocks_used[:, cycle_of]
    draws = jax.random.randint(key_keep, (N_PIX, block_count, BLOCK), 0, 8, dtype=jnp.int32)
    first_pixel = (jnp.arange(BLOCK, dtype=jnp.int32) == 0)[None, None, :]
    keep = (draws < threshold[:, cycle_of][:, :, None]) | first_pixel
    labels = jnp.where(live_block[:, :, None] & keep, cycle_of[None, :, None], -1)
    sector_keys = jax.random.split(key_perm, N_PIX)

    def shuffle(sector_key, sector_labels):
        return sector_labels[jax.random.permutation(sector_key, block_count)]
    mixed = jax.vmap(shuffle)(sector_keys, labels)
    return mixed.reshape(-1).astype(jnp.int32)


def setup_inputs(seed: int = 0) -> dict:
    arg_keys = jax.random.split(jax.random.key(seed), 3)
    frames = draw_frames(jax.random.fold_in(arg_keys[2], 71), 0)
    cycle_map = draw_cycle_map(jax.random.fold_in(arg_keys[2], 71), 0)
    return {"frames": frames, "cycle_map": cycle_map}


def window_sum(padded, length):
    summed = padded[0:length]
    for offset in range(1, 2 * HALF_WIN + 1):
        summed = summed + padded[offset:offset + length]
    return summed


def smooth_count(first_frame, length, total):
    frame_pos = first_frame + jnp.arange(length, dtype=jnp.int32)
    upper = jnp.minimum(frame_pos + HALF_WIN, total - 1)
    lower = jnp.maximum(frame_pos - HALF_WIN, 0)
    return (upper - lower + 1).astype(jnp.float32)


def reference(frames, cycle_map):
    ranking = jnp.argsort(cycle_map, stable=True).astype(jnp.int32)
    sorted_ids = cycle_map[ranking]
    cycle_ids = jnp.arange(CYCLES, dtype=jnp.int32)
    starts = jnp.searchsorted(sorted_ids, cycle_ids, side="left").astype(jnp.int32)
    finish = jnp.searchsorted(sorted_ids, cycle_ids, side="right").astype(jnp.int32)
    slot_count = N_PIX * CAP
    divisor = smooth_count(0, F, F)

    def one_cycle(cycle_index):
        first_slot = starts[cycle_index]
        members = finish[cycle_index] - first_slot
        within = jnp.arange(slot_count, dtype=jnp.int32)
        occupied = (within < members)[None, :]
        pixel_idx = ranking[jnp.minimum(first_slot + within, NPIX - 1)]
        raw_block = frames[:, pixel_idx].astype(jnp.float32)
        padded = jnp.pad(raw_block, ((HALF_WIN, HALF_WIN), (0, 0)))
        summed = window_sum(padded, F)
        local_mean = jnp.where(occupied, summed, jnp.float32(1.0)) / divisor[:, None]
        normed = jnp.where(occupied, raw_block / local_mean, jnp.float32(0.0)).astype(jnp.bfloat16)
        values = normed.astype(jnp.float32)
        gram_sum = jnp.dot(values, values.T, precision=lax.Precision.HIGHEST, preferred_element_type=jnp.float32)
        frame_sum = jnp.sum(values, axis=1)
        number = members.astype(jnp.float32)
        result = number * gram_sum / (frame_sum[:, None] * frame_sum[None, :]) - 1.0
        return result.astype(jnp.bfloat16)

    return lax.map(one_cycle, jnp.arange(CYCLES, dtype=jnp.int32))
```

```python
import functools

import jax
import jax.numpy as jnp
from jax import lax
from jax.experimental import pallas as pl
from jax.experimental.pallas import tpu as pltpu
from jax.sharding import PartitionSpec as P

BLOCK = 128
HALF_WIN = 2
PAD = 8
VMEM_BYTES = 48 * 1024 * 1024


def params(**kw):
    return pltpu.CompilerParams(vmem_limit_bytes=VMEM_BYTES, **kw)


def pack_kernel(cycles, half, move, steps, cm_s, frames_ref, cm_ref, first_ref, rest_ref, cnt_ref):
    step = pl.program_id(0)
    blocks = frames_ref.shape[1] // BLOCK

    @pl.when(step == 0)
    def _():
        @pl.loop(0, cycles)
        def _(q):
            cnt_ref[q] = 0

    def one(i, carry):
        q = cm_s[(step * blocks + i) * BLOCK]

        @pl.when(q >= 0)
        def _():
            rank = cnt_ref[q]
            cnt_ref[q] = rank + 1
            valid = cm_ref[pl.ds(i, 1), :] >= 0
            raw = frames_ref[:, pl.ds(pl.multiple_of(i * BLOCK, BLOCK), BLOCK)]
            kept = jnp.where(valid, raw.astype(jnp.float32), 0.0).astype(jnp.bfloat16)

            @pl.when(rank < half)
            def _():
                first_ref[q, rank] = kept

            @pl.when(rank >= half)
            def _():
                rest_ref[q, rank - half] = kept

        return carry

    lax.fori_loop(0, blocks, one, 0, unroll=4)

    @pl.when(step == steps - 1)
    def _():
        zero = jnp.zeros(first_ref.shape[2:], first_ref.dtype)

        @pl.loop(0, cycles)
        def _(q):
            count = cnt_ref[q]

            @pl.loop(count, half)
            def _(slot):
                first_ref[q, slot] = zero

            @pl.loop(jnp.maximum(count, half), half + move)
            def _(slot):
                rest_ref[q, slot - half] = zero


def pack(frames, cycle_map, cycles, half, move):
    rows, p_sec = frames.shape
    steps = 4
    width = p_sec // steps
    return pl.pallas_call(
        functools.partial(pack_kernel, cycles, half, move, steps),
        grid_spec=pltpu.PrefetchScalarGridSpec(
            num_scalar_prefetch=1,
            grid=(steps,),
            in_specs=[
                pl.BlockSpec((rows, width), lambda s, cm: (0, s)),
                pl.BlockSpec((width // BLOCK, BLOCK), lambda s, cm: (s, 0)),
            ],
            out_specs=[
                pl.BlockSpec((cycles, half, rows, BLOCK), lambda s, cm: (0, 0, 0, 0)),
                pl.BlockSpec((cycles, move, rows, BLOCK), lambda s, cm: (0, 0, 0, 0)),
                pl.BlockSpec(memory_space=pltpu.SMEM),
            ],
        ),
        out_shape=[
            jax.ShapeDtypeStruct((cycles, half, rows, BLOCK), frames.dtype),
            jax.ShapeDtypeStruct((cycles, move, rows, BLOCK), frames.dtype),
            jax.ShapeDtypeStruct((cycles,), jnp.int32),
        ],
        compiler_params=params(),
        name="pack_blocks",
    )(cycle_map, frames, cycle_map.reshape(p_sec // BLOCK, BLOCK))


def fill_kernel(cycles, half, move, cnt_s, first_ref, theirs_ref, out_ref, sems):
    def copies(act):
        @pl.loop(0, cycles)
        def _(q):
            count = cnt_s[q]
            for i in range(move):

                @pl.when(count + i < half)
                def _():
                    act(
                        pltpu.make_async_copy(
                            theirs_ref.at[q, i], out_ref.at[q, count + i], sems.at[q, i]
                        )
                    )

    copies(lambda copy: copy.start())
    copies(lambda copy: copy.wait())


def fill(counts, first, theirs):
    cycles, half = first.shape[:2]
    move = theirs.shape[1]
    return pl.pallas_call(
        functools.partial(fill_kernel, cycles, half, move),
        grid_spec=pltpu.PrefetchScalarGridSpec(
            num_scalar_prefetch=1,
            grid=(),
            in_specs=[pl.BlockSpec(memory_space=pl.ANY)] * 2,
            out_specs=pl.BlockSpec(memory_space=pl.ANY),
            scratch_shapes=[pltpu.SemaphoreType.DMA((cycles, move))],
        ),
        out_shape=jax.ShapeDtypeStruct(first.shape, first.dtype),
        input_output_aliases={1: 0},
        compiler_params=params(),
        name="fill_slots",
    )(counts, first, theirs)


def norm_kernel(total, raw_ref, out_ref, padded):
    chunk = 128
    zero = jnp.zeros((PAD, BLOCK), jnp.float32)
    padded[0:PAD] = zero
    padded[PAD + total : 2 * PAD + total] = zero
    padded[PAD : PAD + total] = raw_ref[:, 0].reshape(total, BLOCK).astype(jnp.float32)
    for start in range(0, total, chunk):
        base = PAD + start
        raw = padded[base : base + chunk]
        summed = raw
        for offset in range(1, HALF_WIN + 1):
            summed = summed + padded[base - offset : base - offset + chunk]
            summed = summed + padded[base + offset : base + offset + chunk]
        if start == 0 or start + chunk == total:
            frame = start + lax.broadcasted_iota(jnp.int32, (chunk, BLOCK), 0)
            upper = jnp.minimum(frame + HALF_WIN, total - 1)
            lower = jnp.maximum(frame - HALF_WIN, 0)
            mean = summed / (upper - lower + 1).astype(jnp.float32)
        else:
            mean = summed * (1.0 / (2 * HALF_WIN + 1))
        normed = jnp.where(summed > 0.0, raw / mean, 0.0)
        out_ref[start : start + chunk] = normed.astype(jnp.bfloat16)


def normalise(received):
    sources, slots, rows, _ = received.shape
    total = sources * rows
    return pl.pallas_call(
        functools.partial(norm_kernel, total),
        grid=(slots,),
        in_specs=[pl.BlockSpec((sources, 1, rows, BLOCK), lambda s: (0, s, 0, 0))],
        out_specs=pl.BlockSpec((total, BLOCK), lambda s: (0, s)),
        out_shape=jax.ShapeDtypeStruct((total, slots * BLOCK), jnp.bfloat16),
        scratch_shapes=[pltpu.VMEM((total + 2 * PAD, BLOCK), jnp.float32)],
        compiler_params=params(),
        cost_estimate=pl.CostEstimate(
            flops=12 * total * slots * BLOCK,
            bytes_accessed=4 * total * slots * BLOCK,
            transcendentals=0,
        ),
        name="normalise",
    )(received)


def dot_nt(a, b):
    return lax.dot_general(a, b, (((1,), (1,)), ((), ())), preferred_element_type=jnp.float32)


def correlate_kernel(rows, number_s, mine_ref, theirs_ref, out_ref):
    first_row = pl.multiple_of(lax.axis_index("pix") * rows, rows)
    column = pl.ds(pl.multiple_of(pl.program_id(0) * out_ref.shape[2], BLOCK), out_ref.shape[2])
    gram = 0.0
    row_sum = 0.0
    col_sum = 0.0
    for ref in (mine_ref, theirs_ref):
        left = ref[pl.ds(first_row, rows), :]
        right = ref[column, :]
        width = ref.shape[1]
        gram += dot_nt(left, right)
        row_sum += dot_nt(left, jnp.ones((BLOCK, width), jnp.bfloat16))
        col_sum += dot_nt(jnp.ones((8, width), jnp.bfloat16), right)
    row_inv = 1.0 / row_sum[:, 0:1]
    col_inv = 1.0 / col_sum[0:1, :]
    result = ((gram * row_inv) * col_inv) * number_s[0] - 1.0
    out_ref[0] = result.astype(jnp.bfloat16)


def correlate(number, mine, theirs, parts):
    total, width = mine.shape
    rows = total // parts
    tile = 256
    return pl.pallas_call(
        functools.partial(correlate_kernel, rows),
        grid_spec=pltpu.PrefetchScalarGridSpec(
            num_scalar_prefetch=1,
            grid=(total // tile,),
            in_specs=[pl.BlockSpec((total, width), lambda s, n: (0, 0))] * 2,
            out_specs=pl.BlockSpec((1, rows, tile), lambda s, n: (0, 0, s)),
        ),
        out_shape=jax.ShapeDtypeStruct((1, rows, total), jnp.bfloat16),
        compiler_params=params(),
        cost_estimate=pl.CostEstimate(
            flops=4 * rows * total * width,
            bytes_accessed=4 * total * width + 2 * rows * total,
            transcendentals=0,
        ),
        name="correlate",
    )(number, mine, theirs)


def body(frames, cycle_map):
    rows, p_sec = frames.shape
    cycles = lax.axis_size("frame")
    parts = lax.axis_size("pix")
    cap_blocks = p_sec // cycles // BLOCK
    half = (cap_blocks + 2) // 2
    move = cap_blocks - half
    swap = [(0, 1), (1, 0)]

    first, rest, counts = pack(frames, cycle_map, cycles, half, move)
    theirs = lax.ppermute(rest, "pix", swap)
    first = fill(counts, first, theirs)
    received = lax.all_to_all(first, "frame", split_axis=0, concat_axis=0, tiled=True)

    own = lax.axis_index("frame")
    pixels = jnp.sum((cycle_map == own).astype(jnp.int32)).reshape(1)
    tally = jnp.concatenate([counts, pixels])
    their_tally = lax.ppermute(tally, "pix", swap)
    number = (tally + their_tally)[cycles:].astype(jnp.float32)
    their_counts = their_tally[:cycles]
    overflow = jnp.max(counts + their_counts) > 2 * half

    def finish(received):
        normed = normalise(received)
        return correlate(number, normed, lax.ppermute(normed, "pix", swap), parts)

    def spill(received, rest):
        moved = jnp.arange(move, dtype=jnp.int32)[None, :] < (half - their_counts)[:, None]
        left = jnp.where(moved[:, :, None, None], jnp.zeros((), rest.dtype), rest)
        more = lax.all_to_all(left, "frame", split_axis=0, concat_axis=0, tiled=True)
        return finish(jnp.concatenate([received, more], axis=1))

    return lax.cond(overflow, spill, lambda received, rest: finish(received), received, rest)


def solution(mesh):
    return jax.shard_map(
        body,
        mesh=mesh,
        in_specs=(P("frame", "pix"), P("pix")),
        out_specs=P("frame", "pix", None),
        check_vma=False,
    )
```

```python
import functools

import jax
import jax.numpy as jnp
from jax import lax
from jax.experimental import pallas as pl
from jax.experimental.pallas import tpu as pltpu
from jax.sharding import PartitionSpec as P

BLOCK = 128
HALF_WIN = 2
PAD = 8
TILE = 256
VMEM_BYTES = 32 * 1024 * 1024
LIST, COUNT, PIXELS = 0, 1, 2
SWAP = [(0, 1), (1, 0)]
WHOLE = pl.BlockSpec(memory_space=pltpu.VMEM)
ANYWHERE = pl.BlockSpec(memory_space=pl.ANY)


def call(kernel, name, out_shape, flops=0, bytes_accessed=0, limit=VMEM_BYTES, **kw):
    return pl.pallas_call(
        kernel,
        out_shape=out_shape,
        compiler_params=pltpu.CompilerParams(vmem_limit_bytes=limit),
        cost_estimate=pl.CostEstimate(
            flops=flops, bytes_accessed=bytes_accessed, transcendentals=0
        ),
        name=name,
        **kw,
    )


def keep(cm_ref, block, wanted):
    valid = (cm_ref[pl.ds(block, 1), :] >= 0) & wanted
    return valid.astype(jnp.float32).astype(jnp.bfloat16)


def take(frames_ref, block):
    return frames_ref[:, pl.ds(pl.multiple_of(block * BLOCK, BLOCK), BLOCK)]


def find_blocks(cm, cap_blocks, meta_ref):
    blocks = cm.shape[0]
    width = meta_ref.shape[1]
    first = cm[:, 0:1]
    member = first == lax.broadcasted_iota(jnp.int32, (blocks, BLOCK), 1)
    member_f = member.astype(jnp.float32)
    row = lax.broadcasted_iota(jnp.int32, (blocks, blocks), 0)
    col = lax.broadcasted_iota(jnp.int32, (blocks, blocks), 1)
    earlier = (col < row).astype(jnp.float32).astype(jnp.bfloat16)
    before = jnp.dot(earlier, member_f.astype(jnp.bfloat16), preferred_element_type=jnp.float32)
    rank = jnp.sum(before * member_f, axis=1, keepdims=True).astype(jnp.int32)
    slot = jnp.where(first >= 0, first * cap_blocks + rank, -1)
    hit = slot == lax.broadcasted_iota(jnp.int32, (blocks, width), 1)
    index = lax.broadcasted_iota(jnp.int32, (blocks, width), 0).astype(jnp.float32)
    pixels = jnp.sum((cm >= 0).astype(jnp.float32), axis=1, keepdims=True)
    meta_ref[...] = jnp.zeros_like(meta_ref)
    meta_ref[LIST : LIST + 1, :] = jnp.sum(
        jnp.where(hit, index, 0.0), axis=0, keepdims=True
    ).astype(jnp.int32)
    meta_ref[COUNT : COUNT + 1, 0:BLOCK] = jnp.sum(member_f, axis=0, keepdims=True).astype(
        jnp.int32
    )
    meta_ref[PIXELS : PIXELS + 1, 0:BLOCK] = jnp.sum(
        member_f * pixels, axis=0, keepdims=True
    ).astype(jnp.int32)


def lead_kernel(n, cap_blocks, lead, cm_hbm, frames_hbm, *refs):
    pieces, (meta_ref, frames_ref, cm_ref, meta_s, sems) = refs[:n], refs[n:]
    get_frames = pltpu.make_async_copy(frames_hbm, frames_ref, sems.at[0])
    get_frames.start()
    get_cm = pltpu.make_async_copy(cm_hbm, cm_ref, sems.at[1])
    get_cm.start()
    get_cm.wait()
    find_blocks(cm_ref[...], cap_blocks, meta_ref)
    to_scalars = pltpu.make_async_copy(meta_ref, meta_s, sems.at[2])
    to_scalars.start()
    to_scalars.wait()
    get_frames.wait()
    me = lax.axis_index("frame")
    for k in range(n):
        q = me ^ k
        count = meta_s[COUNT, q]
        for j in range(lead):
            block = meta_s[LIST, q * cap_blocks + j]
            pieces[k][j] = take(frames_ref, block) * keep(cm_ref, block, j < count)


def pack_lead(frames, cm, n, cap_blocks, lead):
    rows = frames.shape[0]
    blocks = cm.shape[0]
    piece = jax.ShapeDtypeStruct((lead, rows, BLOCK), frames.dtype)
    meta = jax.ShapeDtypeStruct((8, blocks), jnp.int32)
    out = call(
        functools.partial(lead_kernel, n, cap_blocks, lead),
        "pack_lead",
        [piece] * n + [meta],
        in_specs=[ANYWHERE] * 2,
        out_specs=[WHOLE] * (n + 1),
        scratch_shapes=[
            pltpu.VMEM(frames.shape, frames.dtype),
            pltpu.VMEM(cm.shape, cm.dtype),
            pltpu.SMEM(meta.shape, meta.dtype),
            pltpu.SemaphoreType.DMA((3,)),
        ],
    )(pltpu.with_memory_space_constraint(cm, pltpu.HBM),
      pltpu.with_memory_space_constraint(frames, pltpu.HBM))
    return out[:n], out[n]


def move_kernel(n, cap_blocks, half, move, meta_s, frames_ref, cm_ref, *refs):
    out_ref = refs[-1]

    @pl.loop(0, n)
    def _(q):
        count = meta_s[COUNT, q]
        for i in range(move):
            block = meta_s[LIST, q * cap_blocks + half + i]
            out_ref[q, i] = take(frames_ref, block) * keep(cm_ref, block, half + i < count)


def pack_move(meta, frames, cm, after, n, cap_blocks, half, move):
    out = jax.ShapeDtypeStruct((n, move, frames.shape[0], BLOCK), frames.dtype)
    return call(
        functools.partial(move_kernel, n, cap_blocks, half, move),
        "pack_move",
        out,
        in_specs=[pl.BlockSpec(memory_space=pltpu.SMEM), WHOLE, WHOLE] + [ANYWHERE] * len(after),
        out_specs=WHOLE,
        bytes_accessed=4 * 1024 * 1024,
    )(meta, frames, cm, *after)


def tail_kernel(n, cap_blocks, lead, half, move, meta_s, frames_ref, cm_ref, theirs_ref, *refs):
    pieces = refs[-n:]
    me = lax.axis_index("frame")
    for k in range(n):
        q = me ^ k
        count = meta_s[COUNT, q]
        for j in range(lead, half):
            block = meta_s[LIST, q * cap_blocks + j]
            own = take(frames_ref, block) * keep(cm_ref, block, j < count)
            free = jnp.broadcast_to(count <= j, (1, BLOCK))
            free = free.astype(jnp.float32).astype(jnp.bfloat16)
            i = jnp.clip(j - jnp.maximum(count, lead), 0, move - 1)
            pieces[k][j - lead] = own + theirs_ref[q, i] * free


def pack_tail(meta, frames, cm, theirs, after, n, cap_blocks, lead, half, move):
    piece = jax.ShapeDtypeStruct((half - lead, frames.shape[0], BLOCK), frames.dtype)
    return call(
        functools.partial(tail_kernel, n, cap_blocks, lead, half, move),
        "pack_tail",
        [piece] * n,
        in_specs=[pl.BlockSpec(memory_space=pltpu.SMEM)] + [WHOLE] * 3 + [ANYWHERE] * len(after),
        out_specs=[WHOLE] * n,
        bytes_accessed=4 * 1024 * 1024,
    )(meta, frames, cm, theirs, *after)


def norm_kernel(n, partners, *refs):
    pieces, (out_ref, padded) = refs[:n], refs[-2:]
    slots, rows, _ = pieces[0].shape
    total = n * rows
    chunk = 128
    me = lax.axis_index("frame")
    zero = jnp.zeros((PAD, BLOCK), jnp.float32)
    for slot in range(slots):
        padded[slot, 0:PAD] = zero
        padded[slot, PAD + total : 2 * PAD + total] = zero
        for i in range(n):
            source = me ^ partners[i] if partners else i
            place = pl.ds(pl.multiple_of(PAD + source * rows, PAD), rows)
            padded[slot, place] = pieces[i][slot].astype(jnp.float32)
    for slot in range(slots):
        for start in range(0, total, chunk):
            base = PAD + start
            raw = padded[slot, base : base + chunk]
            summed = raw
            for offset in range(1, HALF_WIN + 1):
                summed = summed + padded[slot, base - offset : base - offset + chunk]
                summed = summed + padded[slot, base + offset : base + offset + chunk]
            if start == 0 or start + chunk == total:
                frame = start + lax.broadcasted_iota(jnp.int32, (chunk, BLOCK), 0)
                upper = jnp.minimum(frame + HALF_WIN, total - 1)
                lower = jnp.maximum(frame - HALF_WIN, 0)
                mean = summed / (upper - lower + 1).astype(jnp.float32)
            else:
                mean = summed * (1.0 / (2 * HALF_WIN + 1))
            normed = jnp.where(summed > 0.0, raw / mean, 0.0)
            out_ref[start : start + chunk, slot * BLOCK : (slot + 1) * BLOCK] = normed.astype(
                jnp.bfloat16
            )


def normalise(pieces, partners, after=()):
    n = len(pieces)
    slots, rows, _ = pieces[0].shape
    total = n * rows
    return call(
        functools.partial(norm_kernel, n, partners),
        "normalise",
        jax.ShapeDtypeStruct((total, slots * BLOCK), jnp.bfloat16),
        flops=12 * total * slots * BLOCK,
        bytes_accessed=4 * total * slots * BLOCK,
        in_specs=[WHOLE] * n + [ANYWHERE] * len(after),
        out_specs=WHOLE,
        scratch_shapes=[pltpu.VMEM((slots, total + 2 * PAD, BLOCK), jnp.float32)],
    )(*pieces, *after)


def dot_nt(a, b):
    return lax.dot_general(a, b, (((1,), (1,)), ((), ())), preferred_element_type=jnp.float32)


def add_sums(rows, normed, before, column, row_sum):
    first_row = pl.multiple_of(lax.axis_index("pix") * rows, rows)
    gram, row, col = before
    for ref in normed:
        width = ref.shape[1]
        left = ref[pl.ds(first_row, rows), :]
        right = ref[column, :]
        gram = gram + dot_nt(left, right)
        col = col + dot_nt(jnp.ones((8, width), jnp.bfloat16), right)
        if row_sum:
            row = row + dot_nt(left, jnp.ones((BLOCK, width), jnp.bfloat16))
    return gram, row, col


def partial_kernel(count, *refs):
    normed, (gram_out, row_out, col_out) = refs[:count], refs[-3:]
    before = refs[count:-3]
    rows, total = gram_out.shape
    for start in range(0, total, TILE):
        column = slice(start, start + TILE)
        if before:
            sums = before[0][:, column], before[1][...], before[2][:, column]
        else:
            sums = 0.0, 0.0, 0.0
        gram, row, col = add_sums(rows, normed, sums, column, start == 0)
        gram_out[:, column] = gram
        col_out[:, column] = col
        if start == 0:
            row_out[...] = row


def partial_sums(normed, before, parts):
    total, width = normed[0].shape
    rows = total // parts
    return call(
        functools.partial(partial_kernel, len(normed)),
        "partial_sums",
        [
            jax.ShapeDtypeStruct((rows, total), jnp.float32),
            jax.ShapeDtypeStruct((rows, BLOCK), jnp.float32),
            jax.ShapeDtypeStruct((8, total), jnp.float32),
        ],
        flops=2 * rows * total * width * len(normed),
        bytes_accessed=4 * rows * total,
        in_specs=[WHOLE] * (len(normed) + len(before)),
        out_specs=[WHOLE] * 3,
    )(*normed, *before)


def result_kernel(mine_s, theirs_s, normed, gram_in, row_in, col_in, out_hbm, out_ref, sems):
    rows, total = gram_in.shape
    me = lax.axis_index("frame")
    number = (mine_s[PIXELS, me] + theirs_s[PIXELS, me]).astype(jnp.float32)
    row_inv = None
    copies = []
    for i, start in enumerate(range(0, total, TILE)):
        column = slice(start, start + TILE)
        before = gram_in[:, column], row_in[...], col_in[:, column]
        gram, row, col = add_sums(rows, [normed], before, column, i == 0)
        if i == 0:
            row_inv = 1.0 / row[:, 0:1]
        result = ((gram * row_inv) * (1.0 / col[0:1, :])) * number - 1.0
        out_ref[i] = result.astype(jnp.bfloat16)
        copy = pltpu.make_async_copy(out_ref.at[i], out_hbm.at[0, :, column], sems.at[i])
        copy.start()
        copies.append(copy)
    for copy in copies:
        copy.wait()


def correlate(meta, their_meta, normed, before):
    rows, total = before[0].shape
    tiles = total // TILE
    smem = pl.BlockSpec(memory_space=pltpu.SMEM)
    return call(
        result_kernel,
        "correlate",
        pltpu.HBM((1, rows, total), jnp.bfloat16),
        flops=2 * rows * total * normed.shape[1],
        bytes_accessed=6 * rows * total,
        in_specs=[smem, smem] + [WHOLE] * 4,
        out_specs=ANYWHERE,
        scratch_shapes=[
            pltpu.VMEM((tiles, rows, TILE), jnp.bfloat16),
            pltpu.SemaphoreType.DMA((tiles,)),
        ],
    )(meta, their_meta, normed, *before)


def body(frames, cycle_map):
    p_sec = frames.shape[1]
    n = lax.axis_size("frame")
    parts = lax.axis_size("pix")
    cap_blocks = p_sec // n // BLOCK
    half = (cap_blocks + 2) // 2
    move = cap_blocks - half
    lead = half - move
    cm = cycle_map.reshape(p_sec // BLOCK, BLOCK)

    far, near = list(range(n - 1, n // 2 - 1, -1)), list(range(n // 2 - 1, 0, -1))
    order = [far.pop(0) if i % 2 == 0 else near.pop(0) for i in range(n - 1)]
    order.append(0)

    def send(pieces):
        return [
            lax.ppermute(pieces[k], "frame", [(i, i ^ k) for i in range(n)]) if k else pieces[k]
            for k in order
        ]

    lead_pieces, meta = pack_lead(frames, cm, n, cap_blocks, lead)
    lead_got = send(lead_pieces)
    moving = pack_move(meta, frames, cm, lead_got[: n // 4], n, cap_blocks, half, move)
    theirs = lax.ppermute(moving, "pix", SWAP)
    their_meta = lax.ppermute(meta, "pix", SWAP)
    tail = pack_tail(meta, frames, cm, theirs, lead_got[:-1], n, cap_blocks, lead, half, move)
    tail_got = send(tail)

    normed = normalise(lead_got, order)
    sums = partial_sums([normed, lax.ppermute(normed, "pix", SWAP)], [], parts)
    overflow = jnp.max(meta[COUNT, :n] + their_meta[COUNT, :n]) > 2 * half
    early = [sums[2], overflow.astype(jnp.int32).reshape(1)]
    normed = normalise(tail_got, order, early)
    their_normed = lax.ppermute(normed, "pix", SWAP)
    sums = partial_sums([normed], sums, parts)

    def spill(meta, their_meta, their_normed, moving, *sums):
        moved = half - jnp.maximum(their_meta[COUNT, :n], lead)
        stays = jnp.arange(move, dtype=jnp.int32)[None, :] >= moved[:, None]
        rest = jnp.where(stays[:, :, None, None], moving, jnp.zeros((), moving.dtype))
        rest = lax.all_to_all(rest, "frame", split_axis=0, concat_axis=0, tiled=True)
        normed = normalise([rest[i] for i in range(n)], None)
        sums = partial_sums([normed, lax.ppermute(normed, "pix", SWAP)], sums, parts)
        return correlate(meta, their_meta, their_normed, sums)

    def fits(meta, their_meta, their_normed, moving, *sums):
        return correlate(meta, their_meta, their_normed, sums)

    return lax.cond(overflow, spill, fits, meta, their_meta, their_normed, moving, *sums)


def solution(mesh):
    return jax.shard_map(
        body,
        mesh=mesh,
        in_specs=(P("frame", "pix"), P("pix")),
        out_specs=P("frame", "pix", None),
        check_vma=False,
    )
```

```python
import functools

import jax
import jax.numpy as jnp
from jax import lax
from jax.experimental import pallas as pl
from jax.experimental.pallas import tpu as pltpu
from jax.sharding import PartitionSpec as P

BLOCK = 128
HALF_WIN = 2
PAD = 8
TILE = 256
VMEM_BYTES = 32 * 1024 * 1024
LIST, COUNT, PIXELS = 0, 1, 2
SWAP = [(0, 1), (1, 0)]
WHOLE = pl.BlockSpec(memory_space=pltpu.VMEM)
ANYWHERE = pl.BlockSpec(memory_space=pl.ANY)


def call(kernel, name, out_shape, flops=0, bytes_accessed=0, limit=VMEM_BYTES, **kw):
    return pl.pallas_call(
        kernel,
        out_shape=out_shape,
        compiler_params=pltpu.CompilerParams(vmem_limit_bytes=limit),
        cost_estimate=pl.CostEstimate(
            flops=flops, bytes_accessed=bytes_accessed, transcendentals=0
        ),
        name=name,
        **kw,
    )


def keep(cm_ref, block, wanted):
    valid = (cm_ref[pl.ds(block, 1), :] >= 0) & wanted
    return valid.astype(jnp.float32).astype(jnp.bfloat16)


def take(frames_ref, block):
    return frames_ref[:, pl.ds(pl.multiple_of(block * BLOCK, BLOCK), BLOCK)]


def find_blocks(cm, cap_blocks, meta_ref):
    blocks = cm.shape[0]
    width = meta_ref.shape[1]
    first = cm[:, 0:1]
    member = first == lax.broadcasted_iota(jnp.int32, (blocks, BLOCK), 1)
    member_f = member.astype(jnp.float32)
    row = lax.broadcasted_iota(jnp.int32, (blocks, blocks), 0)
    col = lax.broadcasted_iota(jnp.int32, (blocks, blocks), 1)
    earlier = (col < row).astype(jnp.float32).astype(jnp.bfloat16)
    before = jnp.dot(earlier, member_f.astype(jnp.bfloat16), preferred_element_type=jnp.float32)
    rank = jnp.sum(before * member_f, axis=1, keepdims=True).astype(jnp.int32)
    slot = jnp.where(first >= 0, first * cap_blocks + rank, -1)
    hit = slot == lax.broadcasted_iota(jnp.int32, (blocks, width), 1)
    index = lax.broadcasted_iota(jnp.int32, (blocks, width), 0).astype(jnp.float32)
    pixels = jnp.sum((cm >= 0).astype(jnp.float32), axis=1, keepdims=True)
    meta_ref[...] = jnp.zeros_like(meta_ref)
    meta_ref[LIST : LIST + 1, :] = jnp.sum(
        jnp.where(hit, index, 0.0), axis=0, keepdims=True
    ).astype(jnp.int32)
    meta_ref[COUNT : COUNT + 1, 0:BLOCK] = jnp.sum(member_f, axis=0, keepdims=True).astype(
        jnp.int32
    )
    meta_ref[PIXELS : PIXELS + 1, 0:BLOCK] = jnp.sum(
        member_f * pixels, axis=0, keepdims=True
    ).astype(jnp.int32)


def pack_kernel(n, cap_blocks, half, cm_hbm, frames_hbm, lead_ref, move_ref, meta_ref, *scratch):
    frames_ref, cm_ref, meta_s, sems = scratch
    get_frames = pltpu.make_async_copy(frames_hbm, frames_ref, sems.at[0])
    get_frames.start()
    get_cm = pltpu.make_async_copy(cm_hbm, cm_ref, sems.at[1])
    get_cm.start()
    get_cm.wait()
    find_blocks(cm_ref[...], cap_blocks, meta_ref)
    to_scalars = pltpu.make_async_copy(meta_ref, meta_s, sems.at[2])
    to_scalars.start()
    to_scalars.wait()
    get_frames.wait()
    for out_ref, first in ((move_ref, half), (lead_ref, 0)):
        for q in range(n):
            count = meta_s[COUNT, q]
            for i in range(out_ref.shape[1]):
                block = meta_s[LIST, q * cap_blocks + first + i]
                out_ref[q, i] = take(frames_ref, block) * keep(cm_ref, block, first + i < count)


def pack(frames, cm, n, cap_blocks, half, move):
    rows = frames.shape[0]
    meta = jax.ShapeDtypeStruct((8, cm.shape[0]), jnp.int32)
    return call(
        functools.partial(pack_kernel, n, cap_blocks, half),
        "pack",
        [
            jax.ShapeDtypeStruct((n, half - move, rows, BLOCK), frames.dtype),
            jax.ShapeDtypeStruct((n, move, rows, BLOCK), frames.dtype),
            meta,
        ],
        in_specs=[ANYWHERE] * 2,
        out_specs=[WHOLE] * 3,
        scratch_shapes=[
            pltpu.VMEM(frames.shape, frames.dtype),
            pltpu.VMEM(cm.shape, cm.dtype),
            pltpu.SMEM(meta.shape, meta.dtype),
            pltpu.SemaphoreType.DMA((3,)),
        ],
    )(
        pltpu.with_memory_space_constraint(cm, pltpu.HBM),
        pltpu.with_memory_space_constraint(frames, pltpu.HBM),
    )


def tail_kernel(n, cap_blocks, lead, half, move, meta_s, frames_ref, cm_ref, theirs_ref, out_ref):
    for q in range(n):
        count = meta_s[COUNT, q]
        for j in range(lead, half):
            block = meta_s[LIST, q * cap_blocks + j]
            own = take(frames_ref, block) * keep(cm_ref, block, j < count)
            free = jnp.broadcast_to(count <= j, (1, BLOCK))
            free = free.astype(jnp.float32).astype(jnp.bfloat16)
            i = jnp.clip(j - jnp.maximum(count, lead), 0, move - 1)
            out_ref[q, j - lead] = own + theirs_ref[q, i] * free


def pack_tail(meta, frames, cm, theirs, n, cap_blocks, lead, half, move):
    return call(
        functools.partial(tail_kernel, n, cap_blocks, lead, half, move),
        "pack_tail",
        jax.ShapeDtypeStruct((n, half - lead, frames.shape[0], BLOCK), frames.dtype),
        in_specs=[pl.BlockSpec(memory_space=pltpu.SMEM)] + [WHOLE] * 3,
        out_specs=WHOLE,
        bytes_accessed=4 * 1024 * 1024,
    )(meta, frames, cm, theirs)


def norm_kernel(raw_ref, *refs):
    out_ref, padded = refs[-2:]
    n, slots, rows, _ = raw_ref.shape
    total = n * rows
    chunk = 128
    zero = jnp.zeros((PAD, BLOCK), jnp.float32)
    for slot in range(slots):
        padded[slot, 0:PAD] = zero
        padded[slot, PAD + total : 2 * PAD + total] = zero
        for i in range(n):
            start = PAD + i * rows
            padded[slot, start : start + rows] = raw_ref[i, slot].astype(jnp.float32)
    for slot in range(slots):
        for start in range(0, total, chunk):
            base = PAD + start
            raw = padded[slot, base : base + chunk]
            summed = raw
            for offset in range(1, HALF_WIN + 1):
                summed = summed + padded[slot, base - offset : base - offset + chunk]
                summed = summed + padded[slot, base + offset : base + offset + chunk]
            if start == 0 or start + chunk == total:
                frame = start + lax.broadcasted_iota(jnp.int32, (chunk, BLOCK), 0)
                upper = jnp.minimum(frame + HALF_WIN, total - 1)
                lower = jnp.maximum(frame - HALF_WIN, 0)
                mean = summed / (upper - lower + 1).astype(jnp.float32)
            else:
                mean = summed * (1.0 / (2 * HALF_WIN + 1))
            normed = jnp.where(summed > 0.0, raw / mean, 0.0)
            out_ref[start : start + chunk, slot * BLOCK : (slot + 1) * BLOCK] = normed.astype(
                jnp.bfloat16
            )


def normalise(raw, after=()):
    n, slots, rows, _ = raw.shape
    total = n * rows
    return call(
        norm_kernel,
        "normalise",
        jax.ShapeDtypeStruct((total, slots * BLOCK), jnp.bfloat16),
        flops=12 * total * slots * BLOCK,
        bytes_accessed=4 * total * slots * BLOCK,
        in_specs=[WHOLE] + [ANYWHERE] * len(after),
        out_specs=WHOLE,
        scratch_shapes=[pltpu.VMEM((slots, total + 2 * PAD, BLOCK), jnp.float32)],
    )(raw, *after)


def dot_nt(a, b):
    return lax.dot_general(a, b, (((1,), (1,)), ((), ())), preferred_element_type=jnp.float32)


def add_sums(rows, normed, before, column, row_sum):
    first_row = pl.multiple_of(lax.axis_index("pix") * rows, rows)
    gram, row, col = before
    for ref in normed:
        width = ref.shape[1]
        left = ref[pl.ds(first_row, rows), :]
        right = ref[column, :]
        gram = gram + dot_nt(left, right)
        col = col + dot_nt(jnp.ones((8, width), jnp.bfloat16), right)
        if row_sum:
            row = row + dot_nt(left, jnp.ones((BLOCK, width), jnp.bfloat16))
    return gram, row, col


def partial_kernel(count, *refs):
    normed, (gram_out, row_out, col_out) = refs[:count], refs[-3:]
    before = refs[count:-3]
    rows, total = gram_out.shape
    for start in range(0, total, TILE):
        column = slice(start, start + TILE)
        if before:
            sums = before[0][:, column], before[1][...], before[2][:, column]
        else:
            sums = 0.0, 0.0, 0.0
        gram, row, col = add_sums(rows, normed, sums, column, start == 0)
        gram_out[:, column] = gram
        col_out[:, column] = col
        if start == 0:
            row_out[...] = row


def partial_sums(normed, before, parts):
    total, width = normed[0].shape
    rows = total // parts
    return call(
        functools.partial(partial_kernel, len(normed)),
        "partial_sums",
        [
            jax.ShapeDtypeStruct((rows, total), jnp.float32),
            jax.ShapeDtypeStruct((rows, BLOCK), jnp.float32),
            jax.ShapeDtypeStruct((8, total), jnp.float32),
        ],
        flops=2 * rows * total * width * len(normed),
        bytes_accessed=4 * rows * total,
        in_specs=[WHOLE] * (len(normed) + len(before)),
        out_specs=[WHOLE] * 3,
    )(*normed, *before)


def result_kernel(mine_s, theirs_s, normed, gram_in, row_in, col_in, out_hbm, out_ref, sems):
    rows, total = gram_in.shape
    me = lax.axis_index("frame")
    number = (mine_s[PIXELS, me] + theirs_s[PIXELS, me]).astype(jnp.float32)
    row_inv = None
    copies = []
    for i, start in enumerate(range(0, total, TILE)):
        column = slice(start, start + TILE)
        before = gram_in[:, column], row_in[...], col_in[:, column]
        gram, row, col = add_sums(rows, [normed], before, column, i == 0)
        if i == 0:
            row_inv = 1.0 / row[:, 0:1]
        result = ((gram * row_inv) * (1.0 / col[0:1, :])) * number - 1.0
        out_ref[i] = result.astype(jnp.bfloat16)
        copy = pltpu.make_async_copy(out_ref.at[i], out_hbm.at[0, :, column], sems.at[i])
        copy.start()
        copies.append(copy)
    for copy in copies:
        copy.wait()


def correlate(meta, their_meta, normed, before):
    rows, total = before[0].shape
    tiles = total // TILE
    smem = pl.BlockSpec(memory_space=pltpu.SMEM)
    return call(
        result_kernel,
        "correlate",
        pltpu.HBM((1, rows, total), jnp.bfloat16),
        flops=2 * rows * total * normed.shape[1],
        bytes_accessed=6 * rows * total,
        in_specs=[smem, smem] + [WHOLE] * 4,
        out_specs=ANYWHERE,
        scratch_shapes=[
            pltpu.VMEM((tiles, rows, TILE), jnp.bfloat16),
            pltpu.SemaphoreType.DMA((tiles,)),
        ],
    )(meta, their_meta, normed, *before)


def body(frames, cycle_map):
    p_sec = frames.shape[1]
    n = lax.axis_size("frame")
    parts = lax.axis_size("pix")
    cap_blocks = p_sec // n // BLOCK
    half = (cap_blocks + 2) // 2
    move = cap_blocks - half
    lead = half - move
    cm = cycle_map.reshape(p_sec // BLOCK, BLOCK)

    def send(blocks):
        return lax.all_to_all(blocks, "frame", split_axis=0, concat_axis=0, tiled=True)

    lead_blocks, moving, meta = pack(frames, cm, n, cap_blocks, half, move)
    theirs = lax.ppermute(moving, "pix", SWAP)
    their_meta = lax.ppermute(meta, "pix", SWAP)
    lead_got = send(lead_blocks)
    tail_blocks = pack_tail(meta, frames, cm, theirs, n, cap_blocks, lead, half, move)
    tail_got = send(tail_blocks)

    normed = normalise(lead_got, [tail_blocks])
    sums = partial_sums([normed, lax.ppermute(normed, "pix", SWAP)], [], parts)
    overflow = jnp.max(meta[COUNT, :n] + their_meta[COUNT, :n]) > 2 * half
    early = [sums[2], overflow.astype(jnp.int32).reshape(1)]
    normed = normalise(tail_got, early)
    their_normed = lax.ppermute(normed, "pix", SWAP)
    sums = partial_sums([normed], sums, parts)

    def spill(meta, their_meta, their_normed, moving, *sums):
        moved = half - jnp.maximum(their_meta[COUNT, :n], lead)
        stays = jnp.arange(move, dtype=jnp.int32)[None, :] >= moved[:, None]
        rest = jnp.where(stays[:, :, None, None], moving, jnp.zeros((), moving.dtype))
        normed = normalise(send(rest))
        sums = partial_sums([normed, lax.ppermute(normed, "pix", SWAP)], sums, parts)
        return correlate(meta, their_meta, their_normed, sums)

    def fits(meta, their_meta, their_normed, moving, *sums):
        return correlate(meta, their_meta, their_normed, sums)

    return lax.cond(overflow, spill, fits, meta, their_meta, their_normed, moving, *sums)


def solution(mesh):
    return jax.shard_map(
        body,
        mesh=mesh,
        in_specs=(P("frame", "pix"), P("pix")),
        out_specs=P("frame", "pix", None),
        check_vma=False,
    )
```

```python
import functools

import jax
import jax.numpy as jnp
from jax import lax
from jax.experimental import pallas as pl
from jax.experimental.pallas import tpu as pltpu
from jax.sharding import PartitionSpec as P

BLOCK = 128
HALF_WIN = 2
PAD = 8
TILE = 256
VMEM_BYTES = 32 * 1024 * 1024
LIST, COUNT, PIXELS = 0, 1, 2
SWAP = [(0, 1), (1, 0)]
WHOLE = pl.BlockSpec(memory_space=pltpu.VMEM)
ANYWHERE = pl.BlockSpec(memory_space=pl.ANY)


def call(kernel, name, out_shape, flops=0, bytes_accessed=0, limit=VMEM_BYTES, **kw):
    return pl.pallas_call(
        kernel,
        out_shape=out_shape,
        compiler_params=pltpu.CompilerParams(vmem_limit_bytes=limit),
        cost_estimate=pl.CostEstimate(
            flops=flops, bytes_accessed=bytes_accessed, transcendentals=0
        ),
        name=name,
        **kw,
    )


def keep(cm_ref, block, wanted):
    valid = (cm_ref[pl.ds(block, 1), :] >= 0) & wanted
    return valid.astype(jnp.float32).astype(jnp.bfloat16)


def take(frames_ref, block):
    return frames_ref[:, pl.ds(pl.multiple_of(block * BLOCK, BLOCK), BLOCK)]


def find_blocks(cm, cap_blocks, meta_ref):
    blocks = cm.shape[0]
    width = meta_ref.shape[1]
    first = cm[:, 0:1]
    member = first == lax.broadcasted_iota(jnp.int32, (blocks, BLOCK), 1)
    member_f = member.astype(jnp.float32)
    row = lax.broadcasted_iota(jnp.int32, (blocks, blocks), 0)
    col = lax.broadcasted_iota(jnp.int32, (blocks, blocks), 1)
    earlier = (col < row).astype(jnp.float32).astype(jnp.bfloat16)
    before = jnp.dot(earlier, member_f.astype(jnp.bfloat16), preferred_element_type=jnp.float32)
    rank = jnp.sum(before * member_f, axis=1, keepdims=True).astype(jnp.int32)
    slot = jnp.where(first >= 0, first * cap_blocks + rank, -1)
    hit = slot == lax.broadcasted_iota(jnp.int32, (blocks, width), 1)
    index = lax.broadcasted_iota(jnp.int32, (blocks, width), 0).astype(jnp.float32)
    pixels = jnp.sum((cm >= 0).astype(jnp.float32), axis=1, keepdims=True)
    meta_ref[...] = jnp.zeros_like(meta_ref)
    meta_ref[LIST : LIST + 1, :] = jnp.sum(
        jnp.where(hit, index, 0.0), axis=0, keepdims=True
    ).astype(jnp.int32)
    meta_ref[COUNT : COUNT + 1, 0:BLOCK] = jnp.sum(member_f, axis=0, keepdims=True).astype(
        jnp.int32
    )
    meta_ref[PIXELS : PIXELS + 1, 0:BLOCK] = jnp.sum(
        member_f * pixels, axis=0, keepdims=True
    ).astype(jnp.int32)


def own_kernel(cap_blocks, move, cm_ref, their_cm_ref, frames_hbm, *refs):
    out_hbm, tail_ref, meta_ref, their_meta_ref, frames_ref, lead_ref, meta_s, sems = refs
    n, lead = lead_ref.shape[:2]
    get_frames = pltpu.make_async_copy(frames_hbm, frames_ref, sems.at[0])
    get_frames.start()
    find_blocks(cm_ref[...], cap_blocks, meta_ref)
    to_scalars = pltpu.make_async_copy(meta_ref, meta_s, sems.at[1])
    to_scalars.start()
    find_blocks(their_cm_ref[...], cap_blocks, their_meta_ref)
    to_scalars.wait()
    get_frames.wait()

    def put(out_ref, first):
        for q in range(n):
            count = meta_s[COUNT, q]
            for i in range(out_ref.shape[1]):
                block = meta_s[LIST, q * cap_blocks + first + i]
                out_ref[q, i] = take(frames_ref, block) * keep(cm_ref, block, first + i < count)

    put(lead_ref, 0)
    write = pltpu.make_async_copy(lead_ref, out_hbm.at[:, 0:lead], sems.at[2])
    write.start()
    put(tail_ref, lead)
    write.wait()


def pack_own(cm, their_cm, frames, cap_blocks, half, move):
    rows = frames.shape[0]
    n = cm.shape[0] // cap_blocks
    lead = half - move
    meta = jax.ShapeDtypeStruct((8, cm.shape[0]), jnp.int32)
    out = call(
        functools.partial(own_kernel, cap_blocks, move),
        "pack_own",
        [
            pltpu.HBM((n, half, rows, BLOCK), frames.dtype),
            jax.ShapeDtypeStruct((n, move, rows, BLOCK), frames.dtype),
            meta,
            meta,
        ],
        in_specs=[WHOLE] * 2 + [ANYWHERE],
        out_specs=[ANYWHERE] + [WHOLE] * 3,
        scratch_shapes=[
            pltpu.VMEM(frames.shape, frames.dtype),
            pltpu.VMEM((n, lead, rows, BLOCK), frames.dtype),
            pltpu.SMEM(meta.shape, meta.dtype),
            pltpu.SemaphoreType.DMA((3,)),
        ],
        bytes_accessed=4 * 1024 * 1024,
    )(cm, their_cm, frames)
    return out[0], out[1], out[2:]


def share_kernel(cap_blocks, meta_s, their_meta_s, tail_ref, theirs_ref, their_cm_ref, *refs):
    _, out_hbm, out_ref, sems = refs
    n, move = out_ref.shape[:2]
    half = cap_blocks - move
    lead = half - move
    copies = []
    for q in range(n):
        count, their_count = meta_s[COUNT, q], their_meta_s[COUNT, q]
        for i in range(move):
            rank = half + lead + i - jnp.maximum(count, lead)
            wanted = (lead + i >= count) & (rank < their_count)
            block = their_meta_s[LIST, q * cap_blocks + jnp.clip(rank, 0, cap_blocks - 1)]
            theirs = take(theirs_ref, block) * keep(their_cm_ref, block, wanted)
            out_ref[q, i] = tail_ref[q, i] + theirs
        copies.append(
            pltpu.make_async_copy(out_ref.at[q], out_hbm.at[q, lead:half], sems.at[q])
        )
        copies[-1].start()
    for copy in copies:
        copy.wait()


def share(metas, packed, tail, their_frames, their_cm, cap_blocks):
    n = packed.shape[0]
    return call(
        functools.partial(share_kernel, cap_blocks),
        "share",
        pltpu.HBM(packed.shape, packed.dtype),
        in_specs=[pl.BlockSpec(memory_space=pltpu.SMEM)] * 2 + [WHOLE] * 3 + [ANYWHERE],
        out_specs=ANYWHERE,
        input_output_aliases={5: 0},
        scratch_shapes=[
            pltpu.VMEM(tail.shape, tail.dtype),
            pltpu.SemaphoreType.DMA((n,)),
        ],
        bytes_accessed=4 * 1024 * 1024,
    )(*metas, tail, their_frames, their_cm, packed)


def rest_kernel(cap_blocks, meta_s, their_meta_s, frames_ref, cm_ref, out_ref):
    n, move = out_ref.shape[:2]
    half = cap_blocks - move
    lead = half - move
    for q in range(n):
        count, their_count = meta_s[COUNT, q], their_meta_s[COUNT, q]
        for i in range(move):
            block = meta_s[LIST, q * cap_blocks + half + i]
            wanted = (half + i < count) & (i >= half - jnp.maximum(their_count, lead))
            out_ref[q, i] = take(frames_ref, block) * keep(cm_ref, block, wanted)


def pack_rest(metas, frames, cm, cap_blocks, move):
    n = cm.shape[0] // cap_blocks
    return call(
        functools.partial(rest_kernel, cap_blocks),
        "pack_rest",
        jax.ShapeDtypeStruct((n, move, frames.shape[0], BLOCK), frames.dtype),
        in_specs=[pl.BlockSpec(memory_space=pltpu.SMEM)] * 2 + [WHOLE] * 2,
        out_specs=WHOLE,
    )(*metas, frames, cm)


def norm_kernel(first, raw_ref, *refs):
    out_ref, padded = refs[-2:]
    n, _, rows, _ = raw_ref.shape
    slots = out_ref.shape[1] // BLOCK
    total = n * rows
    chunk = 128
    zero = jnp.zeros((PAD, BLOCK), jnp.float32)
    for slot in range(slots):
        padded[slot, 0:PAD] = zero
        padded[slot, PAD + total : 2 * PAD + total] = zero
        for i in range(n):
            start = PAD + i * rows
            padded[slot, start : start + rows] = raw_ref[i, first + slot].astype(jnp.float32)
    for slot in range(slots):
        for start in range(0, total, chunk):
            base = PAD + start
            raw = padded[slot, base : base + chunk]
            summed = raw
            for offset in range(1, HALF_WIN + 1):
                summed = summed + padded[slot, base - offset : base - offset + chunk]
                summed = summed + padded[slot, base + offset : base + offset + chunk]
            if start == 0 or start + chunk == total:
                frame = start + lax.broadcasted_iota(jnp.int32, (chunk, BLOCK), 0)
                upper = jnp.minimum(frame + HALF_WIN, total - 1)
                lower = jnp.maximum(frame - HALF_WIN, 0)
                mean = summed / (upper - lower + 1).astype(jnp.float32)
            else:
                mean = summed * (1.0 / (2 * HALF_WIN + 1))
            normed = jnp.where(summed > 0.0, raw / mean, 0.0)
            out_ref[start : start + chunk, slot * BLOCK : (slot + 1) * BLOCK] = normed.astype(
                jnp.bfloat16
            )


def normalise(raw, first, slots, after=()):
    n, _, rows, _ = raw.shape
    total = n * rows
    return call(
        functools.partial(norm_kernel, first),
        "normalise",
        jax.ShapeDtypeStruct((total, slots * BLOCK), jnp.bfloat16),
        flops=12 * total * slots * BLOCK,
        bytes_accessed=4 * total * slots * BLOCK,
        in_specs=[WHOLE] + [ANYWHERE] * len(after),
        out_specs=WHOLE,
        scratch_shapes=[pltpu.VMEM((slots, total + 2 * PAD, BLOCK), jnp.float32)],
    )(raw, *after)


def dot_nt(a, b):
    return lax.dot_general(a, b, (((1,), (1,)), ((), ())), preferred_element_type=jnp.float32)


def add_sums(rows, normed, sums, column):
    first_row = pl.multiple_of(lax.axis_index("pix") * rows, rows)
    gram, frame = sums
    for ref in normed:
        right = ref[column, :]
        gram = gram + dot_nt(ref[pl.ds(first_row, rows), :], right)
        frame = frame + dot_nt(jnp.ones((8, ref.shape[1]), jnp.bfloat16), right)
    return gram, frame


def partial_kernel(count, *refs):
    normed, (gram_out, frame_out) = refs[:count], refs[-2:]
    before = refs[count:-2]
    rows, total = gram_out.shape
    for start in range(0, total, TILE):
        column = slice(start, start + TILE)
        sums = [ref[:, column] for ref in before] or [0.0, 0.0]
        gram_out[:, column], frame_out[:, column] = add_sums(rows, normed, sums, column)


def partial_sums(normed, before, parts):
    total, width = normed[0].shape
    rows = total // parts
    return call(
        functools.partial(partial_kernel, len(normed)),
        "partial_sums",
        [
            jax.ShapeDtypeStruct((rows, total), jnp.float32),
            jax.ShapeDtypeStruct((8, total), jnp.float32),
        ],
        flops=2 * rows * total * width * len(normed),
        bytes_accessed=4 * rows * total,
        in_specs=[WHOLE] * (len(normed) + len(before)),
        out_specs=[WHOLE] * 2,
    )(*normed, *before)


def result_kernel(count, meta_ref, their_meta_ref, *refs):
    normed, (gram_in, frame_in, out_hbm, out_ref, frame_ref, sems) = refs[:count], refs[count:]
    rows, total = gram_in.shape
    pixels = meta_ref[PIXELS : PIXELS + 1, 0:BLOCK] + their_meta_ref[PIXELS : PIXELS + 1, 0:BLOCK]
    own = lax.broadcasted_iota(jnp.int32, (1, BLOCK), 1) == lax.axis_index("frame")
    number = jnp.sum(jnp.where(own, pixels, 0).astype(jnp.float32), axis=1, keepdims=True)
    for start in range(0, total, TILE):
        column = slice(start, start + TILE)
        frame = frame_in[:, column]
        for ref in normed:
            frame = frame + dot_nt(jnp.ones((8, ref.shape[1]), jnp.bfloat16), ref[column, :])
        frame_ref[:, column] = frame
    first_row = pl.multiple_of(lax.axis_index("pix") * rows, rows)
    row_sum = jnp.broadcast_to(frame_ref[0:1, pl.ds(first_row, rows)], (BLOCK, rows)).T
    row_inv = 1.0 / row_sum[:, 0:1]
    copies = []
    for i, start in enumerate(range(0, total, TILE)):
        column = slice(start, start + TILE)
        gram = gram_in[:, column]
        for ref in normed:
            gram = gram + dot_nt(ref[pl.ds(first_row, rows), :], ref[column, :])
        col_inv = 1.0 / frame_ref[0:1, column]
        out_ref[i] = (((gram * row_inv) * col_inv) * number - 1.0).astype(jnp.bfloat16)
        copies.append(
            pltpu.make_async_copy(out_ref.at[i], out_hbm.at[0, :, column], sems.at[i])
        )
        copies[-1].start()
    for copy in copies:
        copy.wait()


def correlate(metas, normed, before):
    rows, total = before[0].shape
    tiles = total // TILE
    return call(
        functools.partial(result_kernel, len(normed)),
        "correlate",
        pltpu.HBM((1, rows, total), jnp.bfloat16),
        flops=2 * rows * total * sum(x.shape[1] for x in normed),
        bytes_accessed=6 * rows * total,
        in_specs=[WHOLE] * (4 + len(normed)),
        out_specs=ANYWHERE,
        scratch_shapes=[
            pltpu.VMEM((tiles, rows, TILE), jnp.bfloat16),
            pltpu.VMEM((8, total), jnp.float32),
            pltpu.SemaphoreType.DMA((tiles,)),
        ],
    )(*metas, *normed, *before)


def body(frames, cycle_map):
    p_sec = frames.shape[1]
    n = lax.axis_size("frame")
    parts = lax.axis_size("pix")
    cap_blocks = p_sec // n // BLOCK
    half = (cap_blocks + 2) // 2
    move = cap_blocks - half
    early = half - half // 2
    cm = cycle_map.reshape(p_sec // BLOCK, BLOCK)

    def swap(x):
        return lax.ppermute(x, "pix", SWAP)

    def send(blocks):
        return lax.all_to_all(blocks, "frame", split_axis=0, concat_axis=0, tiled=True)

    their_cm = swap(cm)
    their_frames = swap(frames)
    packed, tail, metas = pack_own(cm, their_cm, frames, cap_blocks, half, move)
    packed = share(metas, packed, tail, their_frames, their_cm, cap_blocks)
    overflow = jnp.max(metas[0][COUNT, :n] + metas[1][COUNT, :n]) > 2 * half
    received = send(packed)

    first = normalise(received, 0, early, [overflow.astype(jnp.int32).reshape(1)])
    their_first = swap(first)
    last = normalise(received, early, half - early, [first])
    their_last = swap(last)
    sums = partial_sums([first, last], [], parts)

    def spill(frames, cm, their_first, their_last, *operands):
        metas, sums = operands[:2], operands[2:]
        normed = normalise(send(pack_rest(metas, frames, cm, cap_blocks, move)), 0, move)
        sums = partial_sums([normed, swap(normed)], sums, parts)
        return correlate(metas, [their_first, their_last], sums)

    def fits(frames, cm, their_first, their_last, *operands):
        return correlate(operands[:2], [their_first, their_last], operands[2:])

    return lax.cond(
        overflow, spill, fits, frames, cm, their_first, their_last, *metas, *sums
    )


def solution(mesh):
    return jax.shard_map(
        body,
        mesh=mesh,
        in_specs=(P("frame", "pix"), P("pix")),
        out_specs=P("frame", "pix", None),
        check_vma=False,
    )
```

```python
import functools

import jax
import jax.numpy as jnp
from jax import lax
from jax.experimental import pallas as pl
from jax.experimental.pallas import tpu as pltpu
from jax.sharding import PartitionSpec as P

BLOCK = 128
HALF_WIN = 2
PAD = 8
TILE = 256
VMEM_BYTES = 32 * 1024 * 1024
LIST, COUNT, PIXELS = 0, 1, 2
SWAP = [(0, 1), (1, 0)]
WHOLE = pl.BlockSpec(memory_space=pltpu.VMEM)
ANYWHERE = pl.BlockSpec(memory_space=pl.ANY)


def call(kernel, name, out_shape, flops=0, bytes_accessed=0, limit=VMEM_BYTES, **kw):
    return pl.pallas_call(
        kernel,
        out_shape=out_shape,
        compiler_params=pltpu.CompilerParams(vmem_limit_bytes=limit),
        cost_estimate=pl.CostEstimate(
            flops=flops, bytes_accessed=bytes_accessed, transcendentals=0
        ),
        name=name,
        **kw,
    )


def place(i, n):
    bits = n.bit_length() - 1
    return sum(((i >> b) & 1) << (bits - 1 - b) for b in range(bits))


def keep(cm_ref, block, wanted):
    valid = (cm_ref[pl.ds(block, 1), :] >= 0) & wanted
    return valid.astype(jnp.float32).astype(jnp.bfloat16)


def take(frames_ref, block):
    return frames_ref[:, pl.ds(pl.multiple_of(block * BLOCK, BLOCK), BLOCK)]


def find_blocks(cm, cap_blocks, meta_ref):
    blocks = cm.shape[0]
    width = meta_ref.shape[1]
    first = cm[:, 0:1]
    member = first == lax.broadcasted_iota(jnp.int32, (blocks, BLOCK), 1)
    member_f = member.astype(jnp.float32)
    row = lax.broadcasted_iota(jnp.int32, (blocks, blocks), 0)
    col = lax.broadcasted_iota(jnp.int32, (blocks, blocks), 1)
    earlier = (col < row).astype(jnp.float32).astype(jnp.bfloat16)
    before = jnp.dot(earlier, member_f.astype(jnp.bfloat16), preferred_element_type=jnp.float32)
    rank = jnp.sum(before * member_f, axis=1, keepdims=True).astype(jnp.int32)
    slot = jnp.where(first >= 0, first * cap_blocks + rank, -1)
    hit = slot == lax.broadcasted_iota(jnp.int32, (blocks, width), 1)
    index = lax.broadcasted_iota(jnp.int32, (blocks, width), 0).astype(jnp.float32)
    pixels = jnp.sum((cm >= 0).astype(jnp.float32), axis=1, keepdims=True)
    meta_ref[...] = jnp.zeros_like(meta_ref)
    meta_ref[LIST : LIST + 1, :] = jnp.sum(
        jnp.where(hit, index, 0.0), axis=0, keepdims=True
    ).astype(jnp.int32)
    meta_ref[COUNT : COUNT + 1, 0:BLOCK] = jnp.sum(member_f, axis=0, keepdims=True).astype(
        jnp.int32
    )
    meta_ref[PIXELS : PIXELS + 1, 0:BLOCK] = jnp.sum(
        member_f * pixels, axis=0, keepdims=True
    ).astype(jnp.int32)


def own_kernel(cap_blocks, move, cm_ref, their_cm_ref, frames_hbm, *refs):
    out_hbm, tail_ref, meta_ref, their_meta_ref, frames_ref, lead_ref, meta_s, sems = refs
    n, lead = lead_ref.shape[:2]
    get_frames = pltpu.make_async_copy(frames_hbm, frames_ref, sems.at[0])
    get_frames.start()
    find_blocks(cm_ref[...], cap_blocks, meta_ref)
    to_scalars = pltpu.make_async_copy(meta_ref, meta_s, sems.at[1])
    to_scalars.start()
    find_blocks(their_cm_ref[...], cap_blocks, their_meta_ref)
    to_scalars.wait()
    get_frames.wait()

    def put(out_ref, first):
        for q in range(n):
            count = meta_s[COUNT, q]
            for i in range(out_ref.shape[1]):
                block = meta_s[LIST, q * cap_blocks + first + i]
                kept = take(frames_ref, block) * keep(cm_ref, block, first + i < count)
                out_ref[place(q, n), i] = kept

    put(lead_ref, 0)
    write = pltpu.make_async_copy(lead_ref, out_hbm.at[:, 0:lead], sems.at[2])
    write.start()
    put(tail_ref, lead)
    write.wait()


def pack_own(cm, their_cm, frames, cap_blocks, half, move):
    rows = frames.shape[0]
    n = cm.shape[0] // cap_blocks
    lead = half - move
    meta = jax.ShapeDtypeStruct((8, cm.shape[0]), jnp.int32)
    out = call(
        functools.partial(own_kernel, cap_blocks, move),
        "pack_own",
        [
            pltpu.HBM((n, half, rows, BLOCK), frames.dtype),
            jax.ShapeDtypeStruct((n, move, rows, BLOCK), frames.dtype),
            meta,
            meta,
        ],
        in_specs=[WHOLE] * 2 + [ANYWHERE],
        out_specs=[ANYWHERE] + [WHOLE] * 3,
        scratch_shapes=[
            pltpu.VMEM(frames.shape, frames.dtype),
            pltpu.VMEM((n, lead, rows, BLOCK), frames.dtype),
            pltpu.SMEM(meta.shape, meta.dtype),
            pltpu.SemaphoreType.DMA((3,)),
        ],
        bytes_accessed=4 * 1024 * 1024,
    )(cm, their_cm, frames)
    return out[0], out[1], out[2:]


def share_kernel(cap_blocks, meta_s, their_meta_s, tail_ref, theirs_ref, their_cm_ref, *refs):
    _, out_hbm, out_ref, sems = refs
    n, move = out_ref.shape[:2]
    half = cap_blocks - move
    lead = half - move
    copies = []
    for q in range(n):
        to = place(q, n)
        count, their_count = meta_s[COUNT, q], their_meta_s[COUNT, q]
        for i in range(move):
            rank = half + lead + i - jnp.maximum(count, lead)
            wanted = (lead + i >= count) & (rank < their_count)
            block = their_meta_s[LIST, q * cap_blocks + jnp.clip(rank, 0, cap_blocks - 1)]
            theirs = take(theirs_ref, block) * keep(their_cm_ref, block, wanted)
            out_ref[to, i] = tail_ref[to, i] + theirs
        copies.append(
            pltpu.make_async_copy(out_ref.at[to], out_hbm.at[to, lead:half], sems.at[to])
        )
        copies[-1].start()
    for copy in copies:
        copy.wait()


def share(metas, packed, tail, their_frames, their_cm, cap_blocks):
    n = packed.shape[0]
    return call(
        functools.partial(share_kernel, cap_blocks),
        "share",
        pltpu.HBM(packed.shape, packed.dtype),
        in_specs=[pl.BlockSpec(memory_space=pltpu.SMEM)] * 2 + [WHOLE] * 3 + [ANYWHERE],
        out_specs=ANYWHERE,
        input_output_aliases={5: 0},
        scratch_shapes=[
            pltpu.VMEM(tail.shape, tail.dtype),
            pltpu.SemaphoreType.DMA((n,)),
        ],
        bytes_accessed=4 * 1024 * 1024,
    )(*metas, tail, their_frames, their_cm, packed)


def rest_kernel(cap_blocks, meta_s, their_meta_s, frames_ref, cm_ref, out_ref):
    n, move = out_ref.shape[:2]
    half = cap_blocks - move
    lead = half - move
    for q in range(n):
        count, their_count = meta_s[COUNT, q], their_meta_s[COUNT, q]
        for i in range(move):
            block = meta_s[LIST, q * cap_blocks + half + i]
            wanted = (half + i < count) & (i >= half - jnp.maximum(their_count, lead))
            out_ref[place(q, n), i] = take(frames_ref, block) * keep(cm_ref, block, wanted)


def pack_rest(metas, frames, cm, cap_blocks, move):
    n = cm.shape[0] // cap_blocks
    return call(
        functools.partial(rest_kernel, cap_blocks),
        "pack_rest",
        jax.ShapeDtypeStruct((n, move, frames.shape[0], BLOCK), frames.dtype),
        in_specs=[pl.BlockSpec(memory_space=pltpu.SMEM)] * 2 + [WHOLE] * 2,
        out_specs=WHOLE,
    )(*metas, frames, cm)


def norm_kernel(first, raw_ref, *refs):
    out_ref, padded = refs[-2:]
    n, _, rows, _ = raw_ref.shape
    slots = out_ref.shape[1] // BLOCK
    total = n * rows
    chunk = 128
    zero = jnp.zeros((PAD, BLOCK), jnp.float32)
    for slot in range(slots):
        padded[slot, 0:PAD] = zero
        padded[slot, PAD + total : 2 * PAD + total] = zero
        for i in range(n):
            start = PAD + i * rows
            padded[slot, start : start + rows] = raw_ref[place(i, n), first + slot].astype(jnp.float32)
    for slot in range(slots):
        for start in range(0, total, chunk):
            base = PAD + start
            raw = padded[slot, base : base + chunk]
            summed = raw
            for offset in range(1, HALF_WIN + 1):
                summed = summed + padded[slot, base - offset : base - offset + chunk]
                summed = summed + padded[slot, base + offset : base + offset + chunk]
            if start == 0 or start + chunk == total:
                frame = start + lax.broadcasted_iota(jnp.int32, (chunk, BLOCK), 0)
                upper = jnp.minimum(frame + HALF_WIN, total - 1)
                lower = jnp.maximum(frame - HALF_WIN, 0)
                mean = summed / (upper - lower + 1).astype(jnp.float32)
            else:
                mean = summed * (1.0 / (2 * HALF_WIN + 1))
            normed = jnp.where(summed > 0.0, raw / mean, 0.0)
            out_ref[start : start + chunk, slot * BLOCK : (slot + 1) * BLOCK] = normed.astype(
                jnp.bfloat16
            )


def normalise(raw, first, slots, after=()):
    n, _, rows, _ = raw.shape
    total = n * rows
    return call(
        functools.partial(norm_kernel, first),
        "normalise",
        jax.ShapeDtypeStruct((total, slots * BLOCK), jnp.bfloat16),
        flops=12 * total * slots * BLOCK,
        bytes_accessed=4 * total * slots * BLOCK,
        in_specs=[WHOLE] + [ANYWHERE] * len(after),
        out_specs=WHOLE,
        scratch_shapes=[pltpu.VMEM((slots, total + 2 * PAD, BLOCK), jnp.float32)],
    )(raw, *after)


def dot_nt(a, b):
    return lax.dot_general(a, b, (((1,), (1,)), ((), ())), preferred_element_type=jnp.float32)


def add_sums(rows, normed, sums, column):
    first_row = pl.multiple_of(lax.axis_index("pix") * rows, rows)
    gram, frame = sums
    for ref in normed:
        right = ref[column, :]
        gram = gram + dot_nt(ref[pl.ds(first_row, rows), :], right)
        frame = frame + dot_nt(jnp.ones((8, ref.shape[1]), jnp.bfloat16), right)
    return gram, frame


def partial_kernel(count, *refs):
    normed, (gram_out, frame_out) = refs[:count], refs[-2:]
    before = refs[count:-2]
    rows, total = gram_out.shape
    for start in range(0, total, TILE):
        column = slice(start, start + TILE)
        sums = [ref[:, column] for ref in before] or [0.0, 0.0]
        gram_out[:, column], frame_out[:, column] = add_sums(rows, normed, sums, column)


def partial_sums(normed, before, parts):
    total, width = normed[0].shape
    rows = total // parts
    return call(
        functools.partial(partial_kernel, len(normed)),
        "partial_sums",
        [
            jax.ShapeDtypeStruct((rows, total), jnp.float32),
            jax.ShapeDtypeStruct((8, total), jnp.float32),
        ],
        flops=2 * rows * total * width * len(normed),
        bytes_accessed=4 * rows * total,
        in_specs=[WHOLE] * (len(normed) + len(before)),
        out_specs=[WHOLE] * 2,
    )(*normed, *before)


def result_kernel(count, meta_ref, their_meta_ref, *refs):
    normed, (gram_in, frame_in, out_hbm, out_ref, frame_ref, sems) = refs[:count], refs[count:]
    rows, total = gram_in.shape
    pixels = meta_ref[PIXELS : PIXELS + 1, 0:BLOCK] + their_meta_ref[PIXELS : PIXELS + 1, 0:BLOCK]
    own = lax.broadcasted_iota(jnp.int32, (1, BLOCK), 1) == lax.axis_index("frame")
    number = jnp.sum(jnp.where(own, pixels, 0).astype(jnp.float32), axis=1, keepdims=True)
    for start in range(0, total, TILE):
        column = slice(start, start + TILE)
        frame = frame_in[:, column]
        for ref in normed:
            frame = frame + dot_nt(jnp.ones((8, ref.shape[1]), jnp.bfloat16), ref[column, :])
        frame_ref[:, column] = frame
    first_row = pl.multiple_of(lax.axis_index("pix") * rows, rows)
    row_sum = jnp.broadcast_to(frame_ref[0:1, pl.ds(first_row, rows)], (BLOCK, rows)).T
    row_inv = 1.0 / row_sum[:, 0:1]
    copies = []
    for i, start in enumerate(range(0, total, TILE)):
        column = slice(start, start + TILE)
        gram = gram_in[:, column]
        for ref in normed:
            gram = gram + dot_nt(ref[pl.ds(first_row, rows), :], ref[column, :])
        col_inv = 1.0 / frame_ref[0:1, column]
        out_ref[i] = (((gram * row_inv) * col_inv) * number - 1.0).astype(jnp.bfloat16)
        copies.append(
            pltpu.make_async_copy(out_ref.at[i], out_hbm.at[0, :, column], sems.at[i])
        )
        copies[-1].start()
    for copy in copies:
        copy.wait()


def correlate(metas, normed, before):
    rows, total = before[0].shape
    tiles = total // TILE
    return call(
        functools.partial(result_kernel, len(normed)),
        "correlate",
        pltpu.HBM((1, rows, total), jnp.bfloat16),
        flops=2 * rows * total * sum(x.shape[1] for x in normed),
        bytes_accessed=6 * rows * total,
        in_specs=[WHOLE] * (4 + len(normed)),
        out_specs=ANYWHERE,
        scratch_shapes=[
            pltpu.VMEM((tiles, rows, TILE), jnp.bfloat16),
            pltpu.VMEM((8, total), jnp.float32),
            pltpu.SemaphoreType.DMA((tiles,)),
        ],
    )(*metas, *normed, *before)


def body(frames, cycle_map):
    p_sec = frames.shape[1]
    n = lax.axis_size("frame")
    parts = lax.axis_size("pix")
    cap_blocks = p_sec // n // BLOCK
    half = (cap_blocks + 2) // 2
    move = cap_blocks - half
    early = half - half // 2
    cm = cycle_map.reshape(p_sec // BLOCK, BLOCK)

    def swap(x):
        return lax.ppermute(x, "pix", SWAP)

    def send(blocks):
        group = [place(i, n) for i in range(n)]
        return lax.all_to_all(
            blocks, "frame", split_axis=0, concat_axis=0, axis_index_groups=[group], tiled=True
        )

    their_cm = swap(cm)
    their_cm, late_frames = lax.optimization_barrier((their_cm, frames))
    their_frames = swap(late_frames)
    packed, tail, metas = pack_own(cm, their_cm, frames, cap_blocks, half, move)
    packed = share(metas, packed, tail, their_frames, their_cm, cap_blocks)
    overflow = jnp.max(metas[0][COUNT, :n] + metas[1][COUNT, :n]) > 2 * half
    received = send(packed)

    first = normalise(received, 0, early, [overflow.astype(jnp.int32).reshape(1)])
    their_first = swap(first)
    last = normalise(received, early, half - early, [first])
    their_last = swap(last)
    sums = partial_sums([first, last], [], parts)

    def spill(frames, cm, their_first, their_last, *operands):
        metas, sums = operands[:2], operands[2:]
        normed = normalise(send(pack_rest(metas, frames, cm, cap_blocks, move)), 0, move)
        sums = partial_sums([normed, swap(normed)], sums, parts)
        return correlate(metas, [their_first, their_last], sums)

    def fits(frames, cm, their_first, their_last, *operands):
        return correlate(operands[:2], [their_first, their_last], operands[2:])

    return lax.cond(
        overflow, spill, fits, frames, cm, their_first, their_last, *metas, *sums
    )


def solution(mesh):
    return jax.shard_map(
        body,
        mesh=mesh,
        in_specs=(P("frame", "pix"), P("pix")),
        out_specs=P("frame", "pix", None),
        check_vma=False,
    )
```

```python
import functools

import jax
import jax.numpy as jnp
from jax import lax
from jax.experimental import pallas as pl
from jax.experimental.pallas import tpu as pltpu
from jax.sharding import PartitionSpec as P

BLOCK = 128
HALF_WIN = 2
PAD = 8
TILE = 256
VMEM_BYTES = 32 * 1024 * 1024
LIST, COUNT, PIXELS = 0, 1, 2
SWAP = [(0, 1), (1, 0)]
WHOLE = pl.BlockSpec(memory_space=pltpu.VMEM)
ANYWHERE = pl.BlockSpec(memory_space=pl.ANY)


def call(kernel, name, out_shape, flops=0, bytes_accessed=0, limit=VMEM_BYTES, **kw):
    return pl.pallas_call(
        kernel,
        out_shape=out_shape,
        compiler_params=pltpu.CompilerParams(vmem_limit_bytes=limit),
        cost_estimate=pl.CostEstimate(
            flops=flops, bytes_accessed=bytes_accessed, transcendentals=0
        ),
        name=name,
        **kw,
    )


def place(i, n):
    bits = n.bit_length() - 1
    return sum(((i >> b) & 1) << (bits - 1 - b) for b in range(bits))


def keep(cm_ref, block, wanted):
    valid = (cm_ref[pl.ds(block, 1), :] >= 0) & wanted
    return valid.astype(jnp.float32).astype(jnp.bfloat16)


def take(frames_ref, block):
    return frames_ref[:, pl.ds(pl.multiple_of(block * BLOCK, BLOCK), BLOCK)]


def find_blocks(cm, cap_blocks, meta_ref):
    blocks = cm.shape[0]
    width = meta_ref.shape[1]
    first = cm[:, 0:1]
    member = first == lax.broadcasted_iota(jnp.int32, (blocks, BLOCK), 1)
    member_f = member.astype(jnp.float32)
    row = lax.broadcasted_iota(jnp.int32, (blocks, blocks), 0)
    col = lax.broadcasted_iota(jnp.int32, (blocks, blocks), 1)
    earlier = (col < row).astype(jnp.float32).astype(jnp.bfloat16)
    before = jnp.dot(earlier, member_f.astype(jnp.bfloat16), preferred_element_type=jnp.float32)
    rank = jnp.sum(before * member_f, axis=1, keepdims=True).astype(jnp.int32)
    slot = jnp.where(first >= 0, first * cap_blocks + rank, -1)
    hit = slot == lax.broadcasted_iota(jnp.int32, (blocks, width), 1)
    index = lax.broadcasted_iota(jnp.int32, (blocks, width), 0).astype(jnp.float32)
    pixels = jnp.sum((cm >= 0).astype(jnp.float32), axis=1, keepdims=True)
    meta_ref[...] = jnp.zeros_like(meta_ref)
    meta_ref[LIST : LIST + 1, :] = jnp.sum(
        jnp.where(hit, index, 0.0), axis=0, keepdims=True
    ).astype(jnp.int32)
    meta_ref[COUNT : COUNT + 1, 0:BLOCK] = jnp.sum(member_f, axis=0, keepdims=True).astype(
        jnp.int32
    )
    meta_ref[PIXELS : PIXELS + 1, 0:BLOCK] = jnp.sum(
        member_f * pixels, axis=0, keepdims=True
    ).astype(jnp.int32)


def move_kernel(cap_blocks, cm_hbm, frames_hbm, out_ref, meta_ref, *scratch):
    frames_ref, cm_ref, meta_s, sems = scratch
    n, move = out_ref.shape[:2]
    half = cap_blocks - move
    get_cm = pltpu.make_async_copy(cm_hbm, cm_ref, sems.at[0])
    get_cm.start()
    get_frames = pltpu.make_async_copy(frames_hbm, frames_ref, sems.at[1])
    get_frames.start()
    get_cm.wait()
    find_blocks(cm_ref[...], cap_blocks, meta_ref)
    to_scalars = pltpu.make_async_copy(meta_ref, meta_s, sems.at[2])
    to_scalars.start()
    to_scalars.wait()
    get_frames.wait()
    for q in range(n):
        count = meta_s[COUNT, q]
        for i in range(move):
            block = meta_s[LIST, q * cap_blocks + half + i]
            out_ref[q, i] = take(frames_ref, block) * keep(cm_ref, block, half + i < count)


def pack_move(cm, frames, cap_blocks, move):
    n = cm.shape[0] // cap_blocks
    meta = jax.ShapeDtypeStruct((8, cm.shape[0]), jnp.int32)
    return call(
        functools.partial(move_kernel, cap_blocks),
        "pack_move",
        [jax.ShapeDtypeStruct((n, move, frames.shape[0], BLOCK), frames.dtype), meta],
        in_specs=[ANYWHERE] * 2,
        out_specs=[WHOLE] * 2,
        scratch_shapes=[
            pltpu.VMEM(frames.shape, frames.dtype),
            pltpu.VMEM(cm.shape, cm.dtype),
            pltpu.SMEM(meta.shape, meta.dtype),
            pltpu.SemaphoreType.DMA((3,)),
        ],
    )(
        pltpu.with_memory_space_constraint(cm, pltpu.HBM),
        pltpu.with_memory_space_constraint(frames, pltpu.HBM),
    )


def own_kernel(cap_blocks, meta_s, cm_ref, frames_ref, out_hbm, tail_ref, lead_ref, sem):
    n, lead = lead_ref.shape[:2]

    def put(out_ref, first):
        for q in range(n):
            count = meta_s[COUNT, q]
            for i in range(out_ref.shape[1]):
                block = meta_s[LIST, q * cap_blocks + first + i]
                kept = take(frames_ref, block) * keep(cm_ref, block, first + i < count)
                out_ref[place(q, n), i] = kept

    put(lead_ref, 0)
    write = pltpu.make_async_copy(lead_ref, out_hbm.at[:, 0:lead], sem)
    write.start()
    put(tail_ref, lead)
    write.wait()


def pack_own(meta, cm, frames, cap_blocks, half, move):
    rows = frames.shape[0]
    n = cm.shape[0] // cap_blocks
    return call(
        functools.partial(own_kernel, cap_blocks),
        "pack_own",
        [
            pltpu.HBM((n, half, rows, BLOCK), frames.dtype),
            jax.ShapeDtypeStruct((n, move, rows, BLOCK), frames.dtype),
        ],
        in_specs=[pl.BlockSpec(memory_space=pltpu.SMEM)] + [WHOLE] * 2,
        out_specs=[ANYWHERE, WHOLE],
        scratch_shapes=[
            pltpu.VMEM((n, half - move, rows, BLOCK), frames.dtype),
            pltpu.SemaphoreType.DMA,
        ],
        bytes_accessed=4 * 1024 * 1024,
    )(meta, cm, frames)


def share_kernel(meta_s, tail_ref, theirs_ref, *refs):
    _, out_hbm, out_ref, sems = refs
    n, move = out_ref.shape[:2]
    half = out_hbm.shape[1]
    lead = half - move
    for q in range(n):
        to = place(q, n)
        count = meta_s[COUNT, q]
        for i in range(move):
            free = jnp.broadcast_to(count <= lead + i, (1, BLOCK))
            free = free.astype(jnp.float32).astype(jnp.bfloat16)
            theirs = theirs_ref[q, jnp.clip(lead + i - jnp.maximum(count, lead), 0, move - 1)]
            out_ref[to, i] = tail_ref[to, i] + theirs * free
        pltpu.make_async_copy(out_ref.at[to], out_hbm.at[to, lead:half], sems.at[to]).start()
    for q in range(n):
        pltpu.make_async_copy(out_ref.at[q], out_hbm.at[q, lead:half], sems.at[q]).wait()


def share(meta, packed, tail, theirs):
    return call(
        share_kernel,
        "share",
        pltpu.HBM(packed.shape, packed.dtype),
        in_specs=[pl.BlockSpec(memory_space=pltpu.SMEM)] + [WHOLE] * 2 + [ANYWHERE],
        out_specs=ANYWHERE,
        input_output_aliases={3: 0},
        scratch_shapes=[
            pltpu.VMEM(tail.shape, tail.dtype),
            pltpu.SemaphoreType.DMA((packed.shape[0],)),
        ],
        bytes_accessed=4 * 1024 * 1024,
    )(meta, tail, theirs, packed)


def norm_kernel(first, raw_ref, *refs):
    out_ref, padded = refs[-2:]
    n, _, rows, _ = raw_ref.shape
    slots = out_ref.shape[1] // BLOCK
    total = n * rows
    chunk = 128
    zero = jnp.zeros((PAD, BLOCK), jnp.float32)
    for slot in range(slots):
        padded[slot, 0:PAD] = zero
        padded[slot, PAD + total : 2 * PAD + total] = zero
        for i in range(n):
            start = PAD + i * rows
            padded[slot, start : start + rows] = raw_ref[place(i, n), first + slot].astype(jnp.float32)
    for slot in range(slots):
        for start in range(0, total, chunk):
            base = PAD + start
            raw = padded[slot, base : base + chunk]
            summed = raw
            for offset in range(1, HALF_WIN + 1):
                summed = summed + padded[slot, base - offset : base - offset + chunk]
                summed = summed + padded[slot, base + offset : base + offset + chunk]
            if start == 0 or start + chunk == total:
                frame = start + lax.broadcasted_iota(jnp.int32, (chunk, BLOCK), 0)
                upper = jnp.minimum(frame + HALF_WIN, total - 1)
                lower = jnp.maximum(frame - HALF_WIN, 0)
                mean = summed / (upper - lower + 1).astype(jnp.float32)
            else:
                mean = summed * (1.0 / (2 * HALF_WIN + 1))
            normed = jnp.where(summed > 0.0, raw / mean, 0.0)
            out_ref[start : start + chunk, slot * BLOCK : (slot + 1) * BLOCK] = normed.astype(
                jnp.bfloat16
            )


def normalise(raw, first, slots, after=()):
    n, _, rows, _ = raw.shape
    total = n * rows
    return call(
        functools.partial(norm_kernel, first),
        "normalise",
        jax.ShapeDtypeStruct((total, slots * BLOCK), jnp.bfloat16),
        flops=12 * total * slots * BLOCK,
        bytes_accessed=4 * total * slots * BLOCK,
        in_specs=[WHOLE] + [ANYWHERE] * len(after),
        out_specs=WHOLE,
        scratch_shapes=[pltpu.VMEM((slots, total + 2 * PAD, BLOCK), jnp.float32)],
    )(raw, *after)


def dot_nt(a, b):
    return lax.dot_general(a, b, (((1,), (1,)), ((), ())), preferred_element_type=jnp.float32)


def add_sums(rows, normed, sums, column):
    first_row = pl.multiple_of(lax.axis_index("pix") * rows, rows)
    gram, frame = sums
    for ref in normed:
        right = ref[column, :]
        gram = gram + dot_nt(ref[pl.ds(first_row, rows), :], right)
        frame = frame + dot_nt(jnp.ones((8, ref.shape[1]), jnp.bfloat16), right)
    return gram, frame


def partial_kernel(count, *refs):
    normed, (gram_out, frame_out) = refs[:count], refs[-2:]
    before = refs[count:-2]
    rows, total = gram_out.shape
    for start in range(0, total, TILE):
        column = slice(start, start + TILE)
        sums = [ref[:, column] for ref in before] or [0.0, 0.0]
        gram_out[:, column], frame_out[:, column] = add_sums(rows, normed, sums, column)


def partial_sums(normed, before, parts):
    total, width = normed[0].shape
    rows = total // parts
    return call(
        functools.partial(partial_kernel, len(normed)),
        "partial_sums",
        [
            jax.ShapeDtypeStruct((rows, total), jnp.float32),
            jax.ShapeDtypeStruct((8, total), jnp.float32),
        ],
        flops=2 * rows * total * width * len(normed),
        bytes_accessed=4 * rows * total,
        in_specs=[WHOLE] * (len(normed) + len(before)),
        out_specs=[WHOLE] * 2,
    )(*normed, *before)


def result_kernel(count, meta_ref, their_meta_ref, *refs):
    normed, (gram_in, frame_in, out_hbm, out_ref, frame_ref, sems) = refs[:count], refs[count:]
    rows, total = gram_in.shape
    pixels = meta_ref[PIXELS : PIXELS + 1, 0:BLOCK] + their_meta_ref[PIXELS : PIXELS + 1, 0:BLOCK]
    own = lax.broadcasted_iota(jnp.int32, (1, BLOCK), 1) == lax.axis_index("frame")
    number = jnp.sum(jnp.where(own, pixels, 0).astype(jnp.float32), axis=1, keepdims=True)
    for start in range(0, total, TILE):
        column = slice(start, start + TILE)
        frame = frame_in[:, column]
        for ref in normed:
            frame = frame + dot_nt(jnp.ones((8, ref.shape[1]), jnp.bfloat16), ref[column, :])
        frame_ref[:, column] = frame
    first_row = pl.multiple_of(lax.axis_index("pix") * rows, rows)
    row_sum = jnp.broadcast_to(frame_ref[0:1, pl.ds(first_row, rows)], (BLOCK, rows)).T
    row_inv = 1.0 / row_sum[:, 0:1]
    copies = []
    for i, start in enumerate(range(0, total, TILE)):
        column = slice(start, start + TILE)
        gram = gram_in[:, column]
        for ref in normed:
            gram = gram + dot_nt(ref[pl.ds(first_row, rows), :], ref[column, :])
        col_inv = 1.0 / frame_ref[0:1, column]
        out_ref[i] = (((gram * row_inv) * col_inv) * number - 1.0).astype(jnp.bfloat16)
        copies.append(
            pltpu.make_async_copy(out_ref.at[i], out_hbm.at[0, :, column], sems.at[i])
        )
        copies[-1].start()
    for copy in copies:
        copy.wait()


def correlate(metas, normed, before):
    rows, total = before[0].shape
    tiles = total // TILE
    return call(
        functools.partial(result_kernel, len(normed)),
        "correlate",
        pltpu.HBM((1, rows, total), jnp.bfloat16),
        flops=2 * rows * total * sum(x.shape[1] for x in normed),
        bytes_accessed=6 * rows * total,
        in_specs=[WHOLE] * (4 + len(normed)),
        out_specs=ANYWHERE,
        scratch_shapes=[
            pltpu.VMEM((tiles, rows, TILE), jnp.bfloat16),
            pltpu.VMEM((8, total), jnp.float32),
            pltpu.SemaphoreType.DMA((tiles,)),
        ],
    )(*metas, *normed, *before)


def body(frames, cycle_map):
    p_sec = frames.shape[1]
    n = lax.axis_size("frame")
    parts = lax.axis_size("pix")
    cap_blocks = p_sec // n // BLOCK
    half = (cap_blocks + 2) // 2
    move = cap_blocks - half
    lead = half - move
    early = half - half // 2
    cm = cycle_map.reshape(p_sec // BLOCK, BLOCK)

    def swap(x):
        return lax.ppermute(x, "pix", SWAP)

    def send(blocks):
        group = [place(i, n) for i in range(n)]
        return lax.all_to_all(
            blocks, "frame", split_axis=0, concat_axis=0, axis_index_groups=[group], tiled=True
        )

    moving, meta = pack_move(cm, frames, cap_blocks, move)
    theirs = swap(moving)
    packed, tail = pack_own(meta, cm, frames, cap_blocks, half, move)
    packed = share(meta, packed, tail, theirs)
    received = send(packed)

    meta, _ = lax.optimization_barrier((meta, packed))
    their_meta = swap(meta)
    counts, their_counts = meta[COUNT, :n], their_meta[COUNT, :n]
    overflow = jnp.max(counts + their_counts) > 2 * half

    first = normalise(received, 0, early, [overflow.astype(jnp.int32).reshape(1)])
    their_first = swap(first)
    last = normalise(received, early, half - early, [first])
    their_last = swap(last)
    sums = partial_sums([first, last], [], parts)
    sums = partial_sums([their_first], sums, parts)

    def spill(moving, meta, their_meta, their_last, *sums):
        moved = half - jnp.maximum(their_meta[COUNT, :n], lead)
        stays = jnp.arange(move, dtype=jnp.int32)[None, :] >= moved[:, None]
        rest = jnp.where(stays[:, :, None, None], moving, jnp.zeros((), moving.dtype))
        rest = jnp.stack([rest[place(i, n)] for i in range(n)])
        normed = normalise(send(rest), 0, move)
        sums = partial_sums([normed, swap(normed)], sums, parts)
        return correlate([meta, their_meta], [their_last], sums)

    def fits(moving, meta, their_meta, their_last, *sums):
        return correlate([meta, their_meta], [their_last], sums)

    return lax.cond(overflow, spill, fits, moving, meta, their_meta, their_last, *sums)


def solution(mesh):
    return jax.shard_map(
        body,
        mesh=mesh,
        in_specs=(P("frame", "pix"), P("pix")),
        out_specs=P("frame", "pix", None),
        check_vma=False,
    )
```

```python
import functools

import jax
import jax.numpy as jnp
from jax import lax
from jax.experimental import pallas as pl
from jax.experimental.pallas import tpu as pltpu
from jax.sharding import PartitionSpec as P

BLOCK = 128
HALF_WIN = 2
PAD = 8
TILE = 256
CHUNK = 128
ONES = 16
VMEM_BYTES = 32 * 1024 * 1024
LIST, COUNT, PIXELS = 0, 1, 2
SWAP = [(0, 1), (1, 0)]
WHOLE = pl.BlockSpec(memory_space=pltpu.VMEM)
ANYWHERE = pl.BlockSpec(memory_space=pl.ANY)


def call(kernel, name, out_shape, flops=0, bytes_accessed=0, limit=VMEM_BYTES, **kw):
    return pl.pallas_call(
        kernel,
        out_shape=out_shape,
        compiler_params=pltpu.CompilerParams(vmem_limit_bytes=limit),
        cost_estimate=pl.CostEstimate(
            flops=flops, bytes_accessed=bytes_accessed, transcendentals=0
        ),
        name=name,
        **kw,
    )


def place(i, n):
    half, quarter = n // 2, n // 4
    low = i % half
    return i // half * half + low % quarter * 2 + low // quarter


def keep(cm_ref, block, wanted):
    valid = (cm_ref[pl.ds(block, 1), :] >= 0) & wanted
    return valid.astype(jnp.float32).astype(jnp.bfloat16)


def take(frames_ref, block):
    return frames_ref[:, pl.ds(pl.multiple_of(block * BLOCK, BLOCK), BLOCK)]


def find_blocks(cm, cap_blocks, meta_ref):
    blocks = cm.shape[0]
    width = meta_ref.shape[1]
    first = cm[:, 0:1]
    member = first == lax.broadcasted_iota(jnp.int32, (blocks, BLOCK), 1)
    member_f = member.astype(jnp.float32)
    row = lax.broadcasted_iota(jnp.int32, (blocks, blocks), 0)
    col = lax.broadcasted_iota(jnp.int32, (blocks, blocks), 1)
    earlier = (col < row).astype(jnp.float32).astype(jnp.bfloat16)
    before = jnp.dot(earlier, member_f.astype(jnp.bfloat16), preferred_element_type=jnp.float32)
    rank = jnp.sum(before * member_f, axis=1, keepdims=True).astype(jnp.int32)
    slot = jnp.where(first >= 0, first * cap_blocks + rank, -1)
    hit = slot == lax.broadcasted_iota(jnp.int32, (blocks, width), 1)
    index = lax.broadcasted_iota(jnp.int32, (blocks, width), 0).astype(jnp.float32)
    pixels = jnp.sum((cm >= 0).astype(jnp.float32), axis=1, keepdims=True)
    meta_ref[...] = jnp.zeros_like(meta_ref)
    meta_ref[LIST : LIST + 1, :] = jnp.sum(
        jnp.where(hit, index, 0.0), axis=0, keepdims=True
    ).astype(jnp.int32)
    meta_ref[COUNT : COUNT + 1, 0:BLOCK] = jnp.sum(member_f, axis=0, keepdims=True).astype(
        jnp.int32
    )
    meta_ref[PIXELS : PIXELS + 1, 0:BLOCK] = jnp.sum(
        member_f * pixels, axis=0, keepdims=True
    ).astype(jnp.int32)


def move_kernel(cap_blocks, cm_hbm, frames_hbm, out_ref, meta_ref, *scratch):
    frames_ref, cm_ref, meta_s, sems = scratch
    n, move = out_ref.shape[:2]
    half = cap_blocks - move
    get_cm = pltpu.make_async_copy(cm_hbm, cm_ref, sems.at[0])
    get_cm.start()
    get_frames = pltpu.make_async_copy(frames_hbm, frames_ref, sems.at[1])
    get_frames.start()
    get_cm.wait()
    find_blocks(cm_ref[...], cap_blocks, meta_ref)
    to_scalars = pltpu.make_async_copy(meta_ref, meta_s, sems.at[2])
    to_scalars.start()
    to_scalars.wait()
    get_frames.wait()
    for q in range(n):
        count = meta_s[COUNT, q]
        for i in range(move):
            block = meta_s[LIST, q * cap_blocks + half + i]
            out_ref[q, i] = take(frames_ref, block) * keep(cm_ref, block, half + i < count)


def pack_move(cm, frames, cap_blocks, move):
    n = cm.shape[0] // cap_blocks
    meta = jax.ShapeDtypeStruct((8, cm.shape[0]), jnp.int32)
    return call(
        functools.partial(move_kernel, cap_blocks),
        "pack_move",
        [jax.ShapeDtypeStruct((n, move, frames.shape[0], BLOCK), frames.dtype), meta],
        in_specs=[ANYWHERE] * 2,
        out_specs=[WHOLE] * 2,
        scratch_shapes=[
            pltpu.VMEM(frames.shape, frames.dtype),
            pltpu.VMEM(cm.shape, cm.dtype),
            pltpu.SMEM(meta.shape, meta.dtype),
            pltpu.SemaphoreType.DMA((3,)),
        ],
    )(
        pltpu.with_memory_space_constraint(cm, pltpu.HBM),
        pltpu.with_memory_space_constraint(frames, pltpu.HBM),
    )


def own_kernel(cap_blocks, meta_s, cm_ref, frames_ref, out_hbm, tail_ref, lead_ref, sem):
    n, lead = lead_ref.shape[:2]

    def put(out_ref, first):
        for q in range(n):
            count = meta_s[COUNT, q]
            for i in range(out_ref.shape[1]):
                block = meta_s[LIST, q * cap_blocks + first + i]
                kept = take(frames_ref, block) * keep(cm_ref, block, first + i < count)
                out_ref[place(q, n), i] = kept

    put(lead_ref, 0)
    write = pltpu.make_async_copy(lead_ref, out_hbm.at[:, 0:lead], sem)
    write.start()
    put(tail_ref, lead)
    write.wait()


def pack_own(meta, cm, frames, cap_blocks, half, move):
    rows = frames.shape[0]
    n = cm.shape[0] // cap_blocks
    return call(
        functools.partial(own_kernel, cap_blocks),
        "pack_own",
        [
            pltpu.HBM((n, half, rows, BLOCK), frames.dtype),
            jax.ShapeDtypeStruct((n, move, rows, BLOCK), frames.dtype),
        ],
        in_specs=[pl.BlockSpec(memory_space=pltpu.SMEM)] + [WHOLE] * 2,
        out_specs=[ANYWHERE, WHOLE],
        scratch_shapes=[
            pltpu.VMEM((n, half - move, rows, BLOCK), frames.dtype),
            pltpu.SemaphoreType.DMA,
        ],
        bytes_accessed=4 * 1024 * 1024,
    )(meta, cm, frames)


def share_kernel(meta_ref, tail_ref, theirs_ref, *refs):
    _, out_hbm, out_ref, sems = refs
    n, move = out_ref.shape[:2]
    half = out_hbm.shape[1]
    lead = half - move
    counts = meta_ref[COUNT : COUNT + 1, 0:BLOCK]
    for q in range(n):
        to = place(q, n)
        count = jnp.broadcast_to(counts[:, q : q + 1], (1, BLOCK))
        used = jnp.maximum(count, lead) - lead
        block = [tail_ref[to, i] for i in range(move)]
        for skip in range(move):
            fits = ((used == skip) & (count < half)).astype(jnp.float32).astype(jnp.bfloat16)
            for i in range(skip, move):
                block[i] = block[i] + theirs_ref[q, i - skip] * fits
        for i in range(move):
            out_ref[to, i] = block[i]
        pltpu.make_async_copy(out_ref.at[to], out_hbm.at[to, lead:half], sems.at[to]).start()
    for q in range(n):
        pltpu.make_async_copy(out_ref.at[q], out_hbm.at[q, lead:half], sems.at[q]).wait()


def share(meta, packed, tail, theirs):
    return call(
        share_kernel,
        "share",
        pltpu.HBM(packed.shape, packed.dtype),
        in_specs=[WHOLE] * 3 + [ANYWHERE],
        out_specs=ANYWHERE,
        input_output_aliases={3: 0},
        scratch_shapes=[
            pltpu.VMEM(tail.shape, tail.dtype),
            pltpu.SemaphoreType.DMA((packed.shape[0],)),
        ],
        bytes_accessed=4 * 1024 * 1024,
    )(meta, tail, theirs, packed)


def lay_out(raw_ref, first, padded):
    n, _, rows, _ = raw_ref.shape
    total = n * rows
    zero = jnp.zeros((PAD, BLOCK), jnp.float32)
    for slot in range(padded.shape[0]):
        padded[slot, 0:PAD] = zero
        padded[slot, PAD + total : 2 * PAD + total] = zero
        for i in range(n):
            start = PAD + i * rows
            padded[slot, start : start + rows] = raw_ref[place(i, n), first + slot].astype(
                jnp.float32
            )


def norm_rows(padded, start, chunk, out_ref):
    total = out_ref.shape[0]
    base = PAD + start
    for slot in range(padded.shape[0]):
        raw = padded[slot, base : base + chunk]
        summed = raw
        for offset in range(1, HALF_WIN + 1):
            summed = summed + padded[slot, base - offset : base - offset + chunk]
            summed = summed + padded[slot, base + offset : base + offset + chunk]
        if start == 0 or start + chunk == total:
            frame = start + lax.broadcasted_iota(jnp.int32, (chunk, BLOCK), 0)
            upper = jnp.minimum(frame + HALF_WIN, total - 1)
            lower = jnp.maximum(frame - HALF_WIN, 0)
            mean = summed / (upper - lower + 1).astype(jnp.float32)
        else:
            mean = summed * (1.0 / (2 * HALF_WIN + 1))
        normed = jnp.where(summed > 0.0, raw / mean, 0.0)
        out_ref[start : start + chunk, slot * BLOCK : (slot + 1) * BLOCK] = normed.astype(
            jnp.bfloat16
        )


def norm_kernel(first, raw_ref, *refs):
    out_ref, padded = refs[-2:]
    lay_out(raw_ref, first, padded)
    for start in range(0, out_ref.shape[0], CHUNK):
        norm_rows(padded, start, CHUNK, out_ref)


def normalise(raw, first, slots, after=()):
    n, _, rows, _ = raw.shape
    total = n * rows
    return call(
        functools.partial(norm_kernel, first),
        "normalise",
        jax.ShapeDtypeStruct((total, slots * BLOCK), jnp.bfloat16),
        flops=12 * total * slots * BLOCK,
        bytes_accessed=4 * total * slots * BLOCK,
        in_specs=[WHOLE] + [ANYWHERE] * len(after),
        out_specs=WHOLE,
        scratch_shapes=[pltpu.VMEM((slots, total + 2 * PAD, BLOCK), jnp.float32)],
    )(raw, *after)


def dot_nt(a, b):
    return lax.dot_general(a, b, (((1,), (1,)), ((), ())), preferred_element_type=jnp.float32)


def set_left(ref, left_ref):
    rows = left_ref.shape[0] - ONES
    first_row = pl.multiple_of(lax.axis_index("pix") * rows, rows)
    left_ref[0:rows] = ref[pl.ds(first_row, rows), :]
    left_ref[rows : rows + ONES] = jnp.ones((ONES, ref.shape[1]), jnp.bfloat16)


def add_sums(pairs, sums, column):
    gram, frame = sums
    rows = pairs[0][0].shape[0] - ONES
    for left_ref, ref in pairs:
        both = dot_nt(left_ref[...], ref[column, :])
        gram = gram + both[0:rows]
        frame = frame + both[rows : rows + 8]
    return gram, frame


def partial_kernel(count, *refs):
    normed, lefts, (gram_out, frame_out) = refs[:count], refs[-count:], refs[-count - 2 : -count]
    before = refs[count : -count - 2]
    for ref, left_ref in zip(normed, lefts):
        set_left(ref, left_ref)
    for start in range(0, gram_out.shape[1], TILE):
        column = slice(start, start + TILE)
        sums = [ref[:, column] for ref in before] or [0.0, 0.0]
        gram_out[:, column], frame_out[:, column] = add_sums(
            list(zip(lefts, normed)), sums, column
        )


def sums_shape(total, parts):
    return [
        jax.ShapeDtypeStruct((total // parts, total), jnp.float32),
        jax.ShapeDtypeStruct((8, total), jnp.float32),
    ]


def partial_sums(normed, before, parts):
    total, width = normed[0].shape
    rows = total // parts
    return call(
        functools.partial(partial_kernel, len(normed)),
        "partial_sums",
        sums_shape(total, parts),
        flops=2 * rows * total * width * len(normed),
        bytes_accessed=4 * rows * total,
        in_specs=[WHOLE] * (len(normed) + len(before)),
        out_specs=[WHOLE] * 2,
        scratch_shapes=[pltpu.VMEM((rows + ONES, x.shape[1]), x.dtype) for x in normed],
    )(*normed, *before)


def norm_sums_kernel(first, raw_ref, done_ref, out_ref, gram_out, frame_out, padded, left_ref):
    total = out_ref.shape[0]
    tiles = total // TILE
    lay_out(raw_ref, first, padded)
    set_left(done_ref, left_ref)
    for i in range(tiles):
        column = slice(i * TILE, (i + 1) * TILE)
        gram_out[:, column], frame_out[:, column] = add_sums(
            [(left_ref, done_ref)], [0.0, 0.0], column
        )
        for start in range(i * TILE, (i + 1) * TILE, CHUNK):
            norm_rows(padded, start, CHUNK, out_ref)


def normalise_and_sum(raw, done, parts):
    n, slots, rows, _ = raw.shape
    total, width = done.shape
    first = width // BLOCK
    return call(
        functools.partial(norm_sums_kernel, first),
        "normalise_and_sum",
        [jax.ShapeDtypeStruct((total, (slots - first) * BLOCK), jnp.bfloat16)]
        + sums_shape(total, parts),
        flops=2 * total // parts * total * width,
        bytes_accessed=4 * total * total // parts,
        in_specs=[WHOLE] * 2,
        out_specs=[WHOLE] * 3,
        scratch_shapes=[
            pltpu.VMEM((slots - first, total + 2 * PAD, BLOCK), jnp.float32),
            pltpu.VMEM((total // parts + ONES, width), jnp.bfloat16),
        ],
    )(raw, done)


def result_kernel(meta_ref, their_meta_ref, normed_ref, gram_in, frame_in, out_hbm, *scratch):
    out_ref, gram_ref, frame_ref, left_ref, sems = scratch
    rows, total = gram_in.shape
    pixels = meta_ref[PIXELS : PIXELS + 1, 0:BLOCK] + their_meta_ref[PIXELS : PIXELS + 1, 0:BLOCK]
    own = lax.broadcasted_iota(jnp.int32, (1, BLOCK), 1) == lax.axis_index("frame")
    number = jnp.sum(jnp.where(own, pixels, 0).astype(jnp.float32), axis=1, keepdims=True)
    set_left(normed_ref, left_ref)
    for start in range(0, total, TILE):
        column = slice(start, start + TILE)
        gram_ref[:, column], frame_ref[:, column] = add_sums(
            [(left_ref, normed_ref)], [gram_in[:, column], frame_in[:, column]], column
        )
    first_row = pl.multiple_of(lax.axis_index("pix") * rows, rows)
    row_sum = jnp.broadcast_to(frame_ref[0:1, pl.ds(first_row, rows)], (BLOCK, rows)).T
    row_inv = 1.0 / row_sum[:, 0:1]
    copies = []
    for i, start in enumerate(range(0, total, TILE)):
        column = slice(start, start + TILE)
        col_inv = 1.0 / frame_ref[0:1, column]
        result = ((gram_ref[:, column] * row_inv) * col_inv) * number - 1.0
        out_ref[i] = result.astype(jnp.bfloat16)
        copies.append(
            pltpu.make_async_copy(out_ref.at[i], out_hbm.at[0, :, column], sems.at[i])
        )
        copies[-1].start()
    for copy in copies:
        copy.wait()


def correlate(metas, normed, before):
    rows, total = before[0].shape
    tiles = total // TILE
    return call(
        result_kernel,
        "correlate",
        pltpu.HBM((1, rows, total), jnp.bfloat16),
        flops=2 * rows * total * normed.shape[1],
        bytes_accessed=6 * rows * total,
        in_specs=[WHOLE] * 5,
        out_specs=ANYWHERE,
        scratch_shapes=[
            pltpu.VMEM((tiles, rows, TILE), jnp.bfloat16),
            pltpu.VMEM((rows, total), jnp.float32),
            pltpu.VMEM((8, total), jnp.float32),
            pltpu.VMEM((rows + ONES, normed.shape[1]), normed.dtype),
            pltpu.SemaphoreType.DMA((tiles,)),
        ],
    )(*metas, normed, *before)


def body(frames, cycle_map):
    p_sec = frames.shape[1]
    n = lax.axis_size("frame")
    parts = lax.axis_size("pix")
    cap_blocks = p_sec // n // BLOCK
    half = (cap_blocks + 2) // 2
    move = cap_blocks - half
    lead = half - move
    early = half - half // 2
    cm = cycle_map.reshape(p_sec // BLOCK, BLOCK)

    def swap(x):
        return lax.ppermute(x, "pix", SWAP)

    group = sorted(range(n), key=lambda i: place(i, n))

    def send(blocks):
        return lax.all_to_all(
            blocks, "frame", split_axis=0, concat_axis=0, axis_index_groups=[group], tiled=True
        )

    moving, meta = pack_move(cm, frames, cap_blocks, move)
    theirs = swap(moving)
    packed, tail = pack_own(meta, cm, frames, cap_blocks, half, move)
    packed = share(meta, packed, tail, theirs)
    received = send(packed)

    meta, _ = lax.optimization_barrier((meta, packed))
    their_meta = swap(meta)
    counts, their_counts = meta[COUNT, :n], their_meta[COUNT, :n]
    overflow = jnp.max(counts + their_counts) > 2 * half

    first = normalise(received, 0, early, [overflow.astype(jnp.int32).reshape(1)])
    their_first = swap(first)
    last, *sums = normalise_and_sum(received, first, parts)
    their_last = swap(last)
    sums = partial_sums([last], sums, parts)
    sums = partial_sums([their_first], sums, parts)

    def spill(moving, meta, their_meta, their_last, *sums):
        moved = half - jnp.maximum(their_meta[COUNT, :n], lead)
        stays = jnp.arange(move, dtype=jnp.int32)[None, :] >= moved[:, None]
        rest = jnp.where(stays[:, :, None, None], moving, jnp.zeros((), moving.dtype))
        rest = jnp.stack([rest[i] for i in group])
        normed = normalise(send(rest), 0, move)
        sums = partial_sums([normed, swap(normed)], sums, parts)
        return correlate([meta, their_meta], their_last, sums)

    def fits(moving, meta, their_meta, their_last, *sums):
        return correlate([meta, their_meta], their_last, sums)

    return lax.cond(overflow, spill, fits, moving, meta, their_meta, their_last, *sums)


def solution(mesh):
    return jax.shard_map(
        body,
        mesh=mesh,
        in_specs=(P("frame", "pix"), P("pix")),
        out_specs=P("frame", "pix", None),
        check_vma=False,
    )
```

```python
import functools

import jax
import jax.numpy as jnp
from jax import lax
from jax.experimental import pallas as pl
from jax.experimental.pallas import tpu as pltpu
from jax.sharding import PartitionSpec as P

BLOCK = 128
HALF_WIN = 2
PAD = 8
TILE = 256
CHUNK = 128
ONES = 16
VMEM_BYTES = 32 * 1024 * 1024
LIST, COUNT, PIXELS = 0, 1, 2
SWAP = [(0, 1), (1, 0)]
WHOLE = pl.BlockSpec(memory_space=pltpu.VMEM)
ANYWHERE = pl.BlockSpec(memory_space=pl.ANY)


def call(kernel, name, out_shape, flops=0, bytes_accessed=0, limit=VMEM_BYTES, **kw):
    return pl.pallas_call(
        kernel,
        out_shape=out_shape,
        compiler_params=pltpu.CompilerParams(vmem_limit_bytes=limit),
        cost_estimate=pl.CostEstimate(
            flops=flops, bytes_accessed=bytes_accessed, transcendentals=0
        ),
        name=name,
        **kw,
    )


def keep(cm_ref, block, wanted):
    valid = (cm_ref[pl.ds(block, 1), :] >= 0) & wanted
    return valid.astype(jnp.float32).astype(jnp.bfloat16)


def take(frames_ref, block):
    return frames_ref[:, pl.ds(pl.multiple_of(block * BLOCK, BLOCK), BLOCK)]


def find_blocks(cm, cap_blocks, meta_ref):
    blocks = cm.shape[0]
    width = meta_ref.shape[1]
    first = cm[:, 0:1]
    member = first == lax.broadcasted_iota(jnp.int32, (blocks, BLOCK), 1)
    member_f = member.astype(jnp.float32)
    row = lax.broadcasted_iota(jnp.int32, (blocks, blocks), 0)
    col = lax.broadcasted_iota(jnp.int32, (blocks, blocks), 1)
    earlier = (col < row).astype(jnp.float32).astype(jnp.bfloat16)
    before = jnp.dot(earlier, member_f.astype(jnp.bfloat16), preferred_element_type=jnp.float32)
    rank = jnp.sum(before * member_f, axis=1, keepdims=True).astype(jnp.int32)
    slot = jnp.where(first >= 0, first * cap_blocks + rank, -1)
    hit = slot == lax.broadcasted_iota(jnp.int32, (blocks, width), 1)
    index = lax.broadcasted_iota(jnp.int32, (blocks, width), 0).astype(jnp.float32)
    pixels = jnp.sum((cm >= 0).astype(jnp.float32), axis=1, keepdims=True)
    meta_ref[...] = jnp.zeros_like(meta_ref)
    meta_ref[LIST : LIST + 1, :] = jnp.sum(
        jnp.where(hit, index, 0.0), axis=0, keepdims=True
    ).astype(jnp.int32)
    meta_ref[COUNT : COUNT + 1, 0:BLOCK] = jnp.sum(member_f, axis=0, keepdims=True).astype(
        jnp.int32
    )
    meta_ref[PIXELS : PIXELS + 1, 0:BLOCK] = jnp.sum(
        member_f * pixels, axis=0, keepdims=True
    ).astype(jnp.int32)


def move_kernel(cap_blocks, cm_hbm, frames_hbm, out_ref, meta_ref, *scratch):
    frames_ref, cm_ref, meta_s, sems = scratch
    n, move = out_ref.shape[:2]
    half = cap_blocks - move
    get_cm = pltpu.make_async_copy(cm_hbm, cm_ref, sems.at[0])
    get_cm.start()
    get_frames = pltpu.make_async_copy(frames_hbm, frames_ref, sems.at[1])
    get_frames.start()
    get_cm.wait()
    find_blocks(cm_ref[...], cap_blocks, meta_ref)
    to_scalars = pltpu.make_async_copy(meta_ref, meta_s, sems.at[2])
    to_scalars.start()
    to_scalars.wait()
    get_frames.wait()
    for q in range(n):
        count = meta_s[COUNT, q]
        for i in range(move):
            block = meta_s[LIST, q * cap_blocks + half + i]
            out_ref[q, i] = take(frames_ref, block) * keep(cm_ref, block, half + i < count)


def pack_move(cm, frames, cap_blocks, move):
    n = cm.shape[0] // cap_blocks
    meta = jax.ShapeDtypeStruct((8, cm.shape[0]), jnp.int32)
    return call(
        functools.partial(move_kernel, cap_blocks),
        "pack_move",
        [jax.ShapeDtypeStruct((n, move, frames.shape[0], BLOCK), frames.dtype), meta],
        in_specs=[ANYWHERE] * 2,
        out_specs=[WHOLE] * 2,
        scratch_shapes=[
            pltpu.VMEM(frames.shape, frames.dtype),
            pltpu.VMEM(cm.shape, cm.dtype),
            pltpu.SMEM(meta.shape, meta.dtype),
            pltpu.SemaphoreType.DMA((3,)),
        ],
    )(
        pltpu.with_memory_space_constraint(cm, pltpu.HBM),
        pltpu.with_memory_space_constraint(frames, pltpu.HBM),
    )


def own_kernel(cap_blocks, meta_s, cm_ref, frames_ref, out_hbm, tail_ref, lead_ref, sem):
    n, lead = lead_ref.shape[:2]

    def put(out_ref, first):
        for q in range(n):
            count = meta_s[COUNT, q]
            for i in range(out_ref.shape[1]):
                block = meta_s[LIST, q * cap_blocks + first + i]
                kept = take(frames_ref, block) * keep(cm_ref, block, first + i < count)
                out_ref[q, i] = kept

    put(lead_ref, 0)
    write = pltpu.make_async_copy(lead_ref, out_hbm.at[:, 0:lead], sem)
    write.start()
    put(tail_ref, lead)
    write.wait()


def pack_own(meta, cm, frames, cap_blocks, half, move):
    rows = frames.shape[0]
    n = cm.shape[0] // cap_blocks
    return call(
        functools.partial(own_kernel, cap_blocks),
        "pack_own",
        [
            pltpu.HBM((n, half, rows, BLOCK), frames.dtype),
            jax.ShapeDtypeStruct((n, move, rows, BLOCK), frames.dtype),
        ],
        in_specs=[pl.BlockSpec(memory_space=pltpu.SMEM)] + [WHOLE] * 2,
        out_specs=[ANYWHERE, WHOLE],
        scratch_shapes=[
            pltpu.VMEM((n, half - move, rows, BLOCK), frames.dtype),
            pltpu.SemaphoreType.DMA,
        ],
        bytes_accessed=4 * 1024 * 1024,
    )(meta, cm, frames)


def share_kernel(meta_ref, tail_ref, theirs_ref, *refs):
    _, out_hbm, out_ref, sems = refs
    n, move = out_ref.shape[:2]
    half = out_hbm.shape[1]
    lead = half - move
    counts = meta_ref[COUNT : COUNT + 1, 0:BLOCK]
    for q in range(n):
        count = jnp.broadcast_to(counts[:, q : q + 1], (1, BLOCK))
        used = jnp.maximum(count, lead) - lead
        block = [tail_ref[q, i] for i in range(move)]
        for skip in range(move):
            fits = ((used == skip) & (count < half)).astype(jnp.float32).astype(jnp.bfloat16)
            for i in range(skip, move):
                block[i] = block[i] + theirs_ref[q, i - skip] * fits
        for i in range(move):
            out_ref[q, i] = block[i]
        pltpu.make_async_copy(out_ref.at[q], out_hbm.at[q, lead:half], sems.at[q]).start()
    for q in range(n):
        pltpu.make_async_copy(out_ref.at[q], out_hbm.at[q, lead:half], sems.at[q]).wait()


def share(meta, packed, tail, theirs):
    return call(
        share_kernel,
        "share",
        pltpu.HBM(packed.shape, packed.dtype),
        in_specs=[WHOLE] * 3 + [ANYWHERE],
        out_specs=ANYWHERE,
        input_output_aliases={3: 0},
        scratch_shapes=[
            pltpu.VMEM(tail.shape, tail.dtype),
            pltpu.SemaphoreType.DMA((packed.shape[0],)),
        ],
        bytes_accessed=4 * 1024 * 1024,
    )(meta, tail, theirs, packed)


def lay_out(raw_ref, first, padded):
    n, _, rows, _ = raw_ref.shape
    total = n * rows
    zero = jnp.zeros((PAD, BLOCK), jnp.float32)
    for slot in range(padded.shape[0]):
        padded[slot, 0:PAD] = zero
        padded[slot, PAD + total : 2 * PAD + total] = zero
        for i in range(n):
            start = PAD + i * rows
            padded[slot, start : start + rows] = raw_ref[i, first + slot].astype(jnp.float32)


def norm_rows(padded, start, chunk, out_ref):
    total = out_ref.shape[0]
    base = PAD + start
    for slot in range(padded.shape[0]):
        raw = padded[slot, base : base + chunk]
        summed = raw
        for offset in range(1, HALF_WIN + 1):
            summed = summed + padded[slot, base - offset : base - offset + chunk]
            summed = summed + padded[slot, base + offset : base + offset + chunk]
        if start == 0 or start + chunk == total:
            frame = start + lax.broadcasted_iota(jnp.int32, (chunk, BLOCK), 0)
            upper = jnp.minimum(frame + HALF_WIN, total - 1)
            lower = jnp.maximum(frame - HALF_WIN, 0)
            mean = summed / (upper - lower + 1).astype(jnp.float32)
        else:
            mean = summed * (1.0 / (2 * HALF_WIN + 1))
        normed = jnp.where(summed > 0.0, raw / mean, 0.0)
        out_ref[start : start + chunk, slot * BLOCK : (slot + 1) * BLOCK] = normed.astype(
            jnp.bfloat16
        )


def norm_kernel(first, raw_ref, *refs):
    out_ref, padded = refs[-2:]
    lay_out(raw_ref, first, padded)
    for start in range(0, out_ref.shape[0], CHUNK):
        norm_rows(padded, start, CHUNK, out_ref)


def normalise(raw, first, slots, after=()):
    n, _, rows, _ = raw.shape
    total = n * rows
    return call(
        functools.partial(norm_kernel, first),
        "normalise",
        jax.ShapeDtypeStruct((total, slots * BLOCK), jnp.bfloat16),
        flops=12 * total * slots * BLOCK,
        bytes_accessed=4 * total * slots * BLOCK,
        in_specs=[WHOLE] + [ANYWHERE] * len(after),
        out_specs=WHOLE,
        scratch_shapes=[pltpu.VMEM((slots, total + 2 * PAD, BLOCK), jnp.float32)],
    )(raw, *after)


def dot_nt(a, b):
    return lax.dot_general(a, b, (((1,), (1,)), ((), ())), preferred_element_type=jnp.float32)


def set_left(ref, left_ref):
    rows = left_ref.shape[0] - ONES
    first_row = pl.multiple_of(lax.axis_index("pix") * rows, rows)
    left_ref[0:rows] = ref[pl.ds(first_row, rows), :]
    left_ref[rows : rows + ONES] = jnp.ones((ONES, ref.shape[1]), jnp.bfloat16)


def add_sums(pairs, sums, column):
    gram, frame = sums
    rows = pairs[0][0].shape[0] - ONES
    for left_ref, ref in pairs:
        both = dot_nt(left_ref[...], ref[column, :])
        gram = gram + both[0:rows]
        frame = frame + both[rows : rows + 8]
    return gram, frame


def partial_kernel(count, *refs):
    normed, lefts, (gram_out, frame_out) = refs[:count], refs[-count:], refs[-count - 2 : -count]
    before = refs[count : -count - 2]
    for ref, left_ref in zip(normed, lefts):
        set_left(ref, left_ref)
    for start in range(0, gram_out.shape[1], TILE):
        column = slice(start, start + TILE)
        sums = [ref[:, column] for ref in before] or [0.0, 0.0]
        gram_out[:, column], frame_out[:, column] = add_sums(
            list(zip(lefts, normed)), sums, column
        )


def sums_shape(total, parts):
    return [
        jax.ShapeDtypeStruct((total // parts, total), jnp.float32),
        jax.ShapeDtypeStruct((8, total), jnp.float32),
    ]


def partial_sums(normed, before, parts):
    total, width = normed[0].shape
    rows = total // parts
    return call(
        functools.partial(partial_kernel, len(normed)),
        "partial_sums",
        sums_shape(total, parts),
        flops=2 * rows * total * width * len(normed),
        bytes_accessed=4 * rows * total,
        in_specs=[WHOLE] * (len(normed) + len(before)),
        out_specs=[WHOLE] * 2,
        scratch_shapes=[pltpu.VMEM((rows + ONES, x.shape[1]), x.dtype) for x in normed],
    )(*normed, *before)


def norm_sums_kernel(first, raw_ref, done_ref, out_ref, gram_out, frame_out, padded, left_ref):
    total = out_ref.shape[0]
    tiles = total // TILE
    lay_out(raw_ref, first, padded)
    set_left(done_ref, left_ref)
    for i in range(tiles):
        column = slice(i * TILE, (i + 1) * TILE)
        gram_out[:, column], frame_out[:, column] = add_sums(
            [(left_ref, done_ref)], [0.0, 0.0], column
        )
        for start in range(i * TILE, (i + 1) * TILE, CHUNK):
            norm_rows(padded, start, CHUNK, out_ref)


def normalise_and_sum(raw, done, parts):
    n, slots, rows, _ = raw.shape
    total, width = done.shape
    first = width // BLOCK
    return call(
        functools.partial(norm_sums_kernel, first),
        "normalise_and_sum",
        [jax.ShapeDtypeStruct((total, (slots - first) * BLOCK), jnp.bfloat16)]
        + sums_shape(total, parts),
        flops=2 * total // parts * total * width,
        bytes_accessed=4 * total * total // parts,
        in_specs=[WHOLE] * 2,
        out_specs=[WHOLE] * 3,
        scratch_shapes=[
            pltpu.VMEM((slots - first, total + 2 * PAD, BLOCK), jnp.float32),
            pltpu.VMEM((total // parts + ONES, width), jnp.bfloat16),
        ],
    )(raw, done)


def result_kernel(meta_ref, their_meta_ref, normed_ref, gram_in, frame_in, out_hbm, *scratch):
    out_ref, frame_ref, sems = scratch
    rows, total = gram_in.shape
    pixels = meta_ref[PIXELS : PIXELS + 1, 0:BLOCK] + their_meta_ref[PIXELS : PIXELS + 1, 0:BLOCK]
    own = lax.broadcasted_iota(jnp.int32, (1, BLOCK), 1) == lax.axis_index("frame")
    number = jnp.sum(jnp.where(own, pixels, 0).astype(jnp.float32), axis=1, keepdims=True)
    ones = jnp.ones((8, normed_ref.shape[1]), jnp.bfloat16)
    frame_ref[...] = frame_in[...] + dot_nt(ones, normed_ref[...])
    first_row = pl.multiple_of(lax.axis_index("pix") * rows, rows)
    row_sum = jnp.broadcast_to(frame_ref[0:1, pl.ds(first_row, rows)], (BLOCK, rows)).T
    row_inv = 1.0 / row_sum[:, 0:1]
    left = normed_ref[pl.ds(first_row, rows), :]
    copies = []
    for i, start in enumerate(range(0, total, TILE)):
        column = slice(start, start + TILE)
        gram = gram_in[:, column] + dot_nt(left, normed_ref[column, :])
        col_inv = 1.0 / frame_ref[0:1, column]
        result = ((gram * row_inv) * col_inv) * number - 1.0
        out_ref[i] = result.astype(jnp.bfloat16)
        copies.append(
            pltpu.make_async_copy(out_ref.at[i], out_hbm.at[0, :, column], sems.at[i])
        )
        copies[-1].start()
    for copy in copies:
        copy.wait()


def correlate(metas, normed, before):
    rows, total = before[0].shape
    tiles = total // TILE
    return call(
        result_kernel,
        "correlate",
        pltpu.HBM((1, rows, total), jnp.bfloat16),
        flops=2 * rows * total * normed.shape[1],
        bytes_accessed=6 * rows * total,
        in_specs=[WHOLE] * 5,
        out_specs=ANYWHERE,
        scratch_shapes=[
            pltpu.VMEM((tiles, rows, TILE), jnp.bfloat16),
            pltpu.VMEM((8, total), jnp.float32),
            pltpu.SemaphoreType.DMA((tiles,)),
        ],
    )(*metas, normed, *before)


def body(frames, cycle_map):
    p_sec = frames.shape[1]
    n = lax.axis_size("frame")
    parts = lax.axis_size("pix")
    cap_blocks = p_sec // n // BLOCK
    half = (cap_blocks + 2) // 2
    move = cap_blocks - half
    lead = half - move
    early = half - half // 2
    cm = cycle_map.reshape(p_sec // BLOCK, BLOCK)

    def swap(x):
        return lax.ppermute(x, "pix", SWAP)

    def send(blocks):
        return lax.all_to_all(blocks, "frame", split_axis=0, concat_axis=0, tiled=True)

    moving, meta = pack_move(cm, frames, cap_blocks, move)
    theirs = swap(moving)
    packed, tail = pack_own(meta, cm, frames, cap_blocks, half, move)
    packed = share(meta, packed, tail, theirs)
    received = send(packed)

    meta, _ = lax.optimization_barrier((meta, packed))
    their_meta = swap(meta)
    counts, their_counts = meta[COUNT, :n], their_meta[COUNT, :n]
    overflow = jnp.max(counts + their_counts) > 2 * half

    first = normalise(received, 0, early, [overflow.astype(jnp.int32).reshape(1)])
    their_first = swap(first)
    last, *sums = normalise_and_sum(received, first, parts)
    their_last = swap(last)
    sums = partial_sums([last], sums, parts)
    sums = partial_sums([their_first], sums, parts)

    def spill(moving, meta, their_meta, their_last, *sums):
        moved = half - jnp.maximum(their_meta[COUNT, :n], lead)
        stays = jnp.arange(move, dtype=jnp.int32)[None, :] >= moved[:, None]
        rest = jnp.where(stays[:, :, None, None], moving, jnp.zeros((), moving.dtype))
        normed = normalise(send(rest), 0, move)
        sums = partial_sums([normed, swap(normed)], sums, parts)
        return correlate([meta, their_meta], their_last, sums)

    def fits(moving, meta, their_meta, their_last, *sums):
        return correlate([meta, their_meta], their_last, sums)

    return lax.cond(overflow, spill, fits, moving, meta, their_meta, their_last, *sums)


def solution(mesh):
    return jax.shard_map(
        body,
        mesh=mesh,
        in_specs=(P("frame", "pix"), P("pix")),
        out_specs=P("frame", "pix", None),
        check_vma=False,
    )
```

```python
import functools

import jax
import jax.numpy as jnp
from jax import lax
from jax.experimental import pallas as pl
from jax.experimental.pallas import tpu as pltpu
from jax.sharding import PartitionSpec as P

BLOCK = 128
HALF_WIN = 2
PAD = 8
TILE = 256
CHUNK = 128
ONES = 16
VMEM_BYTES = 32 * 1024 * 1024
LIST, COUNT, PIXELS = 0, 1, 2
MERGED = 2
SWAP = [(0, 1), (1, 0)]
WHOLE = pl.BlockSpec(memory_space=pltpu.VMEM)
ANYWHERE = pl.BlockSpec(memory_space=pl.ANY)


def call(kernel, name, out_shape, flops=0, bytes_accessed=0, limit=VMEM_BYTES, **kw):
    return pl.pallas_call(
        kernel,
        out_shape=out_shape,
        compiler_params=pltpu.CompilerParams(vmem_limit_bytes=limit),
        cost_estimate=pl.CostEstimate(
            flops=flops, bytes_accessed=bytes_accessed, transcendentals=0
        ),
        name=name,
        **kw,
    )


def dot_nt(a, b):
    return lax.dot_general(a, b, (((1,), (1,)), ((), ())), preferred_element_type=jnp.float32)


def count_half_rows(rows):
    return max(16, rows // 2)


def gate(wanted):
    wanted = jnp.broadcast_to(wanted, (1, BLOCK))
    return wanted.astype(jnp.float32).astype(jnp.bfloat16)


def take(frames_ref, block):
    return frames_ref[:, pl.ds(pl.multiple_of(block * BLOCK, BLOCK), BLOCK)]


def fold(block, right):
    rows = block.shape[0] // 2
    half = BLOCK // 2
    early, late = block[0:rows].astype(jnp.float32), block[rows:].astype(jnp.float32)
    left = lax.broadcasted_iota(jnp.int32, (rows, BLOCK), 1) < half
    if right:
        folded = jnp.where(left, pltpu.roll(early, half, 1), late)
    else:
        folded = jnp.where(left, early, pltpu.roll(late, half, 1))
    spare = count_half_rows(block.shape[0]) - rows
    if spare:
        folded = jnp.concatenate([folded, jnp.zeros((spare, BLOCK), jnp.float32)])
    return folded.astype(jnp.bfloat16)


def unfold(folded, rows):
    half = BLOCK // 2
    early = folded[0 : rows // 2].astype(jnp.float32)
    left = lax.broadcasted_iota(jnp.int32, early.shape, 1) < half
    return jnp.where(left, early, 0.0), jnp.where(left, pltpu.roll(early, half, 1), 0.0)


def find_members(cm):
    blocks = cm.shape[0]
    first = cm[:, 0:1]
    member = first == lax.broadcasted_iota(jnp.int32, (blocks, BLOCK), 1)
    row = lax.broadcasted_iota(jnp.int32, (blocks, blocks), 0)
    col = lax.broadcasted_iota(jnp.int32, (blocks, blocks), 1)
    earlier = (col < row).astype(jnp.float32).astype(jnp.bfloat16)
    pixels = jnp.sum((cm >= 0).astype(jnp.float32), axis=1, keepdims=True)
    return first, member.astype(jnp.float32), earlier, pixels


def sum_before(earlier, member, values):
    before = jnp.dot(
        earlier, (member * values).astype(jnp.bfloat16), preferred_element_type=jnp.float32
    )
    return jnp.sum(before * member, axis=1, keepdims=True)


def find_blocks(cm, cap_blocks, meta_ref):
    blocks = cm.shape[0]
    width = meta_ref.shape[1]
    first, member, earlier, pixels = find_members(cm)
    rank = sum_before(earlier, member, 1.0).astype(jnp.int32)
    slot = jnp.where(first >= 0, first * cap_blocks + rank, -1)
    hit = slot == lax.broadcasted_iota(jnp.int32, (blocks, width), 1)
    index = lax.broadcasted_iota(jnp.int32, (blocks, width), 0).astype(jnp.float32)
    meta_ref[...] = jnp.zeros_like(meta_ref)
    meta_ref[LIST : LIST + 1, :] = jnp.sum(
        jnp.where(hit, index, 0.0), axis=0, keepdims=True
    ).astype(jnp.int32)
    meta_ref[COUNT : COUNT + 1, 0:BLOCK] = jnp.sum(member, axis=0, keepdims=True).astype(
        jnp.int32
    )
    meta_ref[PIXELS : PIXELS + 1, 0:BLOCK] = jnp.sum(
        member * pixels, axis=0, keepdims=True
    ).astype(jnp.int32)


def find_places(cm):
    _, member, earlier, pixels = find_members(cm)
    valid = (cm >= 0).astype(jnp.float32)
    row = lax.broadcasted_iota(jnp.int32, (BLOCK, BLOCK), 0)
    col = lax.broadcasted_iota(jnp.int32, (BLOCK, BLOCK), 1)
    before = (row < col).astype(jnp.float32).astype(jnp.bfloat16)
    place = jnp.dot(valid.astype(jnp.bfloat16), before, preferred_element_type=jnp.float32)
    return jnp.where(cm >= 0, place + sum_before(earlier, member, pixels), -1.0)


def move_kernel(cap_blocks, cm_hbm, frames_hbm, out_ref, meta_ref, *scratch):
    frames_ref, cm_ref, meta_s, sems = scratch
    n = out_ref.shape[0]
    rows = frames_ref.shape[0]
    kept = cap_blocks // 2
    get_cm = pltpu.make_async_copy(cm_hbm, cm_ref, sems.at[0])
    get_cm.start()
    get_frames = pltpu.make_async_copy(frames_hbm, frames_ref, sems.at[1])
    get_frames.start()
    get_cm.wait()
    find_blocks(cm_ref[...], cap_blocks, meta_ref)
    to_scalars = pltpu.make_async_copy(meta_ref, meta_s, sems.at[2])
    to_scalars.start()
    to_scalars.wait()
    get_frames.wait()
    for q in range(n):
        full = gate(meta_s[PIXELS, q] == cap_blocks * BLOCK)
        for i in range(kept + 1, cap_blocks):
            block = meta_s[LIST, q * cap_blocks + i]
            start = (i - kept - 1) * rows
            out_ref[q, start : start + rows] = take(frames_ref, block) * full
        start = (cap_blocks - kept - 1) * rows
        end = start + count_half_rows(rows)
        block = meta_s[LIST, q * cap_blocks + kept]
        out_ref[q, start:end] = fold(take(frames_ref, block), True) * full
        out_ref[q, end : end + 16] = jnp.broadcast_to(full, (16, BLOCK))


def pack_move(cm, frames, cap_blocks):
    rows = frames.shape[0]
    n = cm.shape[0] // cap_blocks
    height = (cap_blocks - cap_blocks // 2 - 1) * rows + count_half_rows(rows) + 16
    meta = jax.ShapeDtypeStruct((8, cm.shape[0]), jnp.int32)
    return call(
        functools.partial(move_kernel, cap_blocks),
        "pack_move",
        [jax.ShapeDtypeStruct((n, height, BLOCK), frames.dtype), meta],
        in_specs=[ANYWHERE] * 2,
        out_specs=[WHOLE] * 2,
        scratch_shapes=[
            pltpu.VMEM(frames.shape, frames.dtype),
            pltpu.VMEM(cm.shape, cm.dtype),
            pltpu.SMEM(meta.shape, meta.dtype),
            pltpu.SemaphoreType.DMA((3,)),
        ],
    )(
        pltpu.with_memory_space_constraint(cm, pltpu.HBM),
        pltpu.with_memory_space_constraint(frames, pltpu.HBM),
    )


def own_kernel(cap_blocks, meta_s, cm_ref, frames_ref, out_ref, place_ref):
    n = out_ref.shape[0]
    rows = frames_ref.shape[0]
    kept = cap_blocks // 2
    place_ref[...] = find_places(cm_ref[...])
    target = lax.broadcasted_iota(jnp.int32, (BLOCK, BLOCK), 0).astype(jnp.float32)
    for q in range(n):
        count, pixels = meta_s[COUNT, q], meta_s[PIXELS, q]
        is_full = pixels == cap_blocks * BLOCK
        full = gate(is_full)
        fits = (pixels <= BLOCK) & (count <= MERGED)
        compact = 0.0
        for i in range(MERGED):
            block = meta_s[LIST, q * cap_blocks + i]
            place = jnp.where(fits & (i < count), place_ref[pl.ds(block, 1), :], -1.0)
            chosen = (target == place).astype(jnp.float32).astype(jnp.bfloat16)
            compact = compact + dot_nt(take(frames_ref, block), chosen)
        block = meta_s[LIST, q * cap_blocks]
        out_ref[q, 0:rows] = compact.astype(jnp.bfloat16) + take(frames_ref, block) * full
        for i in range(1, kept):
            block = meta_s[LIST, q * cap_blocks + i]
            out_ref[q, i * rows : (i + 1) * rows] = take(frames_ref, block) * full
        block = meta_s[LIST, q * cap_blocks + kept]
        out_ref[q, kept * rows :] = fold(take(frames_ref, block), False) * full


def pack_own(meta, cm, frames, cap_blocks):
    rows = frames.shape[0]
    n = cm.shape[0] // cap_blocks
    height = cap_blocks // 2 * rows + count_half_rows(rows)
    return call(
        functools.partial(own_kernel, cap_blocks),
        "pack_own",
        jax.ShapeDtypeStruct((n, height, BLOCK), frames.dtype),
        in_specs=[pl.BlockSpec(memory_space=pltpu.SMEM)] + [WHOLE] * 2,
        out_specs=WHOLE,
        scratch_shapes=[pltpu.VMEM(cm.shape, jnp.float32)],
        bytes_accessed=4 * 1024 * 1024,
    )(meta, cm, frames)


def share_kernel(cap_blocks, rows, meta_ref, own_ref, theirs_ref, out_hbm, out_ref, sems):
    n, height, _ = out_ref.shape
    second = lax.axis_index("pix") != 0
    pixels = meta_ref[PIXELS : PIXELS + 1, 0:BLOCK]
    for q in range(n):
        mine = jnp.broadcast_to(pixels[:, q : q + 1], (1, BLOCK)) == cap_blocks * BLOCK
        theirs = theirs_ref[q, height - rows : height - rows + 16][0:1].astype(jnp.float32) > 0.0
        helps = theirs & (second | jnp.logical_not(mine))
        first = gate(jnp.logical_not(helps & mine))
        own, other = gate(jnp.logical_not(helps)), gate(helps)
        out_ref[q, 0:rows] = own_ref[q, 0:rows] * first
        out_ref[q, rows:] = own_ref[q, rows:] * own + theirs_ref[q, 0 : height - rows] * other
        pltpu.make_async_copy(out_ref.at[q], out_hbm.at[q], sems.at[q]).start()
    for q in range(n):
        pltpu.make_async_copy(out_ref.at[q], out_hbm.at[q], sems.at[q]).wait()


def share(meta, own, theirs, cap_blocks, rows):
    return call(
        functools.partial(share_kernel, cap_blocks, rows),
        "share",
        pltpu.HBM(own.shape, own.dtype),
        in_specs=[WHOLE] * 3,
        out_specs=ANYWHERE,
        scratch_shapes=[
            pltpu.VMEM(own.shape, own.dtype),
            pltpu.SemaphoreType.DMA((own.shape[0],)),
        ],
        bytes_accessed=4 * 1024 * 1024,
    )(meta, own, theirs)


def left_out(meta, their_meta, cap, second):
    mine, theirs = meta[PIXELS] == cap, their_meta[PIXELS] == cap
    fits = (meta[PIXELS] <= BLOCK) & (meta[COUNT] <= MERGED)
    return theirs & (second | jnp.logical_not(mine)) & jnp.logical_not(fits)


def rest_kernel(cap_blocks, meta_s, their_meta_s, frames_ref, cm_ref, out_ref):
    n, _, rows, _ = out_ref.shape
    second = lax.axis_index("pix") != 0
    for q in range(n):
        counts = [[ref[row, q] for row in range(PIXELS + 1)] for ref in (meta_s, their_meta_s)]
        wanted = left_out(*counts, cap_blocks * BLOCK, second)
        for i in range(cap_blocks):
            block = meta_s[LIST, q * cap_blocks + i]
            valid = cm_ref[pl.ds(block, 1), :] >= 0
            out_ref[q, i] = take(frames_ref, block) * gate(
                valid & wanted & (i < meta_s[COUNT, q])
            )


def pack_rest(meta, their_meta, frames, cm, cap_blocks):
    n = cm.shape[0] // cap_blocks
    return call(
        functools.partial(rest_kernel, cap_blocks),
        "pack_rest",
        jax.ShapeDtypeStruct((n, cap_blocks, frames.shape[0], BLOCK), frames.dtype),
        in_specs=[pl.BlockSpec(memory_space=pltpu.SMEM)] * 2 + [WHOLE] * 2,
        out_specs=WHOLE,
    )(meta, their_meta, frames, cm)


def lay_out(raw_ref, rows, first, padded):
    n, height, _ = raw_ref.shape
    total = n * rows
    zero = jnp.zeros((PAD, BLOCK), jnp.float32)
    for i in range(padded.shape[0]):
        slot = first + i
        padded[i, 0:PAD] = zero
        padded[i, PAD + total : 2 * PAD + total] = zero
        for source in range(n):
            start = PAD + source * rows
            if (slot + 1) * rows <= height:
                block = raw_ref[source, slot * rows : (slot + 1) * rows]
                padded[i, start : start + rows] = block.astype(jnp.float32)
            else:
                early, late = unfold(raw_ref[source, slot * rows : height], rows)
                padded[i, start : start + rows // 2] = early
                padded[i, start + rows // 2 : start + rows] = late


def norm_rows(padded, start, chunk, out_ref):
    total = out_ref.shape[0]
    base = PAD + start
    for slot in range(padded.shape[0]):
        raw = padded[slot, base : base + chunk]
        summed = raw
        for offset in range(1, HALF_WIN + 1):
            summed = summed + padded[slot, base - offset : base - offset + chunk]
            summed = summed + padded[slot, base + offset : base + offset + chunk]
        if start == 0 or start + chunk == total:
            frame = start + lax.broadcasted_iota(jnp.int32, (chunk, BLOCK), 0)
            upper = jnp.minimum(frame + HALF_WIN, total - 1)
            lower = jnp.maximum(frame - HALF_WIN, 0)
            mean = summed / (upper - lower + 1).astype(jnp.float32)
        else:
            mean = summed * (1.0 / (2 * HALF_WIN + 1))
        normed = jnp.where(summed > 0.0, raw / mean, 0.0)
        out_ref[start : start + chunk, slot * BLOCK : (slot + 1) * BLOCK] = normed.astype(
            jnp.bfloat16
        )


def norm_kernel(rows, raw_ref, *refs):
    out_ref, padded = refs[-2:]
    lay_out(raw_ref, rows, 0, padded)
    for start in range(0, out_ref.shape[0], CHUNK):
        norm_rows(padded, start, CHUNK, out_ref)


def normalise(raw, total, slots, after=()):
    return call(
        functools.partial(norm_kernel, total // raw.shape[0]),
        "normalise",
        jax.ShapeDtypeStruct((total, slots * BLOCK), jnp.bfloat16),
        flops=12 * total * slots * BLOCK,
        bytes_accessed=4 * total * slots * BLOCK,
        in_specs=[WHOLE] + [ANYWHERE] * len(after),
        out_specs=WHOLE,
        scratch_shapes=[pltpu.VMEM((slots, total + 2 * PAD, BLOCK), jnp.float32)],
    )(raw, *after)


def set_left(ref, left_ref):
    rows = left_ref.shape[0] - ONES
    first_row = pl.multiple_of(lax.axis_index("pix") * rows, rows)
    left_ref[0:rows] = ref[pl.ds(first_row, rows), :]
    left_ref[rows : rows + ONES] = jnp.ones((ONES, ref.shape[1]), jnp.bfloat16)


def add_sums(pairs, sums, column):
    gram, frame = sums
    rows = pairs[0][0].shape[0] - ONES
    for left_ref, ref in pairs:
        both = dot_nt(left_ref[...], ref[column, :])
        gram = gram + both[0:rows]
        frame = frame + both[rows : rows + 8]
    return gram, frame


def partial_kernel(count, *refs):
    normed, lefts, (gram_out, frame_out) = refs[:count], refs[-count:], refs[-count - 2 : -count]
    before = refs[count : -count - 2]
    for ref, left_ref in zip(normed, lefts):
        set_left(ref, left_ref)
    for start in range(0, gram_out.shape[1], TILE):
        column = slice(start, start + TILE)
        sums = [ref[:, column] for ref in before] or [0.0, 0.0]
        gram_out[:, column], frame_out[:, column] = add_sums(
            list(zip(lefts, normed)), sums, column
        )


def sums_shape(total, parts):
    return [
        jax.ShapeDtypeStruct((total // parts, total), jnp.float32),
        jax.ShapeDtypeStruct((8, total), jnp.float32),
    ]


def partial_sums(normed, before, parts):
    total, width = normed[0].shape
    rows = total // parts
    return call(
        functools.partial(partial_kernel, len(normed)),
        "partial_sums",
        sums_shape(total, parts),
        flops=2 * rows * total * width * len(normed),
        bytes_accessed=4 * rows * total,
        in_specs=[WHOLE] * (len(normed) + len(before)),
        out_specs=[WHOLE] * 2,
        scratch_shapes=[pltpu.VMEM((rows + ONES, x.shape[1]), x.dtype) for x in normed],
    )(*normed, *before)


def norm_sums_kernel(rows, first, raw_ref, done_ref, out_ref, gram_out, frame_out, padded, left_ref):
    total = out_ref.shape[0]
    tiles = total // TILE
    lay_out(raw_ref, rows, first, padded)
    set_left(done_ref, left_ref)
    for i in range(tiles):
        column = slice(i * TILE, (i + 1) * TILE)
        gram_out[:, column], frame_out[:, column] = add_sums(
            [(left_ref, done_ref)], [0.0, 0.0], column
        )
        for start in range(i * TILE, (i + 1) * TILE, CHUNK):
            norm_rows(padded, start, CHUNK, out_ref)


def normalise_and_sum(raw, done, slots, parts):
    total, width = done.shape
    first = width // BLOCK
    return call(
        functools.partial(norm_sums_kernel, total // raw.shape[0], first),
        "normalise_and_sum",
        [jax.ShapeDtypeStruct((total, (slots - first) * BLOCK), jnp.bfloat16)]
        + sums_shape(total, parts),
        flops=2 * total // parts * total * width,
        bytes_accessed=4 * total * total // parts,
        in_specs=[WHOLE] * 2,
        out_specs=[WHOLE] * 3,
        scratch_shapes=[
            pltpu.VMEM((slots - first, total + 2 * PAD, BLOCK), jnp.float32),
            pltpu.VMEM((total // parts + ONES, width), jnp.bfloat16),
        ],
    )(raw, done)


def result_kernel(meta_ref, their_meta_ref, normed_ref, gram_in, frame_in, out_hbm, *scratch):
    out_ref, frame_ref, sems = scratch
    rows, total = gram_in.shape
    pixels = meta_ref[PIXELS : PIXELS + 1, 0:BLOCK] + their_meta_ref[PIXELS : PIXELS + 1, 0:BLOCK]
    own = lax.broadcasted_iota(jnp.int32, (1, BLOCK), 1) == lax.axis_index("frame")
    number = jnp.sum(jnp.where(own, pixels, 0).astype(jnp.float32), axis=1, keepdims=True)
    ones = jnp.ones((8, normed_ref.shape[1]), jnp.bfloat16)
    frame_ref[...] = frame_in[...] + dot_nt(ones, normed_ref[...])
    first_row = pl.multiple_of(lax.axis_index("pix") * rows, rows)
    row_sum = jnp.broadcast_to(frame_ref[0:1, pl.ds(first_row, rows)], (BLOCK, rows)).T
    row_inv = 1.0 / row_sum[:, 0:1]
    left = normed_ref[pl.ds(first_row, rows), :]
    copies = []
    for i, start in enumerate(range(0, total, TILE)):
        column = slice(start, start + TILE)
        gram = gram_in[:, column] + dot_nt(left, normed_ref[column, :])
        col_inv = 1.0 / frame_ref[0:1, column]
        result = ((gram * row_inv) * col_inv) * number - 1.0
        out_ref[i] = result.astype(jnp.bfloat16)
        copies.append(
            pltpu.make_async_copy(out_ref.at[i], out_hbm.at[0, :, column], sems.at[i])
        )
        copies[-1].start()
    for copy in copies:
        copy.wait()


def correlate(metas, normed, before):
    rows, total = before[0].shape
    tiles = total // TILE
    return call(
        result_kernel,
        "correlate",
        pltpu.HBM((1, rows, total), jnp.bfloat16),
        flops=2 * rows * total * normed.shape[1],
        bytes_accessed=6 * rows * total,
        in_specs=[WHOLE] * 5,
        out_specs=ANYWHERE,
        scratch_shapes=[
            pltpu.VMEM((tiles, rows, TILE), jnp.bfloat16),
            pltpu.VMEM((8, total), jnp.float32),
            pltpu.SemaphoreType.DMA((tiles,)),
        ],
    )(*metas, normed, *before)


def body(frames, cycle_map):
    rows, p_sec = frames.shape
    n = lax.axis_size("frame")
    parts = lax.axis_size("pix")
    total = n * rows
    cap_blocks = p_sec // n // BLOCK
    slots = cap_blocks // 2 + 1
    early = slots - slots // 2
    cm = cycle_map.reshape(p_sec // BLOCK, BLOCK)

    def swap(x):
        return lax.ppermute(x, "pix", SWAP)

    def send(blocks):
        return lax.all_to_all(blocks, "frame", split_axis=0, concat_axis=0, tiled=True)

    moving, meta = pack_move(cm, frames, cap_blocks)
    theirs = swap(moving)
    packed = share(meta, pack_own(meta, cm, frames, cap_blocks), theirs, cap_blocks, rows)
    received = send(packed)

    meta, _ = lax.optimization_barrier((meta, packed))
    their_meta = swap(meta)
    second = lax.axis_index("pix") != 0
    spills = left_out(meta[:, :n], their_meta[:, :n], cap_blocks * BLOCK, second)
    spills |= left_out(their_meta[:, :n], meta[:, :n], cap_blocks * BLOCK, jnp.logical_not(second))
    overflow = jnp.any(spills)

    first = normalise(received, total, early, [overflow.astype(jnp.int32).reshape(1)])
    their_first = swap(first)
    last, *sums = normalise_and_sum(received, first, slots, parts)
    their_last = swap(last)
    sums = partial_sums([last], sums, parts)
    sums = partial_sums([their_first], sums, parts)

    def spill(frames, cm, meta, their_meta, their_last, *sums):
        rest = send(pack_rest(meta, their_meta, frames, cm, cap_blocks))
        normed = normalise(rest.reshape(n, cap_blocks * rows, BLOCK), total, cap_blocks)
        sums = partial_sums([normed, swap(normed)], sums, parts)
        return correlate([meta, their_meta], their_last, sums)

    def fits(frames, cm, meta, their_meta, their_last, *sums):
        return correlate([meta, their_meta], their_last, sums)

    return lax.cond(overflow, spill, fits, frames, cm, meta, their_meta, their_last, *sums)


def solution(mesh):
    return jax.shard_map(
        body,
        mesh=mesh,
        in_specs=(P("frame", "pix"), P("pix")),
        out_specs=P("frame", "pix", None),
        check_vma=False,
    )
```

```python
import functools

import jax
import jax.numpy as jnp
from jax import lax
from jax.experimental import pallas as pl
from jax.experimental.pallas import tpu as pltpu
from jax.sharding import PartitionSpec as P

BLOCK = 128
HALF_WIN = 2
PAD = 8
TILE = 256
CHUNK = 128
ONES = 16
VMEM_BYTES = 32 * 1024 * 1024
LIST, COUNT, PIXELS = 0, 1, 2
MARK = 16
MERGED = 2
SWAP = [(0, 1), (1, 0)]
WHOLE = pl.BlockSpec(memory_space=pltpu.VMEM)
ANYWHERE = pl.BlockSpec(memory_space=pl.ANY)


def call(kernel, name, out_shape, flops=0, bytes_accessed=0, limit=VMEM_BYTES, **kw):
    return pl.pallas_call(
        kernel,
        out_shape=out_shape,
        compiler_params=pltpu.CompilerParams(vmem_limit_bytes=limit),
        cost_estimate=pl.CostEstimate(
            flops=flops, bytes_accessed=bytes_accessed, transcendentals=0
        ),
        name=name,
        **kw,
    )


def dot_nt(a, b):
    return lax.dot_general(a, b, (((1,), (1,)), ((), ())), preferred_element_type=jnp.float32)


def count_half_rows(rows):
    return max(16, rows // 2)


def gate(wanted):
    wanted = jnp.broadcast_to(wanted, (1, BLOCK))
    return wanted.astype(jnp.float32).astype(jnp.bfloat16)


def take(frames_ref, block):
    return frames_ref[:, pl.ds(pl.multiple_of(block * BLOCK, BLOCK), BLOCK)]


def fold(block, right):
    rows = block.shape[0] // 2
    half = BLOCK // 2
    early, late = block[0:rows].astype(jnp.float32), block[rows:].astype(jnp.float32)
    left = lax.broadcasted_iota(jnp.int32, (rows, BLOCK), 1) < half
    if right:
        folded = jnp.where(left, pltpu.roll(early, half, 1), late)
    else:
        folded = jnp.where(left, early, pltpu.roll(late, half, 1))
    spare = count_half_rows(block.shape[0]) - rows
    if spare:
        folded = jnp.concatenate([folded, jnp.zeros((spare, BLOCK), jnp.float32)])
    return folded.astype(jnp.bfloat16)


def unfold(folded, rows):
    half = BLOCK // 2
    early = folded[0 : rows // 2].astype(jnp.float32)
    left = lax.broadcasted_iota(jnp.int32, early.shape, 1) < half
    return jnp.where(left, early, 0.0), jnp.where(left, pltpu.roll(early, half, 1), 0.0)


def find_members(cm):
    blocks = cm.shape[0]
    first = cm[:, 0:1]
    member = first == lax.broadcasted_iota(jnp.int32, (blocks, BLOCK), 1)
    row = lax.broadcasted_iota(jnp.int32, (blocks, blocks), 0)
    col = lax.broadcasted_iota(jnp.int32, (blocks, blocks), 1)
    earlier = (col < row).astype(jnp.float32).astype(jnp.bfloat16)
    pixels = jnp.sum((cm >= 0).astype(jnp.float32), axis=1, keepdims=True)
    return first, member.astype(jnp.float32), earlier, pixels


def sum_before(earlier, member, values):
    before = jnp.dot(
        earlier, (member * values).astype(jnp.bfloat16), preferred_element_type=jnp.float32
    )
    return jnp.sum(before * member, axis=1, keepdims=True)


def find_blocks(cm, cap_blocks, meta_ref):
    blocks = cm.shape[0]
    width = meta_ref.shape[1]
    first, member, earlier, pixels = find_members(cm)
    rank = sum_before(earlier, member, 1.0).astype(jnp.int32)
    slot = jnp.where(first >= 0, first * cap_blocks + rank, -1)
    hit = slot == lax.broadcasted_iota(jnp.int32, (blocks, width), 1)
    index = lax.broadcasted_iota(jnp.int32, (blocks, width), 0).astype(jnp.float32)
    meta_ref[...] = jnp.zeros_like(meta_ref)
    meta_ref[LIST : LIST + 1, :] = jnp.sum(
        jnp.where(hit, index, 0.0), axis=0, keepdims=True
    ).astype(jnp.int32)
    meta_ref[COUNT : COUNT + 1, 0:BLOCK] = jnp.sum(member, axis=0, keepdims=True).astype(
        jnp.int32
    )
    meta_ref[PIXELS : PIXELS + 1, 0:BLOCK] = jnp.sum(
        member * pixels, axis=0, keepdims=True
    ).astype(jnp.int32)


def find_places(cm):
    _, member, earlier, pixels = find_members(cm)
    valid = (cm >= 0).astype(jnp.float32)
    row = lax.broadcasted_iota(jnp.int32, (BLOCK, BLOCK), 0)
    col = lax.broadcasted_iota(jnp.int32, (BLOCK, BLOCK), 1)
    before = (row < col).astype(jnp.float32).astype(jnp.bfloat16)
    place = jnp.dot(valid.astype(jnp.bfloat16), before, preferred_element_type=jnp.float32)
    return jnp.where(cm >= 0, place + sum_before(earlier, member, pixels), -1.0)


def move_kernel(cap_blocks, cm_hbm, frames_hbm, out_ref, meta_ref, *scratch):
    frames_ref, cm_ref, meta_s, sems = scratch
    n = out_ref.shape[0]
    rows = frames_ref.shape[0]
    kept = cap_blocks // 2
    get_cm = pltpu.make_async_copy(cm_hbm, cm_ref, sems.at[0])
    get_cm.start()
    get_frames = pltpu.make_async_copy(frames_hbm, frames_ref, sems.at[1])
    get_frames.start()
    get_cm.wait()
    find_blocks(cm_ref[...], cap_blocks, meta_ref)
    to_scalars = pltpu.make_async_copy(meta_ref, meta_s, sems.at[2])
    to_scalars.start()
    to_scalars.wait()
    get_frames.wait()
    for q in range(n):
        full = gate(meta_s[PIXELS, q] == cap_blocks * BLOCK)
        for i in range(kept + 1, cap_blocks):
            block = meta_s[LIST, q * cap_blocks + i]
            start = (i - kept - 1) * rows
            out_ref[q, start : start + rows] = take(frames_ref, block) * full
        start = (cap_blocks - kept - 1) * rows
        end = start + count_half_rows(rows)
        block = meta_s[LIST, q * cap_blocks + kept]
        out_ref[q, start:end] = fold(take(frames_ref, block), True) * full
        out_ref[q, end : end + MARK] = jnp.broadcast_to(full, (MARK, BLOCK))


def pack_move(cm, frames, cap_blocks):
    rows = frames.shape[0]
    n = cm.shape[0] // cap_blocks
    height = (cap_blocks - cap_blocks // 2 - 1) * rows + count_half_rows(rows) + MARK
    meta = jax.ShapeDtypeStruct((8, cm.shape[0]), jnp.int32)
    return call(
        functools.partial(move_kernel, cap_blocks),
        "pack_move",
        [jax.ShapeDtypeStruct((n, height, BLOCK), frames.dtype), meta],
        in_specs=[ANYWHERE] * 2,
        out_specs=[WHOLE] * 2,
        scratch_shapes=[
            pltpu.VMEM(frames.shape, frames.dtype),
            pltpu.VMEM(cm.shape, cm.dtype),
            pltpu.SMEM(meta.shape, meta.dtype),
            pltpu.SemaphoreType.DMA((3,)),
        ],
    )(
        pltpu.with_memory_space_constraint(cm, pltpu.HBM),
        pltpu.with_memory_space_constraint(frames, pltpu.HBM),
    )


def own_kernel(cap_blocks, meta_s, cm_ref, frames_ref, out_ref, place_ref):
    n = out_ref.shape[0]
    rows = frames_ref.shape[0]
    kept = cap_blocks // 2
    place_ref[...] = find_places(cm_ref[...])
    target = lax.broadcasted_iota(jnp.int32, (BLOCK, BLOCK), 0).astype(jnp.float32)
    for q in range(n):
        count, pixels = meta_s[COUNT, q], meta_s[PIXELS, q]
        is_full = pixels == cap_blocks * BLOCK
        full = gate(is_full)
        fits = (pixels <= BLOCK) & (count <= MERGED)
        compact = 0.0
        for i in range(MERGED):
            block = meta_s[LIST, q * cap_blocks + i]
            place = jnp.where(fits & (i < count), place_ref[pl.ds(block, 1), :], -1.0)
            chosen = (target == place).astype(jnp.float32).astype(jnp.bfloat16)
            compact = compact + dot_nt(take(frames_ref, block), chosen)
        block = meta_s[LIST, q * cap_blocks]
        out_ref[q, 0:rows] = compact.astype(jnp.bfloat16) + take(frames_ref, block) * full
        for i in range(1, kept):
            block = meta_s[LIST, q * cap_blocks + i]
            out_ref[q, i * rows : (i + 1) * rows] = take(frames_ref, block) * full
        block = meta_s[LIST, q * cap_blocks + kept]
        end = kept * rows + count_half_rows(rows)
        out_ref[q, kept * rows : end] = fold(take(frames_ref, block), False) * full
        out_ref[q, end : end + MARK] = jnp.broadcast_to(full, (MARK, BLOCK))


def pack_own(meta, cm, frames, cap_blocks):
    rows = frames.shape[0]
    n = cm.shape[0] // cap_blocks
    height = cap_blocks // 2 * rows + count_half_rows(rows) + MARK
    return call(
        functools.partial(own_kernel, cap_blocks),
        "pack_own",
        jax.ShapeDtypeStruct((n, height, BLOCK), frames.dtype),
        in_specs=[pl.BlockSpec(memory_space=pltpu.SMEM)] + [WHOLE] * 2,
        out_specs=WHOLE,
        scratch_shapes=[pltpu.VMEM(cm.shape, jnp.float32)],
        bytes_accessed=4 * 1024 * 1024,
    )(meta, cm, frames)


def combine(own_ref, theirs_ref, q, rows, out_ref):
    height = out_ref.shape[0]
    mine = own_ref[q, height : height + MARK][0:1].astype(jnp.float32) > 0.0
    theirs = theirs_ref[q, height - rows : height - rows + MARK][0:1].astype(jnp.float32) > 0.0
    helps = theirs & ((lax.axis_index("pix") != 0) | jnp.logical_not(mine))
    first = gate(jnp.logical_not(helps & mine))
    own, other = gate(jnp.logical_not(helps)), gate(helps)
    out_ref[0:rows] = own_ref[q, 0:rows] * first
    out_ref[rows:] = own_ref[q, rows:height] * own + theirs_ref[q, 0 : height - rows] * other


def far_kernel(rows, own_ref, theirs_ref, *pieces):
    half_n = len(pieces)
    for k, piece in enumerate(pieces):
        combine(own_ref, theirs_ref, lax.axis_index("frame") ^ (half_n + k), rows, piece)


def pack_far(own, theirs, rows):
    n, height, _ = own.shape
    return call(
        functools.partial(far_kernel, rows),
        "pack_far",
        [jax.ShapeDtypeStruct((height - MARK, BLOCK), own.dtype)] * (n // 2),
        in_specs=[WHOLE] * 2,
        out_specs=[WHOLE] * (n // 2),
        bytes_accessed=4 * 1024 * 1024,
    )(own, theirs)


def near_kernel(rows, own_ref, theirs_ref, _, out_hbm, out_ref, sems):
    half_n = out_ref.shape[0]
    base = lax.axis_index("frame") // half_n * half_n
    for i in range(half_n):
        combine(own_ref, theirs_ref, base + i, rows, out_ref.at[i])
        pltpu.make_async_copy(out_ref.at[i], out_hbm.at[i], sems.at[i]).start()
    for i in range(half_n):
        pltpu.make_async_copy(out_ref.at[i], out_hbm.at[i], sems.at[i]).wait()


def pack_near(own, theirs, after, rows):
    n, height, _ = own.shape
    shape = (n // 2, height - MARK, BLOCK)
    return call(
        functools.partial(near_kernel, rows),
        "pack_near",
        pltpu.HBM(shape, own.dtype),
        in_specs=[WHOLE] * 2 + [ANYWHERE],
        out_specs=ANYWHERE,
        scratch_shapes=[pltpu.VMEM(shape, own.dtype), pltpu.SemaphoreType.DMA((n // 2,))],
        bytes_accessed=4 * 1024 * 1024,
    )(own, theirs, after)


def left_out(meta, their_meta, cap, second):
    mine, theirs = meta[PIXELS] == cap, their_meta[PIXELS] == cap
    fits = (meta[PIXELS] <= BLOCK) & (meta[COUNT] <= MERGED)
    return theirs & (second | jnp.logical_not(mine)) & jnp.logical_not(fits)


def rest_kernel(cap_blocks, meta_s, their_meta_s, frames_ref, cm_ref, out_ref):
    n, _, rows, _ = out_ref.shape
    second = lax.axis_index("pix") != 0
    for q in range(n):
        counts = [[ref[row, q] for row in range(PIXELS + 1)] for ref in (meta_s, their_meta_s)]
        wanted = left_out(*counts, cap_blocks * BLOCK, second)
        for i in range(cap_blocks):
            block = meta_s[LIST, q * cap_blocks + i]
            valid = cm_ref[pl.ds(block, 1), :] >= 0
            out_ref[q, i] = take(frames_ref, block) * gate(
                valid & wanted & (i < meta_s[COUNT, q])
            )


def pack_rest(meta, their_meta, frames, cm, cap_blocks):
    n = cm.shape[0] // cap_blocks
    return call(
        functools.partial(rest_kernel, cap_blocks),
        "pack_rest",
        jax.ShapeDtypeStruct((n, cap_blocks, frames.shape[0], BLOCK), frames.dtype),
        in_specs=[pl.BlockSpec(memory_space=pltpu.SMEM)] * 2 + [WHOLE] * 2,
        out_specs=WHOLE,
    )(meta, their_meta, frames, cm)


def list_sources(refs):
    me = lax.axis_index("frame")
    if len(refs) == 1:
        return [(refs[0].at[i], i) for i in range(refs[0].shape[0])]
    half_n = refs[0].shape[0]
    near = [(refs[0].at[i], me // half_n * half_n + i) for i in range(half_n)]
    return near + [(ref, me ^ (half_n + k)) for k, ref in enumerate(refs[1:])]


def lay_out(refs, rows, first, padded):
    sources = list_sources(refs)
    total = len(sources) * rows
    zero = jnp.zeros((PAD, BLOCK), jnp.float32)
    for i in range(padded.shape[0]):
        slot = first + i
        padded[i, 0:PAD] = zero
        padded[i, PAD + total : 2 * PAD + total] = zero
        for ref, device in sources:
            height = ref.shape[0]
            start = pl.multiple_of(PAD + device * rows, PAD)
            if (slot + 1) * rows <= height:
                block = ref[slot * rows : (slot + 1) * rows].astype(jnp.float32)
                padded[i, pl.ds(start, rows)] = block
            else:
                halves = unfold(ref[slot * rows : height], rows)
                for part, values in enumerate(halves):
                    place = pl.ds(pl.multiple_of(start + part * (rows // 2), PAD), rows // 2)
                    padded[i, place] = values


def norm_rows(padded, start, chunk, out_ref):
    total = out_ref.shape[0]
    base = PAD + start
    for slot in range(padded.shape[0]):
        raw = padded[slot, base : base + chunk]
        summed = raw
        for offset in range(1, HALF_WIN + 1):
            summed = summed + padded[slot, base - offset : base - offset + chunk]
            summed = summed + padded[slot, base + offset : base + offset + chunk]
        if start == 0 or start + chunk == total:
            frame = start + lax.broadcasted_iota(jnp.int32, (chunk, BLOCK), 0)
            upper = jnp.minimum(frame + HALF_WIN, total - 1)
            lower = jnp.maximum(frame - HALF_WIN, 0)
            mean = summed / (upper - lower + 1).astype(jnp.float32)
        else:
            mean = summed * (1.0 / (2 * HALF_WIN + 1))
        normed = jnp.where(summed > 0.0, raw / mean, 0.0)
        out_ref[start : start + chunk, slot * BLOCK : (slot + 1) * BLOCK] = normed.astype(
            jnp.bfloat16
        )


def norm_kernel(count, rows, first, *refs):
    out_ref, padded = refs[-2:]
    lay_out(refs[:count], rows, first, padded)
    for start in range(0, out_ref.shape[0], CHUNK):
        norm_rows(padded, start, CHUNK, out_ref)


def normalise(raws, total, first, slots, after=()):
    sources = len(raws) - 1 + raws[0].shape[0]
    return call(
        functools.partial(norm_kernel, len(raws), total // sources, first),
        "normalise",
        jax.ShapeDtypeStruct((total, slots * BLOCK), jnp.bfloat16),
        flops=12 * total * slots * BLOCK,
        bytes_accessed=4 * total * slots * BLOCK,
        in_specs=[WHOLE] * len(raws) + [ANYWHERE] * len(after),
        out_specs=WHOLE,
        scratch_shapes=[pltpu.VMEM((slots, total + 2 * PAD, BLOCK), jnp.float32)],
    )(*raws, *after)


def set_left(ref, left_ref):
    rows = left_ref.shape[0] - ONES
    first_row = pl.multiple_of(lax.axis_index("pix") * rows, rows)
    left_ref[0:rows] = ref[pl.ds(first_row, rows), :]
    left_ref[rows : rows + ONES] = jnp.ones((ONES, ref.shape[1]), jnp.bfloat16)


def add_sums(pairs, sums, column):
    gram, frame = sums
    rows = pairs[0][0].shape[0] - ONES
    for left_ref, ref in pairs:
        both = dot_nt(left_ref[...], ref[column, :])
        gram = gram + both[0:rows]
        frame = frame + both[rows : rows + 8]
    return gram, frame


def partial_kernel(count, *refs):
    normed, lefts, (gram_out, frame_out) = refs[:count], refs[-count:], refs[-count - 2 : -count]
    before = refs[count : -count - 2]
    for ref, left_ref in zip(normed, lefts):
        set_left(ref, left_ref)
    for start in range(0, gram_out.shape[1], TILE):
        column = slice(start, start + TILE)
        sums = [ref[:, column] for ref in before] or [0.0, 0.0]
        gram_out[:, column], frame_out[:, column] = add_sums(
            list(zip(lefts, normed)), sums, column
        )


def sums_shape(total, parts):
    return [
        jax.ShapeDtypeStruct((total // parts, total), jnp.float32),
        jax.ShapeDtypeStruct((8, total), jnp.float32),
    ]


def partial_sums(normed, before, parts):
    total, width = normed[0].shape
    rows = total // parts
    return call(
        functools.partial(partial_kernel, len(normed)),
        "partial_sums",
        sums_shape(total, parts),
        flops=2 * rows * total * width * len(normed),
        bytes_accessed=4 * rows * total,
        in_specs=[WHOLE] * (len(normed) + len(before)),
        out_specs=[WHOLE] * 2,
        scratch_shapes=[pltpu.VMEM((rows + ONES, x.shape[1]), x.dtype) for x in normed],
    )(*normed, *before)


def result_kernel(meta_ref, their_meta_ref, normed_ref, gram_in, frame_in, out_hbm, *scratch):
    out_ref, frame_ref, sems = scratch
    rows, total = gram_in.shape
    pixels = meta_ref[PIXELS : PIXELS + 1, 0:BLOCK] + their_meta_ref[PIXELS : PIXELS + 1, 0:BLOCK]
    own = lax.broadcasted_iota(jnp.int32, (1, BLOCK), 1) == lax.axis_index("frame")
    number = jnp.sum(jnp.where(own, pixels, 0).astype(jnp.float32), axis=1, keepdims=True)
    ones = jnp.ones((8, normed_ref.shape[1]), jnp.bfloat16)
    frame_ref[...] = frame_in[...] + dot_nt(ones, normed_ref[...])
    first_row = pl.multiple_of(lax.axis_index("pix") * rows, rows)
    row_sum = jnp.broadcast_to(frame_ref[0:1, pl.ds(first_row, rows)], (BLOCK, rows)).T
    row_inv = 1.0 / row_sum[:, 0:1]
    left = normed_ref[pl.ds(first_row, rows), :]
    copies = []
    for i, start in enumerate(range(0, total, TILE)):
        column = slice(start, start + TILE)
        gram = gram_in[:, column] + dot_nt(left, normed_ref[column, :])
        col_inv = 1.0 / frame_ref[0:1, column]
        result = ((gram * row_inv) * col_inv) * number - 1.0
        out_ref[i] = result.astype(jnp.bfloat16)
        copies.append(
            pltpu.make_async_copy(out_ref.at[i], out_hbm.at[0, :, column], sems.at[i])
        )
        copies[-1].start()
    for copy in copies:
        copy.wait()


def correlate(metas, normed, before):
    rows, total = before[0].shape
    tiles = total // TILE
    return call(
        result_kernel,
        "correlate",
        pltpu.HBM((1, rows, total), jnp.bfloat16),
        flops=2 * rows * total * normed.shape[1],
        bytes_accessed=6 * rows * total,
        in_specs=[WHOLE] * 5,
        out_specs=ANYWHERE,
        scratch_shapes=[
            pltpu.VMEM((tiles, rows, TILE), jnp.bfloat16),
            pltpu.VMEM((8, total), jnp.float32),
            pltpu.SemaphoreType.DMA((tiles,)),
        ],
    )(*metas, normed, *before)


def body(frames, cycle_map):
    rows, p_sec = frames.shape
    n = lax.axis_size("frame")
    parts = lax.axis_size("pix")
    total = n * rows
    cap_blocks = p_sec // n // BLOCK
    slots = cap_blocks // 2 + 1
    early = slots - slots // 2
    cm = cycle_map.reshape(p_sec // BLOCK, BLOCK)

    def swap(x):
        return lax.ppermute(x, "pix", SWAP)

    def send(blocks, groups):
        return lax.all_to_all(
            blocks, "frame", split_axis=0, concat_axis=0, axis_index_groups=groups, tiled=True
        )

    moving, meta = pack_move(cm, frames, cap_blocks)
    theirs = swap(moving)
    own = pack_own(meta, cm, frames, cap_blocks)
    far = [
        lax.ppermute(piece, "frame", [(i, i ^ (n // 2 + k)) for i in range(n)])
        for k, piece in enumerate(pack_far(own, theirs, rows))
    ]
    near = pack_near(own, theirs, far[0], rows)
    received = [send(near, [list(range(n // 2)), list(range(n // 2, n))])] + far

    meta, _ = lax.optimization_barrier((meta, near))
    their_meta = swap(meta)
    second = lax.axis_index("pix") != 0
    spills = left_out(meta[:, :n], their_meta[:, :n], cap_blocks * BLOCK, second)
    spills |= left_out(their_meta[:, :n], meta[:, :n], cap_blocks * BLOCK, jnp.logical_not(second))
    overflow = jnp.any(spills)

    first = normalise(received, total, 0, early, [overflow.astype(jnp.int32).reshape(1)])
    their_first = swap(first)
    last = normalise(received, total, early, slots - early, [first])
    their_last = swap(last)
    sums = partial_sums([first, last], [], parts)
    sums = partial_sums([their_first], sums, parts)

    def spill(frames, cm, meta, their_meta, their_last, *sums):
        rest = send(pack_rest(meta, their_meta, frames, cm, cap_blocks), None)
        normed = normalise([rest.reshape(n, cap_blocks * rows, BLOCK)], total, 0, cap_blocks)
        sums = partial_sums([normed, swap(normed)], sums, parts)
        return correlate([meta, their_meta], their_last, sums)

    def fits(frames, cm, meta, their_meta, their_last, *sums):
        return correlate([meta, their_meta], their_last, sums)

    return lax.cond(overflow, spill, fits, frames, cm, meta, their_meta, their_last, *sums)


def solution(mesh):
    return jax.shard_map(
        body,
        mesh=mesh,
        in_specs=(P("frame", "pix"), P("pix")),
        out_specs=P("frame", "pix", None),
        check_vma=False,
    )
```

```python
import functools

import jax
import jax.numpy as jnp
from jax import lax
from jax.experimental import pallas as pl
from jax.experimental.pallas import tpu as pltpu
from jax.sharding import PartitionSpec as P

BLOCK = 128
HALF_WIN = 2
PAD = 8
TILE = 256
CHUNK = 128
ONES = 16
VMEM_BYTES = 32 * 1024 * 1024
LIST, COUNT, PIXELS = 0, 1, 2
MERGED = 2
SWAP = [(0, 1), (1, 0)]
WHOLE = pl.BlockSpec(memory_space=pltpu.VMEM)
ANYWHERE = pl.BlockSpec(memory_space=pl.ANY)


def call(kernel, name, out_shape, flops=0, bytes_accessed=0, limit=VMEM_BYTES, **kw):
    return pl.pallas_call(
        kernel,
        out_shape=out_shape,
        compiler_params=pltpu.CompilerParams(vmem_limit_bytes=limit),
        cost_estimate=pl.CostEstimate(
            flops=flops, bytes_accessed=bytes_accessed, transcendentals=0
        ),
        name=name,
        **kw,
    )


def dot_nt(a, b):
    return lax.dot_general(a, b, (((1,), (1,)), ((), ())), preferred_element_type=jnp.float32)


def count_half_rows(rows):
    return max(16, rows // 2)


def gate(wanted):
    wanted = jnp.broadcast_to(wanted, (1, BLOCK))
    return wanted.astype(jnp.float32).astype(jnp.bfloat16)


def take(frames_ref, block):
    return frames_ref[:, pl.ds(pl.multiple_of(block * BLOCK, BLOCK), BLOCK)]


def fold(block, right):
    rows = block.shape[0] // 2
    half = BLOCK // 2
    early, late = block[0:rows].astype(jnp.float32), block[rows:].astype(jnp.float32)
    left = lax.broadcasted_iota(jnp.int32, (rows, BLOCK), 1) < half
    if right:
        folded = jnp.where(left, pltpu.roll(early, half, 1), late)
    else:
        folded = jnp.where(left, early, pltpu.roll(late, half, 1))
    spare = count_half_rows(block.shape[0]) - rows
    if spare:
        folded = jnp.concatenate([folded, jnp.zeros((spare, BLOCK), jnp.float32)])
    return folded.astype(jnp.bfloat16)


def unfold(folded, rows):
    half = BLOCK // 2
    early = folded[0 : rows // 2].astype(jnp.float32)
    left = lax.broadcasted_iota(jnp.int32, early.shape, 1) < half
    return jnp.where(left, early, 0.0), jnp.where(left, pltpu.roll(early, half, 1), 0.0)


def find_members(cm):
    blocks = cm.shape[0]
    first = cm[:, 0:1]
    member = first == lax.broadcasted_iota(jnp.int32, (blocks, BLOCK), 1)
    row = lax.broadcasted_iota(jnp.int32, (blocks, blocks), 0)
    col = lax.broadcasted_iota(jnp.int32, (blocks, blocks), 1)
    earlier = (col < row).astype(jnp.float32).astype(jnp.bfloat16)
    pixels = jnp.sum((cm >= 0).astype(jnp.float32), axis=1, keepdims=True)
    return first, member.astype(jnp.float32), earlier, pixels


def sum_before(earlier, member, values):
    before = jnp.dot(
        earlier, (member * values).astype(jnp.bfloat16), preferred_element_type=jnp.float32
    )
    return jnp.sum(before * member, axis=1, keepdims=True)


def find_blocks(cm, cap_blocks, meta_ref):
    blocks = cm.shape[0]
    width = meta_ref.shape[1]
    first, member, earlier, pixels = find_members(cm)
    rank = sum_before(earlier, member, 1.0).astype(jnp.int32)
    slot = jnp.where(first >= 0, first * cap_blocks + rank, -1)
    hit = slot == lax.broadcasted_iota(jnp.int32, (blocks, width), 1)
    index = lax.broadcasted_iota(jnp.int32, (blocks, width), 0).astype(jnp.float32)
    meta_ref[...] = jnp.zeros_like(meta_ref)
    meta_ref[LIST : LIST + 1, :] = jnp.sum(
        jnp.where(hit, index, 0.0), axis=0, keepdims=True
    ).astype(jnp.int32)
    meta_ref[COUNT : COUNT + 1, 0:BLOCK] = jnp.sum(member, axis=0, keepdims=True).astype(
        jnp.int32
    )
    meta_ref[PIXELS : PIXELS + 1, 0:BLOCK] = jnp.sum(
        member * pixels, axis=0, keepdims=True
    ).astype(jnp.int32)


def find_places(cm):
    _, member, earlier, pixels = find_members(cm)
    valid = (cm >= 0).astype(jnp.float32)
    row = lax.broadcasted_iota(jnp.int32, (BLOCK, BLOCK), 0)
    col = lax.broadcasted_iota(jnp.int32, (BLOCK, BLOCK), 1)
    before = (row < col).astype(jnp.float32).astype(jnp.bfloat16)
    place = jnp.dot(valid.astype(jnp.bfloat16), before, preferred_element_type=jnp.float32)
    return jnp.where(cm >= 0, place + sum_before(earlier, member, pixels), -1.0)


def move_kernel(cap_blocks, cm_hbm, frames_hbm, out_ref, meta_ref, *scratch):
    frames_ref, cm_ref, meta_s, sems = scratch
    n = out_ref.shape[0]
    rows = frames_ref.shape[0]
    kept = cap_blocks // 2
    get_cm = pltpu.make_async_copy(cm_hbm, cm_ref, sems.at[0])
    get_cm.start()
    get_frames = pltpu.make_async_copy(frames_hbm, frames_ref, sems.at[1])
    get_frames.start()
    get_cm.wait()
    find_blocks(cm_ref[...], cap_blocks, meta_ref)
    to_scalars = pltpu.make_async_copy(meta_ref, meta_s, sems.at[2])
    to_scalars.start()
    to_scalars.wait()
    get_frames.wait()
    for q in range(n):
        full = gate(meta_s[PIXELS, q] == cap_blocks * BLOCK)
        for i in range(kept + 1, cap_blocks):
            block = meta_s[LIST, q * cap_blocks + i]
            start = (i - kept - 1) * rows
            out_ref[q, start : start + rows] = take(frames_ref, block) * full
        start = (cap_blocks - kept - 1) * rows
        end = start + count_half_rows(rows)
        block = meta_s[LIST, q * cap_blocks + kept]
        out_ref[q, start:end] = fold(take(frames_ref, block), True) * full
        out_ref[q, end : end + 16] = jnp.broadcast_to(full, (16, BLOCK))


def pack_move(cm, frames, cap_blocks):
    rows = frames.shape[0]
    n = cm.shape[0] // cap_blocks
    height = (cap_blocks - cap_blocks // 2 - 1) * rows + count_half_rows(rows) + 16
    meta = jax.ShapeDtypeStruct((8, cm.shape[0]), jnp.int32)
    return call(
        functools.partial(move_kernel, cap_blocks),
        "pack_move",
        [jax.ShapeDtypeStruct((n, height, BLOCK), frames.dtype), meta],
        in_specs=[ANYWHERE] * 2,
        out_specs=[WHOLE] * 2,
        scratch_shapes=[
            pltpu.VMEM(frames.shape, frames.dtype),
            pltpu.VMEM(cm.shape, cm.dtype),
            pltpu.SMEM(meta.shape, meta.dtype),
            pltpu.SemaphoreType.DMA((3,)),
        ],
    )(
        pltpu.with_memory_space_constraint(cm, pltpu.HBM),
        pltpu.with_memory_space_constraint(frames, pltpu.HBM),
    )


def own_kernel(cap_blocks, meta_s, cm_ref, frames_ref, out_ref, place_ref):
    n = out_ref.shape[0]
    rows = frames_ref.shape[0]
    kept = cap_blocks // 2
    place_ref[...] = find_places(cm_ref[...])
    target = lax.broadcasted_iota(jnp.int32, (BLOCK, BLOCK), 0).astype(jnp.float32)
    for q in range(n):
        count, pixels = meta_s[COUNT, q], meta_s[PIXELS, q]
        is_full = pixels == cap_blocks * BLOCK
        full = gate(is_full)
        fits = (pixels <= BLOCK) & (count <= MERGED)
        compact = 0.0
        for i in range(MERGED):
            block = meta_s[LIST, q * cap_blocks + i]
            place = jnp.where(fits & (i < count), place_ref[pl.ds(block, 1), :], -1.0)
            chosen = (target == place).astype(jnp.float32).astype(jnp.bfloat16)
            compact = compact + dot_nt(take(frames_ref, block), chosen)
        block = meta_s[LIST, q * cap_blocks]
        out_ref[q, 0:rows] = compact.astype(jnp.bfloat16) + take(frames_ref, block) * full
        for i in range(1, kept):
            block = meta_s[LIST, q * cap_blocks + i]
            out_ref[q, i * rows : (i + 1) * rows] = take(frames_ref, block) * full
        block = meta_s[LIST, q * cap_blocks + kept]
        out_ref[q, kept * rows :] = fold(take(frames_ref, block), False) * full


def pack_own(meta, cm, frames, cap_blocks):
    rows = frames.shape[0]
    n = cm.shape[0] // cap_blocks
    height = cap_blocks // 2 * rows + count_half_rows(rows)
    return call(
        functools.partial(own_kernel, cap_blocks),
        "pack_own",
        jax.ShapeDtypeStruct((n, height, BLOCK), frames.dtype),
        in_specs=[pl.BlockSpec(memory_space=pltpu.SMEM)] + [WHOLE] * 2,
        out_specs=WHOLE,
        scratch_shapes=[pltpu.VMEM(cm.shape, jnp.float32)],
        bytes_accessed=4 * 1024 * 1024,
    )(meta, cm, frames)


def share_kernel(cap_blocks, rows, meta_ref, own_ref, theirs_ref, out_ref):
    n, height, _ = out_ref.shape
    second = lax.axis_index("pix") != 0
    pixels = meta_ref[PIXELS : PIXELS + 1, 0:BLOCK]
    for q in range(n):
        mine = jnp.broadcast_to(pixels[:, q : q + 1], (1, BLOCK)) == cap_blocks * BLOCK
        theirs = theirs_ref[q, height - rows : height - rows + 16][0:1].astype(jnp.float32) > 0.0
        helps = theirs & (second | jnp.logical_not(mine))
        first = gate(jnp.logical_not(helps & mine))
        own, other = gate(jnp.logical_not(helps)), gate(helps)
        out_ref[q, 0:rows] = own_ref[q, 0:rows] * first
        out_ref[q, rows:] = own_ref[q, rows:] * own + theirs_ref[q, 0 : height - rows] * other


def share(meta, own, theirs, cap_blocks, rows):
    return call(
        functools.partial(share_kernel, cap_blocks, rows),
        "share",
        pltpu.VMEM(own.shape, own.dtype),
        in_specs=[WHOLE] * 3,
        out_specs=WHOLE,
        bytes_accessed=4 * 1024 * 1024,
    )(meta, own, theirs)


def left_out(meta, their_meta, cap, second):
    mine, theirs = meta[PIXELS] == cap, their_meta[PIXELS] == cap
    fits = (meta[PIXELS] <= BLOCK) & (meta[COUNT] <= MERGED)
    return theirs & (second | jnp.logical_not(mine)) & jnp.logical_not(fits)


def rest_kernel(cap_blocks, meta_s, their_meta_s, frames_hbm, cm_hbm, out_ref, *scratch):
    frames_ref, cm_ref = scratch
    n, _, rows, _ = out_ref.shape
    pltpu.sync_copy(frames_hbm, frames_ref)
    pltpu.sync_copy(cm_hbm, cm_ref)
    second = lax.axis_index("pix") != 0
    for q in range(n):
        counts = [[ref[row, q] for row in range(PIXELS + 1)] for ref in (meta_s, their_meta_s)]
        wanted = left_out(*counts, cap_blocks * BLOCK, second)
        for i in range(cap_blocks):
            block = meta_s[LIST, q * cap_blocks + i]
            valid = cm_ref[pl.ds(block, 1), :] >= 0
            out_ref[q, i] = take(frames_ref, block) * gate(
                valid & wanted & (i < meta_s[COUNT, q])
            )


def pack_rest(meta, their_meta, frames, cm, cap_blocks):
    n = cm.shape[0] // cap_blocks
    return call(
        functools.partial(rest_kernel, cap_blocks),
        "pack_rest",
        jax.ShapeDtypeStruct((n, cap_blocks, frames.shape[0], BLOCK), frames.dtype),
        in_specs=[pl.BlockSpec(memory_space=pltpu.SMEM)] * 2 + [ANYWHERE] * 2,
        out_specs=WHOLE,
        scratch_shapes=[
            pltpu.VMEM(frames.shape, frames.dtype),
            pltpu.VMEM(cm.shape, cm.dtype),
        ],
    )(
        meta,
        their_meta,
        pltpu.with_memory_space_constraint(frames, pltpu.HBM),
        pltpu.with_memory_space_constraint(cm, pltpu.HBM),
    )


def lay_out(raw_ref, rows, first, padded):
    n, height, _ = raw_ref.shape
    total = n * rows
    zero = jnp.zeros((PAD, BLOCK), jnp.float32)
    for i in range(padded.shape[0]):
        slot = first + i
        padded[i, 0:PAD] = zero
        padded[i, PAD + total : 2 * PAD + total] = zero
        for source in range(n):
            start = PAD + source * rows
            if (slot + 1) * rows <= height:
                block = raw_ref[source, slot * rows : (slot + 1) * rows]
                padded[i, start : start + rows] = block.astype(jnp.float32)
            else:
                early, late = unfold(raw_ref[source, slot * rows : height], rows)
                padded[i, start : start + rows // 2] = early
                padded[i, start + rows // 2 : start + rows] = late


def norm_rows(padded, start, chunk, out_ref):
    total = out_ref.shape[0]
    base = PAD + start
    for slot in range(padded.shape[0]):
        raw = padded[slot, base : base + chunk]
        summed = raw
        for offset in range(1, HALF_WIN + 1):
            summed = summed + padded[slot, base - offset : base - offset + chunk]
            summed = summed + padded[slot, base + offset : base + offset + chunk]
        if start == 0 or start + chunk == total:
            frame = start + lax.broadcasted_iota(jnp.int32, (chunk, BLOCK), 0)
            upper = jnp.minimum(frame + HALF_WIN, total - 1)
            lower = jnp.maximum(frame - HALF_WIN, 0)
            mean = summed / (upper - lower + 1).astype(jnp.float32)
        else:
            mean = summed * (1.0 / (2 * HALF_WIN + 1))
        normed = jnp.where(summed > 0.0, raw / mean, 0.0)
        out_ref[start : start + chunk, slot * BLOCK : (slot + 1) * BLOCK] = normed.astype(
            jnp.bfloat16
        )


def norm_kernel(rows, first, raw_ref, *refs):
    out_ref, padded = refs[-2:]
    lay_out(raw_ref, rows, first, padded)
    for start in range(0, out_ref.shape[0], CHUNK):
        norm_rows(padded, start, CHUNK, out_ref)


def normalise(raw, total, first, slots, after=()):
    return call(
        functools.partial(norm_kernel, total // raw.shape[0], first),
        "normalise",
        jax.ShapeDtypeStruct((total, slots * BLOCK), jnp.bfloat16),
        flops=12 * total * slots * BLOCK,
        bytes_accessed=4 * total * slots * BLOCK,
        in_specs=[WHOLE] + [ANYWHERE] * len(after),
        out_specs=WHOLE,
        scratch_shapes=[pltpu.VMEM((slots, total + 2 * PAD, BLOCK), jnp.float32)],
    )(raw, *after)


def set_left(ref, left_ref):
    rows = left_ref.shape[0] - ONES
    first_row = pl.multiple_of(lax.axis_index("pix") * rows, rows)
    left_ref[0:rows] = ref[pl.ds(first_row, rows), :]
    left_ref[rows : rows + ONES] = jnp.ones((ONES, ref.shape[1]), jnp.bfloat16)


def add_sums(pairs, sums, column):
    gram, frame = sums
    rows = pairs[0][0].shape[0] - ONES
    for left_ref, ref in pairs:
        both = dot_nt(left_ref[...], ref[column, :])
        gram = gram + both[0:rows]
        frame = frame + both[rows : rows + 8]
    return gram, frame


def partial_kernel(count, *refs):
    normed, lefts, (gram_out, frame_out) = refs[:count], refs[-count:], refs[-count - 2 : -count]
    before = refs[count : -count - 2]
    for ref, left_ref in zip(normed, lefts):
        set_left(ref, left_ref)
    for start in range(0, gram_out.shape[1], TILE):
        column = slice(start, start + TILE)
        sums = [ref[:, column] for ref in before] or [0.0, 0.0]
        gram_out[:, column], frame_out[:, column] = add_sums(
            list(zip(lefts, normed)), sums, column
        )


def sums_shape(total, parts):
    return [
        jax.ShapeDtypeStruct((total // parts, total), jnp.float32),
        jax.ShapeDtypeStruct((8, total), jnp.float32),
    ]


def partial_sums(normed, before, parts):
    total, width = normed[0].shape
    rows = total // parts
    return call(
        functools.partial(partial_kernel, len(normed)),
        "partial_sums",
        sums_shape(total, parts),
        flops=2 * rows * total * width * len(normed),
        bytes_accessed=4 * rows * total,
        in_specs=[WHOLE] * (len(normed) + len(before)),
        out_specs=[WHOLE] * 2,
        scratch_shapes=[pltpu.VMEM((rows + ONES, x.shape[1]), x.dtype) for x in normed],
    )(*normed, *before)


def result_kernel(meta_ref, their_meta_ref, normed_ref, gram_in, frame_in, out_hbm, *scratch):
    out_ref, frame_ref, sems = scratch
    rows, total = gram_in.shape
    pixels = meta_ref[PIXELS : PIXELS + 1, 0:BLOCK] + their_meta_ref[PIXELS : PIXELS + 1, 0:BLOCK]
    own = lax.broadcasted_iota(jnp.int32, (1, BLOCK), 1) == lax.axis_index("frame")
    number = jnp.sum(jnp.where(own, pixels, 0).astype(jnp.float32), axis=1, keepdims=True)
    ones = jnp.ones((8, normed_ref.shape[1]), jnp.bfloat16)
    frame_ref[...] = frame_in[...] + dot_nt(ones, normed_ref[...])
    first_row = pl.multiple_of(lax.axis_index("pix") * rows, rows)
    row_sum = jnp.broadcast_to(frame_ref[0:1, pl.ds(first_row, rows)], (BLOCK, rows)).T
    row_inv = 1.0 / row_sum[:, 0:1]
    left = normed_ref[pl.ds(first_row, rows), :]
    copies = []
    for i, start in enumerate(range(0, total, TILE)):
        column = slice(start, start + TILE)
        gram = gram_in[:, column] + dot_nt(left, normed_ref[column, :])
        col_inv = 1.0 / frame_ref[0:1, column]
        result = ((gram * row_inv) * col_inv) * number - 1.0
        out_ref[i] = result.astype(jnp.bfloat16)
        copies.append(
            pltpu.make_async_copy(out_ref.at[i], out_hbm.at[0, :, column], sems.at[i])
        )
        copies[-1].start()
    for copy in copies:
        copy.wait()


def correlate(metas, normed, before):
    rows, total = before[0].shape
    tiles = total // TILE
    return call(
        result_kernel,
        "correlate",
        pltpu.HBM((1, rows, total), jnp.bfloat16),
        flops=2 * rows * total * normed.shape[1],
        bytes_accessed=6 * rows * total,
        in_specs=[WHOLE] * 5,
        out_specs=ANYWHERE,
        scratch_shapes=[
            pltpu.VMEM((tiles, rows, TILE), jnp.bfloat16),
            pltpu.VMEM((8, total), jnp.float32),
            pltpu.SemaphoreType.DMA((tiles,)),
        ],
    )(*metas, normed, *before)


def body(frames, cycle_map):
    rows, p_sec = frames.shape
    n = lax.axis_size("frame")
    parts = lax.axis_size("pix")
    total = n * rows
    cap_blocks = p_sec // n // BLOCK
    slots = cap_blocks // 2 + 1
    early = slots - slots // 2
    cm = cycle_map.reshape(p_sec // BLOCK, BLOCK)

    def swap(x):
        return lax.ppermute(x, "pix", SWAP)

    def send(blocks):
        return lax.all_to_all(blocks, "frame", split_axis=0, concat_axis=0, tiled=True)

    moving, meta = pack_move(cm, frames, cap_blocks)
    theirs = swap(moving)
    packed = share(meta, pack_own(meta, cm, frames, cap_blocks), theirs, cap_blocks, rows)
    received = send(packed)

    meta, _ = lax.optimization_barrier((meta, packed))
    their_meta = swap(meta)
    second = lax.axis_index("pix") != 0
    spills = left_out(meta[:, :n], their_meta[:, :n], cap_blocks * BLOCK, second)
    spills |= left_out(their_meta[:, :n], meta[:, :n], cap_blocks * BLOCK, jnp.logical_not(second))
    overflow = jnp.any(spills)

    first = normalise(received, total, 0, early, [overflow.astype(jnp.int32).reshape(1)])
    their_first = swap(first)
    last = normalise(received, total, early, slots - early, [first])
    their_last = swap(last)
    sums = partial_sums([first, last], [], parts)
    sums = partial_sums([their_first], sums, parts)

    def spill(frames, cm, meta, their_meta, their_last, *sums):
        rest = send(pack_rest(meta, their_meta, frames, cm, cap_blocks))
        normed = normalise(rest.reshape(n, cap_blocks * rows, BLOCK), total, 0, cap_blocks)
        sums = partial_sums([normed, swap(normed)], sums, parts)
        return correlate([meta, their_meta], their_last, sums)

    def fits(frames, cm, meta, their_meta, their_last, *sums):
        return correlate([meta, their_meta], their_last, sums)

    return lax.cond(overflow, spill, fits, frames, cm, meta, their_meta, their_last, *sums)


def solution(mesh):
    return jax.shard_map(
        body,
        mesh=mesh,
        in_specs=(P("frame", "pix"), P("pix")),
        out_specs=P("frame", "pix", None),
        check_vma=False,
    )
```

```python
import functools

import jax
import jax.numpy as jnp
from jax import lax
from jax.experimental import pallas as pl
from jax.experimental.pallas import tpu as pltpu
from jax.sharding import PartitionSpec as P

BLOCK = 128
HALF_WIN = 2
PAD = 8
TILE = 256
CHUNK = 128
ONES = 16
VMEM_BYTES = 32 * 1024 * 1024
LIST, COUNT, PIXELS = 0, 1, 2
MERGED = 2
SWAP = [(0, 1), (1, 0)]
WHOLE = pl.BlockSpec(memory_space=pltpu.VMEM)
ANYWHERE = pl.BlockSpec(memory_space=pl.ANY)


def call(kernel, name, out_shape, flops=0, bytes_accessed=0, limit=VMEM_BYTES, **kw):
    return pl.pallas_call(
        kernel,
        out_shape=out_shape,
        compiler_params=pltpu.CompilerParams(vmem_limit_bytes=limit),
        cost_estimate=pl.CostEstimate(
            flops=flops, bytes_accessed=bytes_accessed, transcendentals=0
        ),
        name=name,
        **kw,
    )


def dot_nt(a, b):
    return lax.dot_general(a, b, (((1,), (1,)), ((), ())), preferred_element_type=jnp.float32)


def place(i, n):
    quarter = n // 4
    return i % quarter * 4 + i // quarter


def count_half_rows(rows):
    return max(16, rows // 2)


def gate(wanted):
    wanted = jnp.broadcast_to(wanted, (1, BLOCK))
    return wanted.astype(jnp.float32).astype(jnp.bfloat16)


def take(frames_ref, block):
    return frames_ref[:, pl.ds(pl.multiple_of(block * BLOCK, BLOCK), BLOCK)]


def fold(block, right):
    rows = block.shape[0] // 2
    half = BLOCK // 2
    early, late = block[0:rows].astype(jnp.float32), block[rows:].astype(jnp.float32)
    left = lax.broadcasted_iota(jnp.int32, (rows, BLOCK), 1) < half
    if right:
        folded = jnp.where(left, pltpu.roll(early, half, 1), late)
    else:
        folded = jnp.where(left, early, pltpu.roll(late, half, 1))
    spare = count_half_rows(block.shape[0]) - rows
    if spare:
        folded = jnp.concatenate([folded, jnp.zeros((spare, BLOCK), jnp.float32)])
    return folded.astype(jnp.bfloat16)


def unfold(folded, rows):
    half = BLOCK // 2
    folded = folded[0 : rows // 2].astype(jnp.float32)
    turned = pltpu.roll(folded, half, 1)
    second = lax.axis_index("pix") != 0
    left = lax.broadcasted_iota(jnp.int32, folded.shape, 1) < half
    used = left != second
    early, late = jnp.where(second, turned, folded), jnp.where(second, folded, turned)
    return jnp.where(used, early, 0.0), jnp.where(used, late, 0.0)


def find_members(cm):
    blocks = cm.shape[0]
    first = cm[:, 0:1]
    member = first == lax.broadcasted_iota(jnp.int32, (blocks, BLOCK), 1)
    row = lax.broadcasted_iota(jnp.int32, (blocks, blocks), 0)
    col = lax.broadcasted_iota(jnp.int32, (blocks, blocks), 1)
    earlier = (col < row).astype(jnp.float32).astype(jnp.bfloat16)
    pixels = jnp.sum((cm >= 0).astype(jnp.float32), axis=1, keepdims=True)
    return first, member.astype(jnp.float32), earlier, pixels


def sum_before(earlier, member, values):
    before = jnp.dot(
        earlier, (member * values).astype(jnp.bfloat16), preferred_element_type=jnp.float32
    )
    return jnp.sum(before * member, axis=1, keepdims=True)


def find_blocks(cm, cap_blocks, meta_ref):
    blocks = cm.shape[0]
    width = meta_ref.shape[1]
    first, member, earlier, pixels = find_members(cm)
    rank = sum_before(earlier, member, 1.0).astype(jnp.int32)
    slot = jnp.where(first >= 0, first * cap_blocks + rank, -1)
    hit = slot == lax.broadcasted_iota(jnp.int32, (blocks, width), 1)
    index = lax.broadcasted_iota(jnp.int32, (blocks, width), 0).astype(jnp.float32)
    meta_ref[...] = jnp.zeros_like(meta_ref)
    meta_ref[LIST : LIST + 1, :] = jnp.sum(
        jnp.where(hit, index, 0.0), axis=0, keepdims=True
    ).astype(jnp.int32)
    meta_ref[COUNT : COUNT + 1, 0:BLOCK] = jnp.sum(member, axis=0, keepdims=True).astype(
        jnp.int32
    )
    meta_ref[PIXELS : PIXELS + 1, 0:BLOCK] = jnp.sum(
        member * pixels, axis=0, keepdims=True
    ).astype(jnp.int32)


def find_places(cm):
    _, member, earlier, pixels = find_members(cm)
    valid = (cm >= 0).astype(jnp.float32)
    row = lax.broadcasted_iota(jnp.int32, (BLOCK, BLOCK), 0)
    col = lax.broadcasted_iota(jnp.int32, (BLOCK, BLOCK), 1)
    before = (row < col).astype(jnp.float32).astype(jnp.bfloat16)
    place = jnp.dot(valid.astype(jnp.bfloat16), before, preferred_element_type=jnp.float32)
    return jnp.where(cm >= 0, place + sum_before(earlier, member, pixels), -1.0)


def move_kernel(cap_blocks, cm_hbm, frames_hbm, out_ref, meta_ref, *scratch):
    frames_ref, cm_ref, meta_s, sems = scratch
    n = out_ref.shape[0]
    rows = frames_ref.shape[0]
    kept = cap_blocks // 2
    get_cm = pltpu.make_async_copy(cm_hbm, cm_ref, sems.at[0])
    get_cm.start()
    get_frames = pltpu.make_async_copy(frames_hbm, frames_ref, sems.at[1])
    get_frames.start()
    get_cm.wait()
    find_blocks(cm_ref[...], cap_blocks, meta_ref)
    to_scalars = pltpu.make_async_copy(meta_ref, meta_s, sems.at[2])
    to_scalars.start()
    to_scalars.wait()
    get_frames.wait()
    for q in range(n):
        full = gate(meta_s[PIXELS, q] == cap_blocks * BLOCK)
        for i in range(kept + 1, cap_blocks):
            block = meta_s[LIST, q * cap_blocks + i]
            start = (i - kept - 1) * rows
            out_ref[q, start : start + rows] = take(frames_ref, block) * full
        start = (cap_blocks - kept - 1) * rows
        end = start + count_half_rows(rows)
        block = meta_s[LIST, q * cap_blocks + kept]
        out_ref[q, start:end] = fold(take(frames_ref, block), True) * full
        out_ref[q, end : end + 16] = jnp.broadcast_to(full, (16, BLOCK))


def pack_move(cm, frames, cap_blocks):
    rows = frames.shape[0]
    n = cm.shape[0] // cap_blocks
    height = (cap_blocks - cap_blocks // 2 - 1) * rows + count_half_rows(rows) + 16
    meta = jax.ShapeDtypeStruct((8, cm.shape[0]), jnp.int32)
    return call(
        functools.partial(move_kernel, cap_blocks),
        "pack_move",
        [jax.ShapeDtypeStruct((n, height, BLOCK), frames.dtype), meta],
        in_specs=[ANYWHERE] * 2,
        out_specs=[WHOLE] * 2,
        scratch_shapes=[
            pltpu.VMEM(frames.shape, frames.dtype),
            pltpu.VMEM(cm.shape, cm.dtype),
            pltpu.SMEM(meta.shape, meta.dtype),
            pltpu.SemaphoreType.DMA((3,)),
        ],
    )(
        pltpu.with_memory_space_constraint(cm, pltpu.HBM),
        pltpu.with_memory_space_constraint(frames, pltpu.HBM),
    )


def own_kernel(cap_blocks, meta_s, cm_ref, frames_ref, out_ref, place_ref):
    n = out_ref.shape[0]
    rows = frames_ref.shape[0]
    kept = cap_blocks // 2
    place_ref[...] = find_places(cm_ref[...])
    target = lax.broadcasted_iota(jnp.int32, (BLOCK, BLOCK), 0).astype(jnp.float32)
    for q in range(n):
        count, pixels = meta_s[COUNT, q], meta_s[PIXELS, q]
        is_full = pixels == cap_blocks * BLOCK
        full = gate(is_full)
        fits = (pixels <= BLOCK) & (count <= MERGED)
        compact = 0.0
        for i in range(MERGED):
            block = meta_s[LIST, q * cap_blocks + i]
            place = jnp.where(fits & (i < count), place_ref[pl.ds(block, 1), :], -1.0)
            chosen = (target == place).astype(jnp.float32).astype(jnp.bfloat16)
            compact = compact + dot_nt(take(frames_ref, block), chosen)
        block = meta_s[LIST, q * cap_blocks]
        out_ref[q, 0:rows] = compact.astype(jnp.bfloat16) + take(frames_ref, block) * full
        for i in range(1, kept):
            block = meta_s[LIST, q * cap_blocks + i]
            out_ref[q, i * rows : (i + 1) * rows] = take(frames_ref, block) * full
        block = meta_s[LIST, q * cap_blocks + kept]
        out_ref[q, kept * rows :] = fold(take(frames_ref, block), False) * full


def pack_own(meta, cm, frames, cap_blocks):
    rows = frames.shape[0]
    n = cm.shape[0] // cap_blocks
    height = cap_blocks // 2 * rows + count_half_rows(rows)
    return call(
        functools.partial(own_kernel, cap_blocks),
        "pack_own",
        jax.ShapeDtypeStruct((n, height, BLOCK), frames.dtype),
        in_specs=[pl.BlockSpec(memory_space=pltpu.SMEM)] + [WHOLE] * 2,
        out_specs=WHOLE,
        scratch_shapes=[pltpu.VMEM(cm.shape, jnp.float32)],
        bytes_accessed=4 * 1024 * 1024,
    )(meta, cm, frames)


def share_kernel(cap_blocks, rows, meta_ref, own_ref, theirs_ref, out_ref):
    n, height, _ = out_ref.shape
    second = lax.axis_index("pix") != 0
    pixels = meta_ref[PIXELS : PIXELS + 1, 0:BLOCK]
    for q in range(n):
        mine = jnp.broadcast_to(pixels[:, q : q + 1], (1, BLOCK)) == cap_blocks * BLOCK
        theirs = theirs_ref[q, height - rows : height - rows + 16][0:1].astype(jnp.float32) > 0.0
        helps = theirs & (second | jnp.logical_not(mine))
        first = gate(jnp.logical_not(helps & mine))
        own, other = gate(jnp.logical_not(helps)), gate(helps)
        to = place(q, n)
        out_ref[to, 0:rows] = own_ref[q, 0:rows] * first
        out_ref[to, rows:] = own_ref[q, rows:] * own + theirs_ref[q, 0 : height - rows] * other


def share(meta, own, theirs, cap_blocks, rows):
    return call(
        functools.partial(share_kernel, cap_blocks, rows),
        "share",
        pltpu.VMEM(own.shape, own.dtype),
        in_specs=[WHOLE] * 3,
        out_specs=WHOLE,
        bytes_accessed=4 * 1024 * 1024,
    )(meta, own, theirs)


def left_out(meta, their_meta, cap, second):
    mine, theirs = meta[PIXELS] == cap, their_meta[PIXELS] == cap
    fits = (meta[PIXELS] <= BLOCK) & (meta[COUNT] <= MERGED)
    return theirs & (second | jnp.logical_not(mine)) & jnp.logical_not(fits)


def rest_kernel(cap_blocks, meta_s, their_meta_s, frames_hbm, cm_hbm, out_ref, *scratch):
    frames_ref, cm_ref = scratch
    n, _, rows, _ = out_ref.shape
    pltpu.sync_copy(frames_hbm, frames_ref)
    pltpu.sync_copy(cm_hbm, cm_ref)
    second = lax.axis_index("pix") != 0
    for q in range(n):
        counts = [[ref[row, q] for row in range(PIXELS + 1)] for ref in (meta_s, their_meta_s)]
        wanted = left_out(*counts, cap_blocks * BLOCK, second)
        for i in range(cap_blocks):
            block = meta_s[LIST, q * cap_blocks + i]
            valid = cm_ref[pl.ds(block, 1), :] >= 0
            out_ref[place(q, n), i] = take(frames_ref, block) * gate(
                valid & wanted & (i < meta_s[COUNT, q])
            )


def pack_rest(meta, their_meta, frames, cm, cap_blocks):
    n = cm.shape[0] // cap_blocks
    return call(
        functools.partial(rest_kernel, cap_blocks),
        "pack_rest",
        jax.ShapeDtypeStruct((n, cap_blocks, frames.shape[0], BLOCK), frames.dtype),
        in_specs=[pl.BlockSpec(memory_space=pltpu.SMEM)] * 2 + [ANYWHERE] * 2,
        out_specs=WHOLE,
        scratch_shapes=[
            pltpu.VMEM(frames.shape, frames.dtype),
            pltpu.VMEM(cm.shape, cm.dtype),
        ],
    )(
        meta,
        their_meta,
        pltpu.with_memory_space_constraint(frames, pltpu.HBM),
        pltpu.with_memory_space_constraint(cm, pltpu.HBM),
    )


def lay_out(raw_ref, rows, first, padded):
    n, height, _ = raw_ref.shape
    total = n * rows
    zero = jnp.zeros((PAD, BLOCK), jnp.float32)
    for i in range(padded.shape[0]):
        slot = first + i
        padded[i, 0:PAD] = zero
        padded[i, PAD + total : 2 * PAD + total] = zero
        for source in range(n):
            start = PAD + source * rows
            if (slot + 1) * rows <= height:
                block = raw_ref[place(source, n), slot * rows : (slot + 1) * rows]
                padded[i, start : start + rows] = block.astype(jnp.float32)
            else:
                early, late = unfold(raw_ref[place(source, n), slot * rows : height], rows)
                padded[i, start : start + rows // 2] = early
                padded[i, start + rows // 2 : start + rows] = late


def norm_rows(padded, start, chunk, out_ref):
    total = out_ref.shape[0]
    base = PAD + start
    for slot in range(padded.shape[0]):
        raw = padded[slot, base : base + chunk]
        summed = raw
        for offset in range(1, HALF_WIN + 1):
            summed = summed + padded[slot, base - offset : base - offset + chunk]
            summed = summed + padded[slot, base + offset : base + offset + chunk]
        if start == 0 or start + chunk == total:
            frame = start + lax.broadcasted_iota(jnp.int32, (chunk, BLOCK), 0)
            upper = jnp.minimum(frame + HALF_WIN, total - 1)
            lower = jnp.maximum(frame - HALF_WIN, 0)
            mean = summed / (upper - lower + 1).astype(jnp.float32)
        else:
            mean = summed * (1.0 / (2 * HALF_WIN + 1))
        normed = jnp.where(summed > 0.0, raw / mean, 0.0)
        out_ref[start : start + chunk, slot * BLOCK : (slot + 1) * BLOCK] = normed.astype(
            jnp.bfloat16
        )


def norm_kernel(rows, first, raw_ref, *refs):
    out_ref, padded = refs[-2:]
    lay_out(raw_ref, rows, first, padded)
    for start in range(0, out_ref.shape[0], CHUNK):
        norm_rows(padded, start, CHUNK, out_ref)


def normalise(raw, total, first, slots, after=()):
    return call(
        functools.partial(norm_kernel, total // raw.shape[0], first),
        "normalise",
        jax.ShapeDtypeStruct((total, slots * BLOCK), jnp.bfloat16),
        flops=12 * total * slots * BLOCK,
        bytes_accessed=4 * total * slots * BLOCK,
        in_specs=[WHOLE] + [ANYWHERE] * len(after),
        out_specs=WHOLE,
        scratch_shapes=[pltpu.VMEM((slots, total + 2 * PAD, BLOCK), jnp.float32)],
    )(raw, *after)


def set_left(ref, left_ref):
    rows, width = left_ref.shape[0] - ONES, left_ref.shape[1]
    first_row = pl.multiple_of(lax.axis_index("pix") * rows, rows)
    left_ref[0:rows] = ref[pl.ds(first_row, rows), 0:width]
    left_ref[rows : rows + ONES] = jnp.ones((ONES, width), jnp.bfloat16)


def add_sums(pairs, sums, column):
    gram, frame = sums
    rows = pairs[0][0].shape[0] - ONES
    for left_ref, ref in pairs:
        both = dot_nt(left_ref[...], ref[column, 0 : left_ref.shape[1]])
        gram = gram + both[0:rows]
        frame = frame + both[rows : rows + 8]
    return gram, frame


def partial_kernel(count, *refs):
    normed, lefts, (gram_out, frame_out) = refs[:count], refs[-count:], refs[-count - 2 : -count]
    before = refs[count : -count - 2]
    for ref, left_ref in zip(normed, lefts):
        set_left(ref, left_ref)
    for start in range(0, gram_out.shape[1], TILE):
        column = slice(start, start + TILE)
        sums = [ref[:, column] for ref in before] or [0.0, 0.0]
        gram_out[:, column], frame_out[:, column] = add_sums(
            list(zip(lefts, normed)), sums, column
        )


def sums_shape(total, parts):
    return [
        jax.ShapeDtypeStruct((total // parts, total), jnp.float32),
        jax.ShapeDtypeStruct((8, total), jnp.float32),
    ]


def partial_sums(normed, before, parts, widths=None):
    widths = widths or [x.shape[1] for x in normed]
    total = normed[0].shape[0]
    rows = total // parts
    return call(
        functools.partial(partial_kernel, len(normed)),
        "partial_sums",
        sums_shape(total, parts),
        flops=2 * rows * total * sum(widths),
        bytes_accessed=4 * rows * total,
        in_specs=[WHOLE] * (len(normed) + len(before)),
        out_specs=[WHOLE] * 2,
        scratch_shapes=[pltpu.VMEM((rows + ONES, width), jnp.bfloat16) for width in widths],
    )(*normed, *before)


def result_kernel(meta_ref, their_meta_ref, mine_ref, theirs_ref, gram_in, frame_in, *refs):
    out_hbm, out_ref, frame_ref, normed_ref, sems = refs
    last = slice(mine_ref.shape[1] - BLOCK, mine_ref.shape[1])
    normed_ref[:, 0 : last.start] = theirs_ref[:, 0 : last.start]
    normed_ref[:, last] = theirs_ref[:, last] + mine_ref[:, last]
    rows, total = gram_in.shape
    pixels = meta_ref[PIXELS : PIXELS + 1, 0:BLOCK] + their_meta_ref[PIXELS : PIXELS + 1, 0:BLOCK]
    own = lax.broadcasted_iota(jnp.int32, (1, BLOCK), 1) == lax.axis_index("frame")
    number = jnp.sum(jnp.where(own, pixels, 0).astype(jnp.float32), axis=1, keepdims=True)
    ones = jnp.ones((8, normed_ref.shape[1]), jnp.bfloat16)
    frame_ref[...] = frame_in[...] + dot_nt(ones, normed_ref[...])
    first_row = pl.multiple_of(lax.axis_index("pix") * rows, rows)
    row_sum = jnp.broadcast_to(frame_ref[0:1, pl.ds(first_row, rows)], (BLOCK, rows)).T
    row_inv = 1.0 / row_sum[:, 0:1]
    left = normed_ref[pl.ds(first_row, rows), :]
    copies = []
    for i, start in enumerate(range(0, total, TILE)):
        column = slice(start, start + TILE)
        gram = gram_in[:, column] + dot_nt(left, normed_ref[column, :])
        col_inv = 1.0 / frame_ref[0:1, column]
        result = ((gram * row_inv) * col_inv) * number - 1.0
        out_ref[i] = result.astype(jnp.bfloat16)
        copies.append(
            pltpu.make_async_copy(out_ref.at[i], out_hbm.at[0, :, column], sems.at[i])
        )
        copies[-1].start()
    for copy in copies:
        copy.wait()


def correlate(metas, mine, theirs, before):
    rows, total = before[0].shape
    tiles = total // TILE
    return call(
        result_kernel,
        "correlate",
        pltpu.HBM((1, rows, total), jnp.bfloat16),
        flops=2 * rows * total * theirs.shape[1],
        bytes_accessed=6 * rows * total,
        in_specs=[WHOLE] * 6,
        out_specs=ANYWHERE,
        scratch_shapes=[
            pltpu.VMEM((tiles, rows, TILE), jnp.bfloat16),
            pltpu.VMEM((8, total), jnp.float32),
            pltpu.VMEM(theirs.shape, theirs.dtype),
            pltpu.SemaphoreType.DMA((tiles,)),
        ],
    )(*metas, mine, theirs, *before)


def body(frames, cycle_map):
    rows, p_sec = frames.shape
    n = lax.axis_size("frame")
    parts = lax.axis_size("pix")
    total = n * rows
    cap_blocks = p_sec // n // BLOCK
    slots = cap_blocks // 2 + 1
    early = slots - slots // 2
    cm = cycle_map.reshape(p_sec // BLOCK, BLOCK)

    def swap(x):
        return lax.ppermute(x, "pix", SWAP)

    def send(blocks):
        group = sorted(range(n), key=lambda i: place(i, n))
        return lax.all_to_all(
            blocks, "frame", split_axis=0, concat_axis=0, axis_index_groups=[group], tiled=True
        )

    moving, meta = pack_move(cm, frames, cap_blocks)
    theirs = swap(moving)
    packed = share(meta, pack_own(meta, cm, frames, cap_blocks), theirs, cap_blocks, rows)
    received = send(packed)

    meta, _ = lax.optimization_barrier((meta, packed))
    their_meta = swap(meta)
    second = lax.axis_index("pix") != 0
    spills = left_out(meta[:, :n], their_meta[:, :n], cap_blocks * BLOCK, second)
    spills |= left_out(their_meta[:, :n], meta[:, :n], cap_blocks * BLOCK, jnp.logical_not(second))
    overflow = jnp.any(spills)

    first = normalise(received, total, 0, early, [overflow.astype(jnp.int32).reshape(1)])
    their_first = swap(first)
    last = normalise(received, total, early, slots - early, [first])
    their_last = swap(last)
    widths = [early * BLOCK, (slots - early - 1) * BLOCK]
    sums = partial_sums([first, last], [], parts, widths)
    sums = partial_sums([their_first], sums, parts)

    def spill(frames, cm, meta, their_meta, last, their_last, *sums):
        rest = send(pack_rest(meta, their_meta, frames, cm, cap_blocks))
        normed = normalise(rest.reshape(n, cap_blocks * rows, BLOCK), total, 0, cap_blocks)
        sums = partial_sums([normed, swap(normed)], sums, parts)
        return correlate([meta, their_meta], last, their_last, sums)

    def fits(frames, cm, meta, their_meta, last, their_last, *sums):
        return correlate([meta, their_meta], last, their_last, sums)

    operands = frames, cm, meta, their_meta, last, their_last, *sums
    return lax.cond(overflow, spill, fits, *operands)


def solution(mesh):
    return jax.shard_map(
        body,
        mesh=mesh,
        in_specs=(P("frame", "pix"), P("pix")),
        out_specs=P("frame", "pix", None),
        check_vma=False,
    )
```

```python
import functools

import jax
import jax.numpy as jnp
from jax import lax
from jax.experimental import pallas as pl
from jax.experimental.pallas import tpu as pltpu
from jax.sharding import PartitionSpec as P

BLOCK = 128
HALF_WIN = 2
PAD = 8
TILE = 256
CHUNK = 128
ONES = 16
VMEM_BYTES = 32 * 1024 * 1024
LIST, COUNT, PIXELS = 0, 1, 2
MERGED = 2
BITS = 16
SWAP = [(0, 1), (1, 0)]
WHOLE = pl.BlockSpec(memory_space=pltpu.VMEM)
ANYWHERE = pl.BlockSpec(memory_space=pl.ANY)


def call(kernel, name, out_shape, flops=0, bytes_accessed=0, limit=VMEM_BYTES, **kw):
    return pl.pallas_call(
        kernel,
        out_shape=out_shape,
        compiler_params=pltpu.CompilerParams(vmem_limit_bytes=limit),
        cost_estimate=pl.CostEstimate(
            flops=flops, bytes_accessed=bytes_accessed, transcendentals=0
        ),
        name=name,
        **kw,
    )


def dot_nt(a, b):
    return lax.dot_general(a, b, (((1,), (1,)), ((), ())), preferred_element_type=jnp.float32)


def count_half_rows(rows):
    return max(16, rows // 2)


def gate(wanted):
    wanted = jnp.broadcast_to(wanted, (1, BLOCK))
    return wanted.astype(jnp.float32).astype(jnp.bfloat16)


def take(frames_ref, block):
    return frames_ref[:, pl.ds(pl.multiple_of(block * BLOCK, BLOCK), BLOCK)]


def fold(block, right):
    rows = block.shape[0] // 2
    half = BLOCK // 2
    early, late = block[0:rows].astype(jnp.float32), block[rows:].astype(jnp.float32)
    left = lax.broadcasted_iota(jnp.int32, (rows, BLOCK), 1) < half
    if right:
        folded = jnp.where(left, pltpu.roll(early, half, 1), late)
    else:
        folded = jnp.where(left, early, pltpu.roll(late, half, 1))
    spare = count_half_rows(block.shape[0]) - rows
    if spare:
        folded = jnp.concatenate([folded, jnp.zeros((spare, BLOCK), jnp.float32)])
    return folded.astype(jnp.bfloat16)


def unfold(folded, rows):
    half = BLOCK // 2
    early = folded[0 : rows // 2].astype(jnp.float32)
    left = lax.broadcasted_iota(jnp.int32, early.shape, 1) < half
    return jnp.where(left, early, 0.0), jnp.where(left, pltpu.roll(early, half, 1), 0.0)


def find_members(cm):
    blocks = cm.shape[0]
    first = cm[:, 0:1]
    member = first == lax.broadcasted_iota(jnp.int32, (blocks, BLOCK), 1)
    row = lax.broadcasted_iota(jnp.int32, (blocks, blocks), 0)
    col = lax.broadcasted_iota(jnp.int32, (blocks, blocks), 1)
    earlier = (col < row).astype(jnp.float32).astype(jnp.bfloat16)
    pixels = jnp.sum((cm >= 0).astype(jnp.float32), axis=1, keepdims=True)
    return first, member.astype(jnp.float32), earlier, pixels


def sum_before(earlier, member, values):
    before = jnp.dot(
        earlier, (member * values).astype(jnp.bfloat16), preferred_element_type=jnp.float32
    )
    return jnp.sum(before * member, axis=1, keepdims=True)


def find_blocks(cm, cap_blocks, meta_ref):
    blocks = cm.shape[0]
    width = meta_ref.shape[1]
    first, member, earlier, pixels = find_members(cm)
    rank = sum_before(earlier, member, 1.0).astype(jnp.int32)
    slot = jnp.where(first >= 0, first * cap_blocks + rank, -1)
    hit = slot == lax.broadcasted_iota(jnp.int32, (blocks, width), 1)
    index = lax.broadcasted_iota(jnp.int32, (blocks, width), 0).astype(jnp.float32)
    meta_ref[...] = jnp.zeros_like(meta_ref)
    meta_ref[LIST : LIST + 1, :] = jnp.sum(
        jnp.where(hit, index, 0.0), axis=0, keepdims=True
    ).astype(jnp.int32)
    meta_ref[COUNT : COUNT + 1, 0:BLOCK] = jnp.sum(member, axis=0, keepdims=True).astype(
        jnp.int32
    )
    meta_ref[PIXELS : PIXELS + 1, 0:BLOCK] = jnp.sum(
        member * pixels, axis=0, keepdims=True
    ).astype(jnp.int32)


def find_places(cm):
    _, member, earlier, pixels = find_members(cm)
    valid = (cm >= 0).astype(jnp.float32)
    row = lax.broadcasted_iota(jnp.int32, (BLOCK, BLOCK), 0)
    col = lax.broadcasted_iota(jnp.int32, (BLOCK, BLOCK), 1)
    before = (row < col).astype(jnp.float32).astype(jnp.bfloat16)
    place = jnp.dot(valid.astype(jnp.bfloat16), before, preferred_element_type=jnp.float32)
    return jnp.where(cm >= 0, place + sum_before(earlier, member, pixels), -1.0)


def move_kernel(cap_blocks, cm_hbm, frames_hbm, out_ref, meta_ref, *scratch):
    frames_ref, cm_ref, meta_s, sems = scratch
    n = out_ref.shape[0]
    rows = frames_ref.shape[0]
    kept = cap_blocks // 2
    get_cm = pltpu.make_async_copy(cm_hbm, cm_ref, sems.at[0])
    get_cm.start()
    get_frames = pltpu.make_async_copy(frames_hbm, frames_ref, sems.at[1])
    get_frames.start()
    get_cm.wait()
    find_blocks(cm_ref[...], cap_blocks, meta_ref)
    to_scalars = pltpu.make_async_copy(meta_ref, meta_s, sems.at[2])
    to_scalars.start()
    to_scalars.wait()
    get_frames.wait()
    for q in range(n):
        for i in range(kept + 1, cap_blocks):
            block = meta_s[LIST, q * cap_blocks + i]
            start = (i - kept - 1) * rows
            out_ref[q, start : start + rows] = take(frames_ref, block)
        start = (cap_blocks - kept - 1) * rows
        block = meta_s[LIST, q * cap_blocks + kept]
        out_ref[q, start:] = fold(take(frames_ref, block), True)


def pack_move(cm, frames, cap_blocks):
    rows = frames.shape[0]
    n = cm.shape[0] // cap_blocks
    height = (cap_blocks - cap_blocks // 2 - 1) * rows + count_half_rows(rows)
    meta = jax.ShapeDtypeStruct((8, cm.shape[0]), jnp.int32)
    return call(
        functools.partial(move_kernel, cap_blocks),
        "pack_move",
        [jax.ShapeDtypeStruct((n, height, BLOCK), frames.dtype), meta],
        in_specs=[ANYWHERE] * 2,
        out_specs=[WHOLE] * 2,
        scratch_shapes=[
            pltpu.VMEM(frames.shape, frames.dtype),
            pltpu.VMEM(cm.shape, cm.dtype),
            pltpu.SMEM(meta.shape, meta.dtype),
            pltpu.SemaphoreType.DMA((3,)),
        ],
    )(
        pltpu.with_memory_space_constraint(cm, pltpu.HBM),
        pltpu.with_memory_space_constraint(frames, pltpu.HBM),
    )


def own_kernel(cap_blocks, meta_s, cm_ref, frames_ref, out_hbm, out_ref, place_ref, sems):
    n = out_ref.shape[0]
    rows = frames_ref.shape[0]
    kept = cap_blocks // 2
    place_ref[...] = find_places(cm_ref[...])
    target = lax.broadcasted_iota(jnp.int32, (BLOCK, BLOCK), 0).astype(jnp.float32)
    for q in range(n):
        count, pixels = meta_s[COUNT, q], meta_s[PIXELS, q]
        is_full = pixels == cap_blocks * BLOCK
        full = gate(is_full)
        fits = (pixels <= BLOCK) & (count <= MERGED)
        compact = 0.0
        for i in range(MERGED):
            block = meta_s[LIST, q * cap_blocks + i]
            place = jnp.where(fits & (i < count), place_ref[pl.ds(block, 1), :], -1.0)
            chosen = (target == place).astype(jnp.float32).astype(jnp.bfloat16)
            compact = compact + dot_nt(take(frames_ref, block), chosen)
        block = meta_s[LIST, q * cap_blocks]
        out_ref[q, 0:rows] = compact.astype(jnp.bfloat16) + take(frames_ref, block) * full
        for i in range(1, kept):
            block = meta_s[LIST, q * cap_blocks + i]
            out_ref[q, i * rows : (i + 1) * rows] = take(frames_ref, block)
        block = meta_s[LIST, q * cap_blocks + kept]
        out_ref[q, kept * rows :] = fold(take(frames_ref, block), False)
        pltpu.make_async_copy(out_ref.at[q], out_hbm.at[q], sems.at[q]).start()
    for q in range(n):
        pltpu.make_async_copy(out_ref.at[q], out_hbm.at[q], sems.at[q]).wait()


def pack_own(meta, cm, frames, cap_blocks):
    rows = frames.shape[0]
    n = cm.shape[0] // cap_blocks
    shape = (n, cap_blocks // 2 * rows + count_half_rows(rows), BLOCK)
    return call(
        functools.partial(own_kernel, cap_blocks),
        "pack_own",
        pltpu.HBM(shape, frames.dtype),
        in_specs=[pl.BlockSpec(memory_space=pltpu.SMEM)] + [WHOLE] * 2,
        out_specs=ANYWHERE,
        scratch_shapes=[
            pltpu.VMEM(shape, frames.dtype),
            pltpu.VMEM(cm.shape, jnp.float32),
            pltpu.SemaphoreType.DMA((n,)),
        ],
        bytes_accessed=4 * 1024 * 1024,
    )(meta, cm, frames)


def share_kernel(cap_blocks, meta_ref, theirs_ref, _, out_hbm, sems):
    n, height, _ = out_hbm.shape
    rows = height - theirs_ref.shape[1]
    lane = lax.broadcasted_iota(jnp.int32, (1, BLOCK), 1)
    helped = meta_ref[PIXELS : PIXELS + 1, 0:BLOCK] != cap_blocks * BLOCK
    masks = []
    for base in range(0, n, BITS):
        inside = helped & (lane >= base) & (lane < base + BITS)
        bits = jnp.left_shift(1, jnp.clip(lane - base, 0, BITS - 1))
        masks.append(jnp.sum(jnp.where(inside, bits, 0).astype(jnp.float32)).astype(jnp.int32))

    def copies(act):
        for q in range(n):

            @pl.when((masks[q // BITS] >> (q % BITS)) & 1 == 1)
            def _():
                act(
                    pltpu.make_async_copy(
                        theirs_ref.at[q], out_hbm.at[q, rows:height], sems.at[q]
                    )
                )

    copies(lambda copy: copy.start())
    copies(lambda copy: copy.wait())


def share(meta, own, theirs, cap_blocks):
    return call(
        functools.partial(share_kernel, cap_blocks),
        "share",
        pltpu.HBM(own.shape, own.dtype),
        in_specs=[WHOLE] * 2 + [ANYWHERE],
        out_specs=ANYWHERE,
        input_output_aliases={2: 0},
        scratch_shapes=[pltpu.SemaphoreType.DMA((own.shape[0],))],
        bytes_accessed=4 * 1024 * 1024,
    )(meta, theirs, own)


def left_out(meta, their_meta, cap):
    mine, theirs = meta[PIXELS] == cap, their_meta[PIXELS] == cap
    fits = (meta[PIXELS] <= BLOCK) & (meta[COUNT] <= MERGED)
    return jnp.logical_not(mine | fits), mine & theirs


def rest_kernel(cap_blocks, meta_s, their_meta_s, frames_hbm, cm_hbm, out_ref, *scratch):
    frames_ref, cm_ref = scratch
    n, _, rows, _ = out_ref.shape
    kept = cap_blocks // 2
    pltpu.sync_copy(frames_hbm, frames_ref)
    pltpu.sync_copy(cm_hbm, cm_ref)
    right = lax.broadcasted_iota(jnp.int32, (1, BLOCK), 1) >= BLOCK // 2
    for q in range(n):
        counts = [[ref[row, q] for row in range(PIXELS + 1)] for ref in (meta_s, their_meta_s)]
        large, twice = left_out(*counts, cap_blocks * BLOCK)
        for i in range(cap_blocks):
            block = meta_s[LIST, q * cap_blocks + i]
            wanted = jnp.broadcast_to(large, (1, BLOCK))
            if i >= kept:
                wanted |= twice & right if i == kept else twice
            valid = (cm_ref[pl.ds(block, 1), :] >= 0) & (i < meta_s[COUNT, q])
            out_ref[q, i] = take(frames_ref, block) * gate(valid & wanted)


def pack_rest(meta, their_meta, frames, cm, cap_blocks):
    n = cm.shape[0] // cap_blocks
    return call(
        functools.partial(rest_kernel, cap_blocks),
        "pack_rest",
        jax.ShapeDtypeStruct((n, cap_blocks, frames.shape[0], BLOCK), frames.dtype),
        in_specs=[pl.BlockSpec(memory_space=pltpu.SMEM)] * 2 + [ANYWHERE] * 2,
        out_specs=WHOLE,
        scratch_shapes=[
            pltpu.VMEM(frames.shape, frames.dtype),
            pltpu.VMEM(cm.shape, cm.dtype),
        ],
    )(
        meta,
        their_meta,
        pltpu.with_memory_space_constraint(frames, pltpu.HBM),
        pltpu.with_memory_space_constraint(cm, pltpu.HBM),
    )


def lay_out(raw_ref, rows, first, padded):
    n, height, _ = raw_ref.shape
    total = n * rows
    zero = jnp.zeros((PAD, BLOCK), jnp.float32)
    for i in range(padded.shape[0]):
        slot = first + i
        padded[i, 0:PAD] = zero
        padded[i, PAD + total : 2 * PAD + total] = zero
        for source in range(n):
            start = PAD + source * rows
            if (slot + 1) * rows <= height:
                block = raw_ref[source, slot * rows : (slot + 1) * rows]
                padded[i, start : start + rows] = block.astype(jnp.float32)
            else:
                early, late = unfold(raw_ref[source, slot * rows : height], rows)
                padded[i, start : start + rows // 2] = early
                padded[i, start + rows // 2 : start + rows] = late


def norm_rows(padded, start, chunk, out_ref):
    total = out_ref.shape[0]
    base = PAD + start
    for slot in range(padded.shape[0]):
        raw = padded[slot, base : base + chunk]
        summed = raw
        for offset in range(1, HALF_WIN + 1):
            summed = summed + padded[slot, base - offset : base - offset + chunk]
            summed = summed + padded[slot, base + offset : base + offset + chunk]
        if start == 0 or start + chunk == total:
            frame = start + lax.broadcasted_iota(jnp.int32, (chunk, BLOCK), 0)
            upper = jnp.minimum(frame + HALF_WIN, total - 1)
            lower = jnp.maximum(frame - HALF_WIN, 0)
            mean = summed / (upper - lower + 1).astype(jnp.float32)
        else:
            mean = summed * (1.0 / (2 * HALF_WIN + 1))
        normed = jnp.where(summed > 0.0, raw / mean, 0.0)
        out_ref[start : start + chunk, slot * BLOCK : (slot + 1) * BLOCK] = normed.astype(
            jnp.bfloat16
        )


def norm_kernel(rows, first, raw_ref, *refs):
    out_ref, padded = refs[-2:]
    lay_out(raw_ref, rows, first, padded)
    for start in range(0, out_ref.shape[0], CHUNK):
        norm_rows(padded, start, CHUNK, out_ref)


def normalise(raw, total, first, slots, after=()):
    return call(
        functools.partial(norm_kernel, total // raw.shape[0], first),
        "normalise",
        jax.ShapeDtypeStruct((total, slots * BLOCK), jnp.bfloat16),
        flops=12 * total * slots * BLOCK,
        bytes_accessed=4 * total * slots * BLOCK,
        in_specs=[WHOLE] + [ANYWHERE] * len(after),
        out_specs=WHOLE,
        scratch_shapes=[pltpu.VMEM((slots, total + 2 * PAD, BLOCK), jnp.float32)],
    )(raw, *after)


def set_left(ref, left_ref):
    rows = left_ref.shape[0] - ONES
    first_row = pl.multiple_of(lax.axis_index("pix") * rows, rows)
    left_ref[0:rows] = ref[pl.ds(first_row, rows), :]
    left_ref[rows : rows + ONES] = jnp.ones((ONES, ref.shape[1]), jnp.bfloat16)


def add_sums(pairs, sums, column):
    gram, frame = sums
    rows = pairs[0][0].shape[0] - ONES
    for left_ref, ref in pairs:
        both = dot_nt(left_ref[...], ref[column, :])
        gram = gram + both[0:rows]
        frame = frame + both[rows : rows + 8]
    return gram, frame


def partial_kernel(count, *refs):
    normed, lefts, (gram_out, frame_out) = refs[:count], refs[-count:], refs[-count - 2 : -count]
    before = refs[count : -count - 2]
    for ref, left_ref in zip(normed, lefts):
        set_left(ref, left_ref)
    for start in range(0, gram_out.shape[1], TILE):
        column = slice(start, start + TILE)
        sums = [ref[:, column] for ref in before] or [0.0, 0.0]
        gram_out[:, column], frame_out[:, column] = add_sums(
            list(zip(lefts, normed)), sums, column
        )


def sums_shape(total, parts):
    return [
        jax.ShapeDtypeStruct((total // parts, total), jnp.float32),
        jax.ShapeDtypeStruct((8, total), jnp.float32),
    ]


def partial_sums(normed, before, parts):
    total, width = normed[0].shape
    rows = total // parts
    return call(
        functools.partial(partial_kernel, len(normed)),
        "partial_sums",
        sums_shape(total, parts),
        flops=2 * rows * total * width * len(normed),
        bytes_accessed=4 * rows * total,
        in_specs=[WHOLE] * (len(normed) + len(before)),
        out_specs=[WHOLE] * 2,
        scratch_shapes=[pltpu.VMEM((rows + ONES, x.shape[1]), x.dtype) for x in normed],
    )(*normed, *before)


def result_kernel(meta_ref, their_meta_ref, normed_ref, gram_in, frame_in, out_hbm, *scratch):
    out_ref, frame_ref, sems = scratch
    rows, total = gram_in.shape
    pixels = meta_ref[PIXELS : PIXELS + 1, 0:BLOCK] + their_meta_ref[PIXELS : PIXELS + 1, 0:BLOCK]
    own = lax.broadcasted_iota(jnp.int32, (1, BLOCK), 1) == lax.axis_index("frame")
    number = jnp.sum(jnp.where(own, pixels, 0).astype(jnp.float32), axis=1, keepdims=True)
    ones = jnp.ones((8, normed_ref.shape[1]), jnp.bfloat16)
    frame_ref[...] = frame_in[...] + dot_nt(ones, normed_ref[...])
    first_row = pl.multiple_of(lax.axis_index("pix") * rows, rows)
    row_sum = jnp.broadcast_to(frame_ref[0:1, pl.ds(first_row, rows)], (BLOCK, rows)).T
    row_inv = 1.0 / row_sum[:, 0:1]
    left = normed_ref[pl.ds(first_row, rows), :]
    copies = []
    for i, start in enumerate(range(0, total, TILE)):
        column = slice(start, start + TILE)
        gram = gram_in[:, column] + dot_nt(left, normed_ref[column, :])
        col_inv = 1.0 / frame_ref[0:1, column]
        result = ((gram * row_inv) * col_inv) * number - 1.0
        out_ref[i] = result.astype(jnp.bfloat16)
        copies.append(
            pltpu.make_async_copy(out_ref.at[i], out_hbm.at[0, :, column], sems.at[i])
        )
        copies[-1].start()
    for copy in copies:
        copy.wait()


def correlate(metas, normed, before):
    rows, total = before[0].shape
    tiles = total // TILE
    return call(
        result_kernel,
        "correlate",
        pltpu.HBM((1, rows, total), jnp.bfloat16),
        flops=2 * rows * total * normed.shape[1],
        bytes_accessed=6 * rows * total,
        in_specs=[WHOLE] * 5,
        out_specs=ANYWHERE,
        scratch_shapes=[
            pltpu.VMEM((tiles, rows, TILE), jnp.bfloat16),
            pltpu.VMEM((8, total), jnp.float32),
            pltpu.SemaphoreType.DMA((tiles,)),
        ],
    )(*metas, normed, *before)


def body(frames, cycle_map):
    rows, p_sec = frames.shape
    n = lax.axis_size("frame")
    parts = lax.axis_size("pix")
    total = n * rows
    cap_blocks = p_sec // n // BLOCK
    slots = cap_blocks // 2 + 1
    early = slots - slots // 2
    cm = cycle_map.reshape(p_sec // BLOCK, BLOCK)

    def swap(x):
        return lax.ppermute(x, "pix", SWAP)

    def send(blocks):
        return lax.all_to_all(blocks, "frame", split_axis=0, concat_axis=0, tiled=True)

    moving, meta = pack_move(cm, frames, cap_blocks)
    theirs = swap(moving)
    packed = share(meta, pack_own(meta, cm, frames, cap_blocks), theirs, cap_blocks)
    received = send(packed)

    meta, _ = lax.optimization_barrier((meta, packed))
    their_meta = swap(meta)
    cap = cap_blocks * BLOCK
    large, twice = left_out(meta[:, :n], their_meta[:, :n], cap)
    overflow = jnp.any(large | twice | left_out(their_meta[:, :n], meta[:, :n], cap)[0])

    first = normalise(received, total, 0, early, [overflow.astype(jnp.int32).reshape(1)])
    their_first = swap(first)
    last = normalise(received, total, early, slots - early, [first])
    their_last = swap(last)
    sums = partial_sums([first, last], [], parts)
    sums = partial_sums([their_first], sums, parts)

    def spill(frames, cm, meta, their_meta, their_last, *sums):
        rest = send(pack_rest(meta, their_meta, frames, cm, cap_blocks))
        normed = normalise(rest.reshape(n, cap_blocks * rows, BLOCK), total, 0, cap_blocks)
        sums = partial_sums([normed, swap(normed)], sums, parts)
        return correlate([meta, their_meta], their_last, sums)

    def fits(frames, cm, meta, their_meta, their_last, *sums):
        return correlate([meta, their_meta], their_last, sums)

    return lax.cond(overflow, spill, fits, frames, cm, meta, their_meta, their_last, *sums)


def solution(mesh):
    return jax.shard_map(
        body,
        mesh=mesh,
        in_specs=(P("frame", "pix"), P("pix")),
        out_specs=P("frame", "pix", None),
        check_vma=False,
    )
```

```python
import functools

import jax
import jax.numpy as jnp
from jax import lax
from jax.experimental import pallas as pl
from jax.experimental.pallas import tpu as pltpu
from jax.sharding import PartitionSpec as P

BLOCK = 128
HALF_WIN = 2
PAD = 8
TILE = 256
CHUNK = 128
ONES = 16
VMEM_BYTES = 32 * 1024 * 1024
LIST, COUNT, PIXELS = 0, 1, 2
MERGED = 2
BITS = 16
SWAP = [(0, 1), (1, 0)]
WHOLE = pl.BlockSpec(memory_space=pltpu.VMEM)
ANYWHERE = pl.BlockSpec(memory_space=pl.ANY)


def call(kernel, name, out_shape, flops=0, bytes_accessed=0, limit=VMEM_BYTES, **kw):
    return pl.pallas_call(
        kernel,
        out_shape=out_shape,
        compiler_params=pltpu.CompilerParams(vmem_limit_bytes=limit),
        cost_estimate=pl.CostEstimate(
            flops=flops, bytes_accessed=bytes_accessed, transcendentals=0
        ),
        name=name,
        **kw,
    )


def dot_nt(a, b):
    return lax.dot_general(a, b, (((1,), (1,)), ((), ())), preferred_element_type=jnp.float32)


def count_half_rows(rows):
    return max(16, rows // 2)


def gate(wanted):
    wanted = jnp.broadcast_to(wanted, (1, BLOCK))
    return wanted.astype(jnp.float32).astype(jnp.bfloat16)


def take(frames_ref, block):
    return frames_ref[:, pl.ds(pl.multiple_of(block * BLOCK, BLOCK), BLOCK)]


def fold(block, right):
    rows = block.shape[0] // 2
    half = BLOCK // 2
    early, late = block[0:rows].astype(jnp.float32), block[rows:].astype(jnp.float32)
    left = lax.broadcasted_iota(jnp.int32, (rows, BLOCK), 1) < half
    if right:
        folded = jnp.where(left, pltpu.roll(early, half, 1), late)
    else:
        folded = jnp.where(left, early, pltpu.roll(late, half, 1))
    spare = count_half_rows(block.shape[0]) - rows
    if spare:
        folded = jnp.concatenate([folded, jnp.zeros((spare, BLOCK), jnp.float32)])
    return folded.astype(jnp.bfloat16)


def unfold(folded, rows):
    half = BLOCK // 2
    early = folded[0 : rows // 2].astype(jnp.float32)
    left = lax.broadcasted_iota(jnp.int32, early.shape, 1) < half
    return jnp.where(left, early, 0.0), jnp.where(left, pltpu.roll(early, half, 1), 0.0)


def find_members(cm):
    blocks = cm.shape[0]
    first = cm[:, 0:1]
    member = first == lax.broadcasted_iota(jnp.int32, (blocks, BLOCK), 1)
    row = lax.broadcasted_iota(jnp.int32, (blocks, blocks), 0)
    col = lax.broadcasted_iota(jnp.int32, (blocks, blocks), 1)
    earlier = (col < row).astype(jnp.float32).astype(jnp.bfloat16)
    pixels = jnp.sum((cm >= 0).astype(jnp.float32), axis=1, keepdims=True)
    return first, member.astype(jnp.float32), earlier, pixels


def sum_before(earlier, member, values):
    before = jnp.dot(
        earlier, (member * values).astype(jnp.bfloat16), preferred_element_type=jnp.float32
    )
    return jnp.sum(before * member, axis=1, keepdims=True)


def find_blocks(cm, cap_blocks, meta_ref):
    blocks = cm.shape[0]
    width = meta_ref.shape[1]
    first, member, earlier, pixels = find_members(cm)
    rank = sum_before(earlier, member, 1.0).astype(jnp.int32)
    slot = jnp.where(first >= 0, first * cap_blocks + rank, -1)
    hit = slot == lax.broadcasted_iota(jnp.int32, (blocks, width), 1)
    index = lax.broadcasted_iota(jnp.int32, (blocks, width), 0).astype(jnp.float32)
    meta_ref[...] = jnp.zeros_like(meta_ref)
    meta_ref[LIST : LIST + 1, :] = jnp.sum(
        jnp.where(hit, index, 0.0), axis=0, keepdims=True
    ).astype(jnp.int32)
    meta_ref[COUNT : COUNT + 1, 0:BLOCK] = jnp.sum(member, axis=0, keepdims=True).astype(
        jnp.int32
    )
    meta_ref[PIXELS : PIXELS + 1, 0:BLOCK] = jnp.sum(
        member * pixels, axis=0, keepdims=True
    ).astype(jnp.int32)


def find_places(cm):
    _, member, earlier, pixels = find_members(cm)
    valid = (cm >= 0).astype(jnp.float32)
    row = lax.broadcasted_iota(jnp.int32, (BLOCK, BLOCK), 0)
    col = lax.broadcasted_iota(jnp.int32, (BLOCK, BLOCK), 1)
    before = (row < col).astype(jnp.float32).astype(jnp.bfloat16)
    place = jnp.dot(valid.astype(jnp.bfloat16), before, preferred_element_type=jnp.float32)
    return jnp.where(cm >= 0, place + sum_before(earlier, member, pixels), -1.0)


def move_kernel(cap_blocks, cm_hbm, frames_hbm, out_ref, meta_ref, *scratch):
    frames_ref, cm_ref, meta_s, sems = scratch
    n = out_ref.shape[0]
    rows = frames_ref.shape[0]
    kept = cap_blocks // 2
    get_cm = pltpu.make_async_copy(cm_hbm, cm_ref, sems.at[0])
    get_cm.start()
    get_frames = pltpu.make_async_copy(frames_hbm, frames_ref, sems.at[1])
    get_frames.start()
    get_cm.wait()
    find_blocks(cm_ref[...], cap_blocks, meta_ref)
    to_scalars = pltpu.make_async_copy(meta_ref, meta_s, sems.at[2])
    to_scalars.start()
    to_scalars.wait()
    get_frames.wait()
    for q in range(n):
        for i in range(kept + 1, cap_blocks):
            block = meta_s[LIST, q * cap_blocks + i]
            start = (i - kept - 1) * rows
            out_ref[q, start : start + rows] = take(frames_ref, block)
        start = (cap_blocks - kept - 1) * rows
        block = meta_s[LIST, q * cap_blocks + kept]
        out_ref[q, start:] = fold(take(frames_ref, block), True)


def pack_move(cm, frames, cap_blocks):
    rows = frames.shape[0]
    n = cm.shape[0] // cap_blocks
    height = (cap_blocks - cap_blocks // 2 - 1) * rows + count_half_rows(rows)
    meta = jax.ShapeDtypeStruct((8, cm.shape[0]), jnp.int32)
    return call(
        functools.partial(move_kernel, cap_blocks),
        "pack_move",
        [jax.ShapeDtypeStruct((n, height, BLOCK), frames.dtype), meta],
        in_specs=[ANYWHERE] * 2,
        out_specs=[WHOLE] * 2,
        scratch_shapes=[
            pltpu.VMEM(frames.shape, frames.dtype),
            pltpu.VMEM(cm.shape, cm.dtype),
            pltpu.SMEM(meta.shape, meta.dtype),
            pltpu.SemaphoreType.DMA((3,)),
        ],
    )(
        pltpu.with_memory_space_constraint(cm, pltpu.HBM),
        pltpu.with_memory_space_constraint(frames, pltpu.HBM),
    )


def own_kernel(cap_blocks, meta_s, cm_ref, frames_ref, out_hbm, head_ref, *scratch):
    tail_ref, place_ref, sems = scratch
    n, rows, _ = head_ref.shape
    kept = cap_blocks // 2

    def write(q):
        return pltpu.make_async_copy(tail_ref.at[q], out_hbm.at[q, rows:], sems.at[q])

    for q in range(n):
        for i in range(1, kept):
            block = meta_s[LIST, q * cap_blocks + i]
            tail_ref[q, (i - 1) * rows : i * rows] = take(frames_ref, block)
        block = meta_s[LIST, q * cap_blocks + kept]
        tail_ref[q, (kept - 1) * rows :] = fold(take(frames_ref, block), False)
        write(q).start()
    place_ref[...] = find_places(cm_ref[...])
    target = lax.broadcasted_iota(jnp.int32, (BLOCK, BLOCK), 0).astype(jnp.float32)
    for q in range(n):
        count, pixels = meta_s[COUNT, q], meta_s[PIXELS, q]
        full = gate(pixels == cap_blocks * BLOCK)
        fits = (pixels <= BLOCK) & (count <= MERGED)
        compact = 0.0
        for i in range(MERGED):
            block = meta_s[LIST, q * cap_blocks + i]
            place = jnp.where(fits & (i < count), place_ref[pl.ds(block, 1), :], -1.0)
            chosen = (target == place).astype(jnp.float32).astype(jnp.bfloat16)
            compact = compact + dot_nt(take(frames_ref, block), chosen)
        block = meta_s[LIST, q * cap_blocks]
        head_ref[q] = compact.astype(jnp.bfloat16) + take(frames_ref, block) * full
    for q in range(n):
        write(q).wait()


def pack_own(meta, cm, frames, cap_blocks):
    rows = frames.shape[0]
    n = cm.shape[0] // cap_blocks
    tail = (cap_blocks // 2 - 1) * rows + count_half_rows(rows)
    return call(
        functools.partial(own_kernel, cap_blocks),
        "pack_own",
        [
            pltpu.HBM((n, rows + tail, BLOCK), frames.dtype),
            jax.ShapeDtypeStruct((n, rows, BLOCK), frames.dtype),
        ],
        in_specs=[pl.BlockSpec(memory_space=pltpu.SMEM)] + [WHOLE] * 2,
        out_specs=[ANYWHERE, WHOLE],
        scratch_shapes=[
            pltpu.VMEM((n, tail, BLOCK), frames.dtype),
            pltpu.VMEM(cm.shape, jnp.float32),
            pltpu.SemaphoreType.DMA((n,)),
        ],
        bytes_accessed=4 * 1024 * 1024,
    )(meta, cm, frames)


def share_kernel(cap_blocks, meta_ref, head_ref, theirs_ref, _, out_hbm, sems, head_sem):
    n, height, _ = out_hbm.shape
    rows = head_ref.shape[1]
    head = pltpu.make_async_copy(head_ref, out_hbm.at[:, 0:rows], head_sem)
    head.start()
    lane = lax.broadcasted_iota(jnp.int32, (1, BLOCK), 1)
    helped = meta_ref[PIXELS : PIXELS + 1, 0:BLOCK] != cap_blocks * BLOCK
    masks = []
    for base in range(0, n, BITS):
        inside = helped & (lane >= base) & (lane < base + BITS)
        bits = jnp.left_shift(1, jnp.clip(lane - base, 0, BITS - 1))
        masks.append(jnp.sum(jnp.where(inside, bits, 0).astype(jnp.float32)).astype(jnp.int32))

    def copies(act):
        for q in range(n):

            @pl.when((masks[q // BITS] >> (q % BITS)) & 1 == 1)
            def _():
                act(
                    pltpu.make_async_copy(
                        theirs_ref.at[q], out_hbm.at[q, rows:height], sems.at[q]
                    )
                )

    copies(lambda copy: copy.start())
    copies(lambda copy: copy.wait())
    head.wait()


def share(meta, own, head, theirs, cap_blocks):
    return call(
        functools.partial(share_kernel, cap_blocks),
        "share",
        pltpu.HBM(own.shape, own.dtype),
        in_specs=[WHOLE] * 3 + [ANYWHERE],
        out_specs=ANYWHERE,
        input_output_aliases={3: 0},
        scratch_shapes=[pltpu.SemaphoreType.DMA((own.shape[0],)), pltpu.SemaphoreType.DMA],
        bytes_accessed=4 * 1024 * 1024,
    )(meta, head, theirs, own)


def left_out(meta, their_meta, cap):
    mine, theirs = meta[PIXELS] == cap, their_meta[PIXELS] == cap
    fits = (meta[PIXELS] <= BLOCK) & (meta[COUNT] <= MERGED)
    return jnp.logical_not(mine | fits), mine & theirs


def rest_kernel(cap_blocks, meta_s, their_meta_s, frames_hbm, cm_hbm, out_ref, *scratch):
    frames_ref, cm_ref = scratch
    n, _, rows, _ = out_ref.shape
    kept = cap_blocks // 2
    pltpu.sync_copy(frames_hbm, frames_ref)
    pltpu.sync_copy(cm_hbm, cm_ref)
    right = lax.broadcasted_iota(jnp.int32, (1, BLOCK), 1) >= BLOCK // 2
    for q in range(n):
        counts = [[ref[row, q] for row in range(PIXELS + 1)] for ref in (meta_s, their_meta_s)]
        large, twice = left_out(*counts, cap_blocks * BLOCK)
        for i in range(cap_blocks):
            block = meta_s[LIST, q * cap_blocks + i]
            wanted = jnp.broadcast_to(large, (1, BLOCK))
            if i >= kept:
                wanted |= twice & right if i == kept else twice
            valid = (cm_ref[pl.ds(block, 1), :] >= 0) & (i < meta_s[COUNT, q])
            out_ref[q, i] = take(frames_ref, block) * gate(valid & wanted)


def pack_rest(meta, their_meta, frames, cm, cap_blocks):
    n = cm.shape[0] // cap_blocks
    return call(
        functools.partial(rest_kernel, cap_blocks),
        "pack_rest",
        jax.ShapeDtypeStruct((n, cap_blocks, frames.shape[0], BLOCK), frames.dtype),
        in_specs=[pl.BlockSpec(memory_space=pltpu.SMEM)] * 2 + [ANYWHERE] * 2,
        out_specs=WHOLE,
        scratch_shapes=[
            pltpu.VMEM(frames.shape, frames.dtype),
            pltpu.VMEM(cm.shape, cm.dtype),
        ],
    )(
        meta,
        their_meta,
        pltpu.with_memory_space_constraint(frames, pltpu.HBM),
        pltpu.with_memory_space_constraint(cm, pltpu.HBM),
    )


def lay_out(raw_ref, rows, first, padded):
    n, height, _ = raw_ref.shape
    total = n * rows
    zero = jnp.zeros((PAD, BLOCK), jnp.float32)
    for i in range(padded.shape[0]):
        slot = first + i
        padded[i, 0:PAD] = zero
        padded[i, PAD + total : 2 * PAD + total] = zero
        for source in range(n):
            start = PAD + source * rows
            if (slot + 1) * rows <= height:
                block = raw_ref[source, slot * rows : (slot + 1) * rows]
                padded[i, start : start + rows] = block.astype(jnp.float32)
            else:
                early, late = unfold(raw_ref[source, slot * rows : height], rows)
                padded[i, start : start + rows // 2] = early
                padded[i, start + rows // 2 : start + rows] = late


def norm_rows(padded, start, chunk, out_ref):
    total = out_ref.shape[0]
    base = PAD + start
    for slot in range(padded.shape[0]):
        raw = padded[slot, base : base + chunk]
        summed = raw
        for offset in range(1, HALF_WIN + 1):
            summed = summed + padded[slot, base - offset : base - offset + chunk]
            summed = summed + padded[slot, base + offset : base + offset + chunk]
        if start == 0 or start + chunk == total:
            frame = start + lax.broadcasted_iota(jnp.int32, (chunk, BLOCK), 0)
            upper = jnp.minimum(frame + HALF_WIN, total - 1)
            lower = jnp.maximum(frame - HALF_WIN, 0)
            mean = summed / (upper - lower + 1).astype(jnp.float32)
        else:
            mean = summed * (1.0 / (2 * HALF_WIN + 1))
        normed = jnp.where(summed > 0.0, raw / mean, 0.0)
        out_ref[start : start + chunk, slot * BLOCK : (slot + 1) * BLOCK] = normed.astype(
            jnp.bfloat16
        )


def norm_kernel(rows, first, raw_ref, *refs):
    out_ref, padded = refs[-2:]
    lay_out(raw_ref, rows, first, padded)
    for start in range(0, out_ref.shape[0], CHUNK):
        norm_rows(padded, start, CHUNK, out_ref)


def normalise(raw, total, first, slots, after=()):
    return call(
        functools.partial(norm_kernel, total // raw.shape[0], first),
        "normalise",
        jax.ShapeDtypeStruct((total, slots * BLOCK), jnp.bfloat16),
        flops=12 * total * slots * BLOCK,
        bytes_accessed=4 * total * slots * BLOCK,
        in_specs=[WHOLE] + [ANYWHERE] * len(after),
        out_specs=WHOLE,
        scratch_shapes=[pltpu.VMEM((slots, total + 2 * PAD, BLOCK), jnp.float32)],
    )(raw, *after)


def set_left(ref, left_ref):
    rows = left_ref.shape[0] - ONES
    first_row = pl.multiple_of(lax.axis_index("pix") * rows, rows)
    left_ref[0:rows] = ref[pl.ds(first_row, rows), :]
    left_ref[rows : rows + ONES] = jnp.ones((ONES, ref.shape[1]), jnp.bfloat16)


def add_sums(pairs, sums, column):
    gram, frame = sums
    rows = pairs[0][0].shape[0] - ONES
    for left_ref, ref in pairs:
        both = dot_nt(left_ref[...], ref[column, :])
        gram = gram + both[0:rows]
        frame = frame + both[rows : rows + 8]
    return gram, frame


def partial_kernel(count, *refs):
    normed, lefts, (gram_out, frame_out) = refs[:count], refs[-count:], refs[-count - 2 : -count]
    before = refs[count : -count - 2]
    for ref, left_ref in zip(normed, lefts):
        set_left(ref, left_ref)
    for start in range(0, gram_out.shape[1], TILE):
        column = slice(start, start + TILE)
        sums = [ref[:, column] for ref in before] or [0.0, 0.0]
        gram_out[:, column], frame_out[:, column] = add_sums(
            list(zip(lefts, normed)), sums, column
        )


def sums_shape(total, parts):
    return [
        jax.ShapeDtypeStruct((total // parts, total), jnp.float32),
        jax.ShapeDtypeStruct((8, total), jnp.float32),
    ]


def partial_sums(normed, before, parts):
    total, width = normed[0].shape
    rows = total // parts
    return call(
        functools.partial(partial_kernel, len(normed)),
        "partial_sums",
        sums_shape(total, parts),
        flops=2 * rows * total * width * len(normed),
        bytes_accessed=4 * rows * total,
        in_specs=[WHOLE] * (len(normed) + len(before)),
        out_specs=[WHOLE] * 2,
        scratch_shapes=[pltpu.VMEM((rows + ONES, x.shape[1]), x.dtype) for x in normed],
    )(*normed, *before)


def result_kernel(meta_ref, their_meta_ref, normed_ref, gram_in, frame_in, out_hbm, *scratch):
    out_ref, frame_ref, sems = scratch
    rows, total = gram_in.shape
    pixels = meta_ref[PIXELS : PIXELS + 1, 0:BLOCK] + their_meta_ref[PIXELS : PIXELS + 1, 0:BLOCK]
    own = lax.broadcasted_iota(jnp.int32, (1, BLOCK), 1) == lax.axis_index("frame")
    number = jnp.sum(jnp.where(own, pixels, 0).astype(jnp.float32), axis=1, keepdims=True)
    ones = jnp.ones((8, normed_ref.shape[1]), jnp.bfloat16)
    frame_ref[...] = frame_in[...] + dot_nt(ones, normed_ref[...])
    first_row = pl.multiple_of(lax.axis_index("pix") * rows, rows)
    row_sum = jnp.broadcast_to(frame_ref[0:1, pl.ds(first_row, rows)], (BLOCK, rows)).T
    row_inv = 1.0 / row_sum[:, 0:1]
    left = normed_ref[pl.ds(first_row, rows), :]
    copies = []
    for i, start in enumerate(range(0, total, TILE)):
        column = slice(start, start + TILE)
        gram = gram_in[:, column] + dot_nt(left, normed_ref[column, :])
        col_inv = 1.0 / frame_ref[0:1, column]
        result = ((gram * row_inv) * col_inv) * number - 1.0
        out_ref[i] = result.astype(jnp.bfloat16)
        copies.append(
            pltpu.make_async_copy(out_ref.at[i], out_hbm.at[0, :, column], sems.at[i])
        )
        copies[-1].start()
    for copy in copies:
        copy.wait()


def correlate(metas, normed, before):
    rows, total = before[0].shape
    tiles = total // TILE
    return call(
        result_kernel,
        "correlate",
        pltpu.HBM((1, rows, total), jnp.bfloat16),
        flops=2 * rows * total * normed.shape[1],
        bytes_accessed=6 * rows * total,
        in_specs=[WHOLE] * 5,
        out_specs=ANYWHERE,
        scratch_shapes=[
            pltpu.VMEM((tiles, rows, TILE), jnp.bfloat16),
            pltpu.VMEM((8, total), jnp.float32),
            pltpu.SemaphoreType.DMA((tiles,)),
        ],
    )(*metas, normed, *before)


def body(frames, cycle_map):
    rows, p_sec = frames.shape
    n = lax.axis_size("frame")
    parts = lax.axis_size("pix")
    total = n * rows
    cap_blocks = p_sec // n // BLOCK
    slots = cap_blocks // 2 + 1
    early = slots - slots // 2
    cm = cycle_map.reshape(p_sec // BLOCK, BLOCK)

    def swap(x):
        return lax.ppermute(x, "pix", SWAP)

    def send(blocks):
        return lax.all_to_all(blocks, "frame", split_axis=0, concat_axis=0, tiled=True)

    moving, meta = pack_move(cm, frames, cap_blocks)
    theirs = swap(moving)
    packed = share(meta, *pack_own(meta, cm, frames, cap_blocks), theirs, cap_blocks)
    received = send(packed)

    meta, _ = lax.optimization_barrier((meta, packed))
    their_meta = swap(meta)
    cap = cap_blocks * BLOCK
    large, twice = left_out(meta[:, :n], their_meta[:, :n], cap)
    overflow = jnp.any(large | twice | left_out(their_meta[:, :n], meta[:, :n], cap)[0])

    first = normalise(received, total, 0, early, [overflow.astype(jnp.int32).reshape(1)])
    their_first = swap(first)
    last = normalise(received, total, early, slots - early, [first])
    their_last = swap(last)
    sums = partial_sums([first, last], [], parts)
    sums = partial_sums([their_first], sums, parts)

    def spill(frames, cm, meta, their_meta, their_last, *sums):
        rest = send(pack_rest(meta, their_meta, frames, cm, cap_blocks))
        normed = normalise(rest.reshape(n, cap_blocks * rows, BLOCK), total, 0, cap_blocks)
        sums = partial_sums([normed, swap(normed)], sums, parts)
        return correlate([meta, their_meta], their_last, sums)

    def fits(frames, cm, meta, their_meta, their_last, *sums):
        return correlate([meta, their_meta], their_last, sums)

    return lax.cond(overflow, spill, fits, frames, cm, meta, their_meta, their_last, *sums)


def solution(mesh):
    return jax.shard_map(
        body,
        mesh=mesh,
        in_specs=(P("frame", "pix"), P("pix")),
        out_specs=P("frame", "pix", None),
        check_vma=False,
    )
```

```python
import functools

import jax
import jax.numpy as jnp
from jax import lax
from jax.experimental import pallas as pl
from jax.experimental.pallas import tpu as pltpu
from jax.sharding import PartitionSpec as P

BLOCK = 128
HALF_WIN = 2
PAD = 8
TILE = 256
CHUNK = 128
ONES = 16
VMEM_BYTES = 32 * 1024 * 1024
LIST, COUNT, PIXELS = 0, 1, 2
MERGED = 2
BITS = 16
SWAP = [(0, 1), (1, 0)]
WHOLE = pl.BlockSpec(memory_space=pltpu.VMEM)
ANYWHERE = pl.BlockSpec(memory_space=pl.ANY)


def call(kernel, name, out_shape, flops=0, bytes_accessed=0, limit=VMEM_BYTES, **kw):
    return pl.pallas_call(
        kernel,
        out_shape=out_shape,
        compiler_params=pltpu.CompilerParams(vmem_limit_bytes=limit),
        cost_estimate=pl.CostEstimate(
            flops=flops, bytes_accessed=bytes_accessed, transcendentals=0
        ),
        name=name,
        **kw,
    )


def dot_nt(a, b):
    return lax.dot_general(a, b, (((1,), (1,)), ((), ())), preferred_element_type=jnp.float32)


def count_half_rows(rows):
    return max(16, rows // 2)


def gate(wanted):
    wanted = jnp.broadcast_to(wanted, (1, BLOCK))
    return wanted.astype(jnp.float32).astype(jnp.bfloat16)


def take(frames_ref, block):
    return frames_ref[:, pl.ds(pl.multiple_of(block * BLOCK, BLOCK), BLOCK)]


def fold(block, right):
    rows = block.shape[0] // 2
    half = BLOCK // 2
    early, late = block[0:rows].astype(jnp.float32), block[rows:].astype(jnp.float32)
    left = lax.broadcasted_iota(jnp.int32, (rows, BLOCK), 1) < half
    if right:
        folded = jnp.where(left, pltpu.roll(early, half, 1), late)
    else:
        folded = jnp.where(left, early, pltpu.roll(late, half, 1))
    spare = count_half_rows(block.shape[0]) - rows
    if spare:
        folded = jnp.concatenate([folded, jnp.zeros((spare, BLOCK), jnp.float32)])
    return folded.astype(jnp.bfloat16)


def unfold(folded, rows):
    half = BLOCK // 2
    early = folded[0 : rows // 2].astype(jnp.float32)
    left = lax.broadcasted_iota(jnp.int32, early.shape, 1) < half
    return jnp.where(left, early, 0.0), jnp.where(left, pltpu.roll(early, half, 1), 0.0)


def find_members(cm):
    blocks = cm.shape[0]
    first = cm[:, 0:1]
    member = first == lax.broadcasted_iota(jnp.int32, (blocks, BLOCK), 1)
    row = lax.broadcasted_iota(jnp.int32, (blocks, blocks), 0)
    col = lax.broadcasted_iota(jnp.int32, (blocks, blocks), 1)
    earlier = (col < row).astype(jnp.float32).astype(jnp.bfloat16)
    pixels = jnp.sum((cm >= 0).astype(jnp.float32), axis=1, keepdims=True)
    return first, member.astype(jnp.float32), earlier, pixels


def sum_before(earlier, member, values):
    before = jnp.dot(
        earlier, (member * values).astype(jnp.bfloat16), preferred_element_type=jnp.float32
    )
    return jnp.sum(before * member, axis=1, keepdims=True)


def find_blocks(cm, cap_blocks, meta_ref):
    blocks = cm.shape[0]
    width = meta_ref.shape[1]
    first, member, earlier, pixels = find_members(cm)
    rank = sum_before(earlier, member, 1.0).astype(jnp.int32)
    slot = jnp.where(first >= 0, first * cap_blocks + rank, -1)
    hit = slot == lax.broadcasted_iota(jnp.int32, (blocks, width), 1)
    index = lax.broadcasted_iota(jnp.int32, (blocks, width), 0).astype(jnp.float32)
    meta_ref[...] = jnp.zeros_like(meta_ref)
    meta_ref[LIST : LIST + 1, :] = jnp.sum(
        jnp.where(hit, index, 0.0), axis=0, keepdims=True
    ).astype(jnp.int32)
    meta_ref[COUNT : COUNT + 1, 0:BLOCK] = jnp.sum(member, axis=0, keepdims=True).astype(
        jnp.int32
    )
    meta_ref[PIXELS : PIXELS + 1, 0:BLOCK] = jnp.sum(
        member * pixels, axis=0, keepdims=True
    ).astype(jnp.int32)


def find_places(cm):
    _, member, earlier, pixels = find_members(cm)
    valid = (cm >= 0).astype(jnp.float32)
    row = lax.broadcasted_iota(jnp.int32, (BLOCK, BLOCK), 0)
    col = lax.broadcasted_iota(jnp.int32, (BLOCK, BLOCK), 1)
    before = (row < col).astype(jnp.float32).astype(jnp.bfloat16)
    place = jnp.dot(valid.astype(jnp.bfloat16), before, preferred_element_type=jnp.float32)
    return jnp.where(cm >= 0, place + sum_before(earlier, member, pixels), -1.0)


def move_kernel(cap_blocks, cm_hbm, frames_hbm, out_ref, meta_ref, *scratch):
    frames_ref, cm_ref, meta_s, sems = scratch
    n = out_ref.shape[0]
    rows = frames_ref.shape[0]
    kept = cap_blocks // 2
    get_cm = pltpu.make_async_copy(cm_hbm, cm_ref, sems.at[0])
    get_cm.start()
    get_frames = pltpu.make_async_copy(frames_hbm, frames_ref, sems.at[1])
    get_frames.start()
    get_cm.wait()
    find_blocks(cm_ref[...], cap_blocks, meta_ref)
    to_scalars = pltpu.make_async_copy(meta_ref, meta_s, sems.at[2])
    to_scalars.start()
    to_scalars.wait()
    get_frames.wait()
    for q in range(n):
        for i in range(kept + 1, cap_blocks):
            block = meta_s[LIST, q * cap_blocks + i]
            start = (i - kept - 1) * rows
            out_ref[q, start : start + rows] = take(frames_ref, block)
        start = (cap_blocks - kept - 1) * rows
        block = meta_s[LIST, q * cap_blocks + kept]
        out_ref[q, start:] = fold(take(frames_ref, block), True)


def pack_move(cm, frames, cap_blocks):
    rows = frames.shape[0]
    n = cm.shape[0] // cap_blocks
    height = (cap_blocks - cap_blocks // 2 - 1) * rows + count_half_rows(rows)
    meta = jax.ShapeDtypeStruct((8, cm.shape[0]), jnp.int32)
    return call(
        functools.partial(move_kernel, cap_blocks),
        "pack_move",
        [jax.ShapeDtypeStruct((n, height, BLOCK), frames.dtype), meta],
        in_specs=[ANYWHERE] * 2,
        out_specs=[WHOLE] * 2,
        scratch_shapes=[
            pltpu.VMEM(frames.shape, frames.dtype),
            pltpu.VMEM(cm.shape, cm.dtype),
            pltpu.SMEM(meta.shape, meta.dtype),
            pltpu.SemaphoreType.DMA((3,)),
        ],
    )(
        pltpu.with_memory_space_constraint(cm, pltpu.HBM),
        pltpu.with_memory_space_constraint(frames, pltpu.HBM),
    )


def own_kernel(cap_blocks, meta_s, cm_ref, frames_ref, out_hbm, head_ref, *scratch):
    tail_ref, place_ref, sem = scratch
    n, rows, _ = head_ref.shape
    kept = cap_blocks // 2
    for q in range(n):
        for i in range(1, kept):
            block = meta_s[LIST, q * cap_blocks + i]
            tail_ref[q, (i - 1) * rows : i * rows] = take(frames_ref, block)
        block = meta_s[LIST, q * cap_blocks + kept]
        tail_ref[q, (kept - 1) * rows :] = fold(take(frames_ref, block), False)
    write = pltpu.make_async_copy(tail_ref, out_hbm.at[:, rows:], sem)
    write.start()
    place_ref[...] = find_places(cm_ref[...])
    target = lax.broadcasted_iota(jnp.int32, (BLOCK, BLOCK), 0).astype(jnp.float32)
    for q in range(n):
        count, pixels = meta_s[COUNT, q], meta_s[PIXELS, q]
        full = gate(pixels == cap_blocks * BLOCK)
        fits = (pixels <= BLOCK) & (count <= MERGED)
        compact = 0.0
        for i in range(MERGED):
            block = meta_s[LIST, q * cap_blocks + i]
            place = jnp.where(fits & (i < count), place_ref[pl.ds(block, 1), :], -1.0)
            chosen = (target == place).astype(jnp.float32).astype(jnp.bfloat16)
            compact = compact + dot_nt(take(frames_ref, block), chosen)
        block = meta_s[LIST, q * cap_blocks]
        head_ref[q] = compact.astype(jnp.bfloat16) + take(frames_ref, block) * full
    write.wait()


def pack_own(meta, cm, frames, cap_blocks):
    rows = frames.shape[0]
    n = cm.shape[0] // cap_blocks
    tail = (cap_blocks // 2 - 1) * rows + count_half_rows(rows)
    return call(
        functools.partial(own_kernel, cap_blocks),
        "pack_own",
        [
            pltpu.HBM((n, rows + tail, BLOCK), frames.dtype),
            jax.ShapeDtypeStruct((n, rows, BLOCK), frames.dtype),
        ],
        in_specs=[pl.BlockSpec(memory_space=pltpu.SMEM)] + [WHOLE] * 2,
        out_specs=[ANYWHERE, WHOLE],
        scratch_shapes=[
            pltpu.VMEM((n, tail, BLOCK), frames.dtype),
            pltpu.VMEM(cm.shape, jnp.float32),
            pltpu.SemaphoreType.DMA,
        ],
        bytes_accessed=4 * 1024 * 1024,
    )(meta, cm, frames)


def share_kernel(cap_blocks, meta_ref, head_ref, theirs_ref, _, out_hbm, sems, head_sem):
    n, height, _ = out_hbm.shape
    rows = head_ref.shape[1]
    head = pltpu.make_async_copy(head_ref, out_hbm.at[:, 0:rows], head_sem)
    head.start()
    lane = lax.broadcasted_iota(jnp.int32, (1, BLOCK), 1)
    helped = meta_ref[PIXELS : PIXELS + 1, 0:BLOCK] != cap_blocks * BLOCK
    masks = []
    for base in range(0, n, BITS):
        inside = helped & (lane >= base) & (lane < base + BITS)
        bits = jnp.left_shift(1, jnp.clip(lane - base, 0, BITS - 1))
        masks.append(jnp.sum(jnp.where(inside, bits, 0).astype(jnp.float32)).astype(jnp.int32))

    def copies(act):
        for q in range(n):

            @pl.when((masks[q // BITS] >> (q % BITS)) & 1 == 1)
            def _():
                act(
                    pltpu.make_async_copy(
                        theirs_ref.at[q], out_hbm.at[q, rows:height], sems.at[q]
                    )
                )

    copies(lambda copy: copy.start())
    copies(lambda copy: copy.wait())
    head.wait()


def share(meta, own, head, theirs, cap_blocks):
    return call(
        functools.partial(share_kernel, cap_blocks),
        "share",
        pltpu.HBM(own.shape, own.dtype),
        in_specs=[WHOLE] * 3 + [ANYWHERE],
        out_specs=ANYWHERE,
        input_output_aliases={3: 0},
        scratch_shapes=[pltpu.SemaphoreType.DMA((own.shape[0],)), pltpu.SemaphoreType.DMA],
        bytes_accessed=4 * 1024 * 1024,
    )(meta, head, theirs, own)


def left_out(meta, their_meta, cap):
    mine, theirs = meta[PIXELS] == cap, their_meta[PIXELS] == cap
    fits = (meta[PIXELS] <= BLOCK) & (meta[COUNT] <= MERGED)
    return jnp.logical_not(mine | fits), mine & theirs


def rest_kernel(cap_blocks, meta_s, their_meta_s, frames_hbm, cm_hbm, out_ref, *scratch):
    frames_ref, cm_ref = scratch
    n, _, rows, _ = out_ref.shape
    kept = cap_blocks // 2
    pltpu.sync_copy(frames_hbm, frames_ref)
    pltpu.sync_copy(cm_hbm, cm_ref)
    right = lax.broadcasted_iota(jnp.int32, (1, BLOCK), 1) >= BLOCK // 2
    for q in range(n):
        counts = [[ref[row, q] for row in range(PIXELS + 1)] for ref in (meta_s, their_meta_s)]
        large, twice = left_out(*counts, cap_blocks * BLOCK)
        for i in range(cap_blocks):
            block = meta_s[LIST, q * cap_blocks + i]
            wanted = jnp.broadcast_to(large, (1, BLOCK))
            if i >= kept:
                wanted |= twice & right if i == kept else twice
            valid = (cm_ref[pl.ds(block, 1), :] >= 0) & (i < meta_s[COUNT, q])
            out_ref[q, i] = take(frames_ref, block) * gate(valid & wanted)


def pack_rest(meta, their_meta, frames, cm, cap_blocks):
    n = cm.shape[0] // cap_blocks
    return call(
        functools.partial(rest_kernel, cap_blocks),
        "pack_rest",
        jax.ShapeDtypeStruct((n, cap_blocks, frames.shape[0], BLOCK), frames.dtype),
        in_specs=[pl.BlockSpec(memory_space=pltpu.SMEM)] * 2 + [ANYWHERE] * 2,
        out_specs=WHOLE,
        scratch_shapes=[
            pltpu.VMEM(frames.shape, frames.dtype),
            pltpu.VMEM(cm.shape, cm.dtype),
        ],
    )(
        meta,
        their_meta,
        pltpu.with_memory_space_constraint(frames, pltpu.HBM),
        pltpu.with_memory_space_constraint(cm, pltpu.HBM),
    )


def lay_out(raw_ref, rows, first, padded):
    n, height, _ = raw_ref.shape
    total = n * rows
    zero = jnp.zeros((PAD, BLOCK), jnp.float32)
    for i in range(padded.shape[0]):
        slot = first + i
        padded[i, 0:PAD] = zero
        padded[i, PAD + total : 2 * PAD + total] = zero
        for source in range(n):
            start = PAD + source * rows
            if (slot + 1) * rows <= height:
                block = raw_ref[source, slot * rows : (slot + 1) * rows]
                padded[i, start : start + rows] = block.astype(jnp.float32)
            else:
                early, late = unfold(raw_ref[source, slot * rows : height], rows)
                padded[i, start : start + rows // 2] = early
                padded[i, start + rows // 2 : start + rows] = late


def norm_rows(padded, start, chunk, out_ref):
    total = out_ref.shape[0]
    base = PAD + start
    for slot in range(padded.shape[0]):
        raw = padded[slot, base : base + chunk]
        summed = raw
        for offset in range(1, HALF_WIN + 1):
            summed = summed + padded[slot, base - offset : base - offset + chunk]
            summed = summed + padded[slot, base + offset : base + offset + chunk]
        if start == 0 or start + chunk == total:
            frame = start + lax.broadcasted_iota(jnp.int32, (chunk, BLOCK), 0)
            upper = jnp.minimum(frame + HALF_WIN, total - 1)
            lower = jnp.maximum(frame - HALF_WIN, 0)
            mean = summed / (upper - lower + 1).astype(jnp.float32)
        else:
            mean = summed * (1.0 / (2 * HALF_WIN + 1))
        normed = jnp.where(summed > 0.0, raw / mean, 0.0)
        out_ref[start : start + chunk, slot * BLOCK : (slot + 1) * BLOCK] = normed.astype(
            jnp.bfloat16
        )


def norm_kernel(rows, first, raw_ref, *refs):
    out_ref, padded = refs[-2:]
    lay_out(raw_ref, rows, first, padded)
    for start in range(0, out_ref.shape[0], CHUNK):
        norm_rows(padded, start, CHUNK, out_ref)


def normalise(raw, total, first, slots, after=()):
    return call(
        functools.partial(norm_kernel, total // raw.shape[0], first),
        "normalise",
        jax.ShapeDtypeStruct((total, slots * BLOCK), jnp.bfloat16),
        flops=12 * total * slots * BLOCK,
        bytes_accessed=4 * total * slots * BLOCK,
        in_specs=[WHOLE] + [ANYWHERE] * len(after),
        out_specs=WHOLE,
        scratch_shapes=[pltpu.VMEM((slots, total + 2 * PAD, BLOCK), jnp.float32)],
    )(raw, *after)


def set_left(ref, left_ref):
    rows = left_ref.shape[0] - ONES
    first_row = pl.multiple_of(lax.axis_index("pix") * rows, rows)
    left_ref[0:rows] = ref[pl.ds(first_row, rows), :]
    left_ref[rows : rows + ONES] = jnp.ones((ONES, ref.shape[1]), jnp.bfloat16)


def add_sums(pairs, sums, column):
    gram, frame = sums
    rows = pairs[0][0].shape[0] - ONES
    for left_ref, ref in pairs:
        both = dot_nt(left_ref[...], ref[column, :])
        gram = gram + both[0:rows]
        frame = frame + both[rows : rows + 8]
    return gram, frame


def partial_kernel(count, *refs):
    normed, lefts, (gram_out, frame_out) = refs[:count], refs[-count:], refs[-count - 2 : -count]
    before = refs[count : -count - 2]
    for ref, left_ref in zip(normed, lefts):
        set_left(ref, left_ref)
    for start in range(0, gram_out.shape[1], TILE):
        column = slice(start, start + TILE)
        sums = [ref[:, column] for ref in before] or [0.0, 0.0]
        gram_out[:, column], frame_out[:, column] = add_sums(
            list(zip(lefts, normed)), sums, column
        )


def sums_shape(total, parts):
    return [
        jax.ShapeDtypeStruct((total // parts, total), jnp.float32),
        jax.ShapeDtypeStruct((8, total), jnp.float32),
    ]


def partial_sums(normed, before, parts):
    total, width = normed[0].shape
    rows = total // parts
    return call(
        functools.partial(partial_kernel, len(normed)),
        "partial_sums",
        sums_shape(total, parts),
        flops=2 * rows * total * width * len(normed),
        bytes_accessed=4 * rows * total,
        in_specs=[WHOLE] * (len(normed) + len(before)),
        out_specs=[WHOLE] * 2,
        scratch_shapes=[pltpu.VMEM((rows + ONES, x.shape[1]), x.dtype) for x in normed],
    )(*normed, *before)


def result_kernel(meta_ref, their_meta_ref, normed_ref, gram_in, frame_in, out_hbm, *scratch):
    out_ref, frame_ref, sems = scratch
    rows, total = gram_in.shape
    pixels = meta_ref[PIXELS : PIXELS + 1, 0:BLOCK] + their_meta_ref[PIXELS : PIXELS + 1, 0:BLOCK]
    own = lax.broadcasted_iota(jnp.int32, (1, BLOCK), 1) == lax.axis_index("frame")
    number = jnp.sum(jnp.where(own, pixels, 0).astype(jnp.float32), axis=1, keepdims=True)
    ones = jnp.ones((8, normed_ref.shape[1]), jnp.bfloat16)
    frame_ref[...] = frame_in[...] + dot_nt(ones, normed_ref[...])
    first_row = pl.multiple_of(lax.axis_index("pix") * rows, rows)
    row_sum = jnp.broadcast_to(frame_ref[0:1, pl.ds(first_row, rows)], (BLOCK, rows)).T
    row_inv = 1.0 / row_sum[:, 0:1]
    left = normed_ref[pl.ds(first_row, rows), :]
    copies = []
    for i, start in enumerate(range(0, total, TILE)):
        column = slice(start, start + TILE)
        gram = gram_in[:, column] + dot_nt(left, normed_ref[column, :])
        col_inv = 1.0 / frame_ref[0:1, column]
        result = ((gram * row_inv) * col_inv) * number - 1.0
        out_ref[i] = result.astype(jnp.bfloat16)
        copies.append(
            pltpu.make_async_copy(out_ref.at[i], out_hbm.at[0, :, column], sems.at[i])
        )
        copies[-1].start()
    for copy in copies:
        copy.wait()


def correlate(metas, normed, before):
    rows, total = before[0].shape
    tiles = total // TILE
    return call(
        result_kernel,
        "correlate",
        pltpu.HBM((1, rows, total), jnp.bfloat16),
        flops=2 * rows * total * normed.shape[1],
        bytes_accessed=6 * rows * total,
        in_specs=[WHOLE] * 5,
        out_specs=ANYWHERE,
        scratch_shapes=[
            pltpu.VMEM((tiles, rows, TILE), jnp.bfloat16),
            pltpu.VMEM((8, total), jnp.float32),
            pltpu.SemaphoreType.DMA((tiles,)),
        ],
    )(*metas, normed, *before)


def body(frames, cycle_map):
    rows, p_sec = frames.shape
    n = lax.axis_size("frame")
    parts = lax.axis_size("pix")
    total = n * rows
    cap_blocks = p_sec // n // BLOCK
    slots = cap_blocks // 2 + 1
    early = slots - slots // 2
    cm = cycle_map.reshape(p_sec // BLOCK, BLOCK)

    def swap(x):
        return lax.ppermute(x, "pix", SWAP)

    def send(blocks):
        return lax.all_to_all(blocks, "frame", split_axis=0, concat_axis=0, tiled=True)

    moving, meta = pack_move(cm, frames, cap_blocks)
    theirs = swap(moving)
    packed = share(meta, *pack_own(meta, cm, frames, cap_blocks), theirs, cap_blocks)
    received = send(packed)

    meta, _ = lax.optimization_barrier((meta, packed))
    their_meta = swap(meta)
    cap = cap_blocks * BLOCK
    large, twice = left_out(meta[:, :n], their_meta[:, :n], cap)
    overflow = jnp.any(large | twice | left_out(their_meta[:, :n], meta[:, :n], cap)[0])

    first = normalise(received, total, 0, early, [overflow.astype(jnp.int32).reshape(1)])
    their_first = swap(first)
    last = normalise(received, total, early, slots - early, [first])
    their_last = swap(last)
    sums = partial_sums([first, last], [], parts)
    sums = partial_sums([their_first], sums, parts)

    def spill(frames, cm, meta, their_meta, their_last, *sums):
        rest = send(pack_rest(meta, their_meta, frames, cm, cap_blocks))
        normed = normalise(rest.reshape(n, cap_blocks * rows, BLOCK), total, 0, cap_blocks)
        sums = partial_sums([normed, swap(normed)], sums, parts)
        return correlate([meta, their_meta], their_last, sums)

    def fits(frames, cm, meta, their_meta, their_last, *sums):
        return correlate([meta, their_meta], their_last, sums)

    return lax.cond(overflow, spill, fits, frames, cm, meta, their_meta, their_last, *sums)


def solution(mesh):
    return jax.shard_map(
        body,
        mesh=mesh,
        in_specs=(P("frame", "pix"), P("pix")),
        out_specs=P("frame", "pix", None),
        check_vma=False,
    )
```

```python
import functools

import jax
import jax.numpy as jnp
from jax import lax
from jax.experimental import pallas as pl
from jax.experimental.pallas import tpu as pltpu
from jax.sharding import PartitionSpec as P

BLOCK = 128
HALF_WIN = 2
PAD = 8
TILE = 256
CHUNK = 128
ONES = 16
VMEM_BYTES = 32 * 1024 * 1024
LIST, COUNT, PIXELS = 0, 1, 2
MERGED = 2
BITS = 16
SWAP = [(0, 1), (1, 0)]
WHOLE = pl.BlockSpec(memory_space=pltpu.VMEM)
ANYWHERE = pl.BlockSpec(memory_space=pl.ANY)


def call(kernel, name, out_shape, flops=0, bytes_accessed=0, limit=VMEM_BYTES, **kw):
    return pl.pallas_call(
        kernel,
        out_shape=out_shape,
        compiler_params=pltpu.CompilerParams(vmem_limit_bytes=limit),
        cost_estimate=pl.CostEstimate(
            flops=flops, bytes_accessed=bytes_accessed, transcendentals=0
        ),
        name=name,
        **kw,
    )


def dot_nt(a, b):
    return lax.dot_general(a, b, (((1,), (1,)), ((), ())), preferred_element_type=jnp.float32)


def count_half_rows(rows):
    return max(16, rows // 2)


def gate(wanted):
    wanted = jnp.broadcast_to(wanted, (1, BLOCK))
    return wanted.astype(jnp.float32).astype(jnp.bfloat16)


def take(frames_ref, block):
    return frames_ref[:, pl.ds(pl.multiple_of(block * BLOCK, BLOCK), BLOCK)]


def fold(block, right):
    rows = block.shape[0] // 2
    half = BLOCK // 2
    early, late = block[0:rows].astype(jnp.float32), block[rows:].astype(jnp.float32)
    left = lax.broadcasted_iota(jnp.int32, (rows, BLOCK), 1) < half
    if right:
        folded = jnp.where(left, pltpu.roll(early, half, 1), late)
    else:
        folded = jnp.where(left, early, pltpu.roll(late, half, 1))
    spare = count_half_rows(block.shape[0]) - rows
    if spare:
        folded = jnp.concatenate([folded, jnp.zeros((spare, BLOCK), jnp.float32)])
    return folded.astype(jnp.bfloat16)


def unfold(folded, rows):
    half = BLOCK // 2
    early = folded[0 : rows // 2].astype(jnp.float32)
    left = lax.broadcasted_iota(jnp.int32, early.shape, 1) < half
    return jnp.where(left, early, 0.0), jnp.where(left, pltpu.roll(early, half, 1), 0.0)


def find_members(cm):
    blocks = cm.shape[0]
    first = cm[:, 0:1]
    member = first == lax.broadcasted_iota(jnp.int32, (blocks, BLOCK), 1)
    row = lax.broadcasted_iota(jnp.int32, (blocks, blocks), 0)
    col = lax.broadcasted_iota(jnp.int32, (blocks, blocks), 1)
    earlier = (col < row).astype(jnp.float32).astype(jnp.bfloat16)
    pixels = jnp.sum((cm >= 0).astype(jnp.float32), axis=1, keepdims=True)
    return first, member.astype(jnp.float32), earlier, pixels


def sum_before(earlier, member, values):
    before = jnp.dot(
        earlier, (member * values).astype(jnp.bfloat16), preferred_element_type=jnp.float32
    )
    return jnp.sum(before * member, axis=1, keepdims=True)


def find_blocks(cm, cap_blocks, meta_ref):
    blocks = cm.shape[0]
    width = meta_ref.shape[1]
    first, member, earlier, pixels = find_members(cm)
    rank = sum_before(earlier, member, 1.0).astype(jnp.int32)
    slot = jnp.where(first >= 0, first * cap_blocks + rank, -1)
    hit = slot == lax.broadcasted_iota(jnp.int32, (blocks, width), 1)
    index = lax.broadcasted_iota(jnp.int32, (blocks, width), 0).astype(jnp.float32)
    meta_ref[...] = jnp.zeros_like(meta_ref)
    meta_ref[LIST : LIST + 1, :] = jnp.sum(
        jnp.where(hit, index, 0.0), axis=0, keepdims=True
    ).astype(jnp.int32)
    meta_ref[COUNT : COUNT + 1, 0:BLOCK] = jnp.sum(member, axis=0, keepdims=True).astype(
        jnp.int32
    )
    meta_ref[PIXELS : PIXELS + 1, 0:BLOCK] = jnp.sum(
        member * pixels, axis=0, keepdims=True
    ).astype(jnp.int32)


def find_places(cm):
    _, member, earlier, pixels = find_members(cm)
    valid = (cm >= 0).astype(jnp.float32)
    row = lax.broadcasted_iota(jnp.int32, (BLOCK, BLOCK), 0)
    col = lax.broadcasted_iota(jnp.int32, (BLOCK, BLOCK), 1)
    before = (row < col).astype(jnp.float32).astype(jnp.bfloat16)
    place = jnp.dot(valid.astype(jnp.bfloat16), before, preferred_element_type=jnp.float32)
    return jnp.where(cm >= 0, place + sum_before(earlier, member, pixels), -1.0)


def move_kernel(cap_blocks, cm_hbm, frames_hbm, out_ref, meta_ref, *scratch):
    frames_ref, cm_ref, meta_s, sems = scratch
    n = out_ref.shape[0]
    rows = frames_ref.shape[0]
    kept = cap_blocks // 2
    get_cm = pltpu.make_async_copy(cm_hbm, cm_ref, sems.at[0])
    get_cm.start()
    get_frames = pltpu.make_async_copy(frames_hbm, frames_ref, sems.at[1])
    get_frames.start()
    get_cm.wait()
    find_blocks(cm_ref[...], cap_blocks, meta_ref)
    to_scalars = pltpu.make_async_copy(meta_ref, meta_s, sems.at[2])
    to_scalars.start()
    to_scalars.wait()
    get_frames.wait()
    for q in range(n):
        for i in range(kept + 1, cap_blocks):
            block = meta_s[LIST, q * cap_blocks + i]
            start = (i - kept - 1) * rows
            out_ref[q, start : start + rows] = take(frames_ref, block)
        start = (cap_blocks - kept - 1) * rows
        block = meta_s[LIST, q * cap_blocks + kept]
        out_ref[q, start:] = fold(take(frames_ref, block), True)


def pack_move(cm, frames, cap_blocks):
    rows = frames.shape[0]
    n = cm.shape[0] // cap_blocks
    height = (cap_blocks - cap_blocks // 2 - 1) * rows + count_half_rows(rows)
    meta = jax.ShapeDtypeStruct((8, cm.shape[0]), jnp.int32)
    return call(
        functools.partial(move_kernel, cap_blocks),
        "pack_move",
        [jax.ShapeDtypeStruct((n, height, BLOCK), frames.dtype), meta],
        in_specs=[ANYWHERE] * 2,
        out_specs=[WHOLE] * 2,
        scratch_shapes=[
            pltpu.VMEM(frames.shape, frames.dtype),
            pltpu.VMEM(cm.shape, cm.dtype),
            pltpu.SMEM(meta.shape, meta.dtype),
            pltpu.SemaphoreType.DMA((3,)),
        ],
    )(
        pltpu.with_memory_space_constraint(cm, pltpu.HBM),
        pltpu.with_memory_space_constraint(frames, pltpu.HBM),
    )


def own_kernel(cap_blocks, meta_s, cm_ref, frames_ref, out_hbm, head_ref, *scratch):
    tail_ref, place_ref, sems = scratch
    n, rows, _ = head_ref.shape
    kept = cap_blocks // 2
    place_ref[...] = find_places(cm_ref[...])
    target = lax.broadcasted_iota(jnp.int32, (BLOCK, BLOCK), 0).astype(jnp.float32)
    writes = []
    for q in range(n):
        count, pixels = meta_s[COUNT, q], meta_s[PIXELS, q]
        full = gate(pixels == cap_blocks * BLOCK)
        fits = (pixels <= BLOCK) & (count <= MERGED)
        compact = 0.0
        for i in range(MERGED):
            block = meta_s[LIST, q * cap_blocks + i]
            place = jnp.where(fits & (i < count), place_ref[pl.ds(block, 1), :], -1.0)
            chosen = (target == place).astype(jnp.float32).astype(jnp.bfloat16)
            compact = compact + dot_nt(take(frames_ref, block), chosen)
        block = meta_s[LIST, q * cap_blocks]
        head_ref[q] = compact.astype(jnp.bfloat16) + take(frames_ref, block) * full
        for i in range(1, kept):
            block = meta_s[LIST, q * cap_blocks + i]
            tail_ref[q, (i - 1) * rows : i * rows] = take(frames_ref, block)
        block = meta_s[LIST, q * cap_blocks + kept]
        tail_ref[q, (kept - 1) * rows :] = fold(take(frames_ref, block), False)
        if q + 1 in (n * 3 // 4, n):
            part = pl.ds(0, n * 3 // 4) if q + 1 < n else pl.ds(n * 3 // 4, n - n * 3 // 4)
            writes.append(
                pltpu.make_async_copy(
                    tail_ref.at[part], out_hbm.at[part, rows:], sems.at[len(writes)]
                )
            )
            writes[-1].start()
    for write in writes:
        write.wait()


def pack_own(meta, cm, frames, cap_blocks):
    rows = frames.shape[0]
    n = cm.shape[0] // cap_blocks
    tail = (cap_blocks // 2 - 1) * rows + count_half_rows(rows)
    return call(
        functools.partial(own_kernel, cap_blocks),
        "pack_own",
        [
            pltpu.HBM((n, rows + tail, BLOCK), frames.dtype),
            jax.ShapeDtypeStruct((n, rows, BLOCK), frames.dtype),
        ],
        in_specs=[pl.BlockSpec(memory_space=pltpu.SMEM)] + [WHOLE] * 2,
        out_specs=[ANYWHERE, WHOLE],
        scratch_shapes=[
            pltpu.VMEM((n, tail, BLOCK), frames.dtype),
            pltpu.VMEM(cm.shape, jnp.float32),
            pltpu.SemaphoreType.DMA((2,)),
        ],
        bytes_accessed=4 * 1024 * 1024,
    )(meta, cm, frames)


def share_kernel(cap_blocks, meta_ref, head_ref, theirs_ref, _, out_hbm, sems, head_sem):
    n, height, _ = out_hbm.shape
    rows = head_ref.shape[1]
    head = pltpu.make_async_copy(head_ref, out_hbm.at[:, 0:rows], head_sem)
    head.start()
    lane = lax.broadcasted_iota(jnp.int32, (1, BLOCK), 1)
    helped = meta_ref[PIXELS : PIXELS + 1, 0:BLOCK] != cap_blocks * BLOCK
    masks = []
    for base in range(0, n, BITS):
        inside = helped & (lane >= base) & (lane < base + BITS)
        bits = jnp.left_shift(1, jnp.clip(lane - base, 0, BITS - 1))
        masks.append(jnp.sum(jnp.where(inside, bits, 0).astype(jnp.float32)).astype(jnp.int32))

    def copies(act):
        for q in range(n):

            @pl.when((masks[q // BITS] >> (q % BITS)) & 1 == 1)
            def _():
                act(
                    pltpu.make_async_copy(
                        theirs_ref.at[q], out_hbm.at[q, rows:height], sems.at[q]
                    )
                )

    copies(lambda copy: copy.start())
    copies(lambda copy: copy.wait())
    head.wait()


def share(meta, own, head, theirs, cap_blocks):
    return call(
        functools.partial(share_kernel, cap_blocks),
        "share",
        pltpu.HBM(own.shape, own.dtype),
        in_specs=[WHOLE] * 3 + [ANYWHERE],
        out_specs=ANYWHERE,
        input_output_aliases={3: 0},
        scratch_shapes=[pltpu.SemaphoreType.DMA((own.shape[0],)), pltpu.SemaphoreType.DMA],
        bytes_accessed=4 * 1024 * 1024,
    )(meta, head, theirs, own)


def left_out(meta, their_meta, cap):
    mine, theirs = meta[PIXELS] == cap, their_meta[PIXELS] == cap
    fits = (meta[PIXELS] <= BLOCK) & (meta[COUNT] <= MERGED)
    return jnp.logical_not(mine | fits), mine & theirs


def rest_kernel(cap_blocks, meta_s, their_meta_s, frames_hbm, cm_hbm, out_ref, *scratch):
    frames_ref, cm_ref = scratch
    n, _, rows, _ = out_ref.shape
    kept = cap_blocks // 2
    pltpu.sync_copy(frames_hbm, frames_ref)
    pltpu.sync_copy(cm_hbm, cm_ref)
    right = lax.broadcasted_iota(jnp.int32, (1, BLOCK), 1) >= BLOCK // 2
    for q in range(n):
        counts = [[ref[row, q] for row in range(PIXELS + 1)] for ref in (meta_s, their_meta_s)]
        large, twice = left_out(*counts, cap_blocks * BLOCK)
        for i in range(cap_blocks):
            block = meta_s[LIST, q * cap_blocks + i]
            wanted = jnp.broadcast_to(large, (1, BLOCK))
            if i >= kept:
                wanted |= twice & right if i == kept else twice
            valid = (cm_ref[pl.ds(block, 1), :] >= 0) & (i < meta_s[COUNT, q])
            out_ref[q, i] = take(frames_ref, block) * gate(valid & wanted)


def pack_rest(meta, their_meta, frames, cm, cap_blocks):
    n = cm.shape[0] // cap_blocks
    return call(
        functools.partial(rest_kernel, cap_blocks),
        "pack_rest",
        jax.ShapeDtypeStruct((n, cap_blocks, frames.shape[0], BLOCK), frames.dtype),
        in_specs=[pl.BlockSpec(memory_space=pltpu.SMEM)] * 2 + [ANYWHERE] * 2,
        out_specs=WHOLE,
        scratch_shapes=[
            pltpu.VMEM(frames.shape, frames.dtype),
            pltpu.VMEM(cm.shape, cm.dtype),
        ],
    )(
        meta,
        their_meta,
        pltpu.with_memory_space_constraint(frames, pltpu.HBM),
        pltpu.with_memory_space_constraint(cm, pltpu.HBM),
    )


def lay_out(raw_ref, rows, first, padded):
    n, height, _ = raw_ref.shape
    total = n * rows
    zero = jnp.zeros((PAD, BLOCK), jnp.float32)
    for i in range(padded.shape[0]):
        slot = first + i
        padded[i, 0:PAD] = zero
        padded[i, PAD + total : 2 * PAD + total] = zero
        for source in range(n):
            start = PAD + source * rows
            if (slot + 1) * rows <= height:
                block = raw_ref[source, slot * rows : (slot + 1) * rows]
                padded[i, start : start + rows] = block.astype(jnp.float32)
            else:
                early, late = unfold(raw_ref[source, slot * rows : height], rows)
                padded[i, start : start + rows // 2] = early
                padded[i, start + rows // 2 : start + rows] = late


def norm_rows(padded, start, chunk, out_ref):
    total = out_ref.shape[0]
    base = PAD + start
    for slot in range(padded.shape[0]):
        raw = padded[slot, base : base + chunk]
        summed = raw
        for offset in range(1, HALF_WIN + 1):
            summed = summed + padded[slot, base - offset : base - offset + chunk]
            summed = summed + padded[slot, base + offset : base + offset + chunk]
        if start == 0 or start + chunk == total:
            frame = start + lax.broadcasted_iota(jnp.int32, (chunk, BLOCK), 0)
            upper = jnp.minimum(frame + HALF_WIN, total - 1)
            lower = jnp.maximum(frame - HALF_WIN, 0)
            mean = summed / (upper - lower + 1).astype(jnp.float32)
        else:
            mean = summed * (1.0 / (2 * HALF_WIN + 1))
        normed = jnp.where(summed > 0.0, raw / mean, 0.0)
        out_ref[start : start + chunk, slot * BLOCK : (slot + 1) * BLOCK] = normed.astype(
            jnp.bfloat16
        )


def norm_kernel(rows, first, raw_ref, *refs):
    out_ref, padded = refs[-2:]
    lay_out(raw_ref, rows, first, padded)
    for start in range(0, out_ref.shape[0], CHUNK):
        norm_rows(padded, start, CHUNK, out_ref)


def normalise(raw, total, first, slots, after=()):
    return call(
        functools.partial(norm_kernel, total // raw.shape[0], first),
        "normalise",
        jax.ShapeDtypeStruct((total, slots * BLOCK), jnp.bfloat16),
        flops=12 * total * slots * BLOCK,
        bytes_accessed=4 * total * slots * BLOCK,
        in_specs=[WHOLE] + [ANYWHERE] * len(after),
        out_specs=WHOLE,
        scratch_shapes=[pltpu.VMEM((slots, total + 2 * PAD, BLOCK), jnp.float32)],
    )(raw, *after)


def set_left(ref, left_ref):
    rows = left_ref.shape[0] - ONES
    first_row = pl.multiple_of(lax.axis_index("pix") * rows, rows)
    left_ref[0:rows] = ref[pl.ds(first_row, rows), :]
    left_ref[rows : rows + ONES] = jnp.ones((ONES, ref.shape[1]), jnp.bfloat16)


def add_sums(pairs, sums, column):
    gram, frame = sums
    rows = pairs[0][0].shape[0] - ONES
    for left_ref, ref in pairs:
        both = dot_nt(left_ref[...], ref[column, :])
        gram = gram + both[0:rows]
        frame = frame + both[rows : rows + 8]
    return gram, frame


def partial_kernel(count, *refs):
    normed, lefts, (gram_out, frame_out) = refs[:count], refs[-count:], refs[-count - 2 : -count]
    before = refs[count : -count - 2]
    for ref, left_ref in zip(normed, lefts):
        set_left(ref, left_ref)
    for start in range(0, gram_out.shape[1], TILE):
        column = slice(start, start + TILE)
        sums = [ref[:, column] for ref in before] or [0.0, 0.0]
        gram_out[:, column], frame_out[:, column] = add_sums(
            list(zip(lefts, normed)), sums, column
        )


def sums_shape(total, parts):
    return [
        jax.ShapeDtypeStruct((total // parts, total), jnp.float32),
        jax.ShapeDtypeStruct((8, total), jnp.float32),
    ]


def partial_sums(normed, before, parts):
    total, width = normed[0].shape
    rows = total // parts
    return call(
        functools.partial(partial_kernel, len(normed)),
        "partial_sums",
        sums_shape(total, parts),
        flops=2 * rows * total * width * len(normed),
        bytes_accessed=4 * rows * total,
        in_specs=[WHOLE] * (len(normed) + len(before)),
        out_specs=[WHOLE] * 2,
        scratch_shapes=[pltpu.VMEM((rows + ONES, x.shape[1]), x.dtype) for x in normed],
    )(*normed, *before)


def result_kernel(meta_ref, their_meta_ref, normed_ref, gram_in, frame_in, out_hbm, *scratch):
    out_ref, frame_ref, sems = scratch
    rows, total = gram_in.shape
    pixels = meta_ref[PIXELS : PIXELS + 1, 0:BLOCK] + their_meta_ref[PIXELS : PIXELS + 1, 0:BLOCK]
    own = lax.broadcasted_iota(jnp.int32, (1, BLOCK), 1) == lax.axis_index("frame")
    number = jnp.sum(jnp.where(own, pixels, 0).astype(jnp.float32), axis=1, keepdims=True)
    ones = jnp.ones((8, normed_ref.shape[1]), jnp.bfloat16)
    frame_ref[...] = frame_in[...] + dot_nt(ones, normed_ref[...])
    first_row = pl.multiple_of(lax.axis_index("pix") * rows, rows)
    row_sum = jnp.broadcast_to(frame_ref[0:1, pl.ds(first_row, rows)], (BLOCK, rows)).T
    row_inv = 1.0 / row_sum[:, 0:1]
    left = normed_ref[pl.ds(first_row, rows), :]
    copies = []
    for i, start in enumerate(range(0, total, TILE)):
        column = slice(start, start + TILE)
        gram = gram_in[:, column] + dot_nt(left, normed_ref[column, :])
        col_inv = 1.0 / frame_ref[0:1, column]
        result = ((gram * row_inv) * col_inv) * number - 1.0
        out_ref[i] = result.astype(jnp.bfloat16)
        copies.append(
            pltpu.make_async_copy(out_ref.at[i], out_hbm.at[0, :, column], sems.at[i])
        )
        copies[-1].start()
    for copy in copies:
        copy.wait()


def correlate(metas, normed, before):
    rows, total = before[0].shape
    tiles = total // TILE
    return call(
        result_kernel,
        "correlate",
        pltpu.HBM((1, rows, total), jnp.bfloat16),
        flops=2 * rows * total * normed.shape[1],
        bytes_accessed=6 * rows * total,
        in_specs=[WHOLE] * 5,
        out_specs=ANYWHERE,
        scratch_shapes=[
            pltpu.VMEM((tiles, rows, TILE), jnp.bfloat16),
            pltpu.VMEM((8, total), jnp.float32),
            pltpu.SemaphoreType.DMA((tiles,)),
        ],
    )(*metas, normed, *before)


def body(frames, cycle_map):
    rows, p_sec = frames.shape
    n = lax.axis_size("frame")
    parts = lax.axis_size("pix")
    total = n * rows
    cap_blocks = p_sec // n // BLOCK
    slots = cap_blocks // 2 + 1
    early = slots - slots // 2
    cm = cycle_map.reshape(p_sec // BLOCK, BLOCK)

    def swap(x):
        return lax.ppermute(x, "pix", SWAP)

    def send(blocks):
        return lax.all_to_all(blocks, "frame", split_axis=0, concat_axis=0, tiled=True)

    moving, meta = pack_move(cm, frames, cap_blocks)
    theirs = swap(moving)
    packed = share(meta, *pack_own(meta, cm, frames, cap_blocks), theirs, cap_blocks)
    received = send(packed)

    meta, _ = lax.optimization_barrier((meta, packed))
    their_meta = swap(meta)
    cap = cap_blocks * BLOCK
    large, twice = left_out(meta[:, :n], their_meta[:, :n], cap)
    overflow = jnp.any(large | twice | left_out(their_meta[:, :n], meta[:, :n], cap)[0])

    first = normalise(received, total, 0, early, [overflow.astype(jnp.int32).reshape(1)])
    their_first = swap(first)
    last = normalise(received, total, early, slots - early, [first])
    their_last = swap(last)
    sums = partial_sums([first, last], [], parts)
    sums = partial_sums([their_first], sums, parts)

    def spill(frames, cm, meta, their_meta, their_last, *sums):
        rest = send(pack_rest(meta, their_meta, frames, cm, cap_blocks))
        normed = normalise(rest.reshape(n, cap_blocks * rows, BLOCK), total, 0, cap_blocks)
        sums = partial_sums([normed, swap(normed)], sums, parts)
        return correlate([meta, their_meta], their_last, sums)

    def fits(frames, cm, meta, their_meta, their_last, *sums):
        return correlate([meta, their_meta], their_last, sums)

    return lax.cond(overflow, spill, fits, frames, cm, meta, their_meta, their_last, *sums)


def solution(mesh):
    return jax.shard_map(
        body,
        mesh=mesh,
        in_specs=(P("frame", "pix"), P("pix")),
        out_specs=P("frame", "pix", None),
        check_vma=False,
    )
```

```python
import functools

import jax
import jax.numpy as jnp
from jax import lax
from jax.experimental import pallas as pl
from jax.experimental.pallas import tpu as pltpu
from jax.sharding import PartitionSpec as P

BLOCK = 128
HALF_WIN = 2
PAD = 8
TILE = 256
CHUNK = 128
ONES = 16
VMEM_BYTES = 32 * 1024 * 1024
LIST, COUNT, PIXELS = 0, 1, 2
MERGED = 2
SWAP = [(0, 1), (1, 0)]
WHOLE = pl.BlockSpec(memory_space=pltpu.VMEM)
ANYWHERE = pl.BlockSpec(memory_space=pl.ANY)


def call(kernel, name, out_shape, flops=0, bytes_accessed=0, limit=VMEM_BYTES, **kw):
    return pl.pallas_call(
        kernel,
        out_shape=out_shape,
        compiler_params=pltpu.CompilerParams(vmem_limit_bytes=limit),
        cost_estimate=pl.CostEstimate(
            flops=flops, bytes_accessed=bytes_accessed, transcendentals=0
        ),
        name=name,
        **kw,
    )


def dot_nt(a, b):
    return lax.dot_general(a, b, (((1,), (1,)), ((), ())), preferred_element_type=jnp.float32)


def count_half_rows(rows):
    return max(16, rows // 2)


def gate(wanted):
    wanted = jnp.broadcast_to(wanted, (1, BLOCK))
    return wanted.astype(jnp.float32).astype(jnp.bfloat16)


def take(frames_ref, block):
    return frames_ref[:, pl.ds(pl.multiple_of(block * BLOCK, BLOCK), BLOCK)]


def fold(block, right):
    rows = block.shape[0] // 2
    half = BLOCK // 2
    early, late = block[0:rows].astype(jnp.float32), block[rows:].astype(jnp.float32)
    left = lax.broadcasted_iota(jnp.int32, (rows, BLOCK), 1) < half
    if right:
        folded = jnp.where(left, pltpu.roll(early, half, 1), late)
    else:
        folded = jnp.where(left, early, pltpu.roll(late, half, 1))
    spare = count_half_rows(block.shape[0]) - rows
    if spare:
        folded = jnp.concatenate([folded, jnp.zeros((spare, BLOCK), jnp.float32)])
    return folded.astype(jnp.bfloat16)


def unfold(folded, rows):
    half = BLOCK // 2
    early = folded[0 : rows // 2].astype(jnp.float32)
    left = lax.broadcasted_iota(jnp.int32, early.shape, 1) < half
    return jnp.where(left, early, 0.0), jnp.where(left, pltpu.roll(early, half, 1), 0.0)


def find_members(cm):
    blocks = cm.shape[0]
    first = cm[:, 0:1]
    member = first == lax.broadcasted_iota(jnp.int32, (blocks, BLOCK), 1)
    row = lax.broadcasted_iota(jnp.int32, (blocks, blocks), 0)
    col = lax.broadcasted_iota(jnp.int32, (blocks, blocks), 1)
    earlier = (col < row).astype(jnp.float32).astype(jnp.bfloat16)
    pixels = jnp.sum((cm >= 0).astype(jnp.float32), axis=1, keepdims=True)
    return first, member.astype(jnp.float32), earlier, pixels


def sum_before(earlier, member, values):
    before = jnp.dot(
        earlier, (member * values).astype(jnp.bfloat16), preferred_element_type=jnp.float32
    )
    return jnp.sum(before * member, axis=1, keepdims=True)


def find_blocks(cm, cap_blocks, meta_ref):
    blocks = cm.shape[0]
    width = meta_ref.shape[1]
    first, member, earlier, pixels = find_members(cm)
    rank = sum_before(earlier, member, 1.0).astype(jnp.int32)
    slot = jnp.where(first >= 0, first * cap_blocks + rank, -1)
    hit = slot == lax.broadcasted_iota(jnp.int32, (blocks, width), 1)
    index = lax.broadcasted_iota(jnp.int32, (blocks, width), 0).astype(jnp.float32)
    meta_ref[...] = jnp.zeros_like(meta_ref)
    meta_ref[LIST : LIST + 1, :] = jnp.sum(
        jnp.where(hit, index, 0.0), axis=0, keepdims=True
    ).astype(jnp.int32)
    meta_ref[COUNT : COUNT + 1, 0:BLOCK] = jnp.sum(member, axis=0, keepdims=True).astype(
        jnp.int32
    )
    meta_ref[PIXELS : PIXELS + 1, 0:BLOCK] = jnp.sum(
        member * pixels, axis=0, keepdims=True
    ).astype(jnp.int32)


def find_places(cm):
    _, member, earlier, pixels = find_members(cm)
    valid = (cm >= 0).astype(jnp.float32)
    row = lax.broadcasted_iota(jnp.int32, (BLOCK, BLOCK), 0)
    col = lax.broadcasted_iota(jnp.int32, (BLOCK, BLOCK), 1)
    before = (row < col).astype(jnp.float32).astype(jnp.bfloat16)
    place = jnp.dot(valid.astype(jnp.bfloat16), before, preferred_element_type=jnp.float32)
    return jnp.where(cm >= 0, place + sum_before(earlier, member, pixels), -1.0)


def move_kernel(cap_blocks, cm_hbm, frames_hbm, out_ref, meta_ref, *scratch):
    frames_ref, cm_ref, meta_s, sems = scratch
    n = out_ref.shape[0]
    rows = frames_ref.shape[0]
    kept = cap_blocks // 2
    get_cm = pltpu.make_async_copy(cm_hbm, cm_ref, sems.at[0])
    get_cm.start()
    get_frames = pltpu.make_async_copy(frames_hbm, frames_ref, sems.at[1])
    get_frames.start()
    get_cm.wait()
    find_blocks(cm_ref[...], cap_blocks, meta_ref)
    to_scalars = pltpu.make_async_copy(meta_ref, meta_s, sems.at[2])
    to_scalars.start()
    to_scalars.wait()
    get_frames.wait()
    for q in range(n):
        for i in range(kept + 1, cap_blocks):
            block = meta_s[LIST, q * cap_blocks + i]
            start = (i - kept - 1) * rows
            out_ref[q, start : start + rows] = take(frames_ref, block)
        start = (cap_blocks - kept - 1) * rows
        block = meta_s[LIST, q * cap_blocks + kept]
        out_ref[q, start:] = fold(take(frames_ref, block), True)


def pack_move(cm, frames, cap_blocks):
    rows = frames.shape[0]
    n = cm.shape[0] // cap_blocks
    height = (cap_blocks - cap_blocks // 2 - 1) * rows + count_half_rows(rows)
    meta = jax.ShapeDtypeStruct((8, cm.shape[0]), jnp.int32)
    return call(
        functools.partial(move_kernel, cap_blocks),
        "pack_move",
        [jax.ShapeDtypeStruct((n, height, BLOCK), frames.dtype), meta],
        in_specs=[ANYWHERE] * 2,
        out_specs=[WHOLE] * 2,
        scratch_shapes=[
            pltpu.VMEM(frames.shape, frames.dtype),
            pltpu.VMEM(cm.shape, cm.dtype),
            pltpu.SMEM(meta.shape, meta.dtype),
            pltpu.SemaphoreType.DMA((3,)),
        ],
    )(
        pltpu.with_memory_space_constraint(cm, pltpu.HBM),
        pltpu.with_memory_space_constraint(frames, pltpu.HBM),
    )


def own_kernel(cap_blocks, meta_s, cm_ref, frames_ref, out_ref, place_ref):
    n = out_ref.shape[0]
    rows = frames_ref.shape[0]
    kept = cap_blocks // 2
    place_ref[...] = find_places(cm_ref[...])
    target = lax.broadcasted_iota(jnp.int32, (BLOCK, BLOCK), 0).astype(jnp.float32)
    for q in range(n):
        count, pixels = meta_s[COUNT, q], meta_s[PIXELS, q]
        is_full = pixels == cap_blocks * BLOCK
        full = gate(is_full)
        fits = (pixels <= BLOCK) & (count <= MERGED)
        compact = 0.0
        for i in range(MERGED):
            block = meta_s[LIST, q * cap_blocks + i]
            place = jnp.where(fits & (i < count), place_ref[pl.ds(block, 1), :], -1.0)
            chosen = (target == place).astype(jnp.float32).astype(jnp.bfloat16)
            compact = compact + dot_nt(take(frames_ref, block), chosen)
        block = meta_s[LIST, q * cap_blocks]
        out_ref[q, 0:rows] = compact.astype(jnp.bfloat16) + take(frames_ref, block) * full
        for i in range(1, kept):
            block = meta_s[LIST, q * cap_blocks + i]
            out_ref[q, i * rows : (i + 1) * rows] = take(frames_ref, block) * full
        block = meta_s[LIST, q * cap_blocks + kept]
        out_ref[q, kept * rows :] = fold(take(frames_ref, block), False) * full


def pack_own(meta, cm, frames, cap_blocks):
    rows = frames.shape[0]
    n = cm.shape[0] // cap_blocks
    height = cap_blocks // 2 * rows + count_half_rows(rows)
    return call(
        functools.partial(own_kernel, cap_blocks),
        "pack_own",
        jax.ShapeDtypeStruct((n, height, BLOCK), frames.dtype),
        in_specs=[pl.BlockSpec(memory_space=pltpu.SMEM)] + [WHOLE] * 2,
        out_specs=WHOLE,
        scratch_shapes=[pltpu.VMEM(cm.shape, jnp.float32)],
        bytes_accessed=4 * 1024 * 1024,
    )(meta, cm, frames)


def share_kernel(cap_blocks, meta_ref, own_ref, theirs_ref, out_ref):
    n, height, _ = out_ref.shape
    rows = height - theirs_ref.shape[1]
    helped = meta_ref[PIXELS : PIXELS + 1, 0:BLOCK] != cap_blocks * BLOCK
    out_ref[:, 0:rows] = own_ref[:, 0:rows]
    for q in range(n):
        other = gate(helped[:, q : q + 1])
        out_ref[q, rows:] = own_ref[q, rows:] + theirs_ref[q] * other


def share(meta, own, theirs, cap_blocks):
    return call(
        functools.partial(share_kernel, cap_blocks),
        "share",
        jax.ShapeDtypeStruct(own.shape, own.dtype),
        in_specs=[WHOLE] * 3,
        out_specs=WHOLE,
        bytes_accessed=4 * 1024 * 1024,
    )(meta, own, theirs)


def left_out(meta, their_meta, cap):
    mine, theirs = meta[PIXELS] == cap, their_meta[PIXELS] == cap
    fits = (meta[PIXELS] <= BLOCK) & (meta[COUNT] <= MERGED)
    return jnp.logical_not(mine | fits), mine & theirs


def rest_kernel(cap_blocks, meta_s, their_meta_s, frames_hbm, cm_hbm, out_ref, *scratch):
    frames_ref, cm_ref = scratch
    n, _, rows, _ = out_ref.shape
    kept = cap_blocks // 2
    pltpu.sync_copy(frames_hbm, frames_ref)
    pltpu.sync_copy(cm_hbm, cm_ref)
    right = lax.broadcasted_iota(jnp.int32, (1, BLOCK), 1) >= BLOCK // 2
    for q in range(n):
        counts = [[ref[row, q] for row in range(PIXELS + 1)] for ref in (meta_s, their_meta_s)]
        large, twice = left_out(*counts, cap_blocks * BLOCK)
        for i in range(cap_blocks):
            block = meta_s[LIST, q * cap_blocks + i]
            wanted = jnp.broadcast_to(large, (1, BLOCK))
            if i >= kept:
                wanted |= twice & right if i == kept else twice
            valid = (cm_ref[pl.ds(block, 1), :] >= 0) & (i < meta_s[COUNT, q])
            out_ref[q, i] = take(frames_ref, block) * gate(valid & wanted)


def pack_rest(meta, their_meta, frames, cm, cap_blocks):
    n = cm.shape[0] // cap_blocks
    return call(
        functools.partial(rest_kernel, cap_blocks),
        "pack_rest",
        jax.ShapeDtypeStruct((n, cap_blocks, frames.shape[0], BLOCK), frames.dtype),
        in_specs=[pl.BlockSpec(memory_space=pltpu.SMEM)] * 2 + [ANYWHERE] * 2,
        out_specs=WHOLE,
        scratch_shapes=[
            pltpu.VMEM(frames.shape, frames.dtype),
            pltpu.VMEM(cm.shape, cm.dtype),
        ],
    )(
        meta,
        their_meta,
        pltpu.with_memory_space_constraint(frames, pltpu.HBM),
        pltpu.with_memory_space_constraint(cm, pltpu.HBM),
    )


def lay_out(raw_ref, rows, first, padded):
    n, height, _ = raw_ref.shape
    total = n * rows
    zero = jnp.zeros((PAD, BLOCK), jnp.float32)
    for i in range(padded.shape[0]):
        slot = first + i
        padded[i, 0:PAD] = zero
        padded[i, PAD + total : 2 * PAD + total] = zero
        for source in range(n):
            start = PAD + source * rows
            if (slot + 1) * rows <= height:
                block = raw_ref[source, slot * rows : (slot + 1) * rows]
                padded[i, start : start + rows] = block.astype(jnp.float32)
            else:
                early, late = unfold(raw_ref[source, slot * rows : height], rows)
                padded[i, start : start + rows // 2] = early
                padded[i, start + rows // 2 : start + rows] = late


def norm_rows(padded, start, chunk, out_ref):
    total = out_ref.shape[0]
    base = PAD + start
    for slot in range(padded.shape[0]):
        raw = padded[slot, base : base + chunk]
        summed = raw
        for offset in range(1, HALF_WIN + 1):
            summed = summed + padded[slot, base - offset : base - offset + chunk]
            summed = summed + padded[slot, base + offset : base + offset + chunk]
        if start == 0 or start + chunk == total:
            frame = start + lax.broadcasted_iota(jnp.int32, (chunk, BLOCK), 0)
            upper = jnp.minimum(frame + HALF_WIN, total - 1)
            lower = jnp.maximum(frame - HALF_WIN, 0)
            mean = summed / (upper - lower + 1).astype(jnp.float32)
        else:
            mean = summed * (1.0 / (2 * HALF_WIN + 1))
        normed = jnp.where(summed > 0.0, raw / mean, 0.0)
        out_ref[start : start + chunk, slot * BLOCK : (slot + 1) * BLOCK] = normed.astype(
            jnp.bfloat16
        )


def norm_kernel(rows, first, raw_ref, *refs):
    out_ref, padded = refs[-2:]
    lay_out(raw_ref, rows, first, padded)
    for start in range(0, out_ref.shape[0], CHUNK):
        norm_rows(padded, start, CHUNK, out_ref)


def normalise(raw, total, first, slots, after=()):
    return call(
        functools.partial(norm_kernel, total // raw.shape[0], first),
        "normalise",
        jax.ShapeDtypeStruct((total, slots * BLOCK), jnp.bfloat16),
        flops=12 * total * slots * BLOCK,
        bytes_accessed=4 * total * slots * BLOCK,
        in_specs=[WHOLE] + [ANYWHERE] * len(after),
        out_specs=WHOLE,
        scratch_shapes=[pltpu.VMEM((slots, total + 2 * PAD, BLOCK), jnp.float32)],
    )(raw, *after)


def set_left(ref, left_ref):
    rows = left_ref.shape[0] - ONES
    first_row = pl.multiple_of(lax.axis_index("pix") * rows, rows)
    left_ref[0:rows] = ref[pl.ds(first_row, rows), :]
    left_ref[rows : rows + ONES] = jnp.ones((ONES, ref.shape[1]), jnp.bfloat16)


def add_sums(pairs, sums, column):
    gram, frame = sums
    rows = pairs[0][0].shape[0] - ONES
    for left_ref, ref in pairs:
        both = dot_nt(left_ref[...], ref[column, :])
        gram = gram + both[0:rows]
        frame = frame + both[rows : rows + 8]
    return gram, frame


def partial_kernel(count, *refs):
    normed, lefts, (gram_out, frame_out) = refs[:count], refs[-count:], refs[-count - 2 : -count]
    before = refs[count : -count - 2]
    for ref, left_ref in zip(normed, lefts):
        set_left(ref, left_ref)
    for start in range(0, gram_out.shape[1], TILE):
        column = slice(start, start + TILE)
        sums = [ref[:, column] for ref in before] or [0.0, 0.0]
        gram_out[:, column], frame_out[:, column] = add_sums(
            list(zip(lefts, normed)), sums, column
        )


def sums_shape(total, parts):
    return [
        jax.ShapeDtypeStruct((total // parts, total), jnp.float32),
        jax.ShapeDtypeStruct((8, total), jnp.float32),
    ]


def partial_sums(normed, before, parts):
    total, width = normed[0].shape
    rows = total // parts
    return call(
        functools.partial(partial_kernel, len(normed)),
        "partial_sums",
        sums_shape(total, parts),
        flops=2 * rows * total * width * len(normed),
        bytes_accessed=4 * rows * total,
        in_specs=[WHOLE] * (len(normed) + len(before)),
        out_specs=[WHOLE] * 2,
        scratch_shapes=[pltpu.VMEM((rows + ONES, x.shape[1]), x.dtype) for x in normed],
    )(*normed, *before)


def result_kernel(meta_ref, their_meta_ref, normed_ref, gram_in, frame_in, out_hbm, *scratch):
    out_ref, frame_ref, sems = scratch
    rows, total = gram_in.shape
    pixels = meta_ref[PIXELS : PIXELS + 1, 0:BLOCK] + their_meta_ref[PIXELS : PIXELS + 1, 0:BLOCK]
    own = lax.broadcasted_iota(jnp.int32, (1, BLOCK), 1) == lax.axis_index("frame")
    number = jnp.sum(jnp.where(own, pixels, 0).astype(jnp.float32), axis=1, keepdims=True)
    ones = jnp.ones((8, normed_ref.shape[1]), jnp.bfloat16)
    frame_ref[...] = frame_in[...] + dot_nt(ones, normed_ref[...])
    first_row = pl.multiple_of(lax.axis_index("pix") * rows, rows)
    row_sum = jnp.broadcast_to(frame_ref[0:1, pl.ds(first_row, rows)], (BLOCK, rows)).T
    row_inv = 1.0 / row_sum[:, 0:1]
    left = normed_ref[pl.ds(first_row, rows), :]
    copies = []
    for i, start in enumerate(range(0, total, TILE)):
        column = slice(start, start + TILE)
        gram = gram_in[:, column] + dot_nt(left, normed_ref[column, :])
        col_inv = 1.0 / frame_ref[0:1, column]
        result = ((gram * row_inv) * col_inv) * number - 1.0
        out_ref[i] = result.astype(jnp.bfloat16)
        copies.append(
            pltpu.make_async_copy(out_ref.at[i], out_hbm.at[0, :, column], sems.at[i])
        )
        copies[-1].start()
    for copy in copies:
        copy.wait()


def correlate(metas, normed, before):
    rows, total = before[0].shape
    tiles = total // TILE
    return call(
        result_kernel,
        "correlate",
        pltpu.HBM((1, rows, total), jnp.bfloat16),
        flops=2 * rows * total * normed.shape[1],
        bytes_accessed=6 * rows * total,
        in_specs=[WHOLE] * 5,
        out_specs=ANYWHERE,
        scratch_shapes=[
            pltpu.VMEM((tiles, rows, TILE), jnp.bfloat16),
            pltpu.VMEM((8, total), jnp.float32),
            pltpu.SemaphoreType.DMA((tiles,)),
        ],
    )(*metas, normed, *before)


def body(frames, cycle_map):
    rows, p_sec = frames.shape
    n = lax.axis_size("frame")
    parts = lax.axis_size("pix")
    total = n * rows
    cap_blocks = p_sec // n // BLOCK
    slots = cap_blocks // 2 + 1
    early = slots - slots // 2
    cm = cycle_map.reshape(p_sec // BLOCK, BLOCK)

    def swap(x):
        return lax.ppermute(x, "pix", SWAP)

    def send(blocks):
        return lax.all_to_all(blocks, "frame", split_axis=0, concat_axis=0, tiled=True)

    moving, meta = pack_move(cm, frames, cap_blocks)
    theirs = swap(moving)
    packed = share(meta, pack_own(meta, cm, frames, cap_blocks), theirs, cap_blocks)
    received = send(packed)

    meta, _ = lax.optimization_barrier((meta, packed))
    their_meta = swap(meta)
    cap = cap_blocks * BLOCK
    large, twice = left_out(meta[:, :n], their_meta[:, :n], cap)
    overflow = jnp.any(large | twice | left_out(their_meta[:, :n], meta[:, :n], cap)[0])

    first = normalise(received, total, 0, early, [overflow.astype(jnp.int32).reshape(1)])
    their_first = swap(first)
    last = normalise(received, total, early, slots - early, [first])
    their_last = swap(last)
    sums = partial_sums([first, last], [], parts)
    sums = partial_sums([their_first], sums, parts)

    def spill(frames, cm, meta, their_meta, their_last, *sums):
        rest = send(pack_rest(meta, their_meta, frames, cm, cap_blocks))
        normed = normalise(rest.reshape(n, cap_blocks * rows, BLOCK), total, 0, cap_blocks)
        sums = partial_sums([normed, swap(normed)], sums, parts)
        return correlate([meta, their_meta], their_last, sums)

    def fits(frames, cm, meta, their_meta, their_last, *sums):
        return correlate([meta, their_meta], their_last, sums)

    return lax.cond(overflow, spill, fits, frames, cm, meta, their_meta, their_last, *sums)


def solution(mesh):
    return jax.shard_map(
        body,
        mesh=mesh,
        in_specs=(P("frame", "pix"), P("pix")),
        out_specs=P("frame", "pix", None),
        check_vma=False,
    )
```

```python
import functools

import jax
import jax.numpy as jnp
from jax import lax
from jax.experimental import pallas as pl
from jax.experimental.pallas import tpu as pltpu
from jax.sharding import PartitionSpec as P

BLOCK = 128
HALF_WIN = 2
PAD = 8
TILE = 256
CHUNK = 128
ONES = 16
VMEM_BYTES = 32 * 1024 * 1024
LIST, COUNT, PIXELS = 0, 1, 2
MERGED = 2
SWAP = [(0, 1), (1, 0)]
WHOLE = pl.BlockSpec(memory_space=pltpu.VMEM)
ANYWHERE = pl.BlockSpec(memory_space=pl.ANY)


def call(kernel, name, out_shape, flops=0, bytes_accessed=0, limit=VMEM_BYTES, **kw):
    return pl.pallas_call(
        kernel,
        out_shape=out_shape,
        compiler_params=pltpu.CompilerParams(vmem_limit_bytes=limit),
        cost_estimate=pl.CostEstimate(
            flops=flops, bytes_accessed=bytes_accessed, transcendentals=0
        ),
        name=name,
        **kw,
    )


def dot_nt(a, b):
    return lax.dot_general(a, b, (((1,), (1,)), ((), ())), preferred_element_type=jnp.float32)


def count_half_rows(rows):
    return max(16, rows // 2)


def gate(wanted):
    wanted = jnp.broadcast_to(wanted, (1, BLOCK))
    return wanted.astype(jnp.float32).astype(jnp.bfloat16)


def take(frames_ref, block):
    return frames_ref[:, pl.ds(pl.multiple_of(block * BLOCK, BLOCK), BLOCK)]


def fold(block, right):
    rows = block.shape[0] // 2
    half = BLOCK // 2
    early, late = block[0:rows].astype(jnp.float32), block[rows:].astype(jnp.float32)
    left = lax.broadcasted_iota(jnp.int32, (rows, BLOCK), 1) < half
    if right:
        folded = jnp.where(left, pltpu.roll(early, half, 1), late)
    else:
        folded = jnp.where(left, early, pltpu.roll(late, half, 1))
    spare = count_half_rows(block.shape[0]) - rows
    if spare:
        folded = jnp.concatenate([folded, jnp.zeros((spare, BLOCK), jnp.float32)])
    return folded.astype(jnp.bfloat16)


def unfold(folded, rows):
    half = BLOCK // 2
    early = folded[0 : rows // 2].astype(jnp.float32)
    left = lax.broadcasted_iota(jnp.int32, early.shape, 1) < half
    return jnp.where(left, early, 0.0), jnp.where(left, pltpu.roll(early, half, 1), 0.0)


def find_members(cm):
    blocks = cm.shape[0]
    first = cm[:, 0:1]
    member = first == lax.broadcasted_iota(jnp.int32, (blocks, BLOCK), 1)
    row = lax.broadcasted_iota(jnp.int32, (blocks, blocks), 0)
    col = lax.broadcasted_iota(jnp.int32, (blocks, blocks), 1)
    earlier = (col < row).astype(jnp.float32).astype(jnp.bfloat16)
    pixels = jnp.sum((cm >= 0).astype(jnp.float32), axis=1, keepdims=True)
    return first, member.astype(jnp.float32), earlier, pixels


def sum_before(earlier, member, values):
    before = jnp.dot(
        earlier, (member * values).astype(jnp.bfloat16), preferred_element_type=jnp.float32
    )
    return jnp.sum(before * member, axis=1, keepdims=True)


def find_blocks(cm, cap_blocks, meta_ref):
    blocks = cm.shape[0]
    width = meta_ref.shape[1]
    first, member, earlier, pixels = find_members(cm)
    rank = sum_before(earlier, member, 1.0).astype(jnp.int32)
    slot = jnp.where(first >= 0, first * cap_blocks + rank, -1)
    hit = slot == lax.broadcasted_iota(jnp.int32, (blocks, width), 1)
    index = lax.broadcasted_iota(jnp.int32, (blocks, width), 0).astype(jnp.float32)
    meta_ref[...] = jnp.zeros_like(meta_ref)
    meta_ref[LIST : LIST + 1, :] = jnp.sum(
        jnp.where(hit, index, 0.0), axis=0, keepdims=True
    ).astype(jnp.int32)
    meta_ref[COUNT : COUNT + 1, 0:BLOCK] = jnp.sum(member, axis=0, keepdims=True).astype(
        jnp.int32
    )
    meta_ref[PIXELS : PIXELS + 1, 0:BLOCK] = jnp.sum(
        member * pixels, axis=0, keepdims=True
    ).astype(jnp.int32)


def find_places(cm):
    _, member, earlier, pixels = find_members(cm)
    valid = (cm >= 0).astype(jnp.float32)
    row = lax.broadcasted_iota(jnp.int32, (BLOCK, BLOCK), 0)
    col = lax.broadcasted_iota(jnp.int32, (BLOCK, BLOCK), 1)
    before = (row < col).astype(jnp.float32).astype(jnp.bfloat16)
    place = jnp.dot(valid.astype(jnp.bfloat16), before, preferred_element_type=jnp.float32)
    return jnp.where(cm >= 0, place + sum_before(earlier, member, pixels), -1.0)


def move_kernel(cap_blocks, cm_hbm, frames_hbm, out_ref, meta_ref, *scratch):
    frames_ref, cm_ref, meta_s, sems = scratch
    n = out_ref.shape[0]
    rows = frames_ref.shape[0]
    kept = cap_blocks // 2
    get_cm = pltpu.make_async_copy(cm_hbm, cm_ref, sems.at[0])
    get_cm.start()
    get_frames = pltpu.make_async_copy(frames_hbm, frames_ref, sems.at[1])
    get_frames.start()
    get_cm.wait()
    find_blocks(cm_ref[...], cap_blocks, meta_ref)
    to_scalars = pltpu.make_async_copy(meta_ref, meta_s, sems.at[2])
    to_scalars.start()
    to_scalars.wait()
    get_frames.wait()
    for q in range(n):
        for i in range(kept + 1, cap_blocks):
            block = meta_s[LIST, q * cap_blocks + i]
            start = (i - kept - 1) * rows
            out_ref[q, start : start + rows] = take(frames_ref, block)
        start = (cap_blocks - kept - 1) * rows
        block = meta_s[LIST, q * cap_blocks + kept]
        out_ref[q, start:] = fold(take(frames_ref, block), True)


def pack_move(cm, frames, cap_blocks):
    rows = frames.shape[0]
    n = cm.shape[0] // cap_blocks
    height = (cap_blocks - cap_blocks // 2 - 1) * rows + count_half_rows(rows)
    meta = jax.ShapeDtypeStruct((8, cm.shape[0]), jnp.int32)
    return call(
        functools.partial(move_kernel, cap_blocks),
        "pack_move",
        [jax.ShapeDtypeStruct((n, height, BLOCK), frames.dtype), meta],
        in_specs=[ANYWHERE] * 2,
        out_specs=[WHOLE] * 2,
        scratch_shapes=[
            pltpu.VMEM(frames.shape, frames.dtype),
            pltpu.VMEM(cm.shape, cm.dtype),
            pltpu.SMEM(meta.shape, meta.dtype),
            pltpu.SemaphoreType.DMA((3,)),
        ],
    )(
        pltpu.with_memory_space_constraint(cm, pltpu.HBM),
        pltpu.with_memory_space_constraint(frames, pltpu.HBM),
    )


def own_kernel(cap_blocks, meta_s, cm_ref, frames_ref, out_ref, place_ref):
    n = out_ref.shape[0]
    rows = frames_ref.shape[0]
    kept = cap_blocks // 2
    place_ref[...] = find_places(cm_ref[...])
    target = lax.broadcasted_iota(jnp.int32, (BLOCK, BLOCK), 0).astype(jnp.float32)
    for q in range(n):
        count, pixels = meta_s[COUNT, q], meta_s[PIXELS, q]
        is_full = pixels == cap_blocks * BLOCK
        full = gate(is_full)
        fits = (pixels <= BLOCK) & (count <= MERGED)
        compact = 0.0
        for i in range(MERGED):
            block = meta_s[LIST, q * cap_blocks + i]
            place = jnp.where(fits & (i < count), place_ref[pl.ds(block, 1), :], -1.0)
            chosen = (target == place).astype(jnp.float32).astype(jnp.bfloat16)
            compact = compact + dot_nt(take(frames_ref, block), chosen)
        block = meta_s[LIST, q * cap_blocks]
        out_ref[q, 0:rows] = compact.astype(jnp.bfloat16) + take(frames_ref, block) * full
        for i in range(1, kept):
            block = meta_s[LIST, q * cap_blocks + i]
            out_ref[q, i * rows : (i + 1) * rows] = take(frames_ref, block) * full
        block = meta_s[LIST, q * cap_blocks + kept]
        out_ref[q, kept * rows :] = fold(take(frames_ref, block), False) * full


def pack_own(meta, cm, frames, cap_blocks):
    rows = frames.shape[0]
    n = cm.shape[0] // cap_blocks
    height = cap_blocks // 2 * rows + count_half_rows(rows)
    return call(
        functools.partial(own_kernel, cap_blocks),
        "pack_own",
        jax.ShapeDtypeStruct((n, height, BLOCK), frames.dtype),
        in_specs=[pl.BlockSpec(memory_space=pltpu.SMEM)] + [WHOLE] * 2,
        out_specs=WHOLE,
        scratch_shapes=[pltpu.VMEM(cm.shape, jnp.float32)],
        bytes_accessed=4 * 1024 * 1024,
    )(meta, cm, frames)


def share_kernel(cap_blocks, meta_ref, own_ref, theirs_ref, out_ref):
    n, height, _ = out_ref.shape
    rows = height - theirs_ref.shape[1]
    helped = meta_ref[PIXELS : PIXELS + 1, 0:BLOCK] != cap_blocks * BLOCK
    out_ref[:, 0:rows] = own_ref[:, 0:rows]
    for q in range(n):
        other = gate(helped[:, q : q + 1])
        out_ref[q, rows:] = own_ref[q, rows:] + theirs_ref[q] * other


def share(meta, own, theirs, cap_blocks):
    return call(
        functools.partial(share_kernel, cap_blocks),
        "share",
        jax.ShapeDtypeStruct(own.shape, own.dtype),
        in_specs=[WHOLE] * 3,
        out_specs=WHOLE,
        bytes_accessed=4 * 1024 * 1024,
    )(meta, own, theirs)


def left_out(meta, their_meta, cap):
    mine, theirs = meta[PIXELS] == cap, their_meta[PIXELS] == cap
    fits = (meta[PIXELS] <= BLOCK) & (meta[COUNT] <= MERGED)
    return jnp.logical_not(mine | fits), mine & theirs


def rest_kernel(cap_blocks, meta_s, their_meta_s, frames_hbm, cm_hbm, out_ref, *scratch):
    frames_ref, cm_ref = scratch
    n, _, rows, _ = out_ref.shape
    kept = cap_blocks // 2
    pltpu.sync_copy(frames_hbm, frames_ref)
    pltpu.sync_copy(cm_hbm, cm_ref)
    right = lax.broadcasted_iota(jnp.int32, (1, BLOCK), 1) >= BLOCK // 2
    for q in range(n):
        counts = [[ref[row, q] for row in range(PIXELS + 1)] for ref in (meta_s, their_meta_s)]
        large, twice = left_out(*counts, cap_blocks * BLOCK)
        for i in range(cap_blocks):
            block = meta_s[LIST, q * cap_blocks + i]
            wanted = jnp.broadcast_to(large, (1, BLOCK))
            if i >= kept:
                wanted |= twice & right if i == kept else twice
            valid = (cm_ref[pl.ds(block, 1), :] >= 0) & (i < meta_s[COUNT, q])
            out_ref[q, i] = take(frames_ref, block) * gate(valid & wanted)


def pack_rest(meta, their_meta, frames, cm, cap_blocks):
    n = cm.shape[0] // cap_blocks
    return call(
        functools.partial(rest_kernel, cap_blocks),
        "pack_rest",
        jax.ShapeDtypeStruct((n, cap_blocks, frames.shape[0], BLOCK), frames.dtype),
        in_specs=[pl.BlockSpec(memory_space=pltpu.SMEM)] * 2 + [ANYWHERE] * 2,
        out_specs=WHOLE,
        scratch_shapes=[
            pltpu.VMEM(frames.shape, frames.dtype),
            pltpu.VMEM(cm.shape, cm.dtype),
        ],
    )(
        meta,
        their_meta,
        pltpu.with_memory_space_constraint(frames, pltpu.HBM),
        pltpu.with_memory_space_constraint(cm, pltpu.HBM),
    )


def lay_out(raw_ref, rows, first, whole, padded):
    n, height, _ = raw_ref.shape
    total = n * rows
    zero = jnp.zeros((PAD, BLOCK), jnp.float32)
    for i in range(padded.shape[0]):
        slot = first + i
        padded[i, 0:PAD] = zero
        padded[i, PAD + total : 2 * PAD + total] = zero
        for source in range(n):
            start = PAD + source * rows
            if slot < whole:
                block = raw_ref[source, slot * rows : (slot + 1) * rows]
                padded[i, start : start + rows] = block.astype(jnp.float32)
            else:
                early, late = unfold(raw_ref[source, slot * rows : height], rows)
                padded[i, start : start + rows // 2] = early
                padded[i, start + rows // 2 : start + rows] = late


def norm_rows(padded, start, chunk, out_ref):
    total = out_ref.shape[0]
    base = PAD + start
    for slot in range(padded.shape[0]):
        raw = padded[slot, base : base + chunk]
        summed = raw
        for offset in range(1, HALF_WIN + 1):
            summed = summed + padded[slot, base - offset : base - offset + chunk]
            summed = summed + padded[slot, base + offset : base + offset + chunk]
        if start == 0 or start + chunk == total:
            frame = start + lax.broadcasted_iota(jnp.int32, (chunk, BLOCK), 0)
            upper = jnp.minimum(frame + HALF_WIN, total - 1)
            lower = jnp.maximum(frame - HALF_WIN, 0)
            mean = summed / (upper - lower + 1).astype(jnp.float32)
        else:
            mean = summed * (1.0 / (2 * HALF_WIN + 1))
        normed = jnp.where(summed > 0.0, raw / mean, 0.0)
        out_ref[start : start + chunk, slot * BLOCK : (slot + 1) * BLOCK] = normed.astype(
            jnp.bfloat16
        )


def norm_kernel(rows, first, whole, raw_ref, *refs):
    out_ref, padded = refs[-2:]
    lay_out(raw_ref, rows, first, whole, padded)
    for start in range(0, out_ref.shape[0], CHUNK):
        norm_rows(padded, start, CHUNK, out_ref)


def normalise(raw, total, first, slots, whole, after=()):
    return call(
        functools.partial(norm_kernel, total // raw.shape[0], first, whole),
        "normalise",
        jax.ShapeDtypeStruct((total, slots * BLOCK), jnp.bfloat16),
        flops=12 * total * slots * BLOCK,
        bytes_accessed=4 * total * slots * BLOCK,
        in_specs=[WHOLE] + [ANYWHERE] * len(after),
        out_specs=WHOLE,
        scratch_shapes=[pltpu.VMEM((slots, total + 2 * PAD, BLOCK), jnp.float32)],
    )(raw, *after)


def set_left(ref, left_ref):
    rows = left_ref.shape[0] - ONES
    first_row = pl.multiple_of(lax.axis_index("pix") * rows, rows)
    left_ref[0:rows] = ref[pl.ds(first_row, rows), :]
    left_ref[rows : rows + ONES] = jnp.ones((ONES, ref.shape[1]), jnp.bfloat16)


def add_sums(pairs, sums, column):
    gram, frame = sums
    rows = pairs[0][0].shape[0] - ONES
    for left_ref, ref in pairs:
        both = dot_nt(left_ref[...], ref[column, :])
        gram = gram + both[0:rows]
        frame = frame + both[rows : rows + 8]
    return gram, frame


def partial_kernel(count, *refs):
    normed, lefts, (gram_out, frame_out) = refs[:count], refs[-count:], refs[-count - 2 : -count]
    before = refs[count : -count - 2]
    for ref, left_ref in zip(normed, lefts):
        set_left(ref, left_ref)
    for start in range(0, gram_out.shape[1], TILE):
        column = slice(start, start + TILE)
        sums = [ref[:, column] for ref in before] or [0.0, 0.0]
        gram_out[:, column], frame_out[:, column] = add_sums(
            list(zip(lefts, normed)), sums, column
        )


def sums_shape(total, parts):
    return [
        jax.ShapeDtypeStruct((total // parts, total), jnp.float32),
        jax.ShapeDtypeStruct((8, total), jnp.float32),
    ]


def partial_sums(normed, before, parts):
    total, width = normed[0].shape
    rows = total // parts
    return call(
        functools.partial(partial_kernel, len(normed)),
        "partial_sums",
        sums_shape(total, parts),
        flops=2 * rows * total * width * len(normed),
        bytes_accessed=4 * rows * total,
        in_specs=[WHOLE] * (len(normed) + len(before)),
        out_specs=[WHOLE] * 2,
        scratch_shapes=[pltpu.VMEM((rows + ONES, x.shape[1]), x.dtype) for x in normed],
    )(*normed, *before)


def result_kernel(meta_ref, their_meta_ref, normed_ref, gram_in, frame_in, out_hbm, *scratch):
    out_ref, frame_ref, sems = scratch
    rows, total = gram_in.shape
    pixels = meta_ref[PIXELS : PIXELS + 1, 0:BLOCK] + their_meta_ref[PIXELS : PIXELS + 1, 0:BLOCK]
    own = lax.broadcasted_iota(jnp.int32, (1, BLOCK), 1) == lax.axis_index("frame")
    number = jnp.sum(jnp.where(own, pixels, 0).astype(jnp.float32), axis=1, keepdims=True)
    ones = jnp.ones((8, normed_ref.shape[1]), jnp.bfloat16)
    frame_ref[...] = frame_in[...] + dot_nt(ones, normed_ref[...])
    first_row = pl.multiple_of(lax.axis_index("pix") * rows, rows)
    row_sum = jnp.broadcast_to(frame_ref[0:1, pl.ds(first_row, rows)], (BLOCK, rows)).T
    row_inv = 1.0 / row_sum[:, 0:1]
    left = normed_ref[pl.ds(first_row, rows), :]
    copies = []
    for i, start in enumerate(range(0, total, TILE)):
        column = slice(start, start + TILE)
        gram = gram_in[:, column] + dot_nt(left, normed_ref[column, :])
        col_inv = 1.0 / frame_ref[0:1, column]
        result = ((gram * row_inv) * col_inv) * number - 1.0
        out_ref[i] = result.astype(jnp.bfloat16)
        copies.append(
            pltpu.make_async_copy(out_ref.at[i], out_hbm.at[0, :, column], sems.at[i])
        )
        copies[-1].start()
    for copy in copies:
        copy.wait()


def correlate(metas, normed, before):
    rows, total = before[0].shape
    tiles = total // TILE
    return call(
        result_kernel,
        "correlate",
        pltpu.HBM((1, rows, total), jnp.bfloat16),
        flops=2 * rows * total * normed.shape[1],
        bytes_accessed=6 * rows * total,
        in_specs=[WHOLE] * 5,
        out_specs=ANYWHERE,
        scratch_shapes=[
            pltpu.VMEM((tiles, rows, TILE), jnp.bfloat16),
            pltpu.VMEM((8, total), jnp.float32),
            pltpu.SemaphoreType.DMA((tiles,)),
        ],
    )(*metas, normed, *before)


def body(frames, cycle_map):
    rows, p_sec = frames.shape
    n = lax.axis_size("frame")
    parts = lax.axis_size("pix")
    total = n * rows
    cap_blocks = p_sec // n // BLOCK
    slots = cap_blocks // 2 + 1
    early = slots - slots // 2
    cm = cycle_map.reshape(p_sec // BLOCK, BLOCK)

    def swap(x):
        return lax.ppermute(x, "pix", SWAP)

    def send(blocks):
        return lax.all_to_all(blocks, "frame", split_axis=0, concat_axis=0, tiled=True)

    moving, meta = pack_move(cm, frames, cap_blocks)
    theirs = swap(moving)
    packed = share(meta, pack_own(meta, cm, frames, cap_blocks), theirs, cap_blocks)
    received = send(packed)

    meta, _ = lax.optimization_barrier((meta, packed))
    their_meta = swap(meta)
    cap = cap_blocks * BLOCK
    large, twice = left_out(meta[:, :n], their_meta[:, :n], cap)
    overflow = jnp.any(large | twice | left_out(their_meta[:, :n], meta[:, :n], cap)[0])

    flag = overflow.astype(jnp.int32).reshape(1)
    first = normalise(received, total, 0, early, slots - 1, [flag])
    their_first = swap(first)
    last = normalise(received, total, early, slots - early, slots - 1, [first])
    their_last = swap(last)
    sums = partial_sums([first, last], [], parts)
    sums = partial_sums([their_first], sums, parts)

    def spill(frames, cm, meta, their_meta, their_last, *sums):
        rest = send(pack_rest(meta, their_meta, frames, cm, cap_blocks))
        rest = rest.reshape(n, cap_blocks * rows, BLOCK)
        normed = normalise(rest, total, 0, cap_blocks, cap_blocks)
        sums = partial_sums([normed, swap(normed)], sums, parts)
        return correlate([meta, their_meta], their_last, sums)

    def fits(frames, cm, meta, their_meta, their_last, *sums):
        return correlate([meta, their_meta], their_last, sums)

    return lax.cond(overflow, spill, fits, frames, cm, meta, their_meta, their_last, *sums)


def solution(mesh):
    return jax.shard_map(
        body,
        mesh=mesh,
        in_specs=(P("frame", "pix"), P("pix")),
        out_specs=P("frame", "pix", None),
        check_vma=False,
    )
```

```python
import functools

import jax
import jax.numpy as jnp
from jax import lax
from jax.experimental import pallas as pl
from jax.experimental.pallas import tpu as pltpu
from jax.sharding import PartitionSpec as P

BLOCK = 128
HALF_WIN = 2
PAD = 8
TILE = 256
CHUNK = 128
ONES = 16
VMEM_BYTES = 32 * 1024 * 1024
LIST, COUNT, PIXELS = 0, 1, 2
MERGED = 2
SWAP = [(0, 1), (1, 0)]
WHOLE = pl.BlockSpec(memory_space=pltpu.VMEM)
ANYWHERE = pl.BlockSpec(memory_space=pl.ANY)


def call(kernel, name, out_shape, flops=0, bytes_accessed=0, limit=VMEM_BYTES, **kw):
    return pl.pallas_call(
        kernel,
        out_shape=out_shape,
        compiler_params=pltpu.CompilerParams(vmem_limit_bytes=limit),
        cost_estimate=pl.CostEstimate(
            flops=flops, bytes_accessed=bytes_accessed, transcendentals=0
        ),
        name=name,
        **kw,
    )


def dot_nt(a, b):
    return lax.dot_general(a, b, (((1,), (1,)), ((), ())), preferred_element_type=jnp.float32)


def count_half_rows(rows):
    return max(16, rows // 2)


def gate(wanted):
    wanted = jnp.broadcast_to(wanted, (1, BLOCK))
    return wanted.astype(jnp.float32).astype(jnp.bfloat16)


def take(frames_ref, block):
    return frames_ref[:, pl.ds(pl.multiple_of(block * BLOCK, BLOCK), BLOCK)]


def fold(block, right):
    rows = block.shape[0] // 2
    half = BLOCK // 2
    early, late = block[0:rows].astype(jnp.float32), block[rows:].astype(jnp.float32)
    left = lax.broadcasted_iota(jnp.int32, (rows, BLOCK), 1) < half
    if right:
        folded = jnp.where(left, pltpu.roll(early, half, 1), late)
    else:
        folded = jnp.where(left, early, pltpu.roll(late, half, 1))
    spare = count_half_rows(block.shape[0]) - rows
    if spare:
        folded = jnp.concatenate([folded, jnp.zeros((spare, BLOCK), jnp.float32)])
    return folded.astype(jnp.bfloat16)


def unfold(folded, rows):
    half = BLOCK // 2
    early = folded[0 : rows // 2].astype(jnp.float32)
    left = lax.broadcasted_iota(jnp.int32, early.shape, 1) < half
    return jnp.where(left, early, 0.0), jnp.where(left, pltpu.roll(early, half, 1), 0.0)


def find_members(cm):
    blocks = cm.shape[0]
    first = cm[:, 0:1]
    member = first == lax.broadcasted_iota(jnp.int32, (blocks, BLOCK), 1)
    row = lax.broadcasted_iota(jnp.int32, (blocks, blocks), 0)
    col = lax.broadcasted_iota(jnp.int32, (blocks, blocks), 1)
    earlier = (col < row).astype(jnp.float32).astype(jnp.bfloat16)
    pixels = jnp.sum((cm >= 0).astype(jnp.float32), axis=1, keepdims=True)
    return first, member.astype(jnp.float32), earlier, pixels


def sum_before(earlier, member, values):
    before = jnp.dot(
        earlier, (member * values).astype(jnp.bfloat16), preferred_element_type=jnp.float32
    )
    return jnp.sum(before * member, axis=1, keepdims=True)


def find_blocks(members, cap_blocks, width):
    first, member, earlier, _ = members
    blocks = first.shape[0]
    rank = sum_before(earlier, member, 1.0).astype(jnp.int32)
    slot = jnp.where(first >= 0, first * cap_blocks + rank, -1)
    hit = slot == lax.broadcasted_iota(jnp.int32, (blocks, width), 1)
    index = lax.broadcasted_iota(jnp.int32, (blocks, width), 0).astype(jnp.float32)
    return jnp.sum(jnp.where(hit, index, 0.0), axis=0, keepdims=True).astype(jnp.int32)


def find_places(cm):
    _, member, earlier, pixels = find_members(cm)
    valid = (cm >= 0).astype(jnp.float32)
    row = lax.broadcasted_iota(jnp.int32, (BLOCK, BLOCK), 0)
    col = lax.broadcasted_iota(jnp.int32, (BLOCK, BLOCK), 1)
    before = (row < col).astype(jnp.float32).astype(jnp.bfloat16)
    place = jnp.dot(valid.astype(jnp.bfloat16), before, preferred_element_type=jnp.float32)
    return jnp.where(cm >= 0, place + sum_before(earlier, member, pixels), -1.0)


def move_kernel(cap_blocks, cm_hbm, frames_hbm, out_ref, meta_ref, frames_ref, cm_ref, *scratch):
    list_ref, list_s, sems = scratch
    n = out_ref.shape[0]
    rows = frames_ref.shape[0]
    kept = cap_blocks // 2
    get_cm = pltpu.make_async_copy(cm_hbm, cm_ref, sems.at[0])
    get_cm.start()
    get_frames = pltpu.make_async_copy(frames_hbm, frames_ref, sems.at[1])
    get_frames.start()
    get_cm.wait()
    members = find_members(cm_ref[...])
    found = find_blocks(members, cap_blocks, meta_ref.shape[1])
    list_ref[...] = jnp.broadcast_to(found, list_ref.shape)
    to_scalars = pltpu.make_async_copy(list_ref, list_s, sems.at[2])
    to_scalars.start()
    _, member, _, pixels = members
    meta_ref[...] = jnp.zeros_like(meta_ref)
    meta_ref[LIST : LIST + 1, :] = found
    for row, values in ((COUNT, member), (PIXELS, member * pixels)):
        totals = jnp.sum(values, axis=0, keepdims=True)
        meta_ref[row : row + 1, 0:BLOCK] = totals.astype(jnp.int32)
    to_scalars.wait()
    get_frames.wait()
    for q in range(n):
        for i in range(kept + 1, cap_blocks):
            block = list_s[0, q * cap_blocks + i]
            start = (i - kept - 1) * rows
            out_ref[q, start : start + rows] = take(frames_ref, block)
        start = (cap_blocks - kept - 1) * rows
        block = list_s[0, q * cap_blocks + kept]
        out_ref[q, start:] = fold(take(frames_ref, block), True)


def pack_move(cm, frames, cap_blocks):
    rows = frames.shape[0]
    n = cm.shape[0] // cap_blocks
    height = (cap_blocks - cap_blocks // 2 - 1) * rows + count_half_rows(rows)
    meta = jax.ShapeDtypeStruct((8, cm.shape[0]), jnp.int32)
    return call(
        functools.partial(move_kernel, cap_blocks),
        "pack_move",
        [
            jax.ShapeDtypeStruct((n, height, BLOCK), frames.dtype),
            meta,
            jax.ShapeDtypeStruct(frames.shape, frames.dtype),
            jax.ShapeDtypeStruct(cm.shape, cm.dtype),
        ],
        in_specs=[ANYWHERE] * 2,
        out_specs=[WHOLE] * 4,
        scratch_shapes=[
            pltpu.VMEM(meta.shape, meta.dtype),
            pltpu.SMEM(meta.shape, meta.dtype),
            pltpu.SemaphoreType.DMA((3,)),
        ],
    )(
        pltpu.with_memory_space_constraint(cm, pltpu.HBM),
        pltpu.with_memory_space_constraint(frames, pltpu.HBM),
    )


def own_kernel(cap_blocks, meta_s, cm_ref, frames_ref, out_ref, place_ref):
    n = out_ref.shape[0]
    rows = frames_ref.shape[0]
    kept = cap_blocks // 2
    place_ref[...] = find_places(cm_ref[...])
    target = lax.broadcasted_iota(jnp.int32, (BLOCK, BLOCK), 0).astype(jnp.float32)
    for q in range(n):
        count, pixels = meta_s[COUNT, q], meta_s[PIXELS, q]
        is_full = pixels == cap_blocks * BLOCK
        full = gate(is_full)
        fits = (pixels <= BLOCK) & (count <= MERGED)
        compact = 0.0
        for i in range(MERGED):
            block = meta_s[LIST, q * cap_blocks + i]
            place = jnp.where(fits & (i < count), place_ref[pl.ds(block, 1), :], -1.0)
            chosen = (target == place).astype(jnp.float32).astype(jnp.bfloat16)
            compact = compact + dot_nt(take(frames_ref, block), chosen)
        block = meta_s[LIST, q * cap_blocks]
        out_ref[q, 0:rows] = compact.astype(jnp.bfloat16) + take(frames_ref, block) * full
        for i in range(1, kept):
            block = meta_s[LIST, q * cap_blocks + i]
            out_ref[q, i * rows : (i + 1) * rows] = take(frames_ref, block) * full
        block = meta_s[LIST, q * cap_blocks + kept]
        out_ref[q, kept * rows :] = fold(take(frames_ref, block), False) * full


def pack_own(meta, cm, frames, cap_blocks):
    rows = frames.shape[0]
    n = cm.shape[0] // cap_blocks
    height = cap_blocks // 2 * rows + count_half_rows(rows)
    return call(
        functools.partial(own_kernel, cap_blocks),
        "pack_own",
        jax.ShapeDtypeStruct((n, height, BLOCK), frames.dtype),
        in_specs=[pl.BlockSpec(memory_space=pltpu.SMEM)] + [WHOLE] * 2,
        out_specs=WHOLE,
        scratch_shapes=[pltpu.VMEM(cm.shape, jnp.float32)],
        bytes_accessed=4 * 1024 * 1024,
    )(meta, cm, frames)


def share_kernel(cap_blocks, meta_ref, own_ref, theirs_ref, out_ref):
    n, height, _ = out_ref.shape
    rows = height - theirs_ref.shape[1]
    helped = meta_ref[PIXELS : PIXELS + 1, 0:BLOCK] != cap_blocks * BLOCK
    out_ref[:, 0:rows] = own_ref[:, 0:rows]
    for q in range(n):
        other = gate(helped[:, q : q + 1])
        out_ref[q, rows:] = own_ref[q, rows:] + theirs_ref[q] * other


def share(meta, own, theirs, cap_blocks):
    return call(
        functools.partial(share_kernel, cap_blocks),
        "share",
        jax.ShapeDtypeStruct(own.shape, own.dtype),
        in_specs=[WHOLE] * 3,
        out_specs=WHOLE,
        bytes_accessed=4 * 1024 * 1024,
    )(meta, own, theirs)


def left_out(meta, their_meta, cap):
    mine, theirs = meta[PIXELS] == cap, their_meta[PIXELS] == cap
    fits = (meta[PIXELS] <= BLOCK) & (meta[COUNT] <= MERGED)
    return jnp.logical_not(mine | fits), mine & theirs


def rest_kernel(cap_blocks, meta_s, their_meta_s, frames_hbm, cm_hbm, out_ref, *scratch):
    frames_ref, cm_ref = scratch
    n, _, rows, _ = out_ref.shape
    kept = cap_blocks // 2
    pltpu.sync_copy(frames_hbm, frames_ref)
    pltpu.sync_copy(cm_hbm, cm_ref)
    right = lax.broadcasted_iota(jnp.int32, (1, BLOCK), 1) >= BLOCK // 2
    for q in range(n):
        counts = [[ref[row, q] for row in range(PIXELS + 1)] for ref in (meta_s, their_meta_s)]
        large, twice = left_out(*counts, cap_blocks * BLOCK)
        for i in range(cap_blocks):
            block = meta_s[LIST, q * cap_blocks + i]
            wanted = jnp.broadcast_to(large, (1, BLOCK))
            if i >= kept:
                wanted |= twice & right if i == kept else twice
            valid = (cm_ref[pl.ds(block, 1), :] >= 0) & (i < meta_s[COUNT, q])
            out_ref[q, i] = take(frames_ref, block) * gate(valid & wanted)


def pack_rest(meta, their_meta, frames, cm, cap_blocks):
    n = cm.shape[0] // cap_blocks
    return call(
        functools.partial(rest_kernel, cap_blocks),
        "pack_rest",
        jax.ShapeDtypeStruct((n, cap_blocks, frames.shape[0], BLOCK), frames.dtype),
        in_specs=[pl.BlockSpec(memory_space=pltpu.SMEM)] * 2 + [ANYWHERE] * 2,
        out_specs=WHOLE,
        scratch_shapes=[
            pltpu.VMEM(frames.shape, frames.dtype),
            pltpu.VMEM(cm.shape, cm.dtype),
        ],
    )(
        meta,
        their_meta,
        pltpu.with_memory_space_constraint(frames, pltpu.HBM),
        pltpu.with_memory_space_constraint(cm, pltpu.HBM),
    )


def lay_out(raw_ref, rows, first, whole, padded):
    n, height, _ = raw_ref.shape
    total = n * rows
    zero = jnp.zeros((PAD, BLOCK), jnp.float32)
    for i in range(padded.shape[0]):
        slot = first + i
        padded[i, 0:PAD] = zero
        padded[i, PAD + total : 2 * PAD + total] = zero
        for source in range(n):
            start = PAD + source * rows
            if slot < whole:
                block = raw_ref[source, slot * rows : (slot + 1) * rows]
                padded[i, start : start + rows] = block.astype(jnp.float32)
            else:
                early, late = unfold(raw_ref[source, slot * rows : height], rows)
                padded[i, start : start + rows // 2] = early
                padded[i, start + rows // 2 : start + rows] = late


def norm_rows(padded, start, chunk, out_ref):
    total = out_ref.shape[0]
    base = PAD + start
    for slot in range(padded.shape[0]):
        raw = padded[slot, base : base + chunk]
        summed = raw
        for offset in range(1, HALF_WIN + 1):
            summed = summed + padded[slot, base - offset : base - offset + chunk]
            summed = summed + padded[slot, base + offset : base + offset + chunk]
        if start == 0 or start + chunk == total:
            frame = start + lax.broadcasted_iota(jnp.int32, (chunk, BLOCK), 0)
            upper = jnp.minimum(frame + HALF_WIN, total - 1)
            lower = jnp.maximum(frame - HALF_WIN, 0)
            mean = summed / (upper - lower + 1).astype(jnp.float32)
        else:
            mean = summed * (1.0 / (2 * HALF_WIN + 1))
        normed = jnp.where(summed > 0.0, raw / mean, 0.0)
        out_ref[start : start + chunk, slot * BLOCK : (slot + 1) * BLOCK] = normed.astype(
            jnp.bfloat16
        )


def norm_kernel(rows, first, whole, raw_ref, *refs):
    out_ref, padded = refs[-2:]
    lay_out(raw_ref, rows, first, whole, padded)
    for start in range(0, out_ref.shape[0], CHUNK):
        norm_rows(padded, start, CHUNK, out_ref)


def normalise(raw, total, first, slots, whole, after=()):
    return call(
        functools.partial(norm_kernel, total // raw.shape[0], first, whole),
        "normalise",
        jax.ShapeDtypeStruct((total, slots * BLOCK), jnp.bfloat16),
        flops=12 * total * slots * BLOCK,
        bytes_accessed=4 * total * slots * BLOCK,
        in_specs=[WHOLE] + [ANYWHERE] * len(after),
        out_specs=WHOLE,
        scratch_shapes=[pltpu.VMEM((slots, total + 2 * PAD, BLOCK), jnp.float32)],
    )(raw, *after)


def set_left(ref, left_ref):
    rows = left_ref.shape[0] - ONES
    first_row = pl.multiple_of(lax.axis_index("pix") * rows, rows)
    left_ref[0:rows] = ref[pl.ds(first_row, rows), :]
    left_ref[rows : rows + ONES] = jnp.ones((ONES, ref.shape[1]), jnp.bfloat16)


def add_sums(pairs, sums, column):
    gram, frame = sums
    rows = pairs[0][0].shape[0] - ONES
    for left_ref, ref in pairs:
        both = dot_nt(left_ref[...], ref[column, :])
        gram = gram + both[0:rows]
        frame = frame + both[rows : rows + 8]
    return gram, frame


def partial_kernel(count, *refs):
    normed, lefts, (gram_out, frame_out) = refs[:count], refs[-count:], refs[-count - 2 : -count]
    before = refs[count : -count - 2]
    for ref, left_ref in zip(normed, lefts):
        set_left(ref, left_ref)
    for start in range(0, gram_out.shape[1], TILE):
        column = slice(start, start + TILE)
        sums = [ref[:, column] for ref in before] or [0.0, 0.0]
        gram_out[:, column], frame_out[:, column] = add_sums(
            list(zip(lefts, normed)), sums, column
        )


def sums_shape(total, parts):
    return [
        jax.ShapeDtypeStruct((total // parts, total), jnp.float32),
        jax.ShapeDtypeStruct((8, total), jnp.float32),
    ]


def partial_sums(normed, before, parts):
    total, width = normed[0].shape
    rows = total // parts
    return call(
        functools.partial(partial_kernel, len(normed)),
        "partial_sums",
        sums_shape(total, parts),
        flops=2 * rows * total * width * len(normed),
        bytes_accessed=4 * rows * total,
        in_specs=[WHOLE] * (len(normed) + len(before)),
        out_specs=[WHOLE] * 2,
        scratch_shapes=[pltpu.VMEM((rows + ONES, x.shape[1]), x.dtype) for x in normed],
    )(*normed, *before)


def result_kernel(meta_ref, their_meta_ref, normed_ref, gram_in, frame_in, out_hbm, *scratch):
    out_ref, frame_ref, sems = scratch
    rows, total = gram_in.shape
    pixels = meta_ref[PIXELS : PIXELS + 1, 0:BLOCK] + their_meta_ref[PIXELS : PIXELS + 1, 0:BLOCK]
    own = lax.broadcasted_iota(jnp.int32, (1, BLOCK), 1) == lax.axis_index("frame")
    number = jnp.sum(jnp.where(own, pixels, 0).astype(jnp.float32), axis=1, keepdims=True)
    ones = jnp.ones((8, normed_ref.shape[1]), jnp.bfloat16)
    frame_ref[...] = frame_in[...] + dot_nt(ones, normed_ref[...])
    first_row = pl.multiple_of(lax.axis_index("pix") * rows, rows)
    row_sum = jnp.broadcast_to(frame_ref[0:1, pl.ds(first_row, rows)], (BLOCK, rows)).T
    row_inv = 1.0 / row_sum[:, 0:1]
    left = normed_ref[pl.ds(first_row, rows), :]
    copies = []
    for i, start in enumerate(range(0, total, TILE)):
        column = slice(start, start + TILE)
        gram = gram_in[:, column] + dot_nt(left, normed_ref[column, :])
        col_inv = 1.0 / frame_ref[0:1, column]
        result = ((gram * row_inv) * col_inv) * number - 1.0
        out_ref[i] = result.astype(jnp.bfloat16)
        copies.append(
            pltpu.make_async_copy(out_ref.at[i], out_hbm.at[0, :, column], sems.at[i])
        )
        copies[-1].start()
    for copy in copies:
        copy.wait()


def correlate(metas, normed, before):
    rows, total = before[0].shape
    tiles = total // TILE
    return call(
        result_kernel,
        "correlate",
        pltpu.HBM((1, rows, total), jnp.bfloat16),
        flops=2 * rows * total * normed.shape[1],
        bytes_accessed=6 * rows * total,
        in_specs=[WHOLE] * 5,
        out_specs=ANYWHERE,
        scratch_shapes=[
            pltpu.VMEM((tiles, rows, TILE), jnp.bfloat16),
            pltpu.VMEM((8, total), jnp.float32),
            pltpu.SemaphoreType.DMA((tiles,)),
        ],
    )(*metas, normed, *before)


def body(frames, cycle_map):
    rows, p_sec = frames.shape
    n = lax.axis_size("frame")
    parts = lax.axis_size("pix")
    total = n * rows
    cap_blocks = p_sec // n // BLOCK
    slots = cap_blocks // 2 + 1
    early = slots - slots // 2
    cm = cycle_map.reshape(p_sec // BLOCK, BLOCK)

    def swap(x):
        return lax.ppermute(x, "pix", SWAP)

    def send(blocks):
        return lax.all_to_all(blocks, "frame", split_axis=0, concat_axis=0, tiled=True)

    moving, meta, near_frames, near_cm = pack_move(cm, frames, cap_blocks)
    theirs = swap(moving)
    own = pack_own(meta, near_cm, near_frames, cap_blocks)
    packed = share(meta, own, theirs, cap_blocks)
    received = send(packed)

    meta, _ = lax.optimization_barrier((meta, packed))
    their_meta = swap(meta)
    cap = cap_blocks * BLOCK
    large, twice = left_out(meta[:, :n], their_meta[:, :n], cap)
    overflow = jnp.any(large | twice | left_out(their_meta[:, :n], meta[:, :n], cap)[0])

    flag = overflow.astype(jnp.int32).reshape(1)
    first = normalise(received, total, 0, early, slots - 1, [flag])
    their_first = swap(first)
    last = normalise(received, total, early, slots - early, slots - 1, [first])
    their_last = swap(last)
    sums = partial_sums([first, last], [], parts)
    sums = partial_sums([their_first], sums, parts)

    def spill(frames, cm, meta, their_meta, their_last, *sums):
        rest = send(pack_rest(meta, their_meta, frames, cm, cap_blocks))
        rest = rest.reshape(n, cap_blocks * rows, BLOCK)
        normed = normalise(rest, total, 0, cap_blocks, cap_blocks)
        sums = partial_sums([normed, swap(normed)], sums, parts)
        return correlate([meta, their_meta], their_last, sums)

    def fits(frames, cm, meta, their_meta, their_last, *sums):
        return correlate([meta, their_meta], their_last, sums)

    return lax.cond(overflow, spill, fits, frames, cm, meta, their_meta, their_last, *sums)


def solution(mesh):
    return jax.shard_map(
        body,
        mesh=mesh,
        in_specs=(P("frame", "pix"), P("pix")),
        out_specs=P("frame", "pix", None),
        check_vma=False,
    )
```

```python
import functools

import jax
import jax.numpy as jnp
from jax import lax
from jax.experimental import pallas as pl
from jax.experimental.pallas import tpu as pltpu
from jax.sharding import PartitionSpec as P

BLOCK = 128
HALF_WIN = 2
PAD = 8
TILE = 256
CHUNK = 128
ONES = 16
VMEM_BYTES = 32 * 1024 * 1024
LIST, COUNT, PIXELS = 0, 1, 2
MERGED = 2
SWAP = [(0, 1), (1, 0)]
WHOLE = pl.BlockSpec(memory_space=pltpu.VMEM)
ANYWHERE = pl.BlockSpec(memory_space=pl.ANY)


def call(kernel, name, out_shape, flops=0, bytes_accessed=0, limit=VMEM_BYTES, **kw):
    return pl.pallas_call(
        kernel,
        out_shape=out_shape,
        compiler_params=pltpu.CompilerParams(vmem_limit_bytes=limit),
        cost_estimate=pl.CostEstimate(
            flops=flops, bytes_accessed=bytes_accessed, transcendentals=0
        ),
        name=name,
        **kw,
    )


def dot_nt(a, b):
    return lax.dot_general(a, b, (((1,), (1,)), ((), ())), preferred_element_type=jnp.float32)


def count_half_rows(rows):
    return max(16, rows // 2)


def gate(wanted):
    wanted = jnp.broadcast_to(wanted, (1, BLOCK))
    return wanted.astype(jnp.float32).astype(jnp.bfloat16)


def take(frames_ref, block):
    return frames_ref[:, pl.ds(pl.multiple_of(block * BLOCK, BLOCK), BLOCK)]


def fold(block, right):
    rows = block.shape[0] // 2
    half = BLOCK // 2
    early, late = block[0:rows].astype(jnp.float32), block[rows:].astype(jnp.float32)
    left = lax.broadcasted_iota(jnp.int32, (rows, BLOCK), 1) < half
    if right:
        folded = jnp.where(left, pltpu.roll(early, half, 1), late)
    else:
        folded = jnp.where(left, early, pltpu.roll(late, half, 1))
    spare = count_half_rows(block.shape[0]) - rows
    if spare:
        folded = jnp.concatenate([folded, jnp.zeros((spare, BLOCK), jnp.float32)])
    return folded.astype(jnp.bfloat16)


def unfold(folded, rows):
    half = BLOCK // 2
    early = folded[0 : rows // 2].astype(jnp.float32)
    left = lax.broadcasted_iota(jnp.int32, early.shape, 1) < half
    return jnp.where(left, early, 0.0), jnp.where(left, pltpu.roll(early, half, 1), 0.0)


def find_members(cm):
    blocks = cm.shape[0]
    first = cm[:, 0:1]
    member = first == lax.broadcasted_iota(jnp.int32, (blocks, BLOCK), 1)
    row = lax.broadcasted_iota(jnp.int32, (blocks, blocks), 0)
    col = lax.broadcasted_iota(jnp.int32, (blocks, blocks), 1)
    earlier = (col < row).astype(jnp.float32).astype(jnp.bfloat16)
    pixels = jnp.sum((cm >= 0).astype(jnp.float32), axis=1, keepdims=True)
    return first, member.astype(jnp.float32), earlier, pixels


def sum_before(earlier, member, values):
    before = jnp.dot(
        earlier, (member * values).astype(jnp.bfloat16), preferred_element_type=jnp.float32
    )
    return jnp.sum(before * member, axis=1, keepdims=True)


def find_blocks(members, cap_blocks, width):
    first, member, earlier, _ = members
    blocks = first.shape[0]
    rank = sum_before(earlier, member, 1.0).astype(jnp.int32)
    slot = jnp.where(first >= 0, first * cap_blocks + rank, -1)
    hit = slot == lax.broadcasted_iota(jnp.int32, (blocks, width), 1)
    index = lax.broadcasted_iota(jnp.int32, (blocks, width), 0).astype(jnp.float32)
    return jnp.sum(jnp.where(hit, index, 0.0), axis=0, keepdims=True).astype(jnp.int32)


def find_places(cm):
    _, member, earlier, pixels = find_members(cm)
    valid = (cm >= 0).astype(jnp.float32)
    row = lax.broadcasted_iota(jnp.int32, (BLOCK, BLOCK), 0)
    col = lax.broadcasted_iota(jnp.int32, (BLOCK, BLOCK), 1)
    before = (row < col).astype(jnp.float32).astype(jnp.bfloat16)
    place = jnp.dot(valid.astype(jnp.bfloat16), before, preferred_element_type=jnp.float32)
    return jnp.where(cm >= 0, place + sum_before(earlier, member, pixels), -1.0)


def move_kernel(cap_blocks, cm_hbm, frames_hbm, out_ref, meta_ref, frames_ref, cm_ref, *scratch):
    list_ref, list_s, sems = scratch
    n = out_ref.shape[0]
    rows = frames_ref.shape[0]
    kept = cap_blocks // 2
    get_cm = pltpu.make_async_copy(cm_hbm, cm_ref, sems.at[0])
    get_cm.start()
    get_frames = pltpu.make_async_copy(frames_hbm, frames_ref, sems.at[1])
    get_frames.start()
    get_cm.wait()
    members = find_members(cm_ref[...])
    found = find_blocks(members, cap_blocks, meta_ref.shape[1])
    list_ref[...] = jnp.broadcast_to(found, list_ref.shape)
    to_scalars = pltpu.make_async_copy(list_ref, list_s, sems.at[2])
    to_scalars.start()
    _, member, _, pixels = members
    meta_ref[...] = jnp.zeros_like(meta_ref)
    meta_ref[LIST : LIST + 1, :] = found
    for row, values in ((COUNT, member), (PIXELS, member * pixels)):
        totals = jnp.sum(values, axis=0, keepdims=True)
        meta_ref[row : row + 1, 0:BLOCK] = totals.astype(jnp.int32)
    to_scalars.wait()
    get_frames.wait()
    for q in range(n):
        for i in range(kept + 1, cap_blocks):
            block = list_s[0, q * cap_blocks + i]
            start = (i - kept - 1) * rows
            out_ref[q, start : start + rows] = take(frames_ref, block)
        start = (cap_blocks - kept - 1) * rows
        block = list_s[0, q * cap_blocks + kept]
        out_ref[q, start:] = fold(take(frames_ref, block), True)


def pack_move(cm, frames, cap_blocks):
    rows = frames.shape[0]
    n = cm.shape[0] // cap_blocks
    height = (cap_blocks - cap_blocks // 2 - 1) * rows + count_half_rows(rows)
    meta = jax.ShapeDtypeStruct((8, cm.shape[0]), jnp.int32)
    return call(
        functools.partial(move_kernel, cap_blocks),
        "pack_move",
        [
            jax.ShapeDtypeStruct((n, height, BLOCK), frames.dtype),
            meta,
            jax.ShapeDtypeStruct(frames.shape, frames.dtype),
            jax.ShapeDtypeStruct(cm.shape, cm.dtype),
        ],
        in_specs=[ANYWHERE] * 2,
        out_specs=[WHOLE] * 4,
        scratch_shapes=[
            pltpu.VMEM(meta.shape, meta.dtype),
            pltpu.SMEM(meta.shape, meta.dtype),
            pltpu.SemaphoreType.DMA((3,)),
        ],
    )(
        pltpu.with_memory_space_constraint(cm, pltpu.HBM),
        pltpu.with_memory_space_constraint(frames, pltpu.HBM),
    )


def own_kernel(cap_blocks, meta_s, cm_ref, frames_ref, out_ref, place_ref):
    n = out_ref.shape[0]
    rows = frames_ref.shape[0]
    kept = cap_blocks // 2
    place_ref[...] = find_places(cm_ref[...])
    target = lax.broadcasted_iota(jnp.int32, (BLOCK, BLOCK), 0).astype(jnp.float32)
    for q in range(n):
        count, pixels = meta_s[COUNT, q], meta_s[PIXELS, q]
        is_full = pixels == cap_blocks * BLOCK
        full = gate(is_full)
        fits = (pixels <= BLOCK) & (count <= MERGED)
        compact = 0.0
        for i in range(MERGED):
            block = meta_s[LIST, q * cap_blocks + i]
            place = jnp.where(fits & (i < count), place_ref[pl.ds(block, 1), :], -1.0)
            chosen = (target == place).astype(jnp.float32).astype(jnp.bfloat16)
            compact = compact + dot_nt(take(frames_ref, block), chosen)
        block = meta_s[LIST, q * cap_blocks]
        out_ref[q, 0:rows] = compact.astype(jnp.bfloat16) + take(frames_ref, block) * full
        for i in range(1, kept):
            block = meta_s[LIST, q * cap_blocks + i]
            out_ref[q, i * rows : (i + 1) * rows] = take(frames_ref, block) * full
        block = meta_s[LIST, q * cap_blocks + kept]
        out_ref[q, kept * rows :] = fold(take(frames_ref, block), False) * full


def pack_own(meta, cm, frames, cap_blocks):
    rows = frames.shape[0]
    n = cm.shape[0] // cap_blocks
    height = cap_blocks // 2 * rows + count_half_rows(rows)
    return call(
        functools.partial(own_kernel, cap_blocks),
        "pack_own",
        jax.ShapeDtypeStruct((n, height, BLOCK), frames.dtype),
        in_specs=[pl.BlockSpec(memory_space=pltpu.SMEM)] + [WHOLE] * 2,
        out_specs=WHOLE,
        scratch_shapes=[pltpu.VMEM(cm.shape, jnp.float32)],
        bytes_accessed=4 * 1024 * 1024,
    )(meta, cm, frames)


def share_kernel(cap_blocks, meta_ref, own_ref, theirs_ref, out_ref):
    n, height, _ = out_ref.shape
    rows = height - theirs_ref.shape[1]
    helped = meta_ref[PIXELS : PIXELS + 1, 0:BLOCK] != cap_blocks * BLOCK
    out_ref[:, 0:rows] = own_ref[:, 0:rows]
    for q in range(n):
        other = gate(helped[:, q : q + 1])
        out_ref[q, rows:] = own_ref[q, rows:] + theirs_ref[q] * other


def share(meta, own, theirs, cap_blocks):
    return call(
        functools.partial(share_kernel, cap_blocks),
        "share",
        jax.ShapeDtypeStruct(own.shape, own.dtype),
        in_specs=[WHOLE] * 3,
        out_specs=WHOLE,
        bytes_accessed=4 * 1024 * 1024,
    )(meta, own, theirs)


def left_out(meta, their_meta, cap):
    mine, theirs = meta[PIXELS] == cap, their_meta[PIXELS] == cap
    fits = (meta[PIXELS] <= BLOCK) & (meta[COUNT] <= MERGED)
    return jnp.logical_not(mine | fits), mine & theirs


def rest_kernel(cap_blocks, meta_s, their_meta_s, frames_hbm, cm_hbm, out_ref, *scratch):
    frames_ref, cm_ref = scratch
    n, _, rows, _ = out_ref.shape
    kept = cap_blocks // 2
    pltpu.sync_copy(frames_hbm, frames_ref)
    pltpu.sync_copy(cm_hbm, cm_ref)
    right = lax.broadcasted_iota(jnp.int32, (1, BLOCK), 1) >= BLOCK // 2
    for q in range(n):
        counts = [[ref[row, q] for row in range(PIXELS + 1)] for ref in (meta_s, their_meta_s)]
        large, twice = left_out(*counts, cap_blocks * BLOCK)
        for i in range(cap_blocks):
            block = meta_s[LIST, q * cap_blocks + i]
            wanted = jnp.broadcast_to(large, (1, BLOCK))
            if i >= kept:
                wanted |= twice & right if i == kept else twice
            valid = (cm_ref[pl.ds(block, 1), :] >= 0) & (i < meta_s[COUNT, q])
            out_ref[q, i] = take(frames_ref, block) * gate(valid & wanted)


def pack_rest(meta, their_meta, frames, cm, cap_blocks):
    n = cm.shape[0] // cap_blocks
    return call(
        functools.partial(rest_kernel, cap_blocks),
        "pack_rest",
        jax.ShapeDtypeStruct((n, cap_blocks, frames.shape[0], BLOCK), frames.dtype),
        in_specs=[pl.BlockSpec(memory_space=pltpu.SMEM)] * 2 + [ANYWHERE] * 2,
        out_specs=WHOLE,
        scratch_shapes=[
            pltpu.VMEM(frames.shape, frames.dtype),
            pltpu.VMEM(cm.shape, cm.dtype),
        ],
    )(
        meta,
        their_meta,
        pltpu.with_memory_space_constraint(frames, pltpu.HBM),
        pltpu.with_memory_space_constraint(cm, pltpu.HBM),
    )


def lay_out(raw_ref, rows, first, whole, padded):
    n, height, _ = raw_ref.shape
    total = n * rows
    zero = jnp.zeros((PAD, BLOCK), jnp.float32)
    for i in range(padded.shape[0]):
        slot = first + i
        padded[i, 0:PAD] = zero
        padded[i, PAD + total : 2 * PAD + total] = zero
        for source in range(n):
            start = PAD + source * rows
            if slot < whole:
                block = raw_ref[source, slot * rows : (slot + 1) * rows]
                padded[i, start : start + rows] = block.astype(jnp.float32)
            else:
                early, late = unfold(raw_ref[source, slot * rows : height], rows)
                padded[i, start : start + rows // 2] = early
                padded[i, start + rows // 2 : start + rows] = late


def norm_rows(padded, start, chunk, out_ref):
    total = out_ref.shape[0]
    base = PAD + start
    for slot in range(padded.shape[0]):
        raw = padded[slot, base : base + chunk]
        summed = raw
        for offset in range(1, HALF_WIN + 1):
            summed = summed + padded[slot, base - offset : base - offset + chunk]
            summed = summed + padded[slot, base + offset : base + offset + chunk]
        if start == 0 or start + chunk == total:
            frame = start + lax.broadcasted_iota(jnp.int32, (chunk, BLOCK), 0)
            upper = jnp.minimum(frame + HALF_WIN, total - 1)
            lower = jnp.maximum(frame - HALF_WIN, 0)
            mean = summed / (upper - lower + 1).astype(jnp.float32)
        else:
            mean = summed * (1.0 / (2 * HALF_WIN + 1))
        normed = jnp.where(summed > 0.0, raw / mean, 0.0)
        out_ref[start : start + chunk, slot * BLOCK : (slot + 1) * BLOCK] = normed.astype(
            jnp.bfloat16
        )


def norm_kernel(rows, first, whole, raw_ref, *refs):
    out_ref, padded = refs[-2:]
    lay_out(raw_ref, rows, first, whole, padded)
    for start in range(0, out_ref.shape[0], CHUNK):
        norm_rows(padded, start, CHUNK, out_ref)


def normalise(raw, total, first, slots, whole, after=()):
    return call(
        functools.partial(norm_kernel, total // raw.shape[0], first, whole),
        "normalise",
        jax.ShapeDtypeStruct((total, slots * BLOCK), jnp.bfloat16),
        flops=12 * total * slots * BLOCK,
        bytes_accessed=4 * total * slots * BLOCK,
        in_specs=[WHOLE] + [ANYWHERE] * len(after),
        out_specs=WHOLE,
        scratch_shapes=[pltpu.VMEM((slots, total + 2 * PAD, BLOCK), jnp.float32)],
    )(raw, *after)


def set_left(ref, left_ref):
    rows = left_ref.shape[0] - ONES
    first_row = pl.multiple_of(lax.axis_index("pix") * rows, rows)
    left_ref[0:rows] = ref[pl.ds(first_row, rows), :]
    left_ref[rows : rows + ONES] = jnp.ones((ONES, ref.shape[1]), jnp.bfloat16)


def add_sums(pairs, sums, column):
    gram, frame = sums
    rows = pairs[0][0].shape[0] - ONES
    for left_ref, ref in pairs:
        both = dot_nt(left_ref[...], ref[column, :])
        gram = gram + both[0:rows]
        frame = frame + both[rows : rows + 8]
    return gram, frame


def partial_kernel(count, *refs):
    normed, lefts, (gram_out, frame_out) = refs[:count], refs[-count:], refs[-count - 2 : -count]
    before = refs[count : -count - 2]
    for ref, left_ref in zip(normed, lefts):
        set_left(ref, left_ref)
    for start in range(0, gram_out.shape[1], TILE):
        column = slice(start, start + TILE)
        sums = [ref[:, column] for ref in before] or [0.0, 0.0]
        gram_out[:, column], frame_out[:, column] = add_sums(
            list(zip(lefts, normed)), sums, column
        )


def sums_shape(total, parts):
    return [
        jax.ShapeDtypeStruct((total // parts, total), jnp.float32),
        jax.ShapeDtypeStruct((8, total), jnp.float32),
    ]


def partial_sums(normed, before, parts):
    total, width = normed[0].shape
    rows = total // parts
    return call(
        functools.partial(partial_kernel, len(normed)),
        "partial_sums",
        sums_shape(total, parts),
        flops=2 * rows * total * width * len(normed),
        bytes_accessed=4 * rows * total,
        in_specs=[WHOLE] * (len(normed) + len(before)),
        out_specs=[WHOLE] * 2,
        scratch_shapes=[pltpu.VMEM((rows + ONES, x.shape[1]), x.dtype) for x in normed],
    )(*normed, *before)


def result_kernel(meta_ref, their_meta_ref, normed_ref, gram_in, frame_in, out_hbm, *scratch):
    out_ref, gram_ref, frame_ref, left_ref, sems = scratch
    rows, total = gram_in.shape
    tiles, own_tiles = total // TILE, rows // TILE
    pixels = meta_ref[PIXELS : PIXELS + 1, 0:BLOCK] + their_meta_ref[PIXELS : PIXELS + 1, 0:BLOCK]
    own = lax.broadcasted_iota(jnp.int32, (1, BLOCK), 1) == lax.axis_index("frame")
    number = jnp.sum(jnp.where(own, pixels, 0).astype(jnp.float32), axis=1, keepdims=True)
    set_left(normed_ref, left_ref)
    first_row = lax.axis_index("pix") * rows

    def columns(i):
        return pl.ds(pl.multiple_of(lax.rem(first_row + i * TILE, total), TILE), TILE)

    def sum_up(i):
        column = columns(i)
        before = [gram_in[:, column], frame_in[:, column]]
        return add_sums([(left_ref, normed_ref)], before, column)

    def finish(i, gram, frame):
        result = ((gram * row_inv) * (1.0 / frame[0:1])) * number - 1.0
        out_ref[i] = result.astype(jnp.bfloat16)
        copy = pltpu.make_async_copy(out_ref.at[i], out_hbm.at[0, :, columns(i)], sems.at[i])
        copy.start()
        return copy

    for i in range(own_tiles):
        gram_ref[i], frame_ref[:, i * TILE : (i + 1) * TILE] = sum_up(i)
    row_sum = jnp.broadcast_to(frame_ref[0:1, :], (BLOCK, rows)).T
    row_inv = 1.0 / row_sum[:, 0:1]
    copies = []
    for i in range(tiles):
        if i < own_tiles:
            gram, frame = gram_ref[i], frame_ref[:, i * TILE : (i + 1) * TILE]
        else:
            gram, frame = sum_up(i)
        copies.append(finish(i, gram, frame))
    for copy in copies:
        copy.wait()


def correlate(metas, normed, before):
    rows, total = before[0].shape
    tiles = total // TILE
    return call(
        result_kernel,
        "correlate",
        pltpu.HBM((1, rows, total), jnp.bfloat16),
        flops=2 * rows * total * normed.shape[1],
        bytes_accessed=6 * rows * total,
        in_specs=[WHOLE] * 5,
        out_specs=ANYWHERE,
        scratch_shapes=[
            pltpu.VMEM((tiles, rows, TILE), jnp.bfloat16),
            pltpu.VMEM((rows // TILE, rows, TILE), jnp.float32),
            pltpu.VMEM((8, rows), jnp.float32),
            pltpu.VMEM((rows + ONES, normed.shape[1]), normed.dtype),
            pltpu.SemaphoreType.DMA((tiles,)),
        ],
    )(*metas, normed, *before)


def body(frames, cycle_map):
    rows, p_sec = frames.shape
    n = lax.axis_size("frame")
    parts = lax.axis_size("pix")
    total = n * rows
    cap_blocks = p_sec // n // BLOCK
    slots = cap_blocks // 2 + 1
    early = slots - slots // 2
    cm = cycle_map.reshape(p_sec // BLOCK, BLOCK)

    def swap(x):
        return lax.ppermute(x, "pix", SWAP)

    def send(blocks):
        return lax.all_to_all(blocks, "frame", split_axis=0, concat_axis=0, tiled=True)

    moving, meta, near_frames, near_cm = pack_move(cm, frames, cap_blocks)
    theirs = swap(moving)
    own = pack_own(meta, near_cm, near_frames, cap_blocks)
    packed = share(meta, own, theirs, cap_blocks)
    received = send(packed)

    meta, _ = lax.optimization_barrier((meta, packed))
    their_meta = swap(meta)
    cap = cap_blocks * BLOCK
    large, twice = left_out(meta[:, :n], their_meta[:, :n], cap)
    overflow = jnp.any(large | twice | left_out(their_meta[:, :n], meta[:, :n], cap)[0])

    flag = overflow.astype(jnp.int32).reshape(1)
    first = normalise(received, total, 0, early, slots - 1, [flag])
    their_first = swap(first)
    last = normalise(received, total, early, slots - early, slots - 1, [first])
    their_last = swap(last)
    sums = partial_sums([first, last], [], parts)
    sums = partial_sums([their_first], sums, parts)

    def spill(frames, cm, meta, their_meta, their_last, *sums):
        rest = send(pack_rest(meta, their_meta, frames, cm, cap_blocks))
        rest = rest.reshape(n, cap_blocks * rows, BLOCK)
        normed = normalise(rest, total, 0, cap_blocks, cap_blocks)
        sums = partial_sums([normed, swap(normed)], sums, parts)
        return correlate([meta, their_meta], their_last, sums)

    def fits(frames, cm, meta, their_meta, their_last, *sums):
        return correlate([meta, their_meta], their_last, sums)

    return lax.cond(overflow, spill, fits, frames, cm, meta, their_meta, their_last, *sums)


def solution(mesh):
    return jax.shard_map(
        body,
        mesh=mesh,
        in_specs=(P("frame", "pix"), P("pix")),
        out_specs=P("frame", "pix", None),
        check_vma=False,
    )
```

```python
import functools

import jax
import jax.numpy as jnp
from jax import lax
from jax.experimental import pallas as pl
from jax.experimental.pallas import tpu as pltpu
from jax.sharding import PartitionSpec as P

BLOCK = 128
HALF_WIN = 2
PAD = 8
TILE = 256
CHUNK = 128
ONES = 16
VMEM_BYTES = 32 * 1024 * 1024
LIST, COUNT, PIXELS = 0, 1, 2
MERGED = 2
SWAP = [(0, 1), (1, 0)]
WHOLE = pl.BlockSpec(memory_space=pltpu.VMEM)
ANYWHERE = pl.BlockSpec(memory_space=pl.ANY)


def call(kernel, name, out_shape, flops=0, bytes_accessed=0, limit=VMEM_BYTES, **kw):
    return pl.pallas_call(
        kernel,
        out_shape=out_shape,
        compiler_params=pltpu.CompilerParams(vmem_limit_bytes=limit),
        cost_estimate=pl.CostEstimate(
            flops=flops, bytes_accessed=bytes_accessed, transcendentals=0
        ),
        name=name,
        **kw,
    )


def dot_nt(a, b):
    return lax.dot_general(a, b, (((1,), (1,)), ((), ())), preferred_element_type=jnp.float32)


def list_group(n):
    return sorted(range(n), key=lambda i: (i >= n // 2, i % 2 if i < n // 2 else 0, i))


def count_half_rows(rows):
    return max(16, rows // 2)


def gate(wanted):
    wanted = jnp.broadcast_to(wanted, (1, BLOCK))
    return wanted.astype(jnp.float32).astype(jnp.bfloat16)


def take(frames_ref, block):
    return frames_ref[:, pl.ds(pl.multiple_of(block * BLOCK, BLOCK), BLOCK)]


def fold(block, right):
    rows = block.shape[0] // 2
    half = BLOCK // 2
    early, late = block[0:rows].astype(jnp.float32), block[rows:].astype(jnp.float32)
    left = lax.broadcasted_iota(jnp.int32, (rows, BLOCK), 1) < half
    if right:
        folded = jnp.where(left, pltpu.roll(early, half, 1), late)
    else:
        folded = jnp.where(left, early, pltpu.roll(late, half, 1))
    spare = count_half_rows(block.shape[0]) - rows
    if spare:
        folded = jnp.concatenate([folded, jnp.zeros((spare, BLOCK), jnp.float32)])
    return folded.astype(jnp.bfloat16)


def unfold(folded, rows):
    half = BLOCK // 2
    early = folded[0 : rows // 2].astype(jnp.float32)
    left = lax.broadcasted_iota(jnp.int32, early.shape, 1) < half
    return jnp.where(left, early, 0.0), jnp.where(left, pltpu.roll(early, half, 1), 0.0)


def find_members(cm):
    blocks = cm.shape[0]
    first = cm[:, 0:1]
    member = first == lax.broadcasted_iota(jnp.int32, (blocks, BLOCK), 1)
    row = lax.broadcasted_iota(jnp.int32, (blocks, blocks), 0)
    col = lax.broadcasted_iota(jnp.int32, (blocks, blocks), 1)
    earlier = (col < row).astype(jnp.float32).astype(jnp.bfloat16)
    pixels = jnp.sum((cm >= 0).astype(jnp.float32), axis=1, keepdims=True)
    return first, member.astype(jnp.float32), earlier, pixels


def sum_before(earlier, member, values):
    before = jnp.dot(
        earlier, (member * values).astype(jnp.bfloat16), preferred_element_type=jnp.float32
    )
    return jnp.sum(before * member, axis=1, keepdims=True)


def find_blocks(members, cap_blocks, width):
    first, member, earlier, _ = members
    blocks = first.shape[0]
    rank = sum_before(earlier, member, 1.0).astype(jnp.int32)
    slot = jnp.where(first >= 0, first * cap_blocks + rank, -1)
    hit = slot == lax.broadcasted_iota(jnp.int32, (blocks, width), 1)
    index = lax.broadcasted_iota(jnp.int32, (blocks, width), 0).astype(jnp.float32)
    return jnp.sum(jnp.where(hit, index, 0.0), axis=0, keepdims=True).astype(jnp.int32)


def find_places(cm):
    _, member, earlier, pixels = find_members(cm)
    valid = (cm >= 0).astype(jnp.float32)
    row = lax.broadcasted_iota(jnp.int32, (BLOCK, BLOCK), 0)
    col = lax.broadcasted_iota(jnp.int32, (BLOCK, BLOCK), 1)
    before = (row < col).astype(jnp.float32).astype(jnp.bfloat16)
    place = jnp.dot(valid.astype(jnp.bfloat16), before, preferred_element_type=jnp.float32)
    return jnp.where(cm >= 0, place + sum_before(earlier, member, pixels), -1.0)


def move_kernel(cap_blocks, cm_hbm, frames_hbm, out_ref, meta_ref, frames_ref, cm_ref, *scratch):
    list_ref, list_s, sems = scratch
    n = out_ref.shape[0]
    rows = frames_ref.shape[0]
    kept = cap_blocks // 2
    get_cm = pltpu.make_async_copy(cm_hbm, cm_ref, sems.at[0])
    get_cm.start()
    get_frames = pltpu.make_async_copy(frames_hbm, frames_ref, sems.at[1])
    get_frames.start()
    get_cm.wait()
    members = find_members(cm_ref[...])
    found = find_blocks(members, cap_blocks, meta_ref.shape[1])
    list_ref[...] = jnp.broadcast_to(found, list_ref.shape)
    to_scalars = pltpu.make_async_copy(list_ref, list_s, sems.at[2])
    to_scalars.start()
    _, member, _, pixels = members
    meta_ref[...] = jnp.zeros_like(meta_ref)
    meta_ref[LIST : LIST + 1, :] = found
    for row, values in ((COUNT, member), (PIXELS, member * pixels)):
        totals = jnp.sum(values, axis=0, keepdims=True)
        meta_ref[row : row + 1, 0:BLOCK] = totals.astype(jnp.int32)
    to_scalars.wait()
    get_frames.wait()
    for q in range(n):
        for i in range(kept + 1, cap_blocks):
            block = list_s[0, q * cap_blocks + i]
            start = (i - kept - 1) * rows
            out_ref[q, start : start + rows] = take(frames_ref, block)
        start = (cap_blocks - kept - 1) * rows
        block = list_s[0, q * cap_blocks + kept]
        out_ref[q, start:] = fold(take(frames_ref, block), True)


def pack_move(cm, frames, cap_blocks):
    rows = frames.shape[0]
    n = cm.shape[0] // cap_blocks
    height = (cap_blocks - cap_blocks // 2 - 1) * rows + count_half_rows(rows)
    meta = jax.ShapeDtypeStruct((8, cm.shape[0]), jnp.int32)
    return call(
        functools.partial(move_kernel, cap_blocks),
        "pack_move",
        [
            jax.ShapeDtypeStruct((n, height, BLOCK), frames.dtype),
            meta,
            jax.ShapeDtypeStruct(frames.shape, frames.dtype),
            jax.ShapeDtypeStruct(cm.shape, cm.dtype),
        ],
        in_specs=[ANYWHERE] * 2,
        out_specs=[WHOLE] * 4,
        scratch_shapes=[
            pltpu.VMEM(meta.shape, meta.dtype),
            pltpu.SMEM(meta.shape, meta.dtype),
            pltpu.SemaphoreType.DMA((3,)),
        ],
    )(
        pltpu.with_memory_space_constraint(cm, pltpu.HBM),
        pltpu.with_memory_space_constraint(frames, pltpu.HBM),
    )


def own_kernel(cap_blocks, meta_s, cm_ref, frames_ref, out_ref, place_ref):
    n = out_ref.shape[0]
    rows = frames_ref.shape[0]
    kept = cap_blocks // 2
    place_ref[...] = find_places(cm_ref[...])
    target = lax.broadcasted_iota(jnp.int32, (BLOCK, BLOCK), 0).astype(jnp.float32)
    for q in range(n):
        count, pixels = meta_s[COUNT, q], meta_s[PIXELS, q]
        is_full = pixels == cap_blocks * BLOCK
        full = gate(is_full)
        fits = (pixels <= BLOCK) & (count <= MERGED)
        compact = 0.0
        for i in range(MERGED):
            block = meta_s[LIST, q * cap_blocks + i]
            place = jnp.where(fits & (i < count), place_ref[pl.ds(block, 1), :], -1.0)
            chosen = (target == place).astype(jnp.float32).astype(jnp.bfloat16)
            compact = compact + dot_nt(take(frames_ref, block), chosen)
        block = meta_s[LIST, q * cap_blocks]
        out_ref[q, 0:rows] = compact.astype(jnp.bfloat16) + take(frames_ref, block) * full
        for i in range(1, kept):
            block = meta_s[LIST, q * cap_blocks + i]
            out_ref[q, i * rows : (i + 1) * rows] = take(frames_ref, block) * full
        block = meta_s[LIST, q * cap_blocks + kept]
        out_ref[q, kept * rows :] = fold(take(frames_ref, block), False) * full


def pack_own(meta, cm, frames, cap_blocks):
    rows = frames.shape[0]
    n = cm.shape[0] // cap_blocks
    height = cap_blocks // 2 * rows + count_half_rows(rows)
    return call(
        functools.partial(own_kernel, cap_blocks),
        "pack_own",
        jax.ShapeDtypeStruct((n, height, BLOCK), frames.dtype),
        in_specs=[pl.BlockSpec(memory_space=pltpu.SMEM)] + [WHOLE] * 2,
        out_specs=WHOLE,
        scratch_shapes=[pltpu.VMEM(cm.shape, jnp.float32)],
        bytes_accessed=4 * 1024 * 1024,
    )(meta, cm, frames)


def share_kernel(cap_blocks, meta_ref, own_ref, theirs_ref, out_ref):
    n, height, _ = out_ref.shape
    rows = height - theirs_ref.shape[1]
    helped = meta_ref[PIXELS : PIXELS + 1, 0:BLOCK] != cap_blocks * BLOCK
    for to, q in enumerate(list_group(n)):
        other = gate(helped[:, q : q + 1])
        out_ref[to, 0:rows] = own_ref[q, 0:rows]
        out_ref[to, rows:] = own_ref[q, rows:] + theirs_ref[q] * other


def share(meta, own, theirs, cap_blocks):
    return call(
        functools.partial(share_kernel, cap_blocks),
        "share",
        jax.ShapeDtypeStruct(own.shape, own.dtype),
        in_specs=[WHOLE] * 3,
        out_specs=WHOLE,
        bytes_accessed=4 * 1024 * 1024,
    )(meta, own, theirs)


def left_out(meta, their_meta, cap):
    mine, theirs = meta[PIXELS] == cap, their_meta[PIXELS] == cap
    fits = (meta[PIXELS] <= BLOCK) & (meta[COUNT] <= MERGED)
    return jnp.logical_not(mine | fits), mine & theirs


def rest_kernel(cap_blocks, meta_s, their_meta_s, frames_hbm, cm_hbm, out_ref, *scratch):
    frames_ref, cm_ref = scratch
    n, _, rows, _ = out_ref.shape
    kept = cap_blocks // 2
    pltpu.sync_copy(frames_hbm, frames_ref)
    pltpu.sync_copy(cm_hbm, cm_ref)
    right = lax.broadcasted_iota(jnp.int32, (1, BLOCK), 1) >= BLOCK // 2
    for to, q in enumerate(list_group(n)):
        counts = [[ref[row, q] for row in range(PIXELS + 1)] for ref in (meta_s, their_meta_s)]
        large, twice = left_out(*counts, cap_blocks * BLOCK)
        for i in range(cap_blocks):
            block = meta_s[LIST, q * cap_blocks + i]
            wanted = jnp.broadcast_to(large, (1, BLOCK))
            if i >= kept:
                wanted |= twice & right if i == kept else twice
            valid = (cm_ref[pl.ds(block, 1), :] >= 0) & (i < meta_s[COUNT, q])
            out_ref[to, i] = take(frames_ref, block) * gate(valid & wanted)


def pack_rest(meta, their_meta, frames, cm, cap_blocks):
    n = cm.shape[0] // cap_blocks
    return call(
        functools.partial(rest_kernel, cap_blocks),
        "pack_rest",
        jax.ShapeDtypeStruct((n, cap_blocks, frames.shape[0], BLOCK), frames.dtype),
        in_specs=[pl.BlockSpec(memory_space=pltpu.SMEM)] * 2 + [ANYWHERE] * 2,
        out_specs=WHOLE,
        scratch_shapes=[
            pltpu.VMEM(frames.shape, frames.dtype),
            pltpu.VMEM(cm.shape, cm.dtype),
        ],
    )(
        meta,
        their_meta,
        pltpu.with_memory_space_constraint(frames, pltpu.HBM),
        pltpu.with_memory_space_constraint(cm, pltpu.HBM),
    )


def lay_out(raw_ref, rows, first, whole, padded):
    n, height, _ = raw_ref.shape
    total = n * rows
    zero = jnp.zeros((PAD, BLOCK), jnp.float32)
    for i in range(padded.shape[0]):
        slot = first + i
        padded[i, 0:PAD] = zero
        padded[i, PAD + total : 2 * PAD + total] = zero
        for place, source in enumerate(list_group(n)):
            start = PAD + source * rows
            if slot < whole:
                block = raw_ref[place, slot * rows : (slot + 1) * rows]
                padded[i, start : start + rows] = block.astype(jnp.float32)
            else:
                early, late = unfold(raw_ref[place, slot * rows : height], rows)
                padded[i, start : start + rows // 2] = early
                padded[i, start + rows // 2 : start + rows] = late


def norm_rows(padded, start, chunk, out_ref):
    total = out_ref.shape[0]
    base = PAD + start
    for slot in range(padded.shape[0]):
        raw = padded[slot, base : base + chunk]
        summed = raw
        for offset in range(1, HALF_WIN + 1):
            summed = summed + padded[slot, base - offset : base - offset + chunk]
            summed = summed + padded[slot, base + offset : base + offset + chunk]
        if start == 0 or start + chunk == total:
            frame = start + lax.broadcasted_iota(jnp.int32, (chunk, BLOCK), 0)
            upper = jnp.minimum(frame + HALF_WIN, total - 1)
            lower = jnp.maximum(frame - HALF_WIN, 0)
            mean = summed / (upper - lower + 1).astype(jnp.float32)
        else:
            mean = summed * (1.0 / (2 * HALF_WIN + 1))
        normed = jnp.where(summed > 0.0, raw / mean, 0.0)
        out_ref[start : start + chunk, slot * BLOCK : (slot + 1) * BLOCK] = normed.astype(
            jnp.bfloat16
        )


def norm_kernel(rows, first, whole, raw_ref, *refs):
    out_ref, padded = refs[-2:]
    lay_out(raw_ref, rows, first, whole, padded)
    for start in range(0, out_ref.shape[0], CHUNK):
        norm_rows(padded, start, CHUNK, out_ref)


def normalise(raw, total, first, slots, whole, after=()):
    return call(
        functools.partial(norm_kernel, total // raw.shape[0], first, whole),
        "normalise",
        jax.ShapeDtypeStruct((total, slots * BLOCK), jnp.bfloat16),
        flops=12 * total * slots * BLOCK,
        bytes_accessed=4 * total * slots * BLOCK,
        in_specs=[WHOLE] + [ANYWHERE] * len(after),
        out_specs=WHOLE,
        scratch_shapes=[pltpu.VMEM((slots, total + 2 * PAD, BLOCK), jnp.float32)],
    )(raw, *after)


def set_left(ref, left_ref):
    rows = left_ref.shape[0] - ONES
    first_row = pl.multiple_of(lax.axis_index("pix") * rows, rows)
    left_ref[0:rows] = ref[pl.ds(first_row, rows), :]
    left_ref[rows : rows + ONES] = jnp.ones((ONES, ref.shape[1]), jnp.bfloat16)


def add_sums(pairs, sums, column):
    gram, frame = sums
    rows = pairs[0][0].shape[0] - ONES
    for left_ref, ref in pairs:
        both = dot_nt(left_ref[...], ref[column, :])
        gram = gram + both[0:rows]
        frame = frame + both[rows : rows + 8]
    return gram, frame


def partial_kernel(count, *refs):
    normed, lefts, (gram_out, frame_out) = refs[:count], refs[-count:], refs[-count - 2 : -count]
    before = refs[count : -count - 2]
    for ref, left_ref in zip(normed, lefts):
        set_left(ref, left_ref)
    for start in range(0, gram_out.shape[1], TILE):
        column = slice(start, start + TILE)
        sums = [ref[:, column] for ref in before] or [0.0, 0.0]
        gram_out[:, column], frame_out[:, column] = add_sums(
            list(zip(lefts, normed)), sums, column
        )


def sums_shape(total, parts):
    return [
        jax.ShapeDtypeStruct((total // parts, total), jnp.float32),
        jax.ShapeDtypeStruct((8, total), jnp.float32),
    ]


def partial_sums(normed, before, parts):
    total, width = normed[0].shape
    rows = total // parts
    return call(
        functools.partial(partial_kernel, len(normed)),
        "partial_sums",
        sums_shape(total, parts),
        flops=2 * rows * total * width * len(normed),
        bytes_accessed=4 * rows * total,
        in_specs=[WHOLE] * (len(normed) + len(before)),
        out_specs=[WHOLE] * 2,
        scratch_shapes=[pltpu.VMEM((rows + ONES, x.shape[1]), x.dtype) for x in normed],
    )(*normed, *before)


def result_kernel(meta_ref, their_meta_ref, normed_ref, gram_in, frame_in, out_hbm, *scratch):
    out_ref, frame_ref, sems = scratch
    rows, total = gram_in.shape
    pixels = meta_ref[PIXELS : PIXELS + 1, 0:BLOCK] + their_meta_ref[PIXELS : PIXELS + 1, 0:BLOCK]
    own = lax.broadcasted_iota(jnp.int32, (1, BLOCK), 1) == lax.axis_index("frame")
    number = jnp.sum(jnp.where(own, pixels, 0).astype(jnp.float32), axis=1, keepdims=True)
    ones = jnp.ones((8, normed_ref.shape[1]), jnp.bfloat16)
    frame_ref[...] = frame_in[...] + dot_nt(ones, normed_ref[...])
    first_row = pl.multiple_of(lax.axis_index("pix") * rows, rows)
    row_sum = jnp.broadcast_to(frame_ref[0:1, pl.ds(first_row, rows)], (BLOCK, rows)).T
    row_inv = 1.0 / row_sum[:, 0:1]
    left = normed_ref[pl.ds(first_row, rows), :]
    copies = []
    for i, start in enumerate(range(0, total, TILE)):
        column = slice(start, start + TILE)
        gram = gram_in[:, column] + dot_nt(left, normed_ref[column, :])
        col_inv = 1.0 / frame_ref[0:1, column]
        result = ((gram * row_inv) * col_inv) * number - 1.0
        out_ref[i] = result.astype(jnp.bfloat16)
        copies.append(
            pltpu.make_async_copy(out_ref.at[i], out_hbm.at[0, :, column], sems.at[i])
        )
        copies[-1].start()
    for copy in copies:
        copy.wait()


def correlate(metas, normed, before):
    rows, total = before[0].shape
    tiles = total // TILE
    return call(
        result_kernel,
        "correlate",
        pltpu.HBM((1, rows, total), jnp.bfloat16),
        flops=2 * rows * total * normed.shape[1],
        bytes_accessed=6 * rows * total,
        in_specs=[WHOLE] * 5,
        out_specs=ANYWHERE,
        scratch_shapes=[
            pltpu.VMEM((tiles, rows, TILE), jnp.bfloat16),
            pltpu.VMEM((8, total), jnp.float32),
            pltpu.SemaphoreType.DMA((tiles,)),
        ],
    )(*metas, normed, *before)


def body(frames, cycle_map):
    rows, p_sec = frames.shape
    n = lax.axis_size("frame")
    parts = lax.axis_size("pix")
    total = n * rows
    cap_blocks = p_sec // n // BLOCK
    slots = cap_blocks // 2 + 1
    early = slots - slots // 2
    cm = cycle_map.reshape(p_sec // BLOCK, BLOCK)

    def swap(x):
        return lax.ppermute(x, "pix", SWAP)

    def send(blocks):
        return lax.all_to_all(
            blocks,
            "frame",
            split_axis=0,
            concat_axis=0,
            axis_index_groups=[list_group(n)],
            tiled=True,
        )

    moving, meta, near_frames, near_cm = pack_move(cm, frames, cap_blocks)
    theirs = swap(moving)
    own = pack_own(meta, near_cm, near_frames, cap_blocks)
    packed = share(meta, own, theirs, cap_blocks)
    received = send(packed)

    meta, _ = lax.optimization_barrier((meta, packed))
    their_meta = swap(meta)
    cap = cap_blocks * BLOCK
    large, twice = left_out(meta[:, :n], their_meta[:, :n], cap)
    overflow = jnp.any(large | twice | left_out(their_meta[:, :n], meta[:, :n], cap)[0])

    flag = overflow.astype(jnp.int32).reshape(1)
    first = normalise(received, total, 0, early, slots - 1, [flag])
    their_first = swap(first)
    last = normalise(received, total, early, slots - early, slots - 1, [first])
    their_last = swap(last)
    sums = partial_sums([first, last], [], parts)
    sums = partial_sums([their_first], sums, parts)

    def spill(frames, cm, meta, their_meta, their_last, *sums):
        rest = send(pack_rest(meta, their_meta, frames, cm, cap_blocks))
        rest = rest.reshape(n, cap_blocks * rows, BLOCK)
        normed = normalise(rest, total, 0, cap_blocks, cap_blocks)
        sums = partial_sums([normed, swap(normed)], sums, parts)
        return correlate([meta, their_meta], their_last, sums)

    def fits(frames, cm, meta, their_meta, their_last, *sums):
        return correlate([meta, their_meta], their_last, sums)

    return lax.cond(overflow, spill, fits, frames, cm, meta, their_meta, their_last, *sums)


def solution(mesh):
    return jax.shard_map(
        body,
        mesh=mesh,
        in_specs=(P("frame", "pix"), P("pix")),
        out_specs=P("frame", "pix", None),
        check_vma=False,
    )
```

```python
import functools

import jax
import jax.numpy as jnp
from jax import lax
from jax.experimental import pallas as pl
from jax.experimental.pallas import tpu as pltpu
from jax.sharding import PartitionSpec as P

BLOCK = 128
HALF_WIN = 2
PAD = 8
TILE = 256
CHUNK = 128
ONES = 16
VMEM_BYTES = 32 * 1024 * 1024
LIST, COUNT, PIXELS = 0, 1, 2
MERGED = 2
SWAP = [(0, 1), (1, 0)]
WHOLE = pl.BlockSpec(memory_space=pltpu.VMEM)
ANYWHERE = pl.BlockSpec(memory_space=pl.ANY)


def call(kernel, name, out_shape, flops=0, bytes_accessed=0, limit=VMEM_BYTES, **kw):
    return pl.pallas_call(
        kernel,
        out_shape=out_shape,
        compiler_params=pltpu.CompilerParams(vmem_limit_bytes=limit),
        cost_estimate=pl.CostEstimate(
            flops=flops, bytes_accessed=bytes_accessed, transcendentals=0
        ),
        name=name,
        **kw,
    )


def dot_nt(a, b):
    return lax.dot_general(a, b, (((1,), (1,)), ((), ())), preferred_element_type=jnp.float32)


def list_group(n):
    side = n // 4
    order = sorted(range(n // 2), key=lambda i: (i % side >= side // 2, i))
    return order + list(range(n // 2, n))


def count_half_rows(rows):
    return max(16, rows // 2)


def gate(wanted):
    wanted = jnp.broadcast_to(wanted, (1, BLOCK))
    return wanted.astype(jnp.float32).astype(jnp.bfloat16)


def take(frames_ref, block):
    return frames_ref[:, pl.ds(pl.multiple_of(block * BLOCK, BLOCK), BLOCK)]


def fold(block, right):
    rows = block.shape[0] // 2
    half = BLOCK // 2
    early, late = block[0:rows].astype(jnp.float32), block[rows:].astype(jnp.float32)
    left = lax.broadcasted_iota(jnp.int32, (rows, BLOCK), 1) < half
    if right:
        folded = jnp.where(left, pltpu.roll(early, half, 1), late)
    else:
        folded = jnp.where(left, early, pltpu.roll(late, half, 1))
    spare = count_half_rows(block.shape[0]) - rows
    if spare:
        folded = jnp.concatenate([folded, jnp.zeros((spare, BLOCK), jnp.float32)])
    return folded.astype(jnp.bfloat16)


def unfold(folded, rows):
    half = BLOCK // 2
    early = folded[0 : rows // 2].astype(jnp.float32)
    left = lax.broadcasted_iota(jnp.int32, early.shape, 1) < half
    return jnp.where(left, early, 0.0), jnp.where(left, pltpu.roll(early, half, 1), 0.0)


def find_members(cm):
    blocks = cm.shape[0]
    first = cm[:, 0:1]
    member = first == lax.broadcasted_iota(jnp.int32, (blocks, BLOCK), 1)
    row = lax.broadcasted_iota(jnp.int32, (blocks, blocks), 0)
    col = lax.broadcasted_iota(jnp.int32, (blocks, blocks), 1)
    earlier = (col < row).astype(jnp.float32).astype(jnp.bfloat16)
    pixels = jnp.sum((cm >= 0).astype(jnp.float32), axis=1, keepdims=True)
    return first, member.astype(jnp.float32), earlier, pixels


def sum_before(earlier, member, values):
    before = jnp.dot(
        earlier, (member * values).astype(jnp.bfloat16), preferred_element_type=jnp.float32
    )
    return jnp.sum(before * member, axis=1, keepdims=True)


def find_blocks(members, cap_blocks, width):
    first, member, earlier, _ = members
    blocks = first.shape[0]
    rank = sum_before(earlier, member, 1.0).astype(jnp.int32)
    slot = jnp.where(first >= 0, first * cap_blocks + rank, -1)
    hit = slot == lax.broadcasted_iota(jnp.int32, (blocks, width), 1)
    index = lax.broadcasted_iota(jnp.int32, (blocks, width), 0).astype(jnp.float32)
    return jnp.sum(jnp.where(hit, index, 0.0), axis=0, keepdims=True).astype(jnp.int32)


def find_places(cm):
    _, member, earlier, pixels = find_members(cm)
    valid = (cm >= 0).astype(jnp.float32)
    row = lax.broadcasted_iota(jnp.int32, (BLOCK, BLOCK), 0)
    col = lax.broadcasted_iota(jnp.int32, (BLOCK, BLOCK), 1)
    before = (row < col).astype(jnp.float32).astype(jnp.bfloat16)
    place = jnp.dot(valid.astype(jnp.bfloat16), before, preferred_element_type=jnp.float32)
    return jnp.where(cm >= 0, place + sum_before(earlier, member, pixels), -1.0)


def move_kernel(cap_blocks, cm_hbm, frames_hbm, out_ref, meta_ref, frames_ref, cm_ref, *scratch):
    list_ref, list_s, sems = scratch
    n = out_ref.shape[0]
    rows = frames_ref.shape[0]
    kept = cap_blocks // 2
    get_cm = pltpu.make_async_copy(cm_hbm, cm_ref, sems.at[0])
    get_cm.start()
    get_frames = pltpu.make_async_copy(frames_hbm, frames_ref, sems.at[1])
    get_frames.start()
    get_cm.wait()
    members = find_members(cm_ref[...])
    found = find_blocks(members, cap_blocks, meta_ref.shape[1])
    list_ref[...] = jnp.broadcast_to(found, list_ref.shape)
    to_scalars = pltpu.make_async_copy(list_ref, list_s, sems.at[2])
    to_scalars.start()
    _, member, _, pixels = members
    meta_ref[...] = jnp.zeros_like(meta_ref)
    meta_ref[LIST : LIST + 1, :] = found
    for row, values in ((COUNT, member), (PIXELS, member * pixels)):
        totals = jnp.sum(values, axis=0, keepdims=True)
        meta_ref[row : row + 1, 0:BLOCK] = totals.astype(jnp.int32)
    to_scalars.wait()
    get_frames.wait()
    for q in range(n):
        for i in range(kept + 1, cap_blocks):
            block = list_s[0, q * cap_blocks + i]
            start = (i - kept - 1) * rows
            out_ref[q, start : start + rows] = take(frames_ref, block)
        start = (cap_blocks - kept - 1) * rows
        block = list_s[0, q * cap_blocks + kept]
        out_ref[q, start:] = fold(take(frames_ref, block), True)


def pack_move(cm, frames, cap_blocks):
    rows = frames.shape[0]
    n = cm.shape[0] // cap_blocks
    height = (cap_blocks - cap_blocks // 2 - 1) * rows + count_half_rows(rows)
    meta = jax.ShapeDtypeStruct((8, cm.shape[0]), jnp.int32)
    return call(
        functools.partial(move_kernel, cap_blocks),
        "pack_move",
        [
            jax.ShapeDtypeStruct((n, height, BLOCK), frames.dtype),
            meta,
            jax.ShapeDtypeStruct(frames.shape, frames.dtype),
            jax.ShapeDtypeStruct(cm.shape, cm.dtype),
        ],
        in_specs=[ANYWHERE] * 2,
        out_specs=[WHOLE] * 4,
        scratch_shapes=[
            pltpu.VMEM(meta.shape, meta.dtype),
            pltpu.SMEM(meta.shape, meta.dtype),
            pltpu.SemaphoreType.DMA((3,)),
        ],
    )(
        pltpu.with_memory_space_constraint(cm, pltpu.HBM),
        pltpu.with_memory_space_constraint(frames, pltpu.HBM),
    )


def own_kernel(cap_blocks, meta_s, cm_ref, frames_ref, out_ref, place_ref):
    n = out_ref.shape[0]
    rows = frames_ref.shape[0]
    kept = cap_blocks // 2
    place_ref[...] = find_places(cm_ref[...])
    target = lax.broadcasted_iota(jnp.int32, (BLOCK, BLOCK), 0).astype(jnp.float32)
    for q in range(n):
        count, pixels = meta_s[COUNT, q], meta_s[PIXELS, q]
        is_full = pixels == cap_blocks * BLOCK
        full = gate(is_full)
        fits = (pixels <= BLOCK) & (count <= MERGED)
        compact = 0.0
        for i in range(MERGED):
            block = meta_s[LIST, q * cap_blocks + i]
            place = jnp.where(fits & (i < count), place_ref[pl.ds(block, 1), :], -1.0)
            chosen = (target == place).astype(jnp.float32).astype(jnp.bfloat16)
            compact = compact + dot_nt(take(frames_ref, block), chosen)
        block = meta_s[LIST, q * cap_blocks]
        out_ref[q, 0:rows] = compact.astype(jnp.bfloat16) + take(frames_ref, block) * full
        for i in range(1, kept):
            block = meta_s[LIST, q * cap_blocks + i]
            out_ref[q, i * rows : (i + 1) * rows] = take(frames_ref, block) * full
        block = meta_s[LIST, q * cap_blocks + kept]
        out_ref[q, kept * rows :] = fold(take(frames_ref, block), False) * full


def pack_own(meta, cm, frames, cap_blocks):
    rows = frames.shape[0]
    n = cm.shape[0] // cap_blocks
    height = cap_blocks // 2 * rows + count_half_rows(rows)
    return call(
        functools.partial(own_kernel, cap_blocks),
        "pack_own",
        jax.ShapeDtypeStruct((n, height, BLOCK), frames.dtype),
        in_specs=[pl.BlockSpec(memory_space=pltpu.SMEM)] + [WHOLE] * 2,
        out_specs=WHOLE,
        scratch_shapes=[pltpu.VMEM(cm.shape, jnp.float32)],
        bytes_accessed=4 * 1024 * 1024,
    )(meta, cm, frames)


def share_kernel(cap_blocks, meta_ref, own_ref, theirs_ref, out_ref):
    n, height, _ = out_ref.shape
    rows = height - theirs_ref.shape[1]
    helped = meta_ref[PIXELS : PIXELS + 1, 0:BLOCK] != cap_blocks * BLOCK
    for to, q in enumerate(list_group(n)):
        other = gate(helped[:, q : q + 1])
        out_ref[to, 0:rows] = own_ref[q, 0:rows]
        out_ref[to, rows:] = own_ref[q, rows:] + theirs_ref[q] * other


def share(meta, own, theirs, cap_blocks):
    return call(
        functools.partial(share_kernel, cap_blocks),
        "share",
        jax.ShapeDtypeStruct(own.shape, own.dtype),
        in_specs=[WHOLE] * 3,
        out_specs=WHOLE,
        bytes_accessed=4 * 1024 * 1024,
    )(meta, own, theirs)


def left_out(meta, their_meta, cap):
    mine, theirs = meta[PIXELS] == cap, their_meta[PIXELS] == cap
    fits = (meta[PIXELS] <= BLOCK) & (meta[COUNT] <= MERGED)
    return jnp.logical_not(mine | fits), mine & theirs


def rest_kernel(cap_blocks, meta_s, their_meta_s, frames_hbm, cm_hbm, out_ref, *scratch):
    frames_ref, cm_ref = scratch
    n, _, rows, _ = out_ref.shape
    kept = cap_blocks // 2
    pltpu.sync_copy(frames_hbm, frames_ref)
    pltpu.sync_copy(cm_hbm, cm_ref)
    right = lax.broadcasted_iota(jnp.int32, (1, BLOCK), 1) >= BLOCK // 2
    for to, q in enumerate(list_group(n)):
        counts = [[ref[row, q] for row in range(PIXELS + 1)] for ref in (meta_s, their_meta_s)]
        large, twice = left_out(*counts, cap_blocks * BLOCK)
        for i in range(cap_blocks):
            block = meta_s[LIST, q * cap_blocks + i]
            wanted = jnp.broadcast_to(large, (1, BLOCK))
            if i >= kept:
                wanted |= twice & right if i == kept else twice
            valid = (cm_ref[pl.ds(block, 1), :] >= 0) & (i < meta_s[COUNT, q])
            out_ref[to, i] = take(frames_ref, block) * gate(valid & wanted)


def pack_rest(meta, their_meta, frames, cm, cap_blocks):
    n = cm.shape[0] // cap_blocks
    return call(
        functools.partial(rest_kernel, cap_blocks),
        "pack_rest",
        jax.ShapeDtypeStruct((n, cap_blocks, frames.shape[0], BLOCK), frames.dtype),
        in_specs=[pl.BlockSpec(memory_space=pltpu.SMEM)] * 2 + [ANYWHERE] * 2,
        out_specs=WHOLE,
        scratch_shapes=[
            pltpu.VMEM(frames.shape, frames.dtype),
            pltpu.VMEM(cm.shape, cm.dtype),
        ],
    )(
        meta,
        their_meta,
        pltpu.with_memory_space_constraint(frames, pltpu.HBM),
        pltpu.with_memory_space_constraint(cm, pltpu.HBM),
    )


def lay_out(raw_ref, rows, first, whole, padded):
    n, height, _ = raw_ref.shape
    total = n * rows
    zero = jnp.zeros((PAD, BLOCK), jnp.float32)
    for i in range(padded.shape[0]):
        slot = first + i
        padded[i, 0:PAD] = zero
        padded[i, PAD + total : 2 * PAD + total] = zero
        for place, source in enumerate(list_group(n)):
            start = PAD + source * rows
            if slot < whole:
                block = raw_ref[place, slot * rows : (slot + 1) * rows]
                padded[i, start : start + rows] = block.astype(jnp.float32)
            else:
                early, late = unfold(raw_ref[place, slot * rows : height], rows)
                padded[i, start : start + rows // 2] = early
                padded[i, start + rows // 2 : start + rows] = late


def norm_rows(padded, start, chunk, out_ref):
    total = out_ref.shape[0]
    base = PAD + start
    for slot in range(padded.shape[0]):
        raw = padded[slot, base : base + chunk]
        summed = raw
        for offset in range(1, HALF_WIN + 1):
            summed = summed + padded[slot, base - offset : base - offset + chunk]
            summed = summed + padded[slot, base + offset : base + offset + chunk]
        if start == 0 or start + chunk == total:
            frame = start + lax.broadcasted_iota(jnp.int32, (chunk, BLOCK), 0)
            upper = jnp.minimum(frame + HALF_WIN, total - 1)
            lower = jnp.maximum(frame - HALF_WIN, 0)
            mean = summed / (upper - lower + 1).astype(jnp.float32)
        else:
            mean = summed * (1.0 / (2 * HALF_WIN + 1))
        normed = jnp.where(summed > 0.0, raw / mean, 0.0)
        out_ref[start : start + chunk, slot * BLOCK : (slot + 1) * BLOCK] = normed.astype(
            jnp.bfloat16
        )


def norm_kernel(rows, first, whole, raw_ref, *refs):
    out_ref, padded = refs[-2:]
    lay_out(raw_ref, rows, first, whole, padded)
    for start in range(0, out_ref.shape[0], CHUNK):
        norm_rows(padded, start, CHUNK, out_ref)


def normalise(raw, total, first, slots, whole, after=()):
    return call(
        functools.partial(norm_kernel, total // raw.shape[0], first, whole),
        "normalise",
        jax.ShapeDtypeStruct((total, slots * BLOCK), jnp.bfloat16),
        flops=12 * total * slots * BLOCK,
        bytes_accessed=4 * total * slots * BLOCK,
        in_specs=[WHOLE] + [ANYWHERE] * len(after),
        out_specs=WHOLE,
        scratch_shapes=[pltpu.VMEM((slots, total + 2 * PAD, BLOCK), jnp.float32)],
    )(raw, *after)


def set_left(ref, left_ref):
    rows = left_ref.shape[0] - ONES
    first_row = pl.multiple_of(lax.axis_index("pix") * rows, rows)
    left_ref[0:rows] = ref[pl.ds(first_row, rows), :]
    left_ref[rows : rows + ONES] = jnp.ones((ONES, ref.shape[1]), jnp.bfloat16)


def add_sums(pairs, sums, column):
    gram, frame = sums
    rows = pairs[0][0].shape[0] - ONES
    for left_ref, ref in pairs:
        both = dot_nt(left_ref[...], ref[column, :])
        gram = gram + both[0:rows]
        frame = frame + both[rows : rows + 8]
    return gram, frame


def partial_kernel(count, *refs):
    normed, lefts, (gram_out, frame_out) = refs[:count], refs[-count:], refs[-count - 2 : -count]
    before = refs[count : -count - 2]
    for ref, left_ref in zip(normed, lefts):
        set_left(ref, left_ref)
    for start in range(0, gram_out.shape[1], TILE):
        column = slice(start, start + TILE)
        sums = [ref[:, column] for ref in before] or [0.0, 0.0]
        gram_out[:, column], frame_out[:, column] = add_sums(
            list(zip(lefts, normed)), sums, column
        )


def sums_shape(total, parts):
    return [
        jax.ShapeDtypeStruct((total // parts, total), jnp.float32),
        jax.ShapeDtypeStruct((8, total), jnp.float32),
    ]


def partial_sums(normed, before, parts):
    total, width = normed[0].shape
    rows = total // parts
    return call(
        functools.partial(partial_kernel, len(normed)),
        "partial_sums",
        sums_shape(total, parts),
        flops=2 * rows * total * width * len(normed),
        bytes_accessed=4 * rows * total,
        in_specs=[WHOLE] * (len(normed) + len(before)),
        out_specs=[WHOLE] * 2,
        scratch_shapes=[pltpu.VMEM((rows + ONES, x.shape[1]), x.dtype) for x in normed],
    )(*normed, *before)


def result_kernel(meta_ref, their_meta_ref, normed_ref, gram_in, frame_in, out_hbm, *scratch):
    out_ref, frame_ref, sems = scratch
    rows, total = gram_in.shape
    pixels = meta_ref[PIXELS : PIXELS + 1, 0:BLOCK] + their_meta_ref[PIXELS : PIXELS + 1, 0:BLOCK]
    own = lax.broadcasted_iota(jnp.int32, (1, BLOCK), 1) == lax.axis_index("frame")
    number = jnp.sum(jnp.where(own, pixels, 0).astype(jnp.float32), axis=1, keepdims=True)
    ones = jnp.ones((8, normed_ref.shape[1]), jnp.bfloat16)
    frame_ref[...] = frame_in[...] + dot_nt(ones, normed_ref[...])
    first_row = pl.multiple_of(lax.axis_index("pix") * rows, rows)
    row_sum = jnp.broadcast_to(frame_ref[0:1, pl.ds(first_row, rows)], (BLOCK, rows)).T
    row_inv = 1.0 / row_sum[:, 0:1]
    left = normed_ref[pl.ds(first_row, rows), :]
    copies = []
    for i, start in enumerate(range(0, total, TILE)):
        column = slice(start, start + TILE)
        gram = gram_in[:, column] + dot_nt(left, normed_ref[column, :])
        col_inv = 1.0 / frame_ref[0:1, column]
        result = ((gram * row_inv) * col_inv) * number - 1.0
        out_ref[i] = result.astype(jnp.bfloat16)
        copies.append(
            pltpu.make_async_copy(out_ref.at[i], out_hbm.at[0, :, column], sems.at[i])
        )
        copies[-1].start()
    for copy in copies:
        copy.wait()


def correlate(metas, normed, before):
    rows, total = before[0].shape
    tiles = total // TILE
    return call(
        result_kernel,
        "correlate",
        pltpu.HBM((1, rows, total), jnp.bfloat16),
        flops=2 * rows * total * normed.shape[1],
        bytes_accessed=6 * rows * total,
        in_specs=[WHOLE] * 5,
        out_specs=ANYWHERE,
        scratch_shapes=[
            pltpu.VMEM((tiles, rows, TILE), jnp.bfloat16),
            pltpu.VMEM((8, total), jnp.float32),
            pltpu.SemaphoreType.DMA((tiles,)),
        ],
    )(*metas, normed, *before)


def body(frames, cycle_map):
    rows, p_sec = frames.shape
    n = lax.axis_size("frame")
    parts = lax.axis_size("pix")
    total = n * rows
    cap_blocks = p_sec // n // BLOCK
    slots = cap_blocks // 2 + 1
    early = slots - slots // 2
    cm = cycle_map.reshape(p_sec // BLOCK, BLOCK)

    def swap(x):
        return lax.ppermute(x, "pix", SWAP)

    def send(blocks):
        return lax.all_to_all(
            blocks,
            "frame",
            split_axis=0,
            concat_axis=0,
            axis_index_groups=[list_group(n)],
            tiled=True,
        )

    moving, meta, near_frames, near_cm = pack_move(cm, frames, cap_blocks)
    theirs = swap(moving)
    own = pack_own(meta, near_cm, near_frames, cap_blocks)
    packed = share(meta, own, theirs, cap_blocks)
    received = send(packed)

    meta, _ = lax.optimization_barrier((meta, packed))
    their_meta = swap(meta)
    cap = cap_blocks * BLOCK
    large, twice = left_out(meta[:, :n], their_meta[:, :n], cap)
    overflow = jnp.any(large | twice | left_out(their_meta[:, :n], meta[:, :n], cap)[0])

    flag = overflow.astype(jnp.int32).reshape(1)
    first = normalise(received, total, 0, early, slots - 1, [flag])
    their_first = swap(first)
    last = normalise(received, total, early, slots - early, slots - 1, [first])
    their_last = swap(last)
    sums = partial_sums([first, last], [], parts)
    sums = partial_sums([their_first], sums, parts)

    def spill(frames, cm, meta, their_meta, their_last, *sums):
        rest = send(pack_rest(meta, their_meta, frames, cm, cap_blocks))
        rest = rest.reshape(n, cap_blocks * rows, BLOCK)
        normed = normalise(rest, total, 0, cap_blocks, cap_blocks)
        sums = partial_sums([normed, swap(normed)], sums, parts)
        return correlate([meta, their_meta], their_last, sums)

    def fits(frames, cm, meta, their_meta, their_last, *sums):
        return correlate([meta, their_meta], their_last, sums)

    return lax.cond(overflow, spill, fits, frames, cm, meta, their_meta, their_last, *sums)


def solution(mesh):
    return jax.shard_map(
        body,
        mesh=mesh,
        in_specs=(P("frame", "pix"), P("pix")),
        out_specs=P("frame", "pix", None),
        check_vma=False,
    )
```

```python
import functools

import jax
import jax.numpy as jnp
from jax import lax
from jax.experimental import pallas as pl
from jax.experimental.pallas import tpu as pltpu
from jax.sharding import PartitionSpec as P

BLOCK = 128
HALF_WIN = 2
PAD = 8
TILE = 256
CHUNK = 128
ONES = 16
VMEM_BYTES = 32 * 1024 * 1024
LIST, COUNT, PIXELS = 0, 1, 2
MERGED = 2
SWAP = [(0, 1), (1, 0)]
WHOLE = pl.BlockSpec(memory_space=pltpu.VMEM)
ANYWHERE = pl.BlockSpec(memory_space=pl.ANY)


def call(kernel, name, out_shape, flops=0, bytes_accessed=0, limit=VMEM_BYTES, **kw):
    return pl.pallas_call(
        kernel,
        out_shape=out_shape,
        compiler_params=pltpu.CompilerParams(vmem_limit_bytes=limit),
        cost_estimate=pl.CostEstimate(
            flops=flops, bytes_accessed=bytes_accessed, transcendentals=0
        ),
        name=name,
        **kw,
    )


def dot_nt(a, b):
    return lax.dot_general(a, b, (((1,), (1,)), ((), ())), preferred_element_type=jnp.float32)


def list_group(n):
    half, side = n // 2, n // 4
    first = sorted(range(half), key=lambda i: (i % 2, i))
    return first + sorted(range(half, n), key=lambda i: (i % side >= side // 2, i))


def count_half_rows(rows):
    return max(16, rows // 2)


def gate(wanted):
    wanted = jnp.broadcast_to(wanted, (1, BLOCK))
    return wanted.astype(jnp.float32).astype(jnp.bfloat16)


def take(frames_ref, block):
    return frames_ref[:, pl.ds(pl.multiple_of(block * BLOCK, BLOCK), BLOCK)]


def fold(block, right):
    rows = block.shape[0] // 2
    half = BLOCK // 2
    early, late = block[0:rows].astype(jnp.float32), block[rows:].astype(jnp.float32)
    left = lax.broadcasted_iota(jnp.int32, (rows, BLOCK), 1) < half
    if right:
        folded = jnp.where(left, pltpu.roll(early, half, 1), late)
    else:
        folded = jnp.where(left, early, pltpu.roll(late, half, 1))
    spare = count_half_rows(block.shape[0]) - rows
    if spare:
        folded = jnp.concatenate([folded, jnp.zeros((spare, BLOCK), jnp.float32)])
    return folded.astype(jnp.bfloat16)


def unfold(folded, rows):
    half = BLOCK // 2
    early = folded[0 : rows // 2].astype(jnp.float32)
    left = lax.broadcasted_iota(jnp.int32, early.shape, 1) < half
    return jnp.where(left, early, 0.0), jnp.where(left, pltpu.roll(early, half, 1), 0.0)


def find_members(cm):
    blocks = cm.shape[0]
    first = cm[:, 0:1]
    member = first == lax.broadcasted_iota(jnp.int32, (blocks, BLOCK), 1)
    row = lax.broadcasted_iota(jnp.int32, (blocks, blocks), 0)
    col = lax.broadcasted_iota(jnp.int32, (blocks, blocks), 1)
    earlier = (col < row).astype(jnp.float32).astype(jnp.bfloat16)
    pixels = jnp.sum((cm >= 0).astype(jnp.float32), axis=1, keepdims=True)
    return first, member.astype(jnp.float32), earlier, pixels


def sum_before(earlier, member, values):
    before = jnp.dot(
        earlier, (member * values).astype(jnp.bfloat16), preferred_element_type=jnp.float32
    )
    return jnp.sum(before * member, axis=1, keepdims=True)


def find_blocks(members, cap_blocks, width):
    first, member, earlier, _ = members
    blocks = first.shape[0]
    rank = sum_before(earlier, member, 1.0).astype(jnp.int32)
    slot = jnp.where(first >= 0, first * cap_blocks + rank, -1)
    hit = slot == lax.broadcasted_iota(jnp.int32, (blocks, width), 1)
    index = lax.broadcasted_iota(jnp.int32, (blocks, width), 0).astype(jnp.float32)
    return jnp.sum(jnp.where(hit, index, 0.0), axis=0, keepdims=True).astype(jnp.int32)


def find_places(cm):
    _, member, earlier, pixels = find_members(cm)
    valid = (cm >= 0).astype(jnp.float32)
    row = lax.broadcasted_iota(jnp.int32, (BLOCK, BLOCK), 0)
    col = lax.broadcasted_iota(jnp.int32, (BLOCK, BLOCK), 1)
    before = (row < col).astype(jnp.float32).astype(jnp.bfloat16)
    place = jnp.dot(valid.astype(jnp.bfloat16), before, preferred_element_type=jnp.float32)
    return jnp.where(cm >= 0, place + sum_before(earlier, member, pixels), -1.0)


def move_kernel(cap_blocks, cm_hbm, frames_hbm, out_ref, meta_ref, frames_ref, cm_ref, *scratch):
    list_ref, list_s, sems = scratch
    n = out_ref.shape[0]
    rows = frames_ref.shape[0]
    kept = cap_blocks // 2
    get_cm = pltpu.make_async_copy(cm_hbm, cm_ref, sems.at[0])
    get_cm.start()
    get_frames = pltpu.make_async_copy(frames_hbm, frames_ref, sems.at[1])
    get_frames.start()
    get_cm.wait()
    members = find_members(cm_ref[...])
    found = find_blocks(members, cap_blocks, meta_ref.shape[1])
    list_ref[...] = jnp.broadcast_to(found, list_ref.shape)
    to_scalars = pltpu.make_async_copy(list_ref, list_s, sems.at[2])
    to_scalars.start()
    _, member, _, pixels = members
    meta_ref[...] = jnp.zeros_like(meta_ref)
    meta_ref[LIST : LIST + 1, :] = found
    for row, values in ((COUNT, member), (PIXELS, member * pixels)):
        totals = jnp.sum(values, axis=0, keepdims=True)
        meta_ref[row : row + 1, 0:BLOCK] = totals.astype(jnp.int32)
    to_scalars.wait()
    get_frames.wait()
    for q in range(n):
        for i in range(kept + 1, cap_blocks):
            block = list_s[0, q * cap_blocks + i]
            start = (i - kept - 1) * rows
            out_ref[q, start : start + rows] = take(frames_ref, block)
        start = (cap_blocks - kept - 1) * rows
        block = list_s[0, q * cap_blocks + kept]
        out_ref[q, start:] = fold(take(frames_ref, block), True)


def pack_move(cm, frames, cap_blocks):
    rows = frames.shape[0]
    n = cm.shape[0] // cap_blocks
    height = (cap_blocks - cap_blocks // 2 - 1) * rows + count_half_rows(rows)
    meta = jax.ShapeDtypeStruct((8, cm.shape[0]), jnp.int32)
    return call(
        functools.partial(move_kernel, cap_blocks),
        "pack_move",
        [
            jax.ShapeDtypeStruct((n, height, BLOCK), frames.dtype),
            meta,
            jax.ShapeDtypeStruct(frames.shape, frames.dtype),
            jax.ShapeDtypeStruct(cm.shape, cm.dtype),
        ],
        in_specs=[ANYWHERE] * 2,
        out_specs=[WHOLE] * 4,
        scratch_shapes=[
            pltpu.VMEM(meta.shape, meta.dtype),
            pltpu.SMEM(meta.shape, meta.dtype),
            pltpu.SemaphoreType.DMA((3,)),
        ],
    )(
        pltpu.with_memory_space_constraint(cm, pltpu.HBM),
        pltpu.with_memory_space_constraint(frames, pltpu.HBM),
    )


def own_kernel(cap_blocks, meta_s, cm_ref, frames_ref, out_ref, place_ref):
    n = out_ref.shape[0]
    rows = frames_ref.shape[0]
    kept = cap_blocks // 2
    place_ref[...] = find_places(cm_ref[...])
    target = lax.broadcasted_iota(jnp.int32, (BLOCK, BLOCK), 0).astype(jnp.float32)
    for q in range(n):
        count, pixels = meta_s[COUNT, q], meta_s[PIXELS, q]
        is_full = pixels == cap_blocks * BLOCK
        full = gate(is_full)
        fits = (pixels <= BLOCK) & (count <= MERGED)
        compact = 0.0
        for i in range(MERGED):
            block = meta_s[LIST, q * cap_blocks + i]
            place = jnp.where(fits & (i < count), place_ref[pl.ds(block, 1), :], -1.0)
            chosen = (target == place).astype(jnp.float32).astype(jnp.bfloat16)
            compact = compact + dot_nt(take(frames_ref, block), chosen)
        block = meta_s[LIST, q * cap_blocks]
        out_ref[q, 0:rows] = compact.astype(jnp.bfloat16) + take(frames_ref, block) * full
        for i in range(1, kept):
            block = meta_s[LIST, q * cap_blocks + i]
            out_ref[q, i * rows : (i + 1) * rows] = take(frames_ref, block) * full
        block = meta_s[LIST, q * cap_blocks + kept]
        out_ref[q, kept * rows :] = fold(take(frames_ref, block), False) * full


def pack_own(meta, cm, frames, cap_blocks):
    rows = frames.shape[0]
    n = cm.shape[0] // cap_blocks
    height = cap_blocks // 2 * rows + count_half_rows(rows)
    return call(
        functools.partial(own_kernel, cap_blocks),
        "pack_own",
        jax.ShapeDtypeStruct((n, height, BLOCK), frames.dtype),
        in_specs=[pl.BlockSpec(memory_space=pltpu.SMEM)] + [WHOLE] * 2,
        out_specs=WHOLE,
        scratch_shapes=[pltpu.VMEM(cm.shape, jnp.float32)],
        bytes_accessed=4 * 1024 * 1024,
    )(meta, cm, frames)


def share_kernel(cap_blocks, meta_ref, own_ref, theirs_ref, out_ref):
    n, height, _ = out_ref.shape
    rows = height - theirs_ref.shape[1]
    helped = meta_ref[PIXELS : PIXELS + 1, 0:BLOCK] != cap_blocks * BLOCK
    for to, q in enumerate(list_group(n)):
        other = gate(helped[:, q : q + 1])
        out_ref[to, 0:rows] = own_ref[q, 0:rows]
        out_ref[to, rows:] = own_ref[q, rows:] + theirs_ref[q] * other


def share(meta, own, theirs, cap_blocks):
    return call(
        functools.partial(share_kernel, cap_blocks),
        "share",
        jax.ShapeDtypeStruct(own.shape, own.dtype),
        in_specs=[WHOLE] * 3,
        out_specs=WHOLE,
        bytes_accessed=4 * 1024 * 1024,
    )(meta, own, theirs)


def left_out(meta, their_meta, cap):
    mine, theirs = meta[PIXELS] == cap, their_meta[PIXELS] == cap
    fits = (meta[PIXELS] <= BLOCK) & (meta[COUNT] <= MERGED)
    return jnp.logical_not(mine | fits), mine & theirs


def rest_kernel(cap_blocks, meta_s, their_meta_s, frames_hbm, cm_hbm, out_ref, *scratch):
    frames_ref, cm_ref = scratch
    n, _, rows, _ = out_ref.shape
    kept = cap_blocks // 2
    pltpu.sync_copy(frames_hbm, frames_ref)
    pltpu.sync_copy(cm_hbm, cm_ref)
    right = lax.broadcasted_iota(jnp.int32, (1, BLOCK), 1) >= BLOCK // 2
    for to, q in enumerate(list_group(n)):
        counts = [[ref[row, q] for row in range(PIXELS + 1)] for ref in (meta_s, their_meta_s)]
        large, twice = left_out(*counts, cap_blocks * BLOCK)
        for i in range(cap_blocks):
            block = meta_s[LIST, q * cap_blocks + i]
            wanted = jnp.broadcast_to(large, (1, BLOCK))
            if i >= kept:
                wanted |= twice & right if i == kept else twice
            valid = (cm_ref[pl.ds(block, 1), :] >= 0) & (i < meta_s[COUNT, q])
            out_ref[to, i] = take(frames_ref, block) * gate(valid & wanted)


def pack_rest(meta, their_meta, frames, cm, cap_blocks):
    n = cm.shape[0] // cap_blocks
    return call(
        functools.partial(rest_kernel, cap_blocks),
        "pack_rest",
        jax.ShapeDtypeStruct((n, cap_blocks, frames.shape[0], BLOCK), frames.dtype),
        in_specs=[pl.BlockSpec(memory_space=pltpu.SMEM)] * 2 + [ANYWHERE] * 2,
        out_specs=WHOLE,
        scratch_shapes=[
            pltpu.VMEM(frames.shape, frames.dtype),
            pltpu.VMEM(cm.shape, cm.dtype),
        ],
    )(
        meta,
        their_meta,
        pltpu.with_memory_space_constraint(frames, pltpu.HBM),
        pltpu.with_memory_space_constraint(cm, pltpu.HBM),
    )


def lay_out(raw_ref, rows, first, whole, padded):
    n, height, _ = raw_ref.shape
    total = n * rows
    zero = jnp.zeros((PAD, BLOCK), jnp.float32)
    for i in range(padded.shape[0]):
        slot = first + i
        padded[i, 0:PAD] = zero
        padded[i, PAD + total : 2 * PAD + total] = zero
        for place, source in enumerate(list_group(n)):
            start = PAD + source * rows
            if slot < whole:
                block = raw_ref[place, slot * rows : (slot + 1) * rows]
                padded[i, start : start + rows] = block.astype(jnp.float32)
            else:
                early, late = unfold(raw_ref[place, slot * rows : height], rows)
                padded[i, start : start + rows // 2] = early
                padded[i, start + rows // 2 : start + rows] = late


def norm_rows(padded, start, chunk, out_ref):
    total = out_ref.shape[0]
    base = PAD + start
    for slot in range(padded.shape[0]):
        raw = padded[slot, base : base + chunk]
        summed = raw
        for offset in range(1, HALF_WIN + 1):
            summed = summed + padded[slot, base - offset : base - offset + chunk]
            summed = summed + padded[slot, base + offset : base + offset + chunk]
        if start == 0 or start + chunk == total:
            frame = start + lax.broadcasted_iota(jnp.int32, (chunk, BLOCK), 0)
            upper = jnp.minimum(frame + HALF_WIN, total - 1)
            lower = jnp.maximum(frame - HALF_WIN, 0)
            mean = summed / (upper - lower + 1).astype(jnp.float32)
        else:
            mean = summed * (1.0 / (2 * HALF_WIN + 1))
        normed = jnp.where(summed > 0.0, raw / mean, 0.0)
        out_ref[start : start + chunk, slot * BLOCK : (slot + 1) * BLOCK] = normed.astype(
            jnp.bfloat16
        )


def norm_kernel(rows, first, whole, raw_ref, *refs):
    out_ref, padded = refs[-2:]
    lay_out(raw_ref, rows, first, whole, padded)
    for start in range(0, out_ref.shape[0], CHUNK):
        norm_rows(padded, start, CHUNK, out_ref)


def normalise(raw, total, first, slots, whole, after=()):
    return call(
        functools.partial(norm_kernel, total // raw.shape[0], first, whole),
        "normalise",
        jax.ShapeDtypeStruct((total, slots * BLOCK), jnp.bfloat16),
        flops=12 * total * slots * BLOCK,
        bytes_accessed=4 * total * slots * BLOCK,
        in_specs=[WHOLE] + [ANYWHERE] * len(after),
        out_specs=WHOLE,
        scratch_shapes=[pltpu.VMEM((slots, total + 2 * PAD, BLOCK), jnp.float32)],
    )(raw, *after)


def set_left(ref, left_ref):
    rows = left_ref.shape[0] - ONES
    first_row = pl.multiple_of(lax.axis_index("pix") * rows, rows)
    left_ref[0:rows] = ref[pl.ds(first_row, rows), :]
    left_ref[rows : rows + ONES] = jnp.ones((ONES, ref.shape[1]), jnp.bfloat16)


def add_sums(pairs, sums, column):
    gram, frame = sums
    rows = pairs[0][0].shape[0] - ONES
    for left_ref, ref in pairs:
        both = dot_nt(left_ref[...], ref[column, :])
        gram = gram + both[0:rows]
        frame = frame + both[rows : rows + 8]
    return gram, frame


def partial_kernel(count, *refs):
    normed, lefts, (gram_out, frame_out) = refs[:count], refs[-count:], refs[-count - 2 : -count]
    before = refs[count : -count - 2]
    for ref, left_ref in zip(normed, lefts):
        set_left(ref, left_ref)
    for start in range(0, gram_out.shape[1], TILE):
        column = slice(start, start + TILE)
        sums = [ref[:, column] for ref in before] or [0.0, 0.0]
        gram_out[:, column], frame_out[:, column] = add_sums(
            list(zip(lefts, normed)), sums, column
        )


def sums_shape(total, parts):
    return [
        jax.ShapeDtypeStruct((total // parts, total), jnp.float32),
        jax.ShapeDtypeStruct((8, total), jnp.float32),
    ]


def partial_sums(normed, before, parts):
    total, width = normed[0].shape
    rows = total // parts
    return call(
        functools.partial(partial_kernel, len(normed)),
        "partial_sums",
        sums_shape(total, parts),
        flops=2 * rows * total * width * len(normed),
        bytes_accessed=4 * rows * total,
        in_specs=[WHOLE] * (len(normed) + len(before)),
        out_specs=[WHOLE] * 2,
        scratch_shapes=[pltpu.VMEM((rows + ONES, x.shape[1]), x.dtype) for x in normed],
    )(*normed, *before)


def result_kernel(meta_ref, their_meta_ref, normed_ref, gram_in, frame_in, out_hbm, *scratch):
    out_ref, frame_ref, sems = scratch
    rows, total = gram_in.shape
    pixels = meta_ref[PIXELS : PIXELS + 1, 0:BLOCK] + their_meta_ref[PIXELS : PIXELS + 1, 0:BLOCK]
    own = lax.broadcasted_iota(jnp.int32, (1, BLOCK), 1) == lax.axis_index("frame")
    number = jnp.sum(jnp.where(own, pixels, 0).astype(jnp.float32), axis=1, keepdims=True)
    ones = jnp.ones((8, normed_ref.shape[1]), jnp.bfloat16)
    frame_ref[...] = frame_in[...] + dot_nt(ones, normed_ref[...])
    first_row = pl.multiple_of(lax.axis_index("pix") * rows, rows)
    row_sum = jnp.broadcast_to(frame_ref[0:1, pl.ds(first_row, rows)], (BLOCK, rows)).T
    row_inv = 1.0 / row_sum[:, 0:1]
    left = normed_ref[pl.ds(first_row, rows), :]
    copies = []
    for i, start in enumerate(range(0, total, TILE)):
        column = slice(start, start + TILE)
        gram = gram_in[:, column] + dot_nt(left, normed_ref[column, :])
        col_inv = 1.0 / frame_ref[0:1, column]
        result = ((gram * row_inv) * col_inv) * number - 1.0
        out_ref[i] = result.astype(jnp.bfloat16)
        copies.append(
            pltpu.make_async_copy(out_ref.at[i], out_hbm.at[0, :, column], sems.at[i])
        )
        copies[-1].start()
    for copy in copies:
        copy.wait()


def correlate(metas, normed, before):
    rows, total = before[0].shape
    tiles = total // TILE
    return call(
        result_kernel,
        "correlate",
        pltpu.HBM((1, rows, total), jnp.bfloat16),
        flops=2 * rows * total * normed.shape[1],
        bytes_accessed=6 * rows * total,
        in_specs=[WHOLE] * 5,
        out_specs=ANYWHERE,
        scratch_shapes=[
            pltpu.VMEM((tiles, rows, TILE), jnp.bfloat16),
            pltpu.VMEM((8, total), jnp.float32),
            pltpu.SemaphoreType.DMA((tiles,)),
        ],
    )(*metas, normed, *before)


def body(frames, cycle_map):
    rows, p_sec = frames.shape
    n = lax.axis_size("frame")
    parts = lax.axis_size("pix")
    total = n * rows
    cap_blocks = p_sec // n // BLOCK
    slots = cap_blocks // 2 + 1
    early = slots - slots // 2
    cm = cycle_map.reshape(p_sec // BLOCK, BLOCK)

    def swap(x):
        return lax.ppermute(x, "pix", SWAP)

    def send(blocks):
        return lax.all_to_all(
            blocks,
            "frame",
            split_axis=0,
            concat_axis=0,
            axis_index_groups=[list_group(n)],
            tiled=True,
        )

    moving, meta, near_frames, near_cm = pack_move(cm, frames, cap_blocks)
    theirs = swap(moving)
    own = pack_own(meta, near_cm, near_frames, cap_blocks)
    packed = share(meta, own, theirs, cap_blocks)
    received = send(packed)

    meta, _ = lax.optimization_barrier((meta, packed))
    their_meta = swap(meta)
    cap = cap_blocks * BLOCK
    large, twice = left_out(meta[:, :n], their_meta[:, :n], cap)
    overflow = jnp.any(large | twice | left_out(their_meta[:, :n], meta[:, :n], cap)[0])

    flag = overflow.astype(jnp.int32).reshape(1)
    first = normalise(received, total, 0, early, slots - 1, [flag])
    their_first = swap(first)
    last = normalise(received, total, early, slots - early, slots - 1, [first])
    their_last = swap(last)
    sums = partial_sums([first, last], [], parts)
    sums = partial_sums([their_first], sums, parts)

    def spill(frames, cm, meta, their_meta, their_last, *sums):
        rest = send(pack_rest(meta, their_meta, frames, cm, cap_blocks))
        rest = rest.reshape(n, cap_blocks * rows, BLOCK)
        normed = normalise(rest, total, 0, cap_blocks, cap_blocks)
        sums = partial_sums([normed, swap(normed)], sums, parts)
        return correlate([meta, their_meta], their_last, sums)

    def fits(frames, cm, meta, their_meta, their_last, *sums):
        return correlate([meta, their_meta], their_last, sums)

    return lax.cond(overflow, spill, fits, frames, cm, meta, their_meta, their_last, *sums)


def solution(mesh):
    return jax.shard_map(
        body,
        mesh=mesh,
        in_specs=(P("frame", "pix"), P("pix")),
        out_specs=P("frame", "pix", None),
        check_vma=False,
    )
```

```python
import functools

import jax
import jax.numpy as jnp
from jax import lax
from jax.experimental import pallas as pl
from jax.experimental.pallas import tpu as pltpu
from jax.sharding import PartitionSpec as P

BLOCK = 128
HALF_WIN = 2
PAD = 8
TILE = 256
CHUNK = 128
ONES = 16
VMEM_BYTES = 32 * 1024 * 1024
LIST, COUNT, PIXELS = 0, 1, 2
MERGED = 2
SWAP = [(0, 1), (1, 0)]
WHOLE = pl.BlockSpec(memory_space=pltpu.VMEM)
ANYWHERE = pl.BlockSpec(memory_space=pl.ANY)


def call(kernel, name, out_shape, flops=0, bytes_accessed=0, limit=VMEM_BYTES, **kw):
    return pl.pallas_call(
        kernel,
        out_shape=out_shape,
        compiler_params=pltpu.CompilerParams(vmem_limit_bytes=limit),
        cost_estimate=pl.CostEstimate(
            flops=flops, bytes_accessed=bytes_accessed, transcendentals=0
        ),
        name=name,
        **kw,
    )


def dot_nt(a, b):
    return lax.dot_general(a, b, (((1,), (1,)), ((), ())), preferred_element_type=jnp.float32)


def list_group(n):
    half, side = n // 2, n // 4
    first = sorted(range(half), key=lambda i: (i % side >= side - side // 4, i))
    return first + sorted(range(half, n), key=lambda i: (i % side >= side // 2, i))


def count_half_rows(rows):
    return max(16, rows // 2)


def gate(wanted):
    wanted = jnp.broadcast_to(wanted, (1, BLOCK))
    return wanted.astype(jnp.float32).astype(jnp.bfloat16)


def take(frames_ref, block):
    return frames_ref[:, pl.ds(pl.multiple_of(block * BLOCK, BLOCK), BLOCK)]


def fold(block, right):
    rows = block.shape[0] // 2
    half = BLOCK // 2
    early, late = block[0:rows].astype(jnp.float32), block[rows:].astype(jnp.float32)
    left = lax.broadcasted_iota(jnp.int32, (rows, BLOCK), 1) < half
    if right:
        folded = jnp.where(left, pltpu.roll(early, half, 1), late)
    else:
        folded = jnp.where(left, early, pltpu.roll(late, half, 1))
    spare = count_half_rows(block.shape[0]) - rows
    if spare:
        folded = jnp.concatenate([folded, jnp.zeros((spare, BLOCK), jnp.float32)])
    return folded.astype(jnp.bfloat16)


def unfold(folded, rows):
    half = BLOCK // 2
    early = folded[0 : rows // 2].astype(jnp.float32)
    left = lax.broadcasted_iota(jnp.int32, early.shape, 1) < half
    return jnp.where(left, early, 0.0), jnp.where(left, pltpu.roll(early, half, 1), 0.0)


def find_members(cm):
    blocks = cm.shape[0]
    first = cm[:, 0:1]
    member = first == lax.broadcasted_iota(jnp.int32, (blocks, BLOCK), 1)
    row = lax.broadcasted_iota(jnp.int32, (blocks, blocks), 0)
    col = lax.broadcasted_iota(jnp.int32, (blocks, blocks), 1)
    earlier = (col < row).astype(jnp.float32).astype(jnp.bfloat16)
    pixels = jnp.sum((cm >= 0).astype(jnp.float32), axis=1, keepdims=True)
    return first, member.astype(jnp.float32), earlier, pixels


def sum_before(earlier, member, values):
    before = jnp.dot(
        earlier, (member * values).astype(jnp.bfloat16), preferred_element_type=jnp.float32
    )
    return jnp.sum(before * member, axis=1, keepdims=True)


def find_blocks(members, cap_blocks, width):
    first, member, earlier, _ = members
    blocks = first.shape[0]
    rank = sum_before(earlier, member, 1.0).astype(jnp.int32)
    slot = jnp.where(first >= 0, first * cap_blocks + rank, -1)
    hit = slot == lax.broadcasted_iota(jnp.int32, (blocks, width), 1)
    index = lax.broadcasted_iota(jnp.int32, (blocks, width), 0).astype(jnp.float32)
    return jnp.sum(jnp.where(hit, index, 0.0), axis=0, keepdims=True).astype(jnp.int32)


def find_places(cm):
    _, member, earlier, pixels = find_members(cm)
    valid = (cm >= 0).astype(jnp.float32)
    row = lax.broadcasted_iota(jnp.int32, (BLOCK, BLOCK), 0)
    col = lax.broadcasted_iota(jnp.int32, (BLOCK, BLOCK), 1)
    before = (row < col).astype(jnp.float32).astype(jnp.bfloat16)
    place = jnp.dot(valid.astype(jnp.bfloat16), before, preferred_element_type=jnp.float32)
    return jnp.where(cm >= 0, place + sum_before(earlier, member, pixels), -1.0)


def move_kernel(cap_blocks, cm_hbm, frames_hbm, out_ref, meta_ref, frames_ref, cm_ref, *scratch):
    list_ref, list_s, sems = scratch
    n = out_ref.shape[0]
    rows = frames_ref.shape[0]
    kept = cap_blocks // 2
    get_cm = pltpu.make_async_copy(cm_hbm, cm_ref, sems.at[0])
    get_cm.start()
    get_frames = pltpu.make_async_copy(frames_hbm, frames_ref, sems.at[1])
    get_frames.start()
    get_cm.wait()
    members = find_members(cm_ref[...])
    found = find_blocks(members, cap_blocks, meta_ref.shape[1])
    list_ref[...] = jnp.broadcast_to(found, list_ref.shape)
    to_scalars = pltpu.make_async_copy(list_ref, list_s, sems.at[2])
    to_scalars.start()
    _, member, _, pixels = members
    meta_ref[...] = jnp.zeros_like(meta_ref)
    meta_ref[LIST : LIST + 1, :] = found
    for row, values in ((COUNT, member), (PIXELS, member * pixels)):
        totals = jnp.sum(values, axis=0, keepdims=True)
        meta_ref[row : row + 1, 0:BLOCK] = totals.astype(jnp.int32)
    to_scalars.wait()
    get_frames.wait()
    for q in range(n):
        for i in range(kept + 1, cap_blocks):
            block = list_s[0, q * cap_blocks + i]
            start = (i - kept - 1) * rows
            out_ref[q, start : start + rows] = take(frames_ref, block)
        start = (cap_blocks - kept - 1) * rows
        block = list_s[0, q * cap_blocks + kept]
        out_ref[q, start:] = fold(take(frames_ref, block), True)


def pack_move(cm, frames, cap_blocks):
    rows = frames.shape[0]
    n = cm.shape[0] // cap_blocks
    height = (cap_blocks - cap_blocks // 2 - 1) * rows + count_half_rows(rows)
    meta = jax.ShapeDtypeStruct((8, cm.shape[0]), jnp.int32)
    return call(
        functools.partial(move_kernel, cap_blocks),
        "pack_move",
        [
            jax.ShapeDtypeStruct((n, height, BLOCK), frames.dtype),
            meta,
            jax.ShapeDtypeStruct(frames.shape, frames.dtype),
            jax.ShapeDtypeStruct(cm.shape, cm.dtype),
        ],
        in_specs=[ANYWHERE] * 2,
        out_specs=[WHOLE] * 4,
        scratch_shapes=[
            pltpu.VMEM(meta.shape, meta.dtype),
            pltpu.SMEM(meta.shape, meta.dtype),
            pltpu.SemaphoreType.DMA((3,)),
        ],
    )(
        pltpu.with_memory_space_constraint(cm, pltpu.HBM),
        pltpu.with_memory_space_constraint(frames, pltpu.HBM),
    )


def own_kernel(cap_blocks, meta_s, cm_ref, frames_ref, out_ref, place_ref):
    n = out_ref.shape[0]
    rows = frames_ref.shape[0]
    kept = cap_blocks // 2
    place_ref[...] = find_places(cm_ref[...])
    target = lax.broadcasted_iota(jnp.int32, (BLOCK, BLOCK), 0).astype(jnp.float32)
    for q in range(n):
        count, pixels = meta_s[COUNT, q], meta_s[PIXELS, q]
        is_full = pixels == cap_blocks * BLOCK
        full = gate(is_full)
        fits = (pixels <= BLOCK) & (count <= MERGED)
        compact = 0.0
        for i in range(MERGED):
            block = meta_s[LIST, q * cap_blocks + i]
            place = jnp.where(fits & (i < count), place_ref[pl.ds(block, 1), :], -1.0)
            chosen = (target == place).astype(jnp.float32).astype(jnp.bfloat16)
            compact = compact + dot_nt(take(frames_ref, block), chosen)
        block = meta_s[LIST, q * cap_blocks]
        out_ref[q, 0:rows] = compact.astype(jnp.bfloat16) + take(frames_ref, block) * full
        for i in range(1, kept):
            block = meta_s[LIST, q * cap_blocks + i]
            out_ref[q, i * rows : (i + 1) * rows] = take(frames_ref, block) * full
        block = meta_s[LIST, q * cap_blocks + kept]
        out_ref[q, kept * rows :] = fold(take(frames_ref, block), False) * full


def pack_own(meta, cm, frames, cap_blocks):
    rows = frames.shape[0]
    n = cm.shape[0] // cap_blocks
    height = cap_blocks // 2 * rows + count_half_rows(rows)
    return call(
        functools.partial(own_kernel, cap_blocks),
        "pack_own",
        jax.ShapeDtypeStruct((n, height, BLOCK), frames.dtype),
        in_specs=[pl.BlockSpec(memory_space=pltpu.SMEM)] + [WHOLE] * 2,
        out_specs=WHOLE,
        scratch_shapes=[pltpu.VMEM(cm.shape, jnp.float32)],
        bytes_accessed=4 * 1024 * 1024,
    )(meta, cm, frames)


def share_kernel(cap_blocks, meta_ref, own_ref, theirs_ref, out_ref):
    n, height, _ = out_ref.shape
    rows = height - theirs_ref.shape[1]
    helped = meta_ref[PIXELS : PIXELS + 1, 0:BLOCK] != cap_blocks * BLOCK
    for to, q in enumerate(list_group(n)):
        other = gate(helped[:, q : q + 1])
        out_ref[to, 0:rows] = own_ref[q, 0:rows]
        out_ref[to, rows:] = own_ref[q, rows:] + theirs_ref[q] * other


def share(meta, own, theirs, cap_blocks):
    return call(
        functools.partial(share_kernel, cap_blocks),
        "share",
        jax.ShapeDtypeStruct(own.shape, own.dtype),
        in_specs=[WHOLE] * 3,
        out_specs=WHOLE,
        bytes_accessed=4 * 1024 * 1024,
    )(meta, own, theirs)


def left_out(meta, their_meta, cap):
    mine, theirs = meta[PIXELS] == cap, their_meta[PIXELS] == cap
    fits = (meta[PIXELS] <= BLOCK) & (meta[COUNT] <= MERGED)
    return jnp.logical_not(mine | fits), mine & theirs


def rest_kernel(cap_blocks, meta_s, their_meta_s, frames_hbm, cm_hbm, out_ref, *scratch):
    frames_ref, cm_ref = scratch
    n, _, rows, _ = out_ref.shape
    kept = cap_blocks // 2
    pltpu.sync_copy(frames_hbm, frames_ref)
    pltpu.sync_copy(cm_hbm, cm_ref)
    right = lax.broadcasted_iota(jnp.int32, (1, BLOCK), 1) >= BLOCK // 2
    for to, q in enumerate(list_group(n)):
        counts = [[ref[row, q] for row in range(PIXELS + 1)] for ref in (meta_s, their_meta_s)]
        large, twice = left_out(*counts, cap_blocks * BLOCK)
        for i in range(cap_blocks):
            block = meta_s[LIST, q * cap_blocks + i]
            wanted = jnp.broadcast_to(large, (1, BLOCK))
            if i >= kept:
                wanted |= twice & right if i == kept else twice
            valid = (cm_ref[pl.ds(block, 1), :] >= 0) & (i < meta_s[COUNT, q])
            out_ref[to, i] = take(frames_ref, block) * gate(valid & wanted)


def pack_rest(meta, their_meta, frames, cm, cap_blocks):
    n = cm.shape[0] // cap_blocks
    return call(
        functools.partial(rest_kernel, cap_blocks),
        "pack_rest",
        jax.ShapeDtypeStruct((n, cap_blocks, frames.shape[0], BLOCK), frames.dtype),
        in_specs=[pl.BlockSpec(memory_space=pltpu.SMEM)] * 2 + [ANYWHERE] * 2,
        out_specs=WHOLE,
        scratch_shapes=[
            pltpu.VMEM(frames.shape, frames.dtype),
            pltpu.VMEM(cm.shape, cm.dtype),
        ],
    )(
        meta,
        their_meta,
        pltpu.with_memory_space_constraint(frames, pltpu.HBM),
        pltpu.with_memory_space_constraint(cm, pltpu.HBM),
    )


def lay_out(raw_ref, rows, first, whole, padded):
    n, height, _ = raw_ref.shape
    total = n * rows
    zero = jnp.zeros((PAD, BLOCK), jnp.float32)
    for i in range(padded.shape[0]):
        slot = first + i
        padded[i, 0:PAD] = zero
        padded[i, PAD + total : 2 * PAD + total] = zero
        for place, source in enumerate(list_group(n)):
            start = PAD + source * rows
            if slot < whole:
                block = raw_ref[place, slot * rows : (slot + 1) * rows]
                padded[i, start : start + rows] = block.astype(jnp.float32)
            else:
                early, late = unfold(raw_ref[place, slot * rows : height], rows)
                padded[i, start : start + rows // 2] = early
                padded[i, start + rows // 2 : start + rows] = late


def norm_rows(padded, start, chunk, out_ref):
    total = out_ref.shape[0]
    base = PAD + start
    for slot in range(padded.shape[0]):
        raw = padded[slot, base : base + chunk]
        summed = raw
        for offset in range(1, HALF_WIN + 1):
            summed = summed + padded[slot, base - offset : base - offset + chunk]
            summed = summed + padded[slot, base + offset : base + offset + chunk]
        if start == 0 or start + chunk == total:
            frame = start + lax.broadcasted_iota(jnp.int32, (chunk, BLOCK), 0)
            upper = jnp.minimum(frame + HALF_WIN, total - 1)
            lower = jnp.maximum(frame - HALF_WIN, 0)
            mean = summed / (upper - lower + 1).astype(jnp.float32)
        else:
            mean = summed * (1.0 / (2 * HALF_WIN + 1))
        normed = jnp.where(summed > 0.0, raw / mean, 0.0)
        out_ref[start : start + chunk, slot * BLOCK : (slot + 1) * BLOCK] = normed.astype(
            jnp.bfloat16
        )


def norm_kernel(rows, first, whole, raw_ref, *refs):
    out_ref, padded = refs[-2:]
    lay_out(raw_ref, rows, first, whole, padded)
    for start in range(0, out_ref.shape[0], CHUNK):
        norm_rows(padded, start, CHUNK, out_ref)


def normalise(raw, total, first, slots, whole, after=()):
    return call(
        functools.partial(norm_kernel, total // raw.shape[0], first, whole),
        "normalise",
        jax.ShapeDtypeStruct((total, slots * BLOCK), jnp.bfloat16),
        flops=12 * total * slots * BLOCK,
        bytes_accessed=4 * total * slots * BLOCK,
        in_specs=[WHOLE] + [ANYWHERE] * len(after),
        out_specs=WHOLE,
        scratch_shapes=[pltpu.VMEM((slots, total + 2 * PAD, BLOCK), jnp.float32)],
    )(raw, *after)


def set_left(ref, left_ref):
    rows = left_ref.shape[0] - ONES
    first_row = pl.multiple_of(lax.axis_index("pix") * rows, rows)
    left_ref[0:rows] = ref[pl.ds(first_row, rows), :]
    left_ref[rows : rows + ONES] = jnp.ones((ONES, ref.shape[1]), jnp.bfloat16)


def add_sums(pairs, sums, column):
    gram, frame = sums
    rows = pairs[0][0].shape[0] - ONES
    for left_ref, ref in pairs:
        both = dot_nt(left_ref[...], ref[column, :])
        gram = gram + both[0:rows]
        frame = frame + both[rows : rows + 8]
    return gram, frame


def partial_kernel(count, *refs):
    normed, lefts, (gram_out, frame_out) = refs[:count], refs[-count:], refs[-count - 2 : -count]
    before = refs[count : -count - 2]
    for ref, left_ref in zip(normed, lefts):
        set_left(ref, left_ref)
    for start in range(0, gram_out.shape[1], TILE):
        column = slice(start, start + TILE)
        sums = [ref[:, column] for ref in before] or [0.0, 0.0]
        gram_out[:, column], frame_out[:, column] = add_sums(
            list(zip(lefts, normed)), sums, column
        )


def sums_shape(total, parts):
    return [
        jax.ShapeDtypeStruct((total // parts, total), jnp.float32),
        jax.ShapeDtypeStruct((8, total), jnp.float32),
    ]


def partial_sums(normed, before, parts):
    total, width = normed[0].shape
    rows = total // parts
    return call(
        functools.partial(partial_kernel, len(normed)),
        "partial_sums",
        sums_shape(total, parts),
        flops=2 * rows * total * width * len(normed),
        bytes_accessed=4 * rows * total,
        in_specs=[WHOLE] * (len(normed) + len(before)),
        out_specs=[WHOLE] * 2,
        scratch_shapes=[pltpu.VMEM((rows + ONES, x.shape[1]), x.dtype) for x in normed],
    )(*normed, *before)


def result_kernel(meta_ref, their_meta_ref, normed_ref, gram_in, frame_in, out_hbm, *scratch):
    out_ref, frame_ref, sems = scratch
    rows, total = gram_in.shape
    pixels = meta_ref[PIXELS : PIXELS + 1, 0:BLOCK] + their_meta_ref[PIXELS : PIXELS + 1, 0:BLOCK]
    own = lax.broadcasted_iota(jnp.int32, (1, BLOCK), 1) == lax.axis_index("frame")
    number = jnp.sum(jnp.where(own, pixels, 0).astype(jnp.float32), axis=1, keepdims=True)
    ones = jnp.ones((8, normed_ref.shape[1]), jnp.bfloat16)
    frame_ref[...] = frame_in[...] + dot_nt(ones, normed_ref[...])
    first_row = pl.multiple_of(lax.axis_index("pix") * rows, rows)
    row_sum = jnp.broadcast_to(frame_ref[0:1, pl.ds(first_row, rows)], (BLOCK, rows)).T
    row_inv = 1.0 / row_sum[:, 0:1]
    left = normed_ref[pl.ds(first_row, rows), :]
    copies = []
    for i, start in enumerate(range(0, total, TILE)):
        column = slice(start, start + TILE)
        gram = gram_in[:, column] + dot_nt(left, normed_ref[column, :])
        col_inv = 1.0 / frame_ref[0:1, column]
        result = ((gram * row_inv) * col_inv) * number - 1.0
        out_ref[i] = result.astype(jnp.bfloat16)
        copies.append(
            pltpu.make_async_copy(out_ref.at[i], out_hbm.at[0, :, column], sems.at[i])
        )
        copies[-1].start()
    for copy in copies:
        copy.wait()


def correlate(metas, normed, before):
    rows, total = before[0].shape
    tiles = total // TILE
    return call(
        result_kernel,
        "correlate",
        pltpu.HBM((1, rows, total), jnp.bfloat16),
        flops=2 * rows * total * normed.shape[1],
        bytes_accessed=6 * rows * total,
        in_specs=[WHOLE] * 5,
        out_specs=ANYWHERE,
        scratch_shapes=[
            pltpu.VMEM((tiles, rows, TILE), jnp.bfloat16),
            pltpu.VMEM((8, total), jnp.float32),
            pltpu.SemaphoreType.DMA((tiles,)),
        ],
    )(*metas, normed, *before)


def body(frames, cycle_map):
    rows, p_sec = frames.shape
    n = lax.axis_size("frame")
    parts = lax.axis_size("pix")
    total = n * rows
    cap_blocks = p_sec // n // BLOCK
    slots = cap_blocks // 2 + 1
    early = slots - slots // 2
    cm = cycle_map.reshape(p_sec // BLOCK, BLOCK)

    def swap(x):
        return lax.ppermute(x, "pix", SWAP)

    def send(blocks):
        return lax.all_to_all(
            blocks,
            "frame",
            split_axis=0,
            concat_axis=0,
            axis_index_groups=[list_group(n)],
            tiled=True,
        )

    moving, meta, near_frames, near_cm = pack_move(cm, frames, cap_blocks)
    theirs = swap(moving)
    own = pack_own(meta, near_cm, near_frames, cap_blocks)
    packed = share(meta, own, theirs, cap_blocks)
    received = send(packed)

    meta, _ = lax.optimization_barrier((meta, packed))
    their_meta = swap(meta)
    cap = cap_blocks * BLOCK
    large, twice = left_out(meta[:, :n], their_meta[:, :n], cap)
    overflow = jnp.any(large | twice | left_out(their_meta[:, :n], meta[:, :n], cap)[0])

    flag = overflow.astype(jnp.int32).reshape(1)
    first = normalise(received, total, 0, early, slots - 1, [flag])
    their_first = swap(first)
    last = normalise(received, total, early, slots - early, slots - 1, [first])
    their_last = swap(last)
    sums = partial_sums([first, last], [], parts)
    sums = partial_sums([their_first], sums, parts)

    def spill(frames, cm, meta, their_meta, their_last, *sums):
        rest = send(pack_rest(meta, their_meta, frames, cm, cap_blocks))
        rest = rest.reshape(n, cap_blocks * rows, BLOCK)
        normed = normalise(rest, total, 0, cap_blocks, cap_blocks)
        sums = partial_sums([normed, swap(normed)], sums, parts)
        return correlate([meta, their_meta], their_last, sums)

    def fits(frames, cm, meta, their_meta, their_last, *sums):
        return correlate([meta, their_meta], their_last, sums)

    return lax.cond(overflow, spill, fits, frames, cm, meta, their_meta, their_last, *sums)


def solution(mesh):
    return jax.shard_map(
        body,
        mesh=mesh,
        in_specs=(P("frame", "pix"), P("pix")),
        out_specs=P("frame", "pix", None),
        check_vma=False,
    )
```

```python
import functools

import jax
import jax.numpy as jnp
from jax import lax
from jax.experimental import pallas as pl
from jax.experimental.pallas import tpu as pltpu
from jax.sharding import PartitionSpec as P

BLOCK = 128
HALF_WIN = 2
PAD = 8
TILE = 256
CHUNK = 128
ONES = 16
VMEM_BYTES = 32 * 1024 * 1024
LIST, COUNT, PIXELS = 0, 1, 2
MERGED = 2
SWAP = [(0, 1), (1, 0)]
WHOLE = pl.BlockSpec(memory_space=pltpu.VMEM)
ANYWHERE = pl.BlockSpec(memory_space=pl.ANY)


def call(kernel, name, out_shape, flops=0, bytes_accessed=0, limit=VMEM_BYTES, **kw):
    return pl.pallas_call(
        kernel,
        out_shape=out_shape,
        compiler_params=pltpu.CompilerParams(vmem_limit_bytes=limit),
        cost_estimate=pl.CostEstimate(
            flops=flops, bytes_accessed=bytes_accessed, transcendentals=0
        ),
        name=name,
        **kw,
    )


def dot_nt(a, b):
    return lax.dot_general(a, b, (((1,), (1,)), ((), ())), preferred_element_type=jnp.float32)


def list_group(n):
    half, side = n // 2, n // 4
    first = sorted(range(half), key=lambda i: (i > 1 and i % 2, i))
    return first + sorted(range(half, n), key=lambda i: (i % side >= side // 2, i))


def count_half_rows(rows):
    return max(16, rows // 2)


def gate(wanted):
    wanted = jnp.broadcast_to(wanted, (1, BLOCK))
    return wanted.astype(jnp.float32).astype(jnp.bfloat16)


def take(frames_ref, block):
    return frames_ref[:, pl.ds(pl.multiple_of(block * BLOCK, BLOCK), BLOCK)]


def fold(block, right):
    rows = block.shape[0] // 2
    half = BLOCK // 2
    early, late = block[0:rows].astype(jnp.float32), block[rows:].astype(jnp.float32)
    left = lax.broadcasted_iota(jnp.int32, (rows, BLOCK), 1) < half
    if right:
        folded = jnp.where(left, pltpu.roll(early, half, 1), late)
    else:
        folded = jnp.where(left, early, pltpu.roll(late, half, 1))
    spare = count_half_rows(block.shape[0]) - rows
    if spare:
        folded = jnp.concatenate([folded, jnp.zeros((spare, BLOCK), jnp.float32)])
    return folded.astype(jnp.bfloat16)


def unfold(folded, rows):
    half = BLOCK // 2
    early = folded[0 : rows // 2].astype(jnp.float32)
    left = lax.broadcasted_iota(jnp.int32, early.shape, 1) < half
    return jnp.where(left, early, 0.0), jnp.where(left, pltpu.roll(early, half, 1), 0.0)


def find_members(cm):
    blocks = cm.shape[0]
    first = cm[:, 0:1]
    member = first == lax.broadcasted_iota(jnp.int32, (blocks, BLOCK), 1)
    row = lax.broadcasted_iota(jnp.int32, (blocks, blocks), 0)
    col = lax.broadcasted_iota(jnp.int32, (blocks, blocks), 1)
    earlier = (col < row).astype(jnp.float32).astype(jnp.bfloat16)
    pixels = jnp.sum((cm >= 0).astype(jnp.float32), axis=1, keepdims=True)
    return first, member.astype(jnp.float32), earlier, pixels


def sum_before(earlier, member, values):
    before = jnp.dot(
        earlier, (member * values).astype(jnp.bfloat16), preferred_element_type=jnp.float32
    )
    return jnp.sum(before * member, axis=1, keepdims=True)


def find_blocks(members, cap_blocks, width):
    first, member, earlier, _ = members
    blocks = first.shape[0]
    rank = sum_before(earlier, member, 1.0).astype(jnp.int32)
    slot = jnp.where(first >= 0, first * cap_blocks + rank, -1)
    hit = slot == lax.broadcasted_iota(jnp.int32, (blocks, width), 1)
    index = lax.broadcasted_iota(jnp.int32, (blocks, width), 0).astype(jnp.float32)
    return jnp.sum(jnp.where(hit, index, 0.0), axis=0, keepdims=True).astype(jnp.int32)


def find_places(cm):
    _, member, earlier, pixels = find_members(cm)
    valid = (cm >= 0).astype(jnp.float32)
    row = lax.broadcasted_iota(jnp.int32, (BLOCK, BLOCK), 0)
    col = lax.broadcasted_iota(jnp.int32, (BLOCK, BLOCK), 1)
    before = (row < col).astype(jnp.float32).astype(jnp.bfloat16)
    place = jnp.dot(valid.astype(jnp.bfloat16), before, preferred_element_type=jnp.float32)
    return jnp.where(cm >= 0, place + sum_before(earlier, member, pixels), -1.0)


def move_kernel(cap_blocks, cm_hbm, frames_hbm, out_ref, meta_ref, frames_ref, cm_ref, *scratch):
    list_ref, list_s, sems = scratch
    n = out_ref.shape[0]
    rows = frames_ref.shape[0]
    kept = cap_blocks // 2
    get_cm = pltpu.make_async_copy(cm_hbm, cm_ref, sems.at[0])
    get_cm.start()
    get_frames = pltpu.make_async_copy(frames_hbm, frames_ref, sems.at[1])
    get_frames.start()
    get_cm.wait()
    members = find_members(cm_ref[...])
    found = find_blocks(members, cap_blocks, meta_ref.shape[1])
    list_ref[...] = jnp.broadcast_to(found, list_ref.shape)
    to_scalars = pltpu.make_async_copy(list_ref, list_s, sems.at[2])
    to_scalars.start()
    _, member, _, pixels = members
    meta_ref[...] = jnp.zeros_like(meta_ref)
    meta_ref[LIST : LIST + 1, :] = found
    for row, values in ((COUNT, member), (PIXELS, member * pixels)):
        totals = jnp.sum(values, axis=0, keepdims=True)
        meta_ref[row : row + 1, 0:BLOCK] = totals.astype(jnp.int32)
    to_scalars.wait()
    get_frames.wait()
    for q in range(n):
        for i in range(kept + 1, cap_blocks):
            block = list_s[0, q * cap_blocks + i]
            start = (i - kept - 1) * rows
            out_ref[q, start : start + rows] = take(frames_ref, block)
        start = (cap_blocks - kept - 1) * rows
        block = list_s[0, q * cap_blocks + kept]
        out_ref[q, start:] = fold(take(frames_ref, block), True)


def pack_move(cm, frames, cap_blocks):
    rows = frames.shape[0]
    n = cm.shape[0] // cap_blocks
    height = (cap_blocks - cap_blocks // 2 - 1) * rows + count_half_rows(rows)
    meta = jax.ShapeDtypeStruct((8, cm.shape[0]), jnp.int32)
    return call(
        functools.partial(move_kernel, cap_blocks),
        "pack_move",
        [
            jax.ShapeDtypeStruct((n, height, BLOCK), frames.dtype),
            meta,
            jax.ShapeDtypeStruct(frames.shape, frames.dtype),
            jax.ShapeDtypeStruct(cm.shape, cm.dtype),
        ],
        in_specs=[ANYWHERE] * 2,
        out_specs=[WHOLE] * 4,
        scratch_shapes=[
            pltpu.VMEM(meta.shape, meta.dtype),
            pltpu.SMEM(meta.shape, meta.dtype),
            pltpu.SemaphoreType.DMA((3,)),
        ],
    )(
        pltpu.with_memory_space_constraint(cm, pltpu.HBM),
        pltpu.with_memory_space_constraint(frames, pltpu.HBM),
    )


def own_kernel(cap_blocks, meta_s, cm_ref, frames_ref, out_ref, place_ref):
    n = out_ref.shape[0]
    rows = frames_ref.shape[0]
    kept = cap_blocks // 2
    place_ref[...] = find_places(cm_ref[...])
    target = lax.broadcasted_iota(jnp.int32, (BLOCK, BLOCK), 0).astype(jnp.float32)
    for q in range(n):
        count, pixels = meta_s[COUNT, q], meta_s[PIXELS, q]
        is_full = pixels == cap_blocks * BLOCK
        full = gate(is_full)
        fits = (pixels <= BLOCK) & (count <= MERGED)
        compact = 0.0
        for i in range(MERGED):
            block = meta_s[LIST, q * cap_blocks + i]
            place = jnp.where(fits & (i < count), place_ref[pl.ds(block, 1), :], -1.0)
            chosen = (target == place).astype(jnp.float32).astype(jnp.bfloat16)
            compact = compact + dot_nt(take(frames_ref, block), chosen)
        block = meta_s[LIST, q * cap_blocks]
        out_ref[q, 0:rows] = compact.astype(jnp.bfloat16) + take(frames_ref, block) * full
        for i in range(1, kept):
            block = meta_s[LIST, q * cap_blocks + i]
            out_ref[q, i * rows : (i + 1) * rows] = take(frames_ref, block) * full
        block = meta_s[LIST, q * cap_blocks + kept]
        out_ref[q, kept * rows :] = fold(take(frames_ref, block), False) * full


def pack_own(meta, cm, frames, cap_blocks):
    rows = frames.shape[0]
    n = cm.shape[0] // cap_blocks
    height = cap_blocks // 2 * rows + count_half_rows(rows)
    return call(
        functools.partial(own_kernel, cap_blocks),
        "pack_own",
        jax.ShapeDtypeStruct((n, height, BLOCK), frames.dtype),
        in_specs=[pl.BlockSpec(memory_space=pltpu.SMEM)] + [WHOLE] * 2,
        out_specs=WHOLE,
        scratch_shapes=[pltpu.VMEM(cm.shape, jnp.float32)],
        bytes_accessed=4 * 1024 * 1024,
    )(meta, cm, frames)


def share_kernel(cap_blocks, meta_ref, own_ref, theirs_ref, out_ref):
    n, height, _ = out_ref.shape
    rows = height - theirs_ref.shape[1]
    helped = meta_ref[PIXELS : PIXELS + 1, 0:BLOCK] != cap_blocks * BLOCK
    for to, q in enumerate(list_group(n)):
        other = gate(helped[:, q : q + 1])
        out_ref[to, 0:rows] = own_ref[q, 0:rows]
        out_ref[to, rows:] = own_ref[q, rows:] + theirs_ref[q] * other


def share(meta, own, theirs, cap_blocks):
    return call(
        functools.partial(share_kernel, cap_blocks),
        "share",
        jax.ShapeDtypeStruct(own.shape, own.dtype),
        in_specs=[WHOLE] * 3,
        out_specs=WHOLE,
        bytes_accessed=4 * 1024 * 1024,
    )(meta, own, theirs)


def left_out(meta, their_meta, cap):
    mine, theirs = meta[PIXELS] == cap, their_meta[PIXELS] == cap
    fits = (meta[PIXELS] <= BLOCK) & (meta[COUNT] <= MERGED)
    return jnp.logical_not(mine | fits), mine & theirs


def rest_kernel(cap_blocks, meta_s, their_meta_s, frames_hbm, cm_hbm, out_ref, *scratch):
    frames_ref, cm_ref = scratch
    n, _, rows, _ = out_ref.shape
    kept = cap_blocks // 2
    pltpu.sync_copy(frames_hbm, frames_ref)
    pltpu.sync_copy(cm_hbm, cm_ref)
    right = lax.broadcasted_iota(jnp.int32, (1, BLOCK), 1) >= BLOCK // 2
    for to, q in enumerate(list_group(n)):
        counts = [[ref[row, q] for row in range(PIXELS + 1)] for ref in (meta_s, their_meta_s)]
        large, twice = left_out(*counts, cap_blocks * BLOCK)
        for i in range(cap_blocks):
            block = meta_s[LIST, q * cap_blocks + i]
            wanted = jnp.broadcast_to(large, (1, BLOCK))
            if i >= kept:
                wanted |= twice & right if i == kept else twice
            valid = (cm_ref[pl.ds(block, 1), :] >= 0) & (i < meta_s[COUNT, q])
            out_ref[to, i] = take(frames_ref, block) * gate(valid & wanted)


def pack_rest(meta, their_meta, frames, cm, cap_blocks):
    n = cm.shape[0] // cap_blocks
    return call(
        functools.partial(rest_kernel, cap_blocks),
        "pack_rest",
        jax.ShapeDtypeStruct((n, cap_blocks, frames.shape[0], BLOCK), frames.dtype),
        in_specs=[pl.BlockSpec(memory_space=pltpu.SMEM)] * 2 + [ANYWHERE] * 2,
        out_specs=WHOLE,
        scratch_shapes=[
            pltpu.VMEM(frames.shape, frames.dtype),
            pltpu.VMEM(cm.shape, cm.dtype),
        ],
    )(
        meta,
        their_meta,
        pltpu.with_memory_space_constraint(frames, pltpu.HBM),
        pltpu.with_memory_space_constraint(cm, pltpu.HBM),
    )


def lay_out(raw_ref, rows, first, whole, padded):
    n, height, _ = raw_ref.shape
    total = n * rows
    zero = jnp.zeros((PAD, BLOCK), jnp.float32)
    for i in range(padded.shape[0]):
        slot = first + i
        padded[i, 0:PAD] = zero
        padded[i, PAD + total : 2 * PAD + total] = zero
        for place, source in enumerate(list_group(n)):
            start = PAD + source * rows
            if slot < whole:
                block = raw_ref[place, slot * rows : (slot + 1) * rows]
                padded[i, start : start + rows] = block.astype(jnp.float32)
            else:
                early, late = unfold(raw_ref[place, slot * rows : height], rows)
                padded[i, start : start + rows // 2] = early
                padded[i, start + rows // 2 : start + rows] = late


def norm_rows(padded, start, chunk, out_ref):
    total = out_ref.shape[0]
    base = PAD + start
    for slot in range(padded.shape[0]):
        raw = padded[slot, base : base + chunk]
        summed = raw
        for offset in range(1, HALF_WIN + 1):
            summed = summed + padded[slot, base - offset : base - offset + chunk]
            summed = summed + padded[slot, base + offset : base + offset + chunk]
        if start == 0 or start + chunk == total:
            frame = start + lax.broadcasted_iota(jnp.int32, (chunk, BLOCK), 0)
            upper = jnp.minimum(frame + HALF_WIN, total - 1)
            lower = jnp.maximum(frame - HALF_WIN, 0)
            mean = summed / (upper - lower + 1).astype(jnp.float32)
        else:
            mean = summed * (1.0 / (2 * HALF_WIN + 1))
        normed = jnp.where(summed > 0.0, raw / mean, 0.0)
        out_ref[start : start + chunk, slot * BLOCK : (slot + 1) * BLOCK] = normed.astype(
            jnp.bfloat16
        )


def norm_kernel(rows, first, whole, raw_ref, *refs):
    out_ref, padded = refs[-2:]
    lay_out(raw_ref, rows, first, whole, padded)
    for start in range(0, out_ref.shape[0], CHUNK):
        norm_rows(padded, start, CHUNK, out_ref)


def normalise(raw, total, first, slots, whole, after=()):
    return call(
        functools.partial(norm_kernel, total // raw.shape[0], first, whole),
        "normalise",
        jax.ShapeDtypeStruct((total, slots * BLOCK), jnp.bfloat16),
        flops=12 * total * slots * BLOCK,
        bytes_accessed=4 * total * slots * BLOCK,
        in_specs=[WHOLE] + [ANYWHERE] * len(after),
        out_specs=WHOLE,
        scratch_shapes=[pltpu.VMEM((slots, total + 2 * PAD, BLOCK), jnp.float32)],
    )(raw, *after)


def set_left(ref, left_ref):
    rows = left_ref.shape[0] - ONES
    first_row = pl.multiple_of(lax.axis_index("pix") * rows, rows)
    left_ref[0:rows] = ref[pl.ds(first_row, rows), :]
    left_ref[rows : rows + ONES] = jnp.ones((ONES, ref.shape[1]), jnp.bfloat16)


def add_sums(pairs, sums, column):
    gram, frame = sums
    rows = pairs[0][0].shape[0] - ONES
    for left_ref, ref in pairs:
        both = dot_nt(left_ref[...], ref[column, :])
        gram = gram + both[0:rows]
        frame = frame + both[rows : rows + 8]
    return gram, frame


def partial_kernel(count, *refs):
    normed, lefts, (gram_out, frame_out) = refs[:count], refs[-count:], refs[-count - 2 : -count]
    before = refs[count : -count - 2]
    for ref, left_ref in zip(normed, lefts):
        set_left(ref, left_ref)
    for start in range(0, gram_out.shape[1], TILE):
        column = slice(start, start + TILE)
        sums = [ref[:, column] for ref in before] or [0.0, 0.0]
        gram_out[:, column], frame_out[:, column] = add_sums(
            list(zip(lefts, normed)), sums, column
        )


def sums_shape(total, parts):
    return [
        jax.ShapeDtypeStruct((total // parts, total), jnp.float32),
        jax.ShapeDtypeStruct((8, total), jnp.float32),
    ]


def partial_sums(normed, before, parts):
    total, width = normed[0].shape
    rows = total // parts
    return call(
        functools.partial(partial_kernel, len(normed)),
        "partial_sums",
        sums_shape(total, parts),
        flops=2 * rows * total * width * len(normed),
        bytes_accessed=4 * rows * total,
        in_specs=[WHOLE] * (len(normed) + len(before)),
        out_specs=[WHOLE] * 2,
        scratch_shapes=[pltpu.VMEM((rows + ONES, x.shape[1]), x.dtype) for x in normed],
    )(*normed, *before)


def result_kernel(meta_ref, their_meta_ref, normed_ref, gram_in, frame_in, out_hbm, *scratch):
    out_ref, frame_ref, sems = scratch
    rows, total = gram_in.shape
    pixels = meta_ref[PIXELS : PIXELS + 1, 0:BLOCK] + their_meta_ref[PIXELS : PIXELS + 1, 0:BLOCK]
    own = lax.broadcasted_iota(jnp.int32, (1, BLOCK), 1) == lax.axis_index("frame")
    number = jnp.sum(jnp.where(own, pixels, 0).astype(jnp.float32), axis=1, keepdims=True)
    ones = jnp.ones((8, normed_ref.shape[1]), jnp.bfloat16)
    frame_ref[...] = frame_in[...] + dot_nt(ones, normed_ref[...])
    first_row = pl.multiple_of(lax.axis_index("pix") * rows, rows)
    row_sum = jnp.broadcast_to(frame_ref[0:1, pl.ds(first_row, rows)], (BLOCK, rows)).T
    row_inv = 1.0 / row_sum[:, 0:1]
    left = normed_ref[pl.ds(first_row, rows), :]
    copies = []
    for i, start in enumerate(range(0, total, TILE)):
        column = slice(start, start + TILE)
        gram = gram_in[:, column] + dot_nt(left, normed_ref[column, :])
        col_inv = 1.0 / frame_ref[0:1, column]
        result = ((gram * row_inv) * col_inv) * number - 1.0
        out_ref[i] = result.astype(jnp.bfloat16)
        copies.append(
            pltpu.make_async_copy(out_ref.at[i], out_hbm.at[0, :, column], sems.at[i])
        )
        copies[-1].start()
    for copy in copies:
        copy.wait()


def correlate(metas, normed, before):
    rows, total = before[0].shape
    tiles = total // TILE
    return call(
        result_kernel,
        "correlate",
        pltpu.HBM((1, rows, total), jnp.bfloat16),
        flops=2 * rows * total * normed.shape[1],
        bytes_accessed=6 * rows * total,
        in_specs=[WHOLE] * 5,
        out_specs=ANYWHERE,
        scratch_shapes=[
            pltpu.VMEM((tiles, rows, TILE), jnp.bfloat16),
            pltpu.VMEM((8, total), jnp.float32),
            pltpu.SemaphoreType.DMA((tiles,)),
        ],
    )(*metas, normed, *before)


def body(frames, cycle_map):
    rows, p_sec = frames.shape
    n = lax.axis_size("frame")
    parts = lax.axis_size("pix")
    total = n * rows
    cap_blocks = p_sec // n // BLOCK
    slots = cap_blocks // 2 + 1
    early = slots - slots // 2
    cm = cycle_map.reshape(p_sec // BLOCK, BLOCK)

    def swap(x):
        return lax.ppermute(x, "pix", SWAP)

    def send(blocks):
        return lax.all_to_all(
            blocks,
            "frame",
            split_axis=0,
            concat_axis=0,
            axis_index_groups=[list_group(n)],
            tiled=True,
        )

    moving, meta, near_frames, near_cm = pack_move(cm, frames, cap_blocks)
    theirs = swap(moving)
    own = pack_own(meta, near_cm, near_frames, cap_blocks)
    packed = share(meta, own, theirs, cap_blocks)
    received = send(packed)

    meta, _ = lax.optimization_barrier((meta, packed))
    their_meta = swap(meta)
    cap = cap_blocks * BLOCK
    large, twice = left_out(meta[:, :n], their_meta[:, :n], cap)
    overflow = jnp.any(large | twice | left_out(their_meta[:, :n], meta[:, :n], cap)[0])

    flag = overflow.astype(jnp.int32).reshape(1)
    first = normalise(received, total, 0, early, slots - 1, [flag])
    their_first = swap(first)
    last = normalise(received, total, early, slots - early, slots - 1, [first])
    their_last = swap(last)
    sums = partial_sums([first, last], [], parts)
    sums = partial_sums([their_first], sums, parts)

    def spill(frames, cm, meta, their_meta, their_last, *sums):
        rest = send(pack_rest(meta, their_meta, frames, cm, cap_blocks))
        rest = rest.reshape(n, cap_blocks * rows, BLOCK)
        normed = normalise(rest, total, 0, cap_blocks, cap_blocks)
        sums = partial_sums([normed, swap(normed)], sums, parts)
        return correlate([meta, their_meta], their_last, sums)

    def fits(frames, cm, meta, their_meta, their_last, *sums):
        return correlate([meta, their_meta], their_last, sums)

    return lax.cond(overflow, spill, fits, frames, cm, meta, their_meta, their_last, *sums)


def solution(mesh):
    return jax.shard_map(
        body,
        mesh=mesh,
        in_specs=(P("frame", "pix"), P("pix")),
        out_specs=P("frame", "pix", None),
        check_vma=False,
    )
```
